32 devices in a mesh: dp: 8 (over z, x), shard: 4 (over y, core).
Axes of the slice: x: 2, y: 2, z: 4, core: 2. Of those that a mesh axis runs over, the one named last changes fastest.
Arguments:
- tokens: bfloat16 [16384, 256], P(('dp', 'shard')), may hold values from -6 to 6
- cotangent: bfloat16 [16384, 256], P(('dp', 'shard')), may hold values from -6 to 6
- lengths: int32 [128], replicated, may hold values from 0 to 512, as said below
- seq_owner: int32 [128], replicated, may hold values from 0 to 31, as said below
- qkv_weight: float32 [256, 768], P('shard'), may hold values from -0.375 to 0.375
- out_weight: float32 [256, 256], P('shard'), may hold values from -2 to 2
- up_weight: float32 [256, 1024], P('shard'), may hold values from -0.375 to 0.375
- down_weight: float32 [1024, 256], P('shard'), may hold values from -0.1875 to 0.1875
- gains_biases: float32 [3072], P('shard'), may hold values from -0.35 to 1.7
- qkv_first: float32 [256, 768], P('shard'), may hold values from -16 to 16
- qkv_second: float32 [256, 768], P('shard'), may hold values from 19.16928 to 309.6576
- out_first: float32 [256, 256], P('shard'), may hold values from -6 to 6
- out_second: float32 [256, 256], P('shard'), may hold values from 1.664 to 26.88
- up_first: float32 [256, 1024], P('shard'), may hold values from -32 to 32
- up_second: float32 [256, 1024], P('shard'), may hold values from 53.248 to 860.16
- down_first: float32 [1024, 256], P('shard'), may hold values from -32 to 32
- down_second: float32 [1024, 256], P('shard'), may hold values from 53.248 to 860.16
- small_first: float32 [3072], P('shard'), may hold values from -64 to 64
- small_second: float32 [3072], P('shard'), may hold values from 212.992 to 3440.64
Outputs:
- output: bfloat16 [16384, 256], P(('dp', 'shard'))
- input_grad: float32 [16384, 256], P(('dp', 'shard'))
- qkv_first_next: float32 [256, 768], P('shard')
- qkv_second_next: float32 [256, 768], P('shard')
- qkv_weight_next: float32 [256, 768], P('shard')
- out_first_next: float32 [256, 256], P('shard')
- out_second_next: float32 [256, 256], P('shard')
- out_weight_next: float32 [256, 256], P('shard')
- up_first_next: float32 [256, 1024], P('shard')
- up_second_next: float32 [256, 1024], P('shard')
- up_weight_next: float32 [256, 1024], P('shard')
- down_first_next: float32 [1024, 256], P('shard')
- down_second_next: float32 [1024, 256], P('shard')
- down_weight_next: float32 [1024, 256], P('shard')
- small_first_next: float32 [3072], P('shard')
- small_second_next: float32 [3072], P('shard')
- gains_biases_next: float32 [3072], P('shard')
The draws below stay inside these ranges and needn't reach their ends.
Inputs may be any that keep to these rules, and one draw needn't show every extreme that they name: The sequences that one device owns have lengths adding up to 512 or less. In every draw one device owns a single sequence of 512 tokens and its other sequences have length 0. A length of 0 is an empty sequence. `seq_owner`: each device owns exactly 4 sequences.
All inputs are finite; a program needn't handle non-finite values.
Results may differ from the reference program's by a relative error of at most 0.012.
The reference program's roundings to bfloat16 on the way count: a program that leaves them out, or rounds other values in their place, can miss the bound.
Values may be sent and summed in bfloat16 or wider, within the bound.
No kernel may reach another device: no remote copies, remote signals or barrier semaphores. Data moves between devices by JAX's collectives and lax.ppermute only.
A program may use at most 64 MiB of HBM per device.

```python
import math
import jax
import jax.numpy as jnp
from jax import lax

D = 256
HEADS = 8
HEAD = 32
FF = 1024
CAP = 512
SEQ_DEV = 4
STEP = 10
TOKENS = 16384
SEQS = 128
SMALL = 3072


def deal_sequences(key):
    device_count = SEQS // SEQ_DEV
    subkeys = jax.random.split(key, 4)
    shuffle = jax.random.permutation(subkeys[0], SEQS)
    device_load = CAP * jax.random.randint(subkeys[1], (device_count,), 2, 17) // 16
    busiest = jax.random.randint(subkeys[2], (), 0, device_count)
    row_index = jnp.arange(device_count)
    device_load = jnp.where(row_index == busiest, CAP, device_load)
    cut_points = jnp.sort(jax.random.randint(subkeys[3], (device_count, SEQ_DEV - 1), 0, device_load[:, None] + 1), axis=1)
    borders = jnp.concatenate([jnp.zeros((device_count, 1), jnp.int32), cut_points.astype(jnp.int32), device_load[:, None].astype(jnp.int32)], axis=1)
    pieces = borders[:, 1:] - borders[:, :-1]
    column = jnp.arange(SEQ_DEV)
    lone_piece = jnp.where(column[None, :] == 0, CAP, 0)
    pieces = jnp.where((row_index == busiest)[:, None], lone_piece, pieces)
    seq_sizes = jnp.zeros((SEQS,), jnp.int32).at[shuffle].set(pieces.reshape(-1).astype(jnp.int32))
    holder = jnp.zeros((SEQS,), jnp.int32).at[shuffle].set((jnp.arange(SEQS) // SEQ_DEV).astype(jnp.int32))
    return (seq_sizes, holder)


def draw_lengths(key, part):
    return deal_sequences(key)[0]


def draw_seq_owner(key, part):
    return deal_sequences(key)[1]


def draw_gains_biases(key, part):
    key = jax.random.fold_in(key, 3)
    first_key, second_key = jax.random.split(key)
    position = jnp.arange(SMALL)
    is_gain = (position < D) | (position >= 2 * D) & (position < 3 * D)
    gain_vals = jax.random.uniform(first_key, (SMALL,), jnp.float32, 0.5, 1.5)
    bias_vals = jax.random.uniform(second_key, (SMALL,), jnp.float32, -0.35, 0.35)
    return jnp.where(is_gain, gain_vals, bias_vals).astype(jnp.float32)


def block_levels(key, dims, cuts, smallest, top_value):
    def one(dim, blocks):
        heights = jax.random.uniform(jax.random.fold_in(jax.random.fold_in(key, 6), dim), (blocks,), jnp.float32, smallest / len(cuts), top_value / len(cuts))
        return jnp.repeat(jnp.exp(heights), dims[dim] // blocks).reshape((-1,) + (1,) * (len(dims) - dim - 1))

    loudness = one(*cuts[0])
    for cut in cuts[1:]:
        loudness = loudness * one(*cut)
    return loudness


def centred(stream_key, shape, scale, reach, shards=(), kind=jnp.bfloat16):
    drawn = jax.random.normal(stream_key, shape, jnp.float32) * scale
    if len(shards) > 0:
        drawn = block_levels(stream_key, shape, shards, -0.22, 0.18) * drawn
    return jnp.clip(drawn, min=-reach, max=reach).astype(kind)


def setup_inputs(seed: int = 0) -> dict:
    seeds = jax.random.split(jax.random.key(seed), 20)
    return {
        "tokens": centred(seeds[0], (TOKENS, D), 1.0, 6.0, ((0, 32),)),
        "cotangent": centred(seeds[1], (TOKENS, D), 1.0, 6.0, ((0, 32),)),
        "lengths": draw_lengths(jax.random.fold_in(seeds[19], 71), 0),
        "seq_owner": draw_seq_owner(jax.random.fold_in(seeds[19], 71), 0),
        "qkv_weight": centred(seeds[4], (D, 3 * D), D ** -0.5, 0.375, ((0, 4),), jnp.float32),
        "out_weight": centred(seeds[5], (D, D), (max(16 * D // CAP, 1)) ** -0.5, 2.0, ((0, 4),), jnp.float32),
        "up_weight": centred(seeds[6], (D, FF), D ** -0.5, 0.375, ((0, 4),), jnp.float32),
        "down_weight": centred(seeds[7], (FF, D), FF ** -0.5, 0.1875, ((0, 4),), jnp.float32),
        "gains_biases": draw_gains_biases(jax.random.fold_in(seeds[19], 71), 0),
        "qkv_first": centred(seeds[9], (D, 3 * D), (0.023 * TOKENS ** 0.5), 16.0, ((0, 4),), jnp.float32),
        "qkv_second": jnp.clip(jnp.exp(math.log(309.6576) - 2.7821582 * jax.random.uniform(seeds[10], (D, 3 * D), jnp.float32) ** block_levels(seeds[10], (D, 3 * D), ((0, 4),), -0.2, 0.2)), 19.16928, 309.6576),
        "out_first": centred(seeds[11], (D, D), (0.156 * (TOKENS // CAP) ** 0.5), 6.0, ((0, 4),), jnp.float32),
        "out_second": jnp.clip(jnp.exp(math.log(26.88) - 2.7821581 * jax.random.uniform(seeds[12], (D, D), jnp.float32) ** block_levels(seeds[12], (D, D), ((0, 4),), -0.2, 0.2)), 1.664, 26.88),
        "up_first": centred(seeds[13], (D, FF), (0.039 * TOKENS ** 0.5), 32.0, ((0, 4),), jnp.float32),
        "up_second": jnp.clip(jnp.exp(math.log(860.16) - 2.7821581 * jax.random.uniform(seeds[14], (D, FF), jnp.float32) ** block_levels(seeds[14], (D, FF), ((0, 4),), -0.2, 0.2)), 53.248, 860.16),
        "down_first": centred(seeds[15], (FF, D), (0.039 * TOKENS ** 0.5), 32.0, ((0, 4),), jnp.float32),
        "down_second": jnp.clip(jnp.exp(math.log(860.16) - 2.7821581 * jax.random.uniform(seeds[16], (FF, D), jnp.float32) ** block_levels(seeds[16], (FF, D), ((0, 4),), -0.2, 0.2)), 53.248, 860.16),
        "small_first": centred(seeds[17], (SMALL,), (0.078 * TOKENS ** 0.5), 64.0, ((0, 4),), jnp.float32),
        "small_second": jnp.clip(jnp.exp(math.log(3440.64) - 2.7821581 * jax.random.uniform(seeds[18], (SMALL,), jnp.float32) ** block_levels(seeds[18], (SMALL,), ((0, 4),), -0.2, 0.2)), 212.992, 3440.64),
    }


@jax.custom_vjp
def low(v):
    return lax.optimization_barrier(v.astype(jnp.bfloat16)).astype(jnp.float32)

@jax.custom_vjp
def low_back(v):
    return v

def low_keep(v):
    return (low(v), None)

def low_pass(kept, grad):
    return (grad,)

def back_keep(v):
    return (v, None)

def back_low(kept, grad):
    return (low(grad),)
low.defvjp(low_keep, low_pass)
low_back.defvjp(back_keep, back_low)
exact_mode = lax.Precision.HIGHEST
norm_eps = 1e-05
beta_one = 0.9
beta_two = 0.95
learn_rate = 0.1
adam_eps = 1e-08
matrix_decay = 0.1
masked_score = -1e+30

def layer_norm(values, gain, shift):
    centered = values - lax.optimization_barrier(jnp.mean(values, axis=-1, keepdims=True))
    spread = lax.optimization_barrier(jnp.mean(centered * centered, axis=-1, keepdims=True))
    return centered * lax.rsqrt(spread + norm_eps) * gain + shift

def segments_for(lengths, seq_owner, device):
    own_lengths = jnp.where(seq_owner == device, lengths, 0)
    seq_ends = jnp.cumsum(own_lengths).astype(jnp.int32)
    position = jnp.arange(CAP, dtype=jnp.int32)
    segment = lax.optimization_barrier(jnp.sum((seq_ends[None, :] <= position[:, None]).astype(jnp.int32), axis=1)).astype(jnp.int32)
    live_rows = (position < seq_ends[-1]).astype(jnp.float32)
    return (segment, live_rows)

def block_forward(weights, tokens_block, segment):
    qkv_w, out_w, up_w, down_w, small = weights
    gain_one = small[0:D]
    bias_one = small[D:2 * D]
    gain_two = small[2 * D:3 * D]
    bias_two = small[3 * D:4 * D]
    bias_query = small[4 * D:5 * D]
    bias_value = small[5 * D:6 * D]
    bias_out = small[6 * D:7 * D]
    bias_down = small[7 * D:8 * D]
    bias_up = small[8 * D:]
    hidden_one = low(layer_norm(tokens_block, gain_one, bias_one))
    joined_bias = jnp.concatenate([bias_query, jnp.zeros((D,), jnp.float32), bias_value])
    joined = jnp.dot(hidden_one, qkv_w, precision=exact_mode) + joined_bias
    joined = low_back(low(joined))
    queries = joined[:, :D].reshape(CAP, HEADS, HEAD)
    key_rows = joined[:, D:2 * D].reshape(CAP, HEADS, HEAD)
    value_rows = joined[:, 2 * D:].reshape(CAP, HEADS, HEAD)
    scores = jnp.einsum('qhd,khd->hqk', queries, key_rows, precision=exact_mode) * (1.0 / math.sqrt(HEAD))
    scores = low_back(scores)
    position = jnp.arange(CAP, dtype=jnp.int32)
    allowed = (segment[:, None] == segment[None, :]) & (position[None, :] <= position[:, None])
    scores = jnp.where(allowed[None], scores, masked_score)
    row_max = lax.optimization_barrier(jnp.max(scores, axis=-1, keepdims=True))
    exponent = jnp.exp(scores - row_max)
    probs = low(exponent / lax.optimization_barrier(jnp.sum(exponent, axis=-1, keepdims=True)))
    attended = jnp.einsum('hqk,khd->qhd', probs, value_rows, precision=exact_mode).reshape(CAP, D)
    attended = low_back(low(attended))
    branch_one = low_back(jnp.dot(attended, out_w, precision=exact_mode) + bias_out)
    middle = tokens_block + branch_one
    hidden_two = low(layer_norm(middle, gain_two, bias_two))
    pre_act = low_back(jnp.dot(hidden_two, up_w, precision=exact_mode) + bias_up)
    activated = low(jax.nn.gelu(pre_act, approximate=True))
    branch_two = low_back(jnp.dot(activated, down_w, precision=exact_mode) + bias_down)
    return middle + branch_two

def forward(params, tokens_all, segments):
    weights = tuple((low(param_item) for param_item in params))

    def one_device(carry, inputs):
        tokens_block, segment = inputs
        return (carry, block_forward(weights, tokens_block, segment))
    final_carry, outputs = lax.scan(jax.checkpoint(one_device), jnp.zeros((), jnp.float32), (tokens_all, segments))
    return outputs

def adam_step(weight, grad, first, second, decay_rate):
    first_next = beta_one * first + (1.0 - beta_one) * grad
    second_next = beta_two * second + (1.0 - beta_two) * grad * grad
    first_fix = 1.0 - beta_one ** STEP
    second_fix = 1.0 - beta_two ** STEP
    update = first_next / first_fix / (jnp.sqrt(second_next / second_fix) + adam_eps)
    return (first_next, second_next, weight - learn_rate * (update + decay_rate * weight))

def reference(tokens, cotangent, lengths, seq_owner, qkv_weight, out_weight, up_weight, down_weight, gains_biases, qkv_first, qkv_second, out_first, out_second, up_first, up_second, down_first, down_second, small_first, small_second):
    device_count = tokens.shape[0] // CAP
    devices = jnp.arange(device_count, dtype=jnp.int32)
    segments, live_rows = jax.vmap(lambda device: segments_for(lengths, seq_owner, device))(devices)
    tokens_all = tokens.astype(jnp.float32).reshape(device_count, CAP, D)
    params = (qkv_weight, out_weight, up_weight, down_weight, gains_biases)
    outputs, pull_back = jax.vjp(lambda param_set, inputs_all: forward(param_set, inputs_all, segments), params, tokens_all)
    seed_grad = cotangent.astype(jnp.float32).reshape(device_count, CAP, D) * live_rows[:, :, None]
    param_grads, input_grad = pull_back(seed_grad)
    qkv_new = adam_step(qkv_weight, param_grads[0], qkv_first, qkv_second, matrix_decay)
    out_new = adam_step(out_weight, param_grads[1], out_first, out_second, matrix_decay)
    up_new = adam_step(up_weight, param_grads[2], up_first, up_second, matrix_decay)
    down_new = adam_step(down_weight, param_grads[3], down_first, down_second, matrix_decay)
    small_new = adam_step(gains_biases, param_grads[4], small_first, small_second, 0.0)
    return (outputs.reshape(device_count * CAP, D).astype(jnp.bfloat16), input_grad.reshape(device_count * CAP, D), qkv_new[0], qkv_new[1], qkv_new[2], out_new[0], out_new[1], out_new[2], up_new[0], up_new[1], up_new[2], down_new[0], down_new[1], down_new[2], small_new[0], small_new[1], small_new[2])
```

```python
import math

import jax
import jax.numpy as jnp
from jax import lax
from jax.sharding import PartitionSpec as P

HEAD = 32
PAD = 64
STEP = 10


norm_eps = 1e-05
beta_one = 0.9
beta_two = 0.95
learn_rate = 0.1
adam_eps = 1e-08
matrix_decay = 0.1
masked_score = -1e30


def standardize(values):
    centered = values - jnp.mean(values, axis=-1, keepdims=True)
    root_inv = lax.rsqrt(jnp.mean(centered * centered, axis=-1, keepdims=True) + norm_eps)
    return (centered * root_inv, root_inv)


def norm_back(upstream, normed, root_inv, gain):
    scaled = upstream * gain
    inner_mean = jnp.mean(scaled, axis=-1, keepdims=True)
    cross_mean = jnp.mean(scaled * normed, axis=-1, keepdims=True)
    through = root_inv * (scaled - inner_mean - normed * cross_mean)
    return (through, jnp.sum(upstream * normed, axis=0), jnp.sum(upstream, axis=0))


def contract_rows(left, right):
    return lax.dot_general(
        left, right, (((0,), (0,)), ((), ())), preferred_element_type=jnp.float32
    )


def contract_cols(left, right):
    return lax.dot_general(
        left, right, (((1,), (1,)), ((), ())), preferred_element_type=jnp.float32
    )


def unpack_small(small, width):
    pieces = [small[part_index * width : (part_index + 1) * width] for part_index in range(8)]
    return pieces + [small[8 * width :]]


def gelu_tanh(values):
    return jax.nn.gelu(values, approximate=True)


def adam_step(weight, grad, first, second, decay_rate):
    first_next = beta_one * first + (1.0 - beta_one) * grad
    second_next = beta_two * second + (1.0 - beta_two) * grad * grad
    first_fix = 1.0 - beta_one**STEP
    second_fix = 1.0 - beta_two**STEP
    update = first_next / first_fix / (jnp.sqrt(second_next / second_fix) + adam_eps)
    return (first_next, second_next, weight - learn_rate * (update + decay_rate * weight))


def split_cols(values, width):
    return jnp.concatenate(
        [values[..., at : at + width] for at in range(0, values.shape[-1], width)], axis=-2
    )


def join_cols(values, count):
    shard_count, rows, width = values.shape
    values = values.reshape(shard_count, count, rows // count, width)
    return values.transpose(0, 2, 1, 3).reshape(shard_count * rows // count, count * width)


def exchange(values, axis, mask):
    count = lax.axis_size(axis)
    return lax.ppermute(values, axis, [(index, index ^ mask) for index in range(count)])


def reduce_all(parts):
    low, wide = jnp.bfloat16, jnp.float32
    me = lax.axis_index("shard")
    hold = parts
    mask = 1
    size = parts.shape[0]
    pair = hold.reshape(size // 2, 2, *hold.shape[1:])
    side = me % 2
    keep = lax.dynamic_index_in_dim(pair, side, 1, keepdims=False)
    send = lax.dynamic_index_in_dim(pair, 1 - side, 1, keepdims=False).astype(low)
    hold = keep + exchange(send, "shard", 1).astype(wide)
    side = me // 2
    keep = lax.dynamic_index_in_dim(hold, side, 0, keepdims=False)
    send = lax.dynamic_index_in_dim(hold, 1 - side, 0, keepdims=False).astype(low)
    hold = keep + exchange(send, "shard", 2).astype(wide)
    replicas = lax.axis_size("dp")
    pieces = hold.astype(low).reshape(replicas, -1, hold.shape[-1])
    received = lax.all_to_all(pieces, "dp", 0, 0, tiled=False)
    piece = jnp.sum(received.astype(wide), axis=0).astype(low)
    return lax.all_gather(piece, "dp", axis=0, tiled=True).astype(wide)


def shards(
    tokens,
    cotangent,
    lengths,
    seq_owner,
    qkv_weight,
    out_weight,
    up_weight,
    down_weight,
    gains_biases,
    qkv_first,
    qkv_second,
    out_first,
    out_second,
    up_first,
    up_second,
    down_first,
    down_second,
    small_first,
    small_second,
):
    row_count, model_width = tokens.shape
    head_count = model_width // HEAD
    score_scale = 1.0 / math.sqrt(HEAD)
    block_rows = min(512, row_count)
    device = lax.axis_index(("dp", "shard"))
    own_lengths = jnp.where(seq_owner == device, lengths, 0)
    seq_ends = jnp.cumsum(own_lengths)
    position = jnp.arange(row_count, dtype=jnp.int32)
    segment = jnp.sum((seq_ends[None, :] <= position[:, None]).astype(jnp.int32), axis=1)
    live_rows = (position < seq_ends[-1]).astype(jnp.float32)
    packed = jnp.concatenate(
        [
            split_cols(qkv_weight.astype(jnp.bfloat16), model_width),
            out_weight.astype(jnp.bfloat16),
            split_cols(up_weight.astype(jnp.bfloat16), model_width),
            down_weight.astype(jnp.bfloat16),
            gains_biases.astype(jnp.bfloat16).reshape(-1, model_width),
        ],
        axis=0,
    )
    gathered = lax.all_gather(packed, "shard", axis=0)
    qkv_rows = qkv_weight.shape[0] * 3
    out_rows = out_weight.shape[0]
    up_rows = up_weight.shape[0] * 4
    down_rows = down_weight.shape[0]
    ends = [0, qkv_rows, qkv_rows + out_rows, qkv_rows + out_rows + up_rows]
    ends.append(ends[-1] + down_rows)
    qkv_full = join_cols(gathered[:, ends[0] : ends[1]], 3)
    out_full = gathered[:, ends[1] : ends[2]].reshape(-1, model_width)
    up_full = join_cols(gathered[:, ends[2] : ends[3]], 4)
    down_full = gathered[:, ends[3] : ends[4]].reshape(-1, model_width)
    small_full = gathered[:, ends[4] :].reshape(-1)
    small_parts = unpack_small(small_full.astype(jnp.float32), model_width)
    gain_one, bias_one, gain_two, bias_two, bias_query, bias_value, bias_out, bias_down, bias_up = (
        small_parts
    )
    inputs = tokens.astype(jnp.float32)
    normed_one, root_one = standardize(inputs)
    hidden_one = (normed_one * gain_one + bias_one).astype(jnp.bfloat16)
    joined_bias = jnp.concatenate([bias_query, jnp.zeros_like(bias_query), bias_value])
    joined = (
        jnp.dot(hidden_one, qkv_full, preferred_element_type=jnp.float32) + joined_bias
    ).astype(jnp.bfloat16)
    queries = joined[:, :model_width].reshape(row_count, head_count, HEAD)
    key_rows = joined[:, model_width : 2 * model_width].reshape(row_count, head_count, HEAD)
    value_rows = joined[:, 2 * model_width :].reshape(row_count, head_count, HEAD)

    def block_scores(offset):
        limit = offset + block_rows
        raw_scores = (
            jnp.einsum("qhd,khd->hqk", queries, key_rows, preferred_element_type=jnp.float32)
            * score_scale
        )
        allowed = (segment[offset:limit, None] == segment[None, :limit]) & (
            position[None, :limit] <= position[offset:limit, None]
        )
        return (queries, jnp.where(allowed[None], raw_scores, masked_score))

    offset = 0
    limit = offset + block_rows
    query_block, scores = block_scores(offset)
    row_max = jnp.max(scores, axis=-1, keepdims=True)
    exponent = jnp.exp(scores - row_max)
    total = jnp.sum(exponent, axis=-1, keepdims=True)
    probs_low = (exponent / total).astype(jnp.bfloat16)
    attended_blocks = jnp.einsum(
        "hqk,khd->qhd", probs_low, value_rows, preferred_element_type=jnp.float32
    )
    log_sums = [row_max + jnp.log(total)]
    attended = attended_blocks.reshape(row_count, model_width).astype(jnp.bfloat16)
    middle = inputs + (jnp.dot(attended, out_full, preferred_element_type=jnp.float32) + bias_out)
    normed_two, root_two = standardize(middle)
    hidden_two = (normed_two * gain_two + bias_two).astype(jnp.bfloat16)
    pre_act = jnp.dot(hidden_two, up_full, preferred_element_type=jnp.float32) + bias_up
    activated_full, gelu_pull = jax.vjp(gelu_tanh, pre_act)
    activated = activated_full.astype(jnp.bfloat16)
    output = (
        middle + (jnp.dot(activated, down_full, preferred_element_type=jnp.float32) + bias_down)
    ).astype(jnp.bfloat16)
    qkv_back, out_back, up_back, down_back = qkv_full, out_full, up_full, down_full
    gain_one_back = gain_one
    gain_two_back = gain_two
    seed_grad = cotangent.astype(jnp.float32) * live_rows[:, None]
    down_in = seed_grad.astype(jnp.bfloat16)
    grad_down = contract_rows(activated, down_in)
    bias_down_grad = jnp.sum(down_in.astype(jnp.float32), axis=0)
    act_grad = contract_cols(down_in, down_back)
    up_in = gelu_pull(act_grad)[0].astype(jnp.bfloat16)
    grad_up = contract_rows(hidden_two, up_in)
    bias_up_grad = jnp.sum(up_in.astype(jnp.float32), axis=0)
    hidden_two_grad = contract_cols(up_in, up_back)
    through_two, gain_two_grad, bias_two_grad = norm_back(
        hidden_two_grad, normed_two, root_two, gain_two_back
    )
    middle_grad = seed_grad + through_two
    out_in = middle_grad.astype(jnp.bfloat16)
    grad_out = contract_rows(attended, out_in)
    bias_out_grad = jnp.sum(out_in.astype(jnp.float32), axis=0)
    attended_grad = (
        contract_cols(out_in, out_back).astype(jnp.bfloat16).reshape(row_count, head_count, HEAD)
    )
    key_grad = jnp.zeros((row_count, head_count, HEAD), jnp.float32)
    value_grad = jnp.zeros((row_count, head_count, HEAD), jnp.float32)
    query_grads = []
    for block_index, offset in enumerate(range(0, row_count, block_rows)):
        limit = offset + block_rows
        query_block, scores = block_scores(offset)
        probs = jnp.exp(scores - log_sums[block_index])
        probs_low = probs.astype(jnp.bfloat16)
        value_grad = value_grad.at[:limit].add(
            jnp.einsum("hqk,qhd->khd", probs_low, attended_grad, preferred_element_type=jnp.float32)
        )
        prob_grad = jnp.einsum(
            "qhd,khd->hqk", attended_grad, value_rows, preferred_element_type=jnp.float32
        )
        weighted = jnp.sum(probs * prob_grad, axis=-1, keepdims=True)
        score_grad = (probs * (prob_grad - weighted)).astype(jnp.bfloat16)
        query_grads.append(
            jnp.einsum("hqk,khd->qhd", score_grad, key_rows, preferred_element_type=jnp.float32)
            * score_scale
        )
        key_grad = key_grad.at[:limit].add(
            jnp.einsum("hqk,qhd->khd", score_grad, query_block, preferred_element_type=jnp.float32)
            * score_scale
        )
    query_grad = query_grads[0].reshape(row_count, model_width)
    joined_grad = jnp.concatenate(
        [
            query_grad,
            key_grad.reshape(row_count, model_width),
            value_grad.reshape(row_count, model_width),
        ],
        axis=1,
    ).astype(jnp.bfloat16)
    grad_qkv = contract_rows(hidden_one, joined_grad)
    joined_sum = jnp.sum(joined_grad.astype(jnp.float32), axis=0)
    bias_query_grad = joined_sum[:model_width]
    bias_value_grad = joined_sum[2 * model_width :]
    hidden_one_grad = contract_cols(joined_grad, qkv_back)
    through_one, gain_one_grad, bias_one_grad = norm_back(
        hidden_one_grad, normed_one, root_one, gain_one_back
    )
    input_grad = middle_grad + through_one
    small_grad = jnp.concatenate(
        [
            gain_one_grad,
            bias_one_grad,
            gain_two_grad,
            bias_two_grad,
            bias_query_grad,
            bias_value_grad,
            bias_out_grad,
            bias_down_grad,
            bias_up_grad,
        ]
    )
    shard_count = gathered.shape[0]
    by_shard = lambda grad: grad.reshape(shard_count, -1, grad.shape[-1])
    ffn_parts = jnp.concatenate(
        [by_shard(grad_down), split_cols(by_shard(grad_up), model_width)], axis=1
    )
    small_rows = small_grad.reshape(shard_count, -1, model_width)
    pad_rows = PAD - small_rows.shape[1]
    att_parts = jnp.concatenate(
        [
            by_shard(grad_out),
            split_cols(by_shard(grad_qkv), model_width),
            small_rows,
            jnp.zeros((shard_count, pad_rows, model_width), jnp.float32),
        ],
        axis=1,
    )
    ffn_sum = reduce_all(ffn_parts)
    att_sum = reduce_all(att_parts)
    own_down = ffn_sum[:down_rows]
    own_up = join_cols(ffn_sum[None, down_rows:], 4)
    own_out = att_sum[:out_rows]
    own_qkv = join_cols(att_sum[None, out_rows : out_rows + qkv_rows], 3)
    own_small = att_sum[out_rows + qkv_rows :][: small_rows.shape[1]].reshape(-1)
    owned = (own_qkv, own_out, own_up, own_down, own_small)
    qkv_new = adam_step(qkv_weight, owned[0], qkv_first, qkv_second, matrix_decay)
    out_new = adam_step(out_weight, owned[1], out_first, out_second, matrix_decay)
    up_new = adam_step(up_weight, owned[2], up_first, up_second, matrix_decay)
    down_new = adam_step(down_weight, owned[3], down_first, down_second, matrix_decay)
    small_new = adam_step(gains_biases, owned[4], small_first, small_second, 0.0)
    return (
        output,
        input_grad,
        qkv_new[0],
        qkv_new[1],
        qkv_new[2],
        out_new[0],
        out_new[1],
        out_new[2],
        up_new[0],
        up_new[1],
        up_new[2],
        down_new[0],
        down_new[1],
        down_new[2],
        small_new[0],
        small_new[1],
        small_new[2],
    )


def solution(mesh):
    return jax.shard_map(
        shards,
        mesh=mesh,
        in_specs=(
            P(("dp", "shard"), None),
            P(("dp", "shard"), None),
            P(),
            P(),
            P("shard", None),
            P("shard", None),
            P("shard", None),
            P("shard", None),
            P("shard"),
            P("shard", None),
            P("shard", None),
            P("shard", None),
            P("shard", None),
            P("shard", None),
            P("shard", None),
            P("shard", None),
            P("shard", None),
            P("shard"),
            P("shard"),
        ),
        out_specs=(
            P(("dp", "shard"), None),
            P(("dp", "shard"), None),
            P("shard", None),
            P("shard", None),
            P("shard", None),
            P("shard", None),
            P("shard", None),
            P("shard", None),
            P("shard", None),
            P("shard", None),
            P("shard", None),
            P("shard", None),
            P("shard", None),
            P("shard", None),
            P("shard"),
            P("shard"),
            P("shard"),
        ),
        check_vma=False,
    )
```

```python
import functools
import math

import jax
import jax.numpy as jnp
from jax import lax
from jax.experimental import pallas as pl
from jax.experimental.pallas import tpu as pltpu
from jax.sharding import PartitionSpec as P

HEAD = 32
STEP = 10
LANES = 128
GROUP = 8
SMALL_PAD = 16
TILE_ROWS = 8

norm_eps = 1e-05
beta_one = 0.9
beta_two = 0.95
learn_rate = 0.1
adam_eps = 1e-08
matrix_decay = 0.1
masked_score = -1e30
low = jnp.bfloat16
wide = jnp.float32
log2_e = math.log2(math.e)
score_scale = 1.0 / math.sqrt(HEAD)
tanh_scale = math.sqrt(2.0 / math.pi)
cubic = 0.044715


def dot_nn(left, right):
    return jnp.dot(left, right, preferred_element_type=wide)


def dot_nt(left, right):
    return lax.dot_general(left, right, (((1,), (1,)), ((), ())), preferred_element_type=wide)


def standardize(values):
    centered = values - jnp.mean(values, axis=-1, keepdims=True)
    root_inv = lax.rsqrt(jnp.mean(centered * centered, axis=-1, keepdims=True) + norm_eps)
    return centered * root_inv, root_inv


def norm_back(upstream, normed, root_inv, gain):
    scaled = upstream * gain
    inner_mean = jnp.mean(scaled, axis=-1, keepdims=True)
    cross_mean = jnp.mean(scaled * normed, axis=-1, keepdims=True)
    through = root_inv * (scaled - inner_mean - normed * cross_mean)
    return (
        through,
        jnp.sum(upstream * normed, axis=0, keepdims=True),
        jnp.sum(upstream, axis=0, keepdims=True),
    )


def iota(shape, dim):
    return lax.broadcasted_iota(jnp.int32, shape, dim)


def own_row(lengths, owners, device):
    return jnp.where(owners == device, lengths, 0)


def ends_both(own):
    count = own.shape[1]
    shape = (count, count)
    rows, cols = iota(shape, 0), iota(shape, 1)
    spread = jnp.broadcast_to(own, shape)
    ends_col = jnp.sum(jnp.where(cols <= rows, spread, 0), axis=1, keepdims=True)
    own_col = jnp.sum(jnp.where(cols == rows, spread, 0), axis=1, keepdims=True)
    ends_row = jnp.sum(
        jnp.where(rows <= cols, jnp.broadcast_to(own_col, shape), 0), axis=0, keepdims=True
    )
    return ends_col, ends_row


def fill_mask(bias_ref, own, rows):
    ends_col, ends_row = ends_both(own)
    count = own.shape[1]
    seg_row = jnp.sum(
        (ends_col <= iota((count, rows), 1)).astype(jnp.int32), axis=0, keepdims=True
    )
    seg_col = jnp.sum(
        (ends_row <= iota((rows, count), 0)).astype(jnp.int32), axis=1, keepdims=True
    )
    allowed = (seg_row == seg_col) & (iota((rows, rows), 0) <= iota((rows, rows), 1))
    bias_ref[...] = jnp.where(allowed, 0.0, masked_score)


def fill_small(small_ref, shard, pieces, first_row):
    for offset, piece in enumerate(pieces):
        small_ref[shard ^ offset] = piece[first_row:, :].astype(wide)


def fill_cols(full_ref, shard, pieces, first_row, rows, width):
    blocks = full_ref.shape[1] // width
    for offset, piece in enumerate(pieces):
        at = pl.multiple_of((shard ^ offset) * rows, rows)
        for block in range(blocks):
            start = first_row + block * rows
            full_ref[pl.ds(at, rows), block * width : (block + 1) * width] = piece[
                start : start + rows, :
            ]


def head_mask(head):
    lane = iota((1, LANES), 1)
    first = head * HEAD % LANES
    return ((lane >= first) & (lane < first + HEAD)).astype(wide).astype(low)


def head_tile(head):
    first = head * HEAD // LANES * LANES
    return slice(first, first + LANES)


def query_blocks(rows):
    size = min(256, rows)
    return [(at, at + size) for at in range(0, rows, size)]


def put_blocks(target, row, source, width):
    rows = source.shape[0]
    for block in range(source.shape[1] // width):
        cols = slice(block * width, (block + 1) * width)
        target[row : row + rows, :] = source[:, cols].astype(low)
        row += rows
    return row


def pack_first_kernel(qkv_ref, small_ref, first_ref):
    width = first_ref.shape[1]
    row = put_blocks(first_ref, 0, qkv_ref, width)
    parts = [
        small_ref[block * width : (block + 1) * width].reshape(1, width)
        for block in range(small_ref.shape[0] // width)
    ]
    parts.append(jnp.zeros((SMALL_PAD - len(parts), width), wide))
    first_ref[row:, :] = jnp.concatenate(parts, axis=0).astype(low)


def pack_second_kernel(out_ref, up_ref, down_ref, second_ref):
    width = second_ref.shape[1]
    row = put_blocks(second_ref, 0, out_ref, width)
    row = put_blocks(second_ref, row, up_ref, width)
    put_blocks(second_ref, row, down_ref, width)


def attend_kernel(shards, ids, *refs):
    x_ref, len_ref, owner_ref = refs[:3]
    pieces = refs[3 : 3 + shards]
    joined_ref, out_ref, log_ref, weight_ref, small_ref, bias_ref, att_ref = refs[3 + shards :]
    rows, width = x_ref.shape
    shard = ids[1]
    part = width // shards
    fill_cols(weight_ref, shard, pieces, 0, part, width)
    fill_small(small_ref, shard, pieces, 3 * part)
    gain, shift = small_ref[0, 0:1, :], small_ref[0, 1:2, :]
    bias_query, bias_value = small_ref[1, 1:2, :], small_ref[1, 2:3, :]
    fill_mask(bias_ref, own_row(len_ref[...], owner_ref[...], ids[0]), rows)
    normed, _ = standardize(x_ref[...].astype(wide))
    hidden = (normed * gain + shift).astype(low)
    for block, bias in enumerate((bias_query, None, bias_value)):
        cols = slice(block * width, (block + 1) * width)
        value = dot_nn(hidden, weight_ref[:, cols])
        if bias is not None:
            value = value + bias
        joined_ref[:, cols] = value.astype(low)
    values_t = joined_ref[:, 2 * width :].T
    for head in range(width // HEAD):
        tile = head_tile(head)
        key_tile = joined_ref[:, width + tile.start : width + tile.stop] * head_mask(head)
        feature = slice(head * HEAD, (head + 1) * HEAD)
        for start, stop in query_blocks(rows):
            scores = dot_nt(key_tile[:stop], joined_ref[start:stop, tile])
            scores = scores * (score_scale * log2_e) + bias_ref[:stop, start:stop]
            top = jnp.max(scores, axis=0, keepdims=True)
            exponent = jnp.exp2(scores - top)
            total = jnp.sum(exponent, axis=0, keepdims=True)
            probs = (exponent * (1.0 / total)).astype(low)
            att_ref[feature, start:stop] = dot_nn(values_t[feature, :stop], probs).astype(low)
            log_ref[head : head + 1, start:stop] = top + jnp.log2(total)
    out_ref[...] = att_ref[...].T


def feed_kernel(shards, ids, *refs):
    x_ref, att_ref, seed_ref, len_ref, owner_ref = refs[:5]
    firsts = refs[5 : 5 + shards]
    pieces = refs[5 + shards : 5 + 2 * shards]
    refs = refs[5 + 2 * shards :]
    out_ref, middle_ref, dattend_ref, sums_ref, keep_ref = refs[:5]
    sends = refs[5 : 4 + shards]
    small_ref, out_w, up_w, down_w, grads_ref = refs[4 + shards :]
    rows, width = x_ref.shape
    hidden_count = up_w.shape[1]
    shard = ids[1]
    part = width // shards
    blocks = hidden_count // width
    down_part = hidden_count // shards
    fill_small(small_ref, shard, firsts, 3 * part)
    fill_cols(out_w, shard, pieces, 0, part, width)
    fill_cols(up_w, shard, pieces, part, part, width)
    fill_cols(down_w, shard, pieces, part + blocks * part, down_part, width)
    gain, shift = small_ref[0, 2:3, :], small_ref[1, 0:1, :]
    bias_out, bias_down = small_ref[2, 0:1, :], small_ref[2, 1:2, :]
    bias_up = [small_ref[2, 2:3, :]] + [small_ref[3, row : row + 1, :] for row in range(3)]
    live = jnp.sum(own_row(len_ref[...], owner_ref[...], ids[0]), axis=1, keepdims=True)
    live_rows = (iota((rows, 1), 0) < live).astype(wide)
    seed = seed_ref[...].astype(wide) * live_rows
    seed_low = seed.astype(low)
    attended = att_ref[...]
    middle = x_ref[...].astype(wide) + (dot_nn(attended, out_w[...]) + bias_out)
    normed, root = standardize(middle)
    hidden = (normed * gain + shift).astype(low)
    hidden_t = hidden.T
    result = middle + bias_down
    dhidden = jnp.zeros((rows, width), wide)
    sums_ref[...] = jnp.zeros(sums_ref.shape, wide)
    for block in range(blocks):
        cols = slice(block * width, (block + 1) * width)
        pre = dot_nn(hidden, up_w[:, cols]) + bias_up[block]
        square = pre * pre
        bend = jnp.tanh(tanh_scale * (pre + cubic * (pre * square)))
        half = 0.5 * (1.0 + bend)
        act = (pre * half).astype(low)
        slope = half + (0.5 * tanh_scale) * pre * (1.0 - bend * bend) * (
            1.0 + (3.0 * cubic) * square
        )
        dpre = (dot_nt(seed_low, down_w[cols, :]) * slope).astype(low)
        result = result + dot_nn(act, down_w[cols, :])
        dhidden = dhidden + dot_nt(dpre, up_w[:, cols])
        grad_down = dot_nn(act.T, seed_low)
        grad_up = dot_nn(hidden_t, dpre)
        for piece in range(width // down_part):
            target = block * (width // down_part) + piece
            at = part + blocks * part
            grads_ref[target, at : at + down_part, :] = grad_down[
                piece * down_part : (piece + 1) * down_part, :
            ]
        for target in range(shards):
            at = part + block * part
            grads_ref[target, at : at + part, :] = grad_up[target * part : (target + 1) * part, :]
        sums_ref[4 + block : 5 + block, :] = jnp.sum(dpre.astype(wide), axis=0, keepdims=True)
    out_ref[...] = result.astype(low)
    through, gain_grad, shift_grad = norm_back(dhidden, normed, root, gain)
    dmiddle = seed + through
    middle_ref[...] = dmiddle
    dmiddle_low = dmiddle.astype(low)
    grad_out = dot_nn(attended.T, dmiddle_low)
    for target in range(shards):
        grads_ref[target, :part, :] = grad_out[target * part : (target + 1) * part, :]
    dattend_ref[...] = dot_nt(dmiddle_low, out_w[...]).astype(low)
    sums_ref[0:1, :] = gain_grad
    sums_ref[1:2, :] = shift_grad
    sums_ref[2:3, :] = jnp.sum(dmiddle_low.astype(wide), axis=0, keepdims=True)
    sums_ref[3:4, :] = jnp.sum(seed_low.astype(wide), axis=0, keepdims=True)
    keep_ref[...] = grads_ref[shard]
    for offset in range(1, shards):
        sends[offset - 1][...] = grads_ref[shard ^ offset].astype(low)


def attend_back_kernel(shards, ids, *refs):
    x_ref, joined_ref, dattend_ref, log_ref, middle_ref, sums_in, len_ref, owner_ref = refs[:8]
    pieces = refs[8 : 8 + shards]
    refs = refs[8 + shards :]
    dx_ref, keep_ref = refs[:2]
    sends = refs[2 : 1 + shards]
    weight_ref, small_ref, bias_ref, dquery_t, dkey, dvalue, djoined, grads_ref = refs[1 + shards :]
    rows, width = x_ref.shape
    shard = ids[1]
    part = width // shards
    fill_cols(weight_ref, shard, pieces, 0, part, width)
    fill_small(small_ref, shard, pieces, 3 * part)
    gain, shift = small_ref[0, 0:1, :], small_ref[0, 1:2, :]
    fill_mask(bias_ref, own_row(len_ref[...], owner_ref[...], ids[0]), rows)
    keys_t = joined_ref[:, width : 2 * width].T
    dkey[...] = jnp.zeros(dkey.shape, wide)
    dvalue[...] = jnp.zeros(dvalue.shape, wide)
    for head in range(width // HEAD):
        tile = head_tile(head)
        mask = head_mask(head)
        key_tile = joined_ref[:, width + tile.start : width + tile.stop] * mask
        value_tile = joined_ref[:, 2 * width + tile.start : 2 * width + tile.stop] * mask
        feature = slice(head * HEAD, (head + 1) * HEAD)
        for start, stop in query_blocks(rows):
            query = joined_ref[start:stop, tile]
            datt = dattend_ref[start:stop, tile]
            scores = dot_nt(key_tile[:stop], query)
            scores = scores * (score_scale * log2_e) + bias_ref[:stop, start:stop]
            probs = jnp.exp2(scores - log_ref[head : head + 1, start:stop])
            dprobs = dot_nt(value_tile[:stop], datt)
            weighted = jnp.sum(probs * dprobs, axis=0, keepdims=True)
            dscores = (probs * (dprobs - weighted)).astype(low)
            dquery_t[feature, start:stop] = (
                dot_nn(keys_t[feature, :stop], dscores) * score_scale
            ).astype(low)
            dvalue[:stop, tile] += dot_nn(probs.astype(low), datt * mask)
            dkey[:stop, tile] += dot_nn(dscores, query * mask)
    djoined[:, :width] = dquery_t[...].T
    djoined[:, width : 2 * width] = (dkey[...] * score_scale).astype(low)
    djoined[:, 2 * width :] = dvalue[...].astype(low)
    normed, root = standardize(x_ref[...].astype(wide))
    hidden_t = (normed * gain + shift).astype(low).T
    dhidden = jnp.zeros((rows, width), wide)
    bias_sums = []
    for block in range(3):
        cols = slice(block * width, (block + 1) * width)
        piece = djoined[:, cols]
        dhidden = dhidden + dot_nt(piece, weight_ref[:, cols])
        grad = dot_nn(hidden_t, piece)
        for target in range(shards):
            grads_ref[target, block * part : (block + 1) * part, :] = grad[
                target * part : (target + 1) * part, :
            ]
        if block != 1:
            bias_sums.append(jnp.sum(piece.astype(wide), axis=0, keepdims=True))
    through, gain_grad, shift_grad = norm_back(dhidden, normed, root, gain)
    dx_ref[...] = middle_ref[...] + through
    sums = [gain_grad, shift_grad, sums_in[0:1, :], sums_in[1:2, :]] + bias_sums
    sums += [sums_in[row : row + 1, :] for row in range(2, 8)]
    per_shard = len(sums) // shards
    for target in range(shards):
        at = 3 * part
        grads_ref[target, at:, :] = jnp.zeros((grads_ref.shape[1] - at, width), wide)
        for row in range(per_shard):
            grads_ref[target, at + row * TILE_ROWS : at + row * TILE_ROWS + 1, :] = sums[
                target * per_shard + row
            ]
    keep_ref[...] = grads_ref[shard]
    for offset in range(1, shards):
        sends[offset - 1][...] = grads_ref[shard ^ offset].astype(low)


def piece_spans(total, tail, group):
    spans = [((total - tail) // group, 0)]
    if tail:
        spans.append((tail // group, total - tail))
    return spans


def split_kernel(shards, tails, *refs):
    pieces_ref = refs[-1]
    group = pieces_ref.shape[0]
    column = 0
    for chunk, tail in enumerate(tails):
        arrived = refs[chunk * shards : (chunk + 1) * shards]
        count = arrived[0].shape[0]
        for rows, first in piece_spans(count, tail, group):
            for index in range(group):
                at = first + index * rows
                total = arrived[0][at : at + rows, :]
                for piece in arrived[1:]:
                    total = total + piece[at : at + rows, :].astype(wide)
                pieces_ref[index, column : column + rows, :] = total.astype(low)
            column += rows


def piece_kernel(arrived_ref, sent_ref):
    total = arrived_ref[0].astype(wide)
    for index in range(1, arrived_ref.shape[0]):
        total = total + arrived_ref[index].astype(wide)
    for index in range(sent_ref.shape[0]):
        sent_ref[index] = total.astype(low)


def add_kernel(mine_ref, other_ref, sent_ref):
    total = (mine_ref[0].astype(wide) + other_ref[...].astype(wide)).astype(low)
    for index in range(sent_ref.shape[0]):
        sent_ref[index] = total


def adam_values(weight, grad, first, second, decay_rate):
    first_next = beta_one * first + (1.0 - beta_one) * grad
    second_next = beta_two * second + (1.0 - beta_two) * grad * grad
    first_fix = 1.0 - beta_one**STEP
    second_fix = 1.0 - beta_two**STEP
    update = (first_next * (1.0 / first_fix)) / (
        jnp.sqrt(second_next * (1.0 / second_fix)) + adam_eps
    )
    return first_next, second_next, weight - learn_rate * (update + decay_rate * weight)


def adam_kernel(spans, layout, *refs):
    pieces_ref = refs[0]
    grad_ref = refs[-1]
    count = len(layout)
    states = refs[1 : 1 + 3 * count]
    results = refs[1 + 3 * count : -1]
    for index in range(pieces_ref.shape[0]):
        value = pieces_ref[index].astype(wide)
        for rows, first, row in spans:
            at = first + index * rows
            grad_ref[at : at + rows, :] = value[row : row + rows, :]
    width = grad_ref.shape[1]
    for array, (first_row, stride, decay) in enumerate(layout):
        weight, first, second = states[3 * array : 3 * array + 3]
        new = results[3 * array : 3 * array + 3]
        vector = len(weight.shape) == 1
        rows = 1 if vector else weight.shape[0]
        for block in range(weight.shape[-1] // width):
            cols = slice(block * width, (block + 1) * width)
            where = cols if vector else (slice(None), cols)
            at = first_row + block * stride
            values = adam_values(
                weight[where].reshape(rows, width),
                grad_ref[at : at + rows, :],
                first[where].reshape(rows, width),
                second[where].reshape(rows, width),
                decay,
            )
            for target, value in zip(new, values):
                target[where] = value.reshape(width) if vector else value


def local_call(kernel, outs, operands, scratch=(), ids=None, flops=0, name=None):
    specs = [pl.BlockSpec(memory_space=pltpu.VMEM)] * len(operands)
    if ids is not None:
        operands = [ids] + list(operands)
        specs = [pl.BlockSpec(memory_space=pltpu.SMEM)] + specs
    outs = [jax.ShapeDtypeStruct(*out) for out in outs]
    moved = sum(
        math.prod(item.shape) * item.dtype.itemsize for item in list(operands) + outs
    )
    return pl.pallas_call(
        kernel,
        out_shape=outs,
        in_specs=specs,
        out_specs=[pl.BlockSpec(memory_space=pltpu.VMEM)] * len(outs),
        scratch_shapes=[pltpu.VMEM(*item) for item in scratch],
        compiler_params=pltpu.CompilerParams(vmem_limit_bytes=40 * 1024 * 1024),
        cost_estimate=pl.CostEstimate(flops=flops, bytes_accessed=moved, transcendentals=0),
        name=name,
    )(*operands)


def exchange(values, axis, mask):
    count = lax.axis_size(axis)
    return lax.ppermute(values, axis, [(index, index ^ mask) for index in range(count)])


def gather_shards(value, shards):
    found = {0: value}
    far = shards // 2
    while far:
        for offset in sorted(found):
            found[offset ^ far] = exchange(found[offset], "shard", far)
        far //= 2
    return [found[offset] for offset in range(shards)]


def swap_all(values, axis):
    return [exchange(value, axis, offset + 1) for offset, value in enumerate(values)]


def swap_pieces(pieces, group):
    replicas = lax.axis_size("dp")
    groups = None
    if replicas > group:
        groups = [list(range(at, at + group)) for at in range(0, replicas, group)]
    return lax.all_to_all(pieces, "dp", 0, 0, axis_index_groups=groups, tiled=True)


def reduce_replicas(chunks, tails, shards):
    replicas = lax.axis_size("dp")
    group = min(GROUP, replicas)
    width = chunks[0][0].shape[1]
    rows = sum(chunk[0].shape[0] for chunk in chunks) // group
    shape = (group, rows, width)
    (pieces,) = local_call(
        functools.partial(split_kernel, shards, tails),
        [(shape, low)],
        [piece for chunk in chunks for piece in chunk],
        name="split_sum",
    )
    (copies,) = local_call(
        piece_kernel, [(shape, low)], [swap_pieces(pieces, group)], name="piece_sum"
    )
    mask = group
    while mask < replicas:
        other = exchange(copies[0], "dp", mask)
        (copies,) = local_call(add_kernel, [(shape, low)], [copies, other], name="far_sum")
        mask *= 2
    return swap_pieces(copies, group)


def adam_call(pieces, counts, tails, states, layout):
    group, _, width = pieces.shape
    spans = []
    first = row = 0
    for total, tail in zip(counts, tails):
        for rows, start in piece_spans(total, tail, group):
            spans.append((rows, first + start, row))
            row += rows
        first += total
    return local_call(
        functools.partial(adam_kernel, spans, layout),
        [(state[0].shape, wide) for state in states for _ in range(3)],
        [pieces] + [item for state in states for item in state],
        [((first, width), wide)],
        name="adam",
    )


def shards_program(
    tokens,
    cotangent,
    lengths,
    seq_owner,
    qkv_weight,
    out_weight,
    up_weight,
    down_weight,
    gains_biases,
    qkv_first,
    qkv_second,
    out_first,
    out_second,
    up_first,
    up_second,
    down_first,
    down_second,
    small_first,
    small_second,
):
    rows, width = tokens.shape
    shards = lax.axis_size("shard")
    heads = width // HEAD
    part = qkv_weight.shape[0]
    hidden_count = up_weight.shape[1]
    device = lax.axis_index(("dp", "shard"))
    ids = jnp.stack([device, lax.axis_index("shard")]).astype(jnp.int32)
    lengths = lengths.reshape(1, -1)
    seq_owner = seq_owner.reshape(1, -1)
    first_rows = 3 * part + SMALL_PAD
    second_rows = part + up_weight.size // width + down_weight.shape[0]
    (first_pack,) = local_call(
        pack_first_kernel,
        [((first_rows, width), low)],
        [qkv_weight, gains_biases],
        name="pack_first",
    )
    firsts = gather_shards(first_pack, shards)
    (second_pack,) = local_call(
        pack_second_kernel,
        [((second_rows, width), low)],
        [out_weight, up_weight, down_weight],
        name="pack_second",
    )
    firsts, second_pack = lax.optimization_barrier((firsts, second_pack))
    seconds = {0: second_pack}
    seconds[2] = exchange(second_pack, "shard", 2)
    seconds[1] = exchange(second_pack, "shard", 1)
    square = (rows, rows)
    joined, attended, log_sums = local_call(
        functools.partial(attend_kernel, shards),
        [((rows, 3 * width), low), ((rows, width), low), ((heads, rows), wide)],
        [tokens, lengths, seq_owner] + firsts,
        [
            ((width, 3 * width), low),
            ((shards, SMALL_PAD, width), wide),
            (square, wide),
            ((width, rows), low),
        ],
        ids,
        flops=heads * rows * rows * 256 * 4,
        name="attend",
    )
    attended, seconds[2] = lax.optimization_barrier((attended, seconds[2]))
    seconds[3] = exchange(seconds[2], "shard", 1)
    seconds = [seconds[offset] for offset in range(shards)]
    output, middle_grad, attended_grad, sums, keep_ffn, *sends_ffn = local_call(
        functools.partial(feed_kernel, shards),
        [
            ((rows, width), low),
            ((rows, width), wide),
            ((rows, width), low),
            ((SMALL_PAD, width), wide),
            ((second_rows, width), wide),
        ]
        + [((second_rows, width), low)] * (shards - 1),
        [tokens, attended, cotangent, lengths, seq_owner] + firsts + seconds,
        [
            ((shards, SMALL_PAD, width), wide),
            ((width, width), low),
            ((width, hidden_count), low),
            ((hidden_count, width), low),
            ((shards, second_rows, width), wide),
        ],
        ids,
        flops=rows * width * (hidden_count * 12 + width * 6),
        name="feed",
    )
    arrived_ffn = swap_all(sends_ffn, "shard")
    tail = GROUP * TILE_ROWS
    att_rows = 3 * part + tail
    input_grad, keep_att, *sends_att = local_call(
        functools.partial(attend_back_kernel, shards),
        [((rows, width), wide), ((att_rows, width), wide)]
        + [((att_rows, width), low)] * (shards - 1),
        [tokens, joined, attended_grad, log_sums, middle_grad, sums, lengths, seq_owner] + firsts,
        [
            ((width, 3 * width), low),
            ((shards, SMALL_PAD, width), wide),
            (square, wide),
            ((width, rows), low),
            ((rows, width), wide),
            ((rows, width), wide),
            ((rows, 3 * width), low),
            ((shards, att_rows, width), wide),
        ],
        ids,
        flops=heads * rows * rows * 256 * 10,
        name="attend_back",
    )
    arrived_att = swap_all(sends_att, "shard")
    tails = (0, tail)
    pieces = reduce_replicas(
        [[keep_ffn] + arrived_ffn, [keep_att] + arrived_att], tails, shards
    )
    blocks = hidden_count // width
    results = adam_call(
        pieces,
        (second_rows, att_rows),
        tails,
        [
            (qkv_weight, qkv_first, qkv_second),
            (out_weight, out_first, out_second),
            (up_weight, up_first, up_second),
            (down_weight, down_first, down_second),
            (gains_biases, small_first, small_second),
        ],
        [
            (second_rows, part, matrix_decay),
            (0, part, matrix_decay),
            (part, part, matrix_decay),
            (part + blocks * part, 0, matrix_decay),
            (second_rows + 3 * part, TILE_ROWS, 0.0),
        ],
    )
    return (output, input_grad, *results)


def solution(mesh):
    rows = P(("dp", "shard"), None)
    matrix = P("shard", None)
    vector = P("shard")
    return jax.shard_map(
        shards_program,
        mesh=mesh,
        in_specs=(rows, rows, P(), P())
        + (matrix,) * 4
        + (vector,)
        + (matrix,) * 8
        + (vector, vector),
        out_specs=(rows, rows) + (matrix,) * 12 + (vector,) * 3,
        check_vma=False,
    )
```

```python
import functools
import math

import jax
import jax.numpy as jnp
from jax import lax
from jax.experimental import pallas as pl
from jax.experimental.pallas import tpu as pltpu
from jax.sharding import PartitionSpec as P

HEAD = 32
STEP = 10
LANES = 128
GROUP = 8
SMALL_PAD = 16
TILE_ROWS = 8

norm_eps = 1e-05
beta_one = 0.9
beta_two = 0.95
learn_rate = 0.1
adam_eps = 1e-08
matrix_decay = 0.1
masked_score = -1e30
low = jnp.bfloat16
wide = jnp.float32
log2_e = math.log2(math.e)
score_scale = 1.0 / math.sqrt(HEAD)
tanh_scale = math.sqrt(2.0 / math.pi)
cubic = 0.044715


def dot_nn(left, right):
    return jnp.dot(left, right, preferred_element_type=wide)


def dot_nt(left, right):
    return lax.dot_general(left, right, (((1,), (1,)), ((), ())), preferred_element_type=wide)


def standardize(values):
    centered = values - jnp.mean(values, axis=-1, keepdims=True)
    root_inv = lax.rsqrt(jnp.mean(centered * centered, axis=-1, keepdims=True) + norm_eps)
    return centered * root_inv, root_inv


def norm_back(upstream, normed, root_inv, gain):
    scaled = upstream * gain
    inner_mean = jnp.mean(scaled, axis=-1, keepdims=True)
    cross_mean = jnp.mean(scaled * normed, axis=-1, keepdims=True)
    through = root_inv * (scaled - inner_mean - normed * cross_mean)
    return (
        through,
        jnp.sum(upstream * normed, axis=0, keepdims=True),
        jnp.sum(upstream, axis=0, keepdims=True),
    )


def iota(shape, dim):
    return lax.broadcasted_iota(jnp.int32, shape, dim)


def own_row(lengths, owners, device):
    return jnp.where(owners == device, lengths, 0)


def ends_both(own):
    count = own.shape[1]
    shape = (count, count)
    rows, cols = iota(shape, 0), iota(shape, 1)
    spread = jnp.broadcast_to(own, shape)
    ends_col = jnp.sum(jnp.where(cols <= rows, spread, 0), axis=1, keepdims=True)
    own_col = jnp.sum(jnp.where(cols == rows, spread, 0), axis=1, keepdims=True)
    ends_row = jnp.sum(
        jnp.where(rows <= cols, jnp.broadcast_to(own_col, shape), 0), axis=0, keepdims=True
    )
    return ends_col, ends_row


def fill_mask(bias_ref, own, rows):
    ends_col, ends_row = ends_both(own)
    count = own.shape[1]
    seg_row = jnp.sum(
        (ends_col <= iota((count, rows), 1)).astype(jnp.int32), axis=0, keepdims=True
    )
    seg_col = jnp.sum(
        (ends_row <= iota((rows, count), 0)).astype(jnp.int32), axis=1, keepdims=True
    )
    allowed = (seg_row == seg_col) & (iota((rows, rows), 0) <= iota((rows, rows), 1))
    bias_ref[...] = jnp.where(allowed, 0.0, masked_score)


def fill_small(small_ref, shard, pieces, first_row):
    for offset, piece in enumerate(pieces):
        small_ref[shard ^ offset] = piece[first_row:, :].astype(wide)


def fill_cols(full_ref, shard, pieces, first_row, rows, width):
    blocks = full_ref.shape[1] // width
    for offset, piece in enumerate(pieces):
        at = pl.multiple_of((shard ^ offset) * rows, rows)
        for block in range(blocks):
            start = first_row + block * rows
            full_ref[pl.ds(at, rows), block * width : (block + 1) * width] = piece[
                start : start + rows, :
            ]


def head_mask(head):
    lane = iota((1, LANES), 1)
    first = head * HEAD % LANES
    return ((lane >= first) & (lane < first + HEAD)).astype(wide).astype(low)


def head_tile(head):
    first = head * HEAD // LANES * LANES
    return slice(first, first + LANES)


def query_blocks(rows):
    size = min(256, rows)
    return [(at, at + size) for at in range(0, rows, size)]


def put_blocks(target, row, source, width):
    rows = source.shape[0]
    for block in range(source.shape[1] // width):
        cols = slice(block * width, (block + 1) * width)
        target[row : row + rows, :] = source[:, cols].astype(low)
        row += rows
    return row


def pack_first_kernel(qkv_ref, small_ref, first_ref):
    width = first_ref.shape[1]
    row = put_blocks(first_ref, 0, qkv_ref, width)
    parts = [
        small_ref[block * width : (block + 1) * width].reshape(1, width)
        for block in range(small_ref.shape[0] // width)
    ]
    parts.append(jnp.zeros((SMALL_PAD - len(parts), width), wide))
    first_ref[row:, :] = jnp.concatenate(parts, axis=0).astype(low)


def pack_second_kernel(out_ref, up_ref, down_ref, second_ref):
    width = second_ref.shape[1]
    row = put_blocks(second_ref, 0, out_ref, width)
    row = put_blocks(second_ref, row, up_ref, width)
    put_blocks(second_ref, row, down_ref, width)


def attend_kernel(shards, ids, *refs):
    x_ref, len_ref, owner_ref = refs[:3]
    pieces = refs[3 : 3 + shards]
    joined_ref, out_ref, log_ref, weight_ref, small_ref, bias_ref, att_ref = refs[3 + shards :]
    rows, width = x_ref.shape
    shard = ids[1]
    part = width // shards
    fill_cols(weight_ref, shard, pieces, 0, part, width)
    fill_small(small_ref, shard, pieces, 3 * part)
    gain, shift = small_ref[0, 0:1, :], small_ref[0, 1:2, :]
    bias_query, bias_value = small_ref[1, 1:2, :], small_ref[1, 2:3, :]
    fill_mask(bias_ref, own_row(len_ref[...], owner_ref[...], ids[0]), rows)
    normed, _ = standardize(x_ref[...].astype(wide))
    hidden = (normed * gain + shift).astype(low)
    for block, bias in enumerate((bias_query, None, bias_value)):
        cols = slice(block * width, (block + 1) * width)
        value = dot_nn(hidden, weight_ref[:, cols])
        if bias is not None:
            value = value + bias
        joined_ref[:, cols] = value.astype(low)
    values_t = joined_ref[:, 2 * width :].T
    for head in range(width // HEAD):
        tile = head_tile(head)
        key_tile = joined_ref[:, width + tile.start : width + tile.stop] * head_mask(head)
        feature = slice(head * HEAD, (head + 1) * HEAD)
        for start, stop in query_blocks(rows):
            scores = dot_nt(key_tile[:stop], joined_ref[start:stop, tile])
            scores = scores * (score_scale * log2_e) + bias_ref[:stop, start:stop]
            top = jnp.max(scores, axis=0, keepdims=True)
            exponent = jnp.exp2(scores - top)
            total = jnp.sum(exponent, axis=0, keepdims=True)
            probs = (exponent * (1.0 / total)).astype(low)
            att_ref[feature, start:stop] = dot_nn(values_t[feature, :stop], probs).astype(low)
            log_ref[head : head + 1, start:stop] = top + jnp.log2(total)
    out_ref[...] = att_ref[...].T


def feed_kernel(shards, ids, *refs):
    x_ref, att_ref, seed_ref, len_ref, owner_ref = refs[:5]
    firsts = refs[5 : 5 + shards]
    pieces = refs[5 + shards : 5 + 2 * shards]
    refs = refs[5 + 2 * shards :]
    out_ref, middle_ref, dattend_ref, sums_ref, keep_ref = refs[:5]
    sends = refs[5 : 4 + shards]
    small_ref, out_w, up_w, down_w, grads_ref = refs[4 + shards :]
    rows, width = x_ref.shape
    hidden_count = up_w.shape[1]
    shard = ids[1]
    part = width // shards
    blocks = hidden_count // width
    down_part = hidden_count // shards
    fill_small(small_ref, shard, firsts, 3 * part)
    fill_cols(out_w, shard, pieces, 0, part, width)
    fill_cols(up_w, shard, pieces, part, part, width)
    fill_cols(down_w, shard, pieces, part + blocks * part, down_part, width)
    gain, shift = small_ref[0, 2:3, :], small_ref[1, 0:1, :]
    bias_out, bias_down = small_ref[2, 0:1, :], small_ref[2, 1:2, :]
    bias_up = [small_ref[2, 2:3, :]] + [small_ref[3, row : row + 1, :] for row in range(3)]
    live = jnp.sum(own_row(len_ref[...], owner_ref[...], ids[0]), axis=1, keepdims=True)
    live_rows = (iota((rows, 1), 0) < live).astype(wide)
    seed = seed_ref[...].astype(wide) * live_rows
    seed_low = seed.astype(low)
    attended = att_ref[...]
    middle = x_ref[...].astype(wide) + (dot_nn(attended, out_w[...]) + bias_out)
    normed, root = standardize(middle)
    hidden = (normed * gain + shift).astype(low)
    hidden_t = hidden.T
    result = middle + bias_down
    dhidden = jnp.zeros((rows, width), wide)
    sums_ref[...] = jnp.zeros(sums_ref.shape, wide)
    for block in range(blocks):
        cols = slice(block * width, (block + 1) * width)
        pre = dot_nn(hidden, up_w[:, cols]) + bias_up[block]
        square = pre * pre
        bend = jnp.tanh(tanh_scale * (pre + cubic * (pre * square)))
        half = 0.5 * (1.0 + bend)
        act = (pre * half).astype(low)
        slope = half + (0.5 * tanh_scale) * pre * (1.0 - bend * bend) * (
            1.0 + (3.0 * cubic) * square
        )
        dpre = (dot_nt(seed_low, down_w[cols, :]) * slope).astype(low)
        result = result + dot_nn(act, down_w[cols, :])
        dhidden = dhidden + dot_nt(dpre, up_w[:, cols])
        grad_down = dot_nn(act.T, seed_low)
        grad_up = dot_nn(hidden_t, dpre)
        for piece in range(width // down_part):
            target = block * (width // down_part) + piece
            at = part + blocks * part
            grads_ref[target, at : at + down_part, :] = grad_down[
                piece * down_part : (piece + 1) * down_part, :
            ]
        for target in range(shards):
            at = part + block * part
            grads_ref[target, at : at + part, :] = grad_up[target * part : (target + 1) * part, :]
        sums_ref[4 + block : 5 + block, :] = jnp.sum(dpre.astype(wide), axis=0, keepdims=True)
    out_ref[...] = result.astype(low)
    through, gain_grad, shift_grad = norm_back(dhidden, normed, root, gain)
    dmiddle = seed + through
    middle_ref[...] = dmiddle
    dmiddle_low = dmiddle.astype(low)
    grad_out = dot_nn(attended.T, dmiddle_low)
    for target in range(shards):
        grads_ref[target, :part, :] = grad_out[target * part : (target + 1) * part, :]
    dattend_ref[...] = dot_nt(dmiddle_low, out_w[...]).astype(low)
    sums_ref[0:1, :] = gain_grad
    sums_ref[1:2, :] = shift_grad
    sums_ref[2:3, :] = jnp.sum(dmiddle_low.astype(wide), axis=0, keepdims=True)
    sums_ref[3:4, :] = jnp.sum(seed_low.astype(wide), axis=0, keepdims=True)
    keep_ref[...] = grads_ref[shard]
    for offset in range(1, shards):
        sends[offset - 1][...] = grads_ref[shard ^ offset].astype(low)


def attend_back_kernel(shards, ids, *refs):
    x_ref, joined_ref, dattend_ref, log_ref, middle_ref, sums_in, len_ref, owner_ref = refs[:8]
    pieces = refs[8 : 8 + shards]
    refs = refs[8 + shards :]
    dx_ref, keep_ref, send_ref = refs[:3]
    weight_ref, small_ref, bias_ref, dquery_t, dkey, dvalue, djoined, grads_ref = refs[3:]
    rows, width = x_ref.shape
    shard = ids[1]
    part = width // shards
    fill_cols(weight_ref, shard, pieces, 0, part, width)
    fill_small(small_ref, shard, pieces, 3 * part)
    gain, shift = small_ref[0, 0:1, :], small_ref[0, 1:2, :]
    fill_mask(bias_ref, own_row(len_ref[...], owner_ref[...], ids[0]), rows)
    keys_t = joined_ref[:, width : 2 * width].T
    dkey[...] = jnp.zeros(dkey.shape, wide)
    dvalue[...] = jnp.zeros(dvalue.shape, wide)
    for head in range(width // HEAD):
        tile = head_tile(head)
        mask = head_mask(head)
        key_tile = joined_ref[:, width + tile.start : width + tile.stop] * mask
        value_tile = joined_ref[:, 2 * width + tile.start : 2 * width + tile.stop] * mask
        feature = slice(head * HEAD, (head + 1) * HEAD)
        for start, stop in query_blocks(rows):
            query = joined_ref[start:stop, tile]
            datt = dattend_ref[start:stop, tile]
            scores = dot_nt(key_tile[:stop], query)
            scores = scores * (score_scale * log2_e) + bias_ref[:stop, start:stop]
            probs = jnp.exp2(scores - log_ref[head : head + 1, start:stop])
            dprobs = dot_nt(value_tile[:stop], datt)
            weighted = jnp.sum(probs * dprobs, axis=0, keepdims=True)
            dscores = (probs * (dprobs - weighted)).astype(low)
            dquery_t[feature, start:stop] = (
                dot_nn(keys_t[feature, :stop], dscores) * score_scale
            ).astype(low)
            dvalue[:stop, tile] += dot_nn(probs.astype(low), datt * mask)
            dkey[:stop, tile] += dot_nn(dscores, query * mask)
    djoined[:, :width] = dquery_t[...].T
    djoined[:, width : 2 * width] = (dkey[...] * score_scale).astype(low)
    djoined[:, 2 * width :] = dvalue[...].astype(low)
    normed, root = standardize(x_ref[...].astype(wide))
    hidden_t = (normed * gain + shift).astype(low).T
    dhidden = jnp.zeros((rows, width), wide)
    bias_sums = []
    for block in range(3):
        cols = slice(block * width, (block + 1) * width)
        piece = djoined[:, cols]
        dhidden = dhidden + dot_nt(piece, weight_ref[:, cols])
        grad = dot_nn(hidden_t, piece)
        for target in range(shards):
            grads_ref[target, block * part : (block + 1) * part, :] = grad[
                target * part : (target + 1) * part, :
            ]
        if block != 1:
            bias_sums.append(jnp.sum(piece.astype(wide), axis=0, keepdims=True))
    through, gain_grad, shift_grad = norm_back(dhidden, normed, root, gain)
    dx_ref[...] = middle_ref[...] + through
    sums = [gain_grad, shift_grad, sums_in[0:1, :], sums_in[1:2, :]] + bias_sums
    sums += [sums_in[row : row + 1, :] for row in range(2, 8)]
    per_shard = len(sums) // shards
    for target in range(shards):
        at = 3 * part
        grads_ref[target, at:, :] = jnp.zeros((grads_ref.shape[1] - at, width), wide)
        for row in range(per_shard):
            grads_ref[target, at + row * TILE_ROWS : at + row * TILE_ROWS + 1, :] = sums[
                target * per_shard + row
            ]
    side = shard % 2
    for pair in range(shards // 2):
        keep_ref[pair] = grads_ref[2 * pair + side]
        send_ref[pair] = grads_ref[2 * pair + 1 - side].astype(low)


def halve_kernel(ids, kept_ref, arrived_ref, keep_ref, send_ref):
    half = ids[1] // 2
    keep_ref[...] = kept_ref[half] + arrived_ref[half].astype(wide)
    send_ref[...] = (kept_ref[1 - half] + arrived_ref[1 - half].astype(wide)).astype(low)


def piece_spans(total, tail, group):
    spans = [((total - tail) // group, 0)]
    if tail:
        spans.append((tail // group, total - tail))
    return spans


def split_kernel(tail, *refs):
    arrived, pieces_ref = refs[:-1], refs[-1]
    group = pieces_ref.shape[0]
    total = arrived[0][...]
    for piece in arrived[1:]:
        total = total + piece[...].astype(wide)
    for index in range(group):
        parts = [
            total[first + index * rows : first + (index + 1) * rows, :]
            for rows, first in piece_spans(total.shape[0], tail, group)
        ]
        pieces_ref[index] = jnp.concatenate(parts, axis=0).astype(low)


def piece_kernel(*refs):
    sent_ref = refs[-1]
    parts = []
    for arrived_ref in refs[:-1]:
        total = arrived_ref[0].astype(wide)
        for index in range(1, arrived_ref.shape[0]):
            total = total + arrived_ref[index].astype(wide)
        parts.append(total)
    result = jnp.concatenate(parts, axis=0).astype(low)
    for index in range(sent_ref.shape[0]):
        sent_ref[index] = result


def add_kernel(mine_ref, other_ref, sent_ref):
    total = (mine_ref[0].astype(wide) + other_ref[...].astype(wide)).astype(low)
    for index in range(sent_ref.shape[0]):
        sent_ref[index] = total


def adam_values(weight, grad, first, second, decay_rate):
    first_next = beta_one * first + (1.0 - beta_one) * grad
    second_next = beta_two * second + (1.0 - beta_two) * grad * grad
    first_fix = 1.0 - beta_one**STEP
    second_fix = 1.0 - beta_two**STEP
    update = (first_next * (1.0 / first_fix)) / (
        jnp.sqrt(second_next * (1.0 / second_fix)) + adam_eps
    )
    return first_next, second_next, weight - learn_rate * (update + decay_rate * weight)


def adam_kernel(spans, layout, *refs):
    pieces_ref = refs[0]
    grad_ref = refs[-1]
    count = len(layout)
    states = refs[1 : 1 + 3 * count]
    results = refs[1 + 3 * count : -1]
    for index in range(pieces_ref.shape[0]):
        value = pieces_ref[index].astype(wide)
        for rows, first, row in spans:
            at = first + index * rows
            grad_ref[at : at + rows, :] = value[row : row + rows, :]
    width = grad_ref.shape[1]
    for array, (first_row, stride, decay) in enumerate(layout):
        weight, first, second = states[3 * array : 3 * array + 3]
        new = results[3 * array : 3 * array + 3]
        vector = len(weight.shape) == 1
        rows = 1 if vector else weight.shape[0]
        for block in range(weight.shape[-1] // width):
            cols = slice(block * width, (block + 1) * width)
            where = cols if vector else (slice(None), cols)
            at = first_row + block * stride
            values = adam_values(
                weight[where].reshape(rows, width),
                grad_ref[at : at + rows, :],
                first[where].reshape(rows, width),
                second[where].reshape(rows, width),
                decay,
            )
            for target, value in zip(new, values):
                target[where] = value.reshape(width) if vector else value


def local_call(kernel, outs, operands, scratch=(), ids=None, flops=0, name=None):
    specs = [pl.BlockSpec(memory_space=pltpu.VMEM)] * len(operands)
    if ids is not None:
        operands = [ids] + list(operands)
        specs = [pl.BlockSpec(memory_space=pltpu.SMEM)] + specs
    outs = [jax.ShapeDtypeStruct(*out) for out in outs]
    moved = sum(
        math.prod(item.shape) * item.dtype.itemsize for item in list(operands) + outs
    )
    return pl.pallas_call(
        kernel,
        out_shape=outs,
        in_specs=specs,
        out_specs=[pl.BlockSpec(memory_space=pltpu.VMEM)] * len(outs),
        scratch_shapes=[pltpu.VMEM(*item) for item in scratch],
        compiler_params=pltpu.CompilerParams(vmem_limit_bytes=40 * 1024 * 1024),
        cost_estimate=pl.CostEstimate(flops=flops, bytes_accessed=moved, transcendentals=0),
        name=name,
    )(*operands)


def exchange(values, axis, mask):
    count = lax.axis_size(axis)
    return lax.ppermute(values, axis, [(index, index ^ mask) for index in range(count)])


def gather_shards(value, shards):
    found = {0: value}
    far = shards // 2
    while far:
        for offset in sorted(found):
            found[offset ^ far] = exchange(found[offset], "shard", far)
        far //= 2
    return [found[offset] for offset in range(shards)]


def swap_all(values, axis):
    return [exchange(value, axis, offset + 1) for offset, value in enumerate(values)]


def swap_pieces(pieces, group):
    replicas = lax.axis_size("dp")
    groups = None
    if replicas > group:
        groups = [list(range(at, at + group)) for at in range(0, replicas, group)]
    return lax.all_to_all(pieces, "dp", 0, 0, axis_index_groups=groups, tiled=True)


def reduce_replicas(chunks, tails):
    replicas = lax.axis_size("dp")
    group = min(GROUP, replicas)
    width = chunks[0][0].shape[1]
    arrived = []
    for chunk, tail in zip(chunks, tails):
        (pieces,) = local_call(
            functools.partial(split_kernel, tail),
            [((group, chunk[0].shape[0] // group, width), low)],
            chunk,
            name="split_sum",
        )
        arrived.append(swap_pieces(pieces, group))
    shape = (group, sum(pieces.shape[1] for pieces in arrived), width)
    (copies,) = local_call(piece_kernel, [(shape, low)], arrived, name="piece_sum")
    mask = group
    while mask < replicas:
        other = exchange(copies[0], "dp", mask)
        (copies,) = local_call(add_kernel, [(shape, low)], [copies, other], name="far_sum")
        mask *= 2
    return swap_pieces(copies, group)


def adam_call(pieces, counts, tails, states, layout):
    group, _, width = pieces.shape
    spans = []
    first = row = 0
    for total, tail in zip(counts, tails):
        for rows, start in piece_spans(total, tail, group):
            spans.append((rows, first + start, row))
            row += rows
        first += total
    return local_call(
        functools.partial(adam_kernel, spans, layout),
        [(state[0].shape, wide) for state in states for _ in range(3)],
        [pieces] + [item for state in states for item in state],
        [((first, width), wide)],
        name="adam",
    )


def shards_program(
    tokens,
    cotangent,
    lengths,
    seq_owner,
    qkv_weight,
    out_weight,
    up_weight,
    down_weight,
    gains_biases,
    qkv_first,
    qkv_second,
    out_first,
    out_second,
    up_first,
    up_second,
    down_first,
    down_second,
    small_first,
    small_second,
):
    rows, width = tokens.shape
    shards = lax.axis_size("shard")
    heads = width // HEAD
    part = qkv_weight.shape[0]
    hidden_count = up_weight.shape[1]
    device = lax.axis_index(("dp", "shard"))
    ids = jnp.stack([device, lax.axis_index("shard")]).astype(jnp.int32)
    lengths = lengths.reshape(1, -1)
    seq_owner = seq_owner.reshape(1, -1)
    first_rows = 3 * part + SMALL_PAD
    second_rows = part + up_weight.size // width + down_weight.shape[0]
    (first_pack,) = local_call(
        pack_first_kernel,
        [((first_rows, width), low)],
        [qkv_weight, gains_biases],
        name="pack_first",
    )
    firsts = gather_shards(first_pack, shards)
    (second_pack,) = local_call(
        pack_second_kernel,
        [((second_rows, width), low)],
        [out_weight, up_weight, down_weight],
        name="pack_second",
    )
    firsts[2], second_pack = lax.optimization_barrier((firsts[2], second_pack))
    seconds = {0: second_pack}
    seconds[2] = exchange(second_pack, "shard", 2)
    seconds[1] = exchange(second_pack, "shard", 1)
    square = (rows, rows)
    joined, attended, log_sums = local_call(
        functools.partial(attend_kernel, shards),
        [((rows, 3 * width), low), ((rows, width), low), ((heads, rows), wide)],
        [tokens, lengths, seq_owner] + firsts,
        [
            ((width, 3 * width), low),
            ((shards, SMALL_PAD, width), wide),
            (square, wide),
            ((width, rows), low),
        ],
        ids,
        flops=heads * rows * rows * 256 * 4,
        name="attend",
    )
    attended, seconds[2] = lax.optimization_barrier((attended, seconds[2]))
    seconds[3] = exchange(seconds[2], "shard", 1)
    seconds = [seconds[offset] for offset in range(shards)]
    output, middle_grad, attended_grad, sums, keep_ffn, *sends_ffn = local_call(
        functools.partial(feed_kernel, shards),
        [
            ((rows, width), low),
            ((rows, width), wide),
            ((rows, width), low),
            ((SMALL_PAD, width), wide),
            ((second_rows, width), wide),
        ]
        + [((second_rows, width), low)] * (shards - 1),
        [tokens, attended, cotangent, lengths, seq_owner] + firsts + seconds,
        [
            ((shards, SMALL_PAD, width), wide),
            ((width, width), low),
            ((width, hidden_count), low),
            ((hidden_count, width), low),
            ((shards, second_rows, width), wide),
        ],
        ids,
        flops=rows * width * (hidden_count * 12 + width * 6),
        name="feed",
    )
    arrived_ffn = swap_all(sends_ffn, "shard")
    tail = GROUP * TILE_ROWS
    att_rows = 3 * part + tail
    input_grad, kept_att, send_att = local_call(
        functools.partial(attend_back_kernel, shards),
        [
            ((rows, width), wide),
            ((shards // 2, att_rows, width), wide),
            ((shards // 2, att_rows, width), low),
        ],
        [tokens, joined, attended_grad, log_sums, middle_grad, sums, lengths, seq_owner] + firsts,
        [
            ((width, 3 * width), low),
            ((shards, SMALL_PAD, width), wide),
            (square, wide),
            ((width, rows), low),
            ((rows, width), wide),
            ((rows, width), wide),
            ((rows, 3 * width), low),
            ((shards, att_rows, width), wide),
        ],
        ids,
        flops=heads * rows * rows * 256 * 10,
        name="attend_back",
    )
    keep_att, send_att = local_call(
        halve_kernel,
        [((att_rows, width), wide), ((att_rows, width), low)],
        [kept_att, exchange(send_att, "shard", 1)],
        ids=ids,
        name="halve",
    )
    arrived_att = [exchange(send_att, "shard", 2)]
    tails = (0, tail)
    pieces = reduce_replicas([[keep_ffn] + arrived_ffn, [keep_att] + arrived_att], tails)
    blocks = hidden_count // width
    results = adam_call(
        pieces,
        (second_rows, att_rows),
        tails,
        [
            (qkv_weight, qkv_first, qkv_second),
            (out_weight, out_first, out_second),
            (up_weight, up_first, up_second),
            (down_weight, down_first, down_second),
            (gains_biases, small_first, small_second),
        ],
        [
            (second_rows, part, matrix_decay),
            (0, part, matrix_decay),
            (part, part, matrix_decay),
            (part + blocks * part, 0, matrix_decay),
            (second_rows + 3 * part, TILE_ROWS, 0.0),
        ],
    )
    return (output, input_grad, *results)


def solution(mesh):
    rows = P(("dp", "shard"), None)
    matrix = P("shard", None)
    vector = P("shard")
    return jax.shard_map(
        shards_program,
        mesh=mesh,
        in_specs=(rows, rows, P(), P())
        + (matrix,) * 4
        + (vector,)
        + (matrix,) * 8
        + (vector, vector),
        out_specs=(rows, rows) + (matrix,) * 12 + (vector,) * 3,
        check_vma=False,
    )
```

```python
import functools
import math

import jax
import jax.numpy as jnp
from jax import lax
from jax.experimental import pallas as pl
from jax.experimental.pallas import tpu as pltpu
from jax.sharding import PartitionSpec as P

HEAD = 32
STEP = 10
LANES = 128
GROUP = 8
SMALL_PAD = 16
TILE_ROWS = 8

norm_eps = 1e-05
beta_one = 0.9
beta_two = 0.95
learn_rate = 0.1
adam_eps = 1e-08
matrix_decay = 0.1
masked_score = -1e30
low = jnp.bfloat16
wide = jnp.float32
log2_e = math.log2(math.e)
score_scale = 1.0 / math.sqrt(HEAD)
tanh_scale = math.sqrt(2.0 / math.pi)
cubic = 0.044715


def dot_nn(left, right):
    return jnp.dot(left, right, preferred_element_type=wide)


def dot_nt(left, right):
    return lax.dot_general(left, right, (((1,), (1,)), ((), ())), preferred_element_type=wide)


def standardize(values):
    centered = values - jnp.mean(values, axis=-1, keepdims=True)
    root_inv = lax.rsqrt(jnp.mean(centered * centered, axis=-1, keepdims=True) + norm_eps)
    return centered * root_inv, root_inv


def norm_back(upstream, normed, root_inv, gain):
    scaled = upstream * gain
    inner_mean = jnp.mean(scaled, axis=-1, keepdims=True)
    cross_mean = jnp.mean(scaled * normed, axis=-1, keepdims=True)
    through = root_inv * (scaled - inner_mean - normed * cross_mean)
    return (
        through,
        jnp.sum(upstream * normed, axis=0, keepdims=True),
        jnp.sum(upstream, axis=0, keepdims=True),
    )


def iota(shape, dim):
    return lax.broadcasted_iota(jnp.int32, shape, dim)


def own_row(lengths, owners, device):
    return jnp.where(owners == device, lengths, 0)


def ends_both(own):
    count = own.shape[1]
    shape = (count, count)
    rows, cols = iota(shape, 0), iota(shape, 1)
    spread = jnp.broadcast_to(own, shape)
    ends_col = jnp.sum(jnp.where(cols <= rows, spread, 0), axis=1, keepdims=True)
    own_col = jnp.sum(jnp.where(cols == rows, spread, 0), axis=1, keepdims=True)
    ends_row = jnp.sum(
        jnp.where(rows <= cols, jnp.broadcast_to(own_col, shape), 0), axis=0, keepdims=True
    )
    return ends_col, ends_row


def fill_mask(bias_ref, own, rows):
    ends_col, ends_row = ends_both(own)
    count = own.shape[1]
    seg_row = jnp.sum(
        (ends_col <= iota((count, rows), 1)).astype(jnp.int32), axis=0, keepdims=True
    )
    seg_col = jnp.sum(
        (ends_row <= iota((rows, count), 0)).astype(jnp.int32), axis=1, keepdims=True
    )
    allowed = (seg_row == seg_col) & (iota((rows, rows), 0) <= iota((rows, rows), 1))
    bias_ref[...] = jnp.where(allowed, 0.0, masked_score)


def fill_small(small_ref, shard, pieces, first_row):
    for offset, piece in enumerate(pieces):
        small_ref[shard ^ offset] = piece[first_row:, :].astype(wide)


def fill_cols(full_ref, shard, pieces, first_row, rows, width):
    blocks = full_ref.shape[1] // width
    for offset, piece in enumerate(pieces):
        at = pl.multiple_of((shard ^ offset) * rows, rows)
        for block in range(blocks):
            start = first_row + block * rows
            full_ref[pl.ds(at, rows), block * width : (block + 1) * width] = piece[
                start : start + rows, :
            ]


def head_mask(head):
    lane = iota((1, LANES), 1)
    first = head * HEAD % LANES
    return ((lane >= first) & (lane < first + HEAD)).astype(wide).astype(low)


def head_tile(head):
    first = head * HEAD // LANES * LANES
    return slice(first, first + LANES)


def query_blocks(rows):
    size = min(256, rows)
    return [(at, at + size) for at in range(0, rows, size)]


def put_blocks(target, row, source, width):
    rows = source.shape[0]
    for block in range(source.shape[1] // width):
        cols = slice(block * width, (block + 1) * width)
        target[row : row + rows, :] = source[:, cols].astype(low)
        row += rows
    return row


def pack_first_kernel(qkv_ref, small_ref, first_ref):
    width = first_ref.shape[1]
    row = put_blocks(first_ref, 0, qkv_ref, width)
    parts = [
        small_ref[block * width : (block + 1) * width].reshape(1, width)
        for block in range(small_ref.shape[0] // width)
    ]
    parts.append(jnp.zeros((SMALL_PAD - len(parts), width), wide))
    first_ref[row:, :] = jnp.concatenate(parts, axis=0).astype(low)


def pack_second_kernel(out_ref, up_ref, down_ref, second_ref):
    width = second_ref.shape[1]
    row = put_blocks(second_ref, 0, out_ref, width)
    row = put_blocks(second_ref, row, up_ref, width)
    put_blocks(second_ref, row, down_ref, width)


def attend_kernel(shards, ids, *refs):
    x_ref, len_ref, owner_ref = refs[:3]
    pieces = refs[3 : 3 + shards]
    joined_ref, out_ref, log_ref, weight_ref, small_ref, bias_ref, att_ref = refs[3 + shards :]
    rows, width = x_ref.shape
    shard = ids[1]
    part = width // shards
    fill_cols(weight_ref, shard, pieces, 0, part, width)
    fill_small(small_ref, shard, pieces, 3 * part)
    gain, shift = small_ref[0, 0:1, :], small_ref[0, 1:2, :]
    bias_query, bias_value = small_ref[1, 1:2, :], small_ref[1, 2:3, :]
    fill_mask(bias_ref, own_row(len_ref[...], owner_ref[...], ids[0]), rows)
    normed, _ = standardize(x_ref[...].astype(wide))
    hidden = (normed * gain + shift).astype(low)
    for block, bias in enumerate((bias_query, None, bias_value)):
        cols = slice(block * width, (block + 1) * width)
        value = dot_nn(hidden, weight_ref[:, cols])
        if bias is not None:
            value = value + bias
        joined_ref[:, cols] = value.astype(low)
    values_t = joined_ref[:, 2 * width :].T
    for head in range(width // HEAD):
        tile = head_tile(head)
        key_tile = joined_ref[:, width + tile.start : width + tile.stop] * head_mask(head)
        feature = slice(head * HEAD, (head + 1) * HEAD)
        for start, stop in query_blocks(rows):
            scores = dot_nt(key_tile[:stop], joined_ref[start:stop, tile])
            scores = scores * (score_scale * log2_e) + bias_ref[:stop, start:stop]
            top = jnp.max(scores, axis=0, keepdims=True)
            exponent = jnp.exp2(scores - top)
            total = jnp.sum(exponent, axis=0, keepdims=True)
            probs = (exponent * (1.0 / total)).astype(low)
            att_ref[feature, start:stop] = dot_nn(values_t[feature, :stop], probs).astype(low)
            log_ref[head : head + 1, start:stop] = top + jnp.log2(total)
    out_ref[...] = att_ref[...].T


def feed_kernel(shards, ids, *refs):
    x_ref, att_ref, seed_ref, len_ref, owner_ref = refs[:5]
    firsts = refs[5 : 5 + shards]
    pieces = refs[5 + shards : 5 + 2 * shards]
    refs = refs[5 + 2 * shards :]
    out_ref, middle_ref, dattend_ref, sums_ref, keep_ref = refs[:5]
    sends = refs[5 : 4 + shards]
    small_ref, out_w, up_w, down_w, grads_ref = refs[4 + shards :]
    rows, width = x_ref.shape
    hidden_count = up_w.shape[1]
    shard = ids[1]
    part = width // shards
    blocks = hidden_count // width
    down_part = hidden_count // shards
    fill_small(small_ref, shard, firsts, 3 * part)
    fill_cols(out_w, shard, pieces, 0, part, width)
    fill_cols(up_w, shard, pieces, part, part, width)
    fill_cols(down_w, shard, pieces, part + blocks * part, down_part, width)
    gain, shift = small_ref[0, 2:3, :], small_ref[1, 0:1, :]
    bias_out, bias_down = small_ref[2, 0:1, :], small_ref[2, 1:2, :]
    bias_up = [small_ref[2, 2:3, :]] + [small_ref[3, row : row + 1, :] for row in range(3)]
    live = jnp.sum(own_row(len_ref[...], owner_ref[...], ids[0]), axis=1, keepdims=True)
    live_rows = (iota((rows, 1), 0) < live).astype(wide)
    seed = seed_ref[...].astype(wide) * live_rows
    seed_low = seed.astype(low)
    attended = att_ref[...]
    middle = x_ref[...].astype(wide) + (dot_nn(attended, out_w[...]) + bias_out)
    normed, root = standardize(middle)
    hidden = (normed * gain + shift).astype(low)
    hidden_t = hidden.T
    result = middle + bias_down
    dhidden = jnp.zeros((rows, width), wide)
    sums_ref[...] = jnp.zeros(sums_ref.shape, wide)
    for block in range(blocks):
        cols = slice(block * width, (block + 1) * width)
        pre = dot_nn(hidden, up_w[:, cols]) + bias_up[block]
        square = pre * pre
        bend = jnp.tanh(tanh_scale * (pre + cubic * (pre * square)))
        half = 0.5 * (1.0 + bend)
        act = (pre * half).astype(low)
        slope = half + (0.5 * tanh_scale) * pre * (1.0 - bend * bend) * (
            1.0 + (3.0 * cubic) * square
        )
        dpre = (dot_nt(seed_low, down_w[cols, :]) * slope).astype(low)
        result = result + dot_nn(act, down_w[cols, :])
        dhidden = dhidden + dot_nt(dpre, up_w[:, cols])
        grad_down = dot_nn(act.T, seed_low)
        grad_up = dot_nn(hidden_t, dpre)
        for piece in range(width // down_part):
            target = block * (width // down_part) + piece
            at = part + blocks * part
            grads_ref[target, at : at + down_part, :] = grad_down[
                piece * down_part : (piece + 1) * down_part, :
            ]
        for target in range(shards):
            at = part + block * part
            grads_ref[target, at : at + part, :] = grad_up[target * part : (target + 1) * part, :]
        sums_ref[4 + block : 5 + block, :] = jnp.sum(dpre.astype(wide), axis=0, keepdims=True)
    out_ref[...] = result.astype(low)
    through, gain_grad, shift_grad = norm_back(dhidden, normed, root, gain)
    dmiddle = seed + through
    middle_ref[...] = dmiddle
    dmiddle_low = dmiddle.astype(low)
    grad_out = dot_nn(attended.T, dmiddle_low)
    for target in range(shards):
        grads_ref[target, :part, :] = grad_out[target * part : (target + 1) * part, :]
    dattend_ref[...] = dot_nt(dmiddle_low, out_w[...]).astype(low)
    sums_ref[0:1, :] = gain_grad
    sums_ref[1:2, :] = shift_grad
    sums_ref[2:3, :] = jnp.sum(dmiddle_low.astype(wide), axis=0, keepdims=True)
    sums_ref[3:4, :] = jnp.sum(seed_low.astype(wide), axis=0, keepdims=True)
    keep_ref[...] = grads_ref[shard]
    for offset in range(1, shards):
        sends[offset - 1][...] = grads_ref[shard ^ offset].astype(low)


def attend_back_kernel(shards, ids, *refs):
    x_ref, joined_ref, dattend_ref, log_ref, middle_ref, sums_in, len_ref, owner_ref = refs[:8]
    pieces = refs[8 : 8 + shards]
    refs = refs[8 + shards :]
    dx_ref, keep_ref, send_ref = refs[:3]
    weight_ref, small_ref, bias_ref, dquery_t, dkey, dvalue, djoined, grads_ref = refs[3:]
    rows, width = x_ref.shape
    shard = ids[1]
    part = width // shards
    fill_cols(weight_ref, shard, pieces, 0, part, width)
    fill_small(small_ref, shard, pieces, 3 * part)
    gain, shift = small_ref[0, 0:1, :], small_ref[0, 1:2, :]
    fill_mask(bias_ref, own_row(len_ref[...], owner_ref[...], ids[0]), rows)
    keys_t = joined_ref[:, width : 2 * width].T
    dkey[...] = jnp.zeros(dkey.shape, wide)
    dvalue[...] = jnp.zeros(dvalue.shape, wide)
    for head in range(width // HEAD):
        tile = head_tile(head)
        mask = head_mask(head)
        key_tile = joined_ref[:, width + tile.start : width + tile.stop] * mask
        value_tile = joined_ref[:, 2 * width + tile.start : 2 * width + tile.stop] * mask
        feature = slice(head * HEAD, (head + 1) * HEAD)
        for start, stop in query_blocks(rows):
            query = joined_ref[start:stop, tile]
            datt = dattend_ref[start:stop, tile]
            scores = dot_nt(key_tile[:stop], query)
            scores = scores * (score_scale * log2_e) + bias_ref[:stop, start:stop]
            probs = jnp.exp2(scores - log_ref[head : head + 1, start:stop])
            dprobs = dot_nt(value_tile[:stop], datt)
            weighted = jnp.sum(probs * dprobs, axis=0, keepdims=True)
            dscores = (probs * (dprobs - weighted)).astype(low)
            dquery_t[feature, start:stop] = (
                dot_nn(keys_t[feature, :stop], dscores) * score_scale
            ).astype(low)
            dvalue[:stop, tile] += dot_nn(probs.astype(low), datt * mask)
            dkey[:stop, tile] += dot_nn(dscores, query * mask)
    djoined[:, :width] = dquery_t[...].T
    djoined[:, width : 2 * width] = (dkey[...] * score_scale).astype(low)
    djoined[:, 2 * width :] = dvalue[...].astype(low)
    normed, root = standardize(x_ref[...].astype(wide))
    hidden_t = (normed * gain + shift).astype(low).T
    dhidden = jnp.zeros((rows, width), wide)
    bias_sums = []
    for block in range(3):
        cols = slice(block * width, (block + 1) * width)
        piece = djoined[:, cols]
        dhidden = dhidden + dot_nt(piece, weight_ref[:, cols])
        grad = dot_nn(hidden_t, piece)
        for target in range(shards):
            grads_ref[target, block * part : (block + 1) * part, :] = grad[
                target * part : (target + 1) * part, :
            ]
        if block != 1:
            bias_sums.append(jnp.sum(piece.astype(wide), axis=0, keepdims=True))
    through, gain_grad, shift_grad = norm_back(dhidden, normed, root, gain)
    dx_ref[...] = middle_ref[...] + through
    sums = [gain_grad, shift_grad, sums_in[0:1, :], sums_in[1:2, :]] + bias_sums
    sums += [sums_in[row : row + 1, :] for row in range(2, 8)]
    per_shard = len(sums) // shards
    for target in range(shards):
        at = 3 * part
        grads_ref[target, at:, :] = jnp.zeros((grads_ref.shape[1] - at, width), wide)
        for row in range(per_shard):
            grads_ref[target, at + row * TILE_ROWS : at + row * TILE_ROWS + 1, :] = sums[
                target * per_shard + row
            ]
    side = shard % 2
    for pair in range(shards // 2):
        keep_ref[pair] = grads_ref[2 * pair + side]
        send_ref[pair] = grads_ref[2 * pair + 1 - side].astype(low)


def halve_kernel(which, bit, ids, *refs):
    count = (len(refs) - 2) // 2
    keep_ref, send_ref = refs[-2:]
    side = (ids[which] >> bit) & 1
    for pair in range(keep_ref.shape[0]):
        for target, index in ((keep_ref, 2 * pair + side), (send_ref, 2 * pair + 1 - side)):
            parts = []
            for chunk in range(count):
                kept, arrived = refs[2 * chunk : 2 * chunk + 2]
                parts.append(kept[index] + arrived[index].astype(wide))
            value = parts[0] if count == 1 else jnp.concatenate(parts, axis=0)
            target[pair] = value.astype(target.dtype)


def piece_spans(total, tail, group):
    spans = [((total - tail) // group, 0)]
    if tail:
        spans.append((tail // group, total - tail))
    return spans


def split_kernel(tail, ids, *refs):
    arrived, keep_ref, send_ref, sum_ref = refs[:-3], *refs[-3:]
    group = sum_ref.shape[0]
    total = arrived[0][...]
    for piece in arrived[1:]:
        total = total + piece[...].astype(wide)
    for index in range(group):
        row = 0
        for rows, first in piece_spans(total.shape[0], tail, group):
            at = first + index * rows
            sum_ref[index, row : row + rows, :] = total[at : at + rows, :]
            row += rows
    side = ids[2] & 1
    for pair in range(group // 2):
        keep_ref[pair] = sum_ref[2 * pair + side]
        send_ref[pair] = sum_ref[2 * pair + 1 - side].astype(low)


def add_kernel(mine_ref, other_ref, sum_ref):
    total = mine_ref[...].astype(wide) + other_ref[...].astype(wide)
    sum_ref[...] = total.astype(low).reshape(sum_ref.shape)


def adam_values(weight, grad, first, second, decay_rate):
    first_next = beta_one * first + (1.0 - beta_one) * grad
    second_next = beta_two * second + (1.0 - beta_two) * grad * grad
    first_fix = 1.0 - beta_one**STEP
    second_fix = 1.0 - beta_two**STEP
    update = (first_next * (1.0 / first_fix)) / (
        jnp.sqrt(second_next * (1.0 / second_fix)) + adam_eps
    )
    return first_next, second_next, weight - learn_rate * (update + decay_rate * weight)


def adam_kernel(group, spans, layout, ids, *refs):
    pieces = refs[:group]
    grad_ref = refs[-1]
    count = len(layout)
    states = refs[group : group + 3 * count]
    results = refs[group + 3 * count : -1]
    for offset, piece in enumerate(pieces):
        value = piece[...].astype(wide)
        index = ids[2] ^ offset
        for rows, first, row in spans:
            at = pl.multiple_of(first + index * rows, TILE_ROWS)
            grad_ref[pl.ds(at, rows), :] = value[row : row + rows, :]
    width = grad_ref.shape[1]
    for array, (first_row, stride, decay) in enumerate(layout):
        weight, first, second = states[3 * array : 3 * array + 3]
        new = results[3 * array : 3 * array + 3]
        vector = len(weight.shape) == 1
        rows = 1 if vector else weight.shape[0]
        for block in range(weight.shape[-1] // width):
            cols = slice(block * width, (block + 1) * width)
            where = cols if vector else (slice(None), cols)
            at = first_row + block * stride
            values = adam_values(
                weight[where].reshape(rows, width),
                grad_ref[at : at + rows, :],
                first[where].reshape(rows, width),
                second[where].reshape(rows, width),
                decay,
            )
            for target, value in zip(new, values):
                target[where] = value.reshape(width) if vector else value


def local_call(kernel, outs, operands, scratch=(), ids=None, flops=0, name=None):
    specs = [pl.BlockSpec(memory_space=pltpu.VMEM)] * len(operands)
    if ids is not None:
        operands = [ids] + list(operands)
        specs = [pl.BlockSpec(memory_space=pltpu.SMEM)] + specs
    outs = [jax.ShapeDtypeStruct(*out) for out in outs]
    moved = sum(
        math.prod(item.shape) * item.dtype.itemsize for item in list(operands) + outs
    )
    return pl.pallas_call(
        kernel,
        out_shape=outs,
        in_specs=specs,
        out_specs=[pl.BlockSpec(memory_space=pltpu.VMEM)] * len(outs),
        scratch_shapes=[pltpu.VMEM(*item) for item in scratch],
        compiler_params=pltpu.CompilerParams(vmem_limit_bytes=40 * 1024 * 1024),
        cost_estimate=pl.CostEstimate(flops=flops, bytes_accessed=moved, transcendentals=0),
        name=name,
    )(*operands)


def exchange(values, axis, mask):
    count = lax.axis_size(axis)
    return lax.ppermute(values, axis, [(index, index ^ mask) for index in range(count)])


def gather_near(value, axis, count):
    found = {0: value}
    far = count // 2
    while far:
        for offset in sorted(found):
            found[offset ^ far] = exchange(found[offset], axis, far)
        far //= 2
    return [found[offset] for offset in range(count)]


def swap_all(values, axis):
    return [exchange(value, axis, offset + 1) for offset, value in enumerate(values)]


def split_chunk(chunk, tail, ids, group):
    rows, width = chunk[0].shape
    half = (group // 2, rows // group, width)
    keep, send = local_call(
        functools.partial(split_kernel, tail),
        [(half, wide), (half, low)],
        chunk,
        [((group,) + half[1:], wide)],
        ids,
        name="split_sum",
    )
    return keep, exchange(send, "dp", 1)


def finish_sum(chunks, ids, group):
    replicas = lax.axis_size("dp")
    half, _, width = chunks[0][0].shape
    rows = sum(chunk[0].shape[1] for chunk in chunks)
    flat = [item for chunk in chunks for item in chunk]
    bit = 1
    while half > 1:
        half //= 2
        keep, send = local_call(
            functools.partial(halve_kernel, 2, bit),
            [((half, rows, width), wide), ((half, rows, width), low)],
            flat,
            ids=ids,
            name="halve_dp",
        )
        flat = [keep, exchange(send, "dp", 1 << bit)]
        bit += 1
    mask = group
    (piece,) = local_call(add_kernel, [((rows, width), low)], flat, name="piece_sum")
    while mask < replicas:
        other = exchange(piece, "dp", mask)
        (piece,) = local_call(add_kernel, [((rows, width), low)], [piece, other], name="far_sum")
        mask *= 2
    return gather_near(piece, "dp", group)


def adam_call(pieces, counts, tails, states, layout, ids):
    group = len(pieces)
    width = pieces[0].shape[1]
    spans = []
    first = row = 0
    for total, tail in zip(counts, tails):
        for rows, start in piece_spans(total, tail, group):
            spans.append((rows, first + start, row))
            row += rows
        first += total
    return local_call(
        functools.partial(adam_kernel, group, spans, layout),
        [(state[0].shape, wide) for state in states for _ in range(3)],
        pieces + [item for state in states for item in state],
        [((first, width), wide)],
        ids,
        name="adam",
    )


def shards_program(
    tokens,
    cotangent,
    lengths,
    seq_owner,
    qkv_weight,
    out_weight,
    up_weight,
    down_weight,
    gains_biases,
    qkv_first,
    qkv_second,
    out_first,
    out_second,
    up_first,
    up_second,
    down_first,
    down_second,
    small_first,
    small_second,
):
    rows, width = tokens.shape
    shards = lax.axis_size("shard")
    heads = width // HEAD
    part = qkv_weight.shape[0]
    hidden_count = up_weight.shape[1]
    device = lax.axis_index(("dp", "shard"))
    group = min(GROUP, lax.axis_size("dp"))
    ids = jnp.stack([device, lax.axis_index("shard"), lax.axis_index("dp") % group])
    ids = ids.astype(jnp.int32)
    lengths = lengths.reshape(1, -1)
    seq_owner = seq_owner.reshape(1, -1)
    first_rows = 3 * part + SMALL_PAD
    second_rows = part + up_weight.size // width + down_weight.shape[0]
    (first_pack,) = local_call(
        pack_first_kernel,
        [((first_rows, width), low)],
        [qkv_weight, gains_biases],
        name="pack_first",
    )
    firsts = gather_near(first_pack, "shard", shards)
    (second_pack,) = local_call(
        pack_second_kernel,
        [((second_rows, width), low)],
        [out_weight, up_weight, down_weight],
        name="pack_second",
    )
    firsts[2], second_pack = lax.optimization_barrier((firsts[2], second_pack))
    seconds = {0: second_pack}
    seconds[2] = exchange(second_pack, "shard", 2)
    seconds[1] = exchange(second_pack, "shard", 1)
    square = (rows, rows)
    joined, attended, log_sums = local_call(
        functools.partial(attend_kernel, shards),
        [((rows, 3 * width), low), ((rows, width), low), ((heads, rows), wide)],
        [tokens, lengths, seq_owner] + firsts,
        [
            ((width, 3 * width), low),
            ((shards, SMALL_PAD, width), wide),
            (square, wide),
            ((width, rows), low),
        ],
        ids,
        flops=heads * rows * rows * 256 * 4,
        name="attend",
    )
    attended, seconds[2] = lax.optimization_barrier((attended, seconds[2]))
    seconds[3] = exchange(seconds[2], "shard", 1)
    seconds = [seconds[offset] for offset in range(shards)]
    output, middle_grad, attended_grad, sums, keep_ffn, *sends_ffn = local_call(
        functools.partial(feed_kernel, shards),
        [
            ((rows, width), low),
            ((rows, width), wide),
            ((rows, width), low),
            ((SMALL_PAD, width), wide),
            ((second_rows, width), wide),
        ]
        + [((second_rows, width), low)] * (shards - 1),
        [tokens, attended, cotangent, lengths, seq_owner] + firsts + seconds,
        [
            ((shards, SMALL_PAD, width), wide),
            ((width, width), low),
            ((width, hidden_count), low),
            ((hidden_count, width), low),
            ((shards, second_rows, width), wide),
        ],
        ids,
        flops=rows * width * (hidden_count * 12 + width * 6),
        name="feed",
    )
    arrived_ffn = swap_all(sends_ffn, "shard")
    tail = GROUP * TILE_ROWS
    att_rows = 3 * part + tail
    input_grad, kept_att, send_att = local_call(
        functools.partial(attend_back_kernel, shards),
        [
            ((rows, width), wide),
            ((shards // 2, att_rows, width), wide),
            ((shards // 2, att_rows, width), low),
        ],
        [tokens, joined, attended_grad, log_sums, middle_grad, sums, lengths, seq_owner] + firsts,
        [
            ((width, 3 * width), low),
            ((shards, SMALL_PAD, width), wide),
            (square, wide),
            ((width, rows), low),
            ((rows, width), wide),
            ((rows, width), wide),
            ((rows, 3 * width), low),
            ((shards, att_rows, width), wide),
        ],
        ids,
        flops=heads * rows * rows * 256 * 10,
        name="attend_back",
    )
    arrived_pair = exchange(send_att, "shard", 1)
    arrived_pair, arrived_ffn = lax.optimization_barrier((arrived_pair, arrived_ffn))
    keep_att, send_att = local_call(
        functools.partial(halve_kernel, 1, 1),
        [((1, att_rows, width), wide), ((1, att_rows, width), low)],
        [kept_att, arrived_pair],
        ids=ids,
        name="halve",
    )
    tails = (0, tail)
    arrived_att = exchange(send_att, "shard", 2)
    chunk_ffn = split_chunk([keep_ffn] + arrived_ffn, 0, ids, group)
    chunk_att = split_chunk([keep_att[0], arrived_att[0]], tail, ids, group)
    pieces = finish_sum([chunk_ffn, chunk_att], ids, group)
    blocks = hidden_count // width
    results = adam_call(
        pieces,
        (second_rows, att_rows),
        tails,
        [
            (qkv_weight, qkv_first, qkv_second),
            (out_weight, out_first, out_second),
            (up_weight, up_first, up_second),
            (down_weight, down_first, down_second),
            (gains_biases, small_first, small_second),
        ],
        [
            (second_rows, part, matrix_decay),
            (0, part, matrix_decay),
            (part, part, matrix_decay),
            (part + blocks * part, 0, matrix_decay),
            (second_rows + 3 * part, TILE_ROWS, 0.0),
        ],
        ids,
    )
    return (output, input_grad, *results)


def solution(mesh):
    rows = P(("dp", "shard"), None)
    matrix = P("shard", None)
    vector = P("shard")
    return jax.shard_map(
        shards_program,
        mesh=mesh,
        in_specs=(rows, rows, P(), P())
        + (matrix,) * 4
        + (vector,)
        + (matrix,) * 8
        + (vector, vector),
        out_specs=(rows, rows) + (matrix,) * 12 + (vector,) * 3,
        check_vma=False,
    )
```

```python
import functools
import math

import jax
import jax.numpy as jnp
from jax import lax
from jax.experimental import pallas as pl
from jax.experimental.pallas import tpu as pltpu
from jax.sharding import PartitionSpec as P

HEAD = 32
STEP = 10
LANES = 128
GROUP = 8
SMALL_PAD = 16
TILE_ROWS = 8

norm_eps = 1e-05
beta_one = 0.9
beta_two = 0.95
learn_rate = 0.1
adam_eps = 1e-08
matrix_decay = 0.1
masked_score = -1e30
low = jnp.bfloat16
wide = jnp.float32
log2_e = math.log2(math.e)
score_scale = 1.0 / math.sqrt(HEAD)
tanh_scale = math.sqrt(2.0 / math.pi)
cubic = 0.044715


def dot_nn(left, right):
    return jnp.dot(left, right, preferred_element_type=wide)


def dot_nt(left, right):
    return lax.dot_general(left, right, (((1,), (1,)), ((), ())), preferred_element_type=wide)


def standardize(values):
    centered = values - jnp.mean(values, axis=-1, keepdims=True)
    root_inv = lax.rsqrt(jnp.mean(centered * centered, axis=-1, keepdims=True) + norm_eps)
    return centered * root_inv, root_inv


def norm_back(upstream, normed, root_inv, gain):
    scaled = upstream * gain
    inner_mean = jnp.mean(scaled, axis=-1, keepdims=True)
    cross_mean = jnp.mean(scaled * normed, axis=-1, keepdims=True)
    through = root_inv * (scaled - inner_mean - normed * cross_mean)
    return (
        through,
        jnp.sum(upstream * normed, axis=0, keepdims=True),
        jnp.sum(upstream, axis=0, keepdims=True),
    )


def iota(shape, dim):
    return lax.broadcasted_iota(jnp.int32, shape, dim)


def own_row(lengths, owners, device):
    return jnp.where(owners == device, lengths, 0)


def ends_both(own):
    count = own.shape[1]
    shape = (count, count)
    rows, cols = iota(shape, 0), iota(shape, 1)
    spread = jnp.broadcast_to(own, shape)
    ends_col = jnp.sum(jnp.where(cols <= rows, spread, 0), axis=1, keepdims=True)
    own_col = jnp.sum(jnp.where(cols == rows, spread, 0), axis=1, keepdims=True)
    ends_row = jnp.sum(
        jnp.where(rows <= cols, jnp.broadcast_to(own_col, shape), 0), axis=0, keepdims=True
    )
    return ends_col, ends_row


def fill_mask(bias_ref, own, rows):
    ends_col, ends_row = ends_both(own)
    count = own.shape[1]
    seg_row = jnp.sum(
        (ends_col <= iota((count, rows), 1)).astype(jnp.int32), axis=0, keepdims=True
    )
    seg_col = jnp.sum(
        (ends_row <= iota((rows, count), 0)).astype(jnp.int32), axis=1, keepdims=True
    )
    allowed = (seg_row == seg_col) & (iota((rows, rows), 0) <= iota((rows, rows), 1))
    bias_ref[...] = jnp.where(allowed, 0.0, masked_score)


def fill_small(small_ref, shard, pieces, first_row):
    for offset, piece in enumerate(pieces):
        small_ref[shard ^ offset] = piece[first_row:, :].astype(wide)


def fill_cols(full_ref, shard, pieces, first_row, rows, width):
    blocks = full_ref.shape[1] // width
    for offset, piece in enumerate(pieces):
        at = pl.multiple_of((shard ^ offset) * rows, rows)
        for block in range(blocks):
            start = first_row + block * rows
            full_ref[pl.ds(at, rows), block * width : (block + 1) * width] = piece[
                start : start + rows, :
            ]


def head_mask(head):
    lane = iota((1, LANES), 1)
    first = head * HEAD % LANES
    return ((lane >= first) & (lane < first + HEAD)).astype(wide).astype(low)


def head_tile(head):
    first = head * HEAD // LANES * LANES
    return slice(first, first + LANES)


def query_blocks(rows):
    size = min(256, rows)
    return [(at, at + size) for at in range(0, rows, size)]


def put_blocks(target, row, source, width):
    rows = source.shape[0]
    for block in range(source.shape[1] // width):
        cols = slice(block * width, (block + 1) * width)
        target[row : row + rows, :] = source[:, cols].astype(low)
        row += rows
    return row


def fetch_all(sources, buffers, sems):
    copies = [
        pltpu.make_async_copy(source, buffer, sems.at[index])
        for index, (source, buffer) in enumerate(zip(sources, buffers))
    ]
    for copy in copies:
        copy.start()
    return copies


def pack_first_kernel(qkv_ref, small_ref, first_ref, qkv_buf, small_buf, sems):
    width = first_ref.shape[1]
    small_copy, qkv_copy = fetch_all((small_ref, qkv_ref), (small_buf, qkv_buf), sems)
    small_copy.wait()
    parts = [
        small_buf[block * width : (block + 1) * width].reshape(1, width)
        for block in range(small_buf.shape[0] // width)
    ]
    parts.append(jnp.zeros((SMALL_PAD - len(parts), width), wide))
    first_ref[first_ref.shape[0] - SMALL_PAD :, :] = jnp.concatenate(parts, axis=0).astype(low)
    qkv_copy.wait()
    put_blocks(first_ref, 0, qkv_buf, width)


def pack_second_kernel(out_ref, up_ref, down_ref, second_ref, out_buf, up_buf, down_buf, sems):
    width = second_ref.shape[1]
    buffers = (out_buf, up_buf, down_buf)
    copies = fetch_all((out_ref, up_ref, down_ref), buffers, sems)
    row = 0
    for copy, buffer in zip(copies, buffers):
        copy.wait()
        row = put_blocks(second_ref, row, buffer, width)


def prepare_kernel(shards, x_ref, seed_ref, len_ref, owner_ref, bias_ref, norm_ref, root_ref, low_ref):
    rows = x_ref.shape[0]
    device = lax.axis_index("dp") * shards + lax.axis_index("shard")
    own = own_row(len_ref[...], owner_ref[...], device)
    fill_mask(bias_ref, own, rows)
    normed, root = standardize(x_ref[...].astype(wide))
    norm_ref[...] = normed
    root_ref[...] = root
    live = jnp.sum(own, axis=1, keepdims=True)
    live_rows = (iota((rows, 1), 0) < live).astype(wide)
    low_ref[...] = (seed_ref[...].astype(wide) * live_rows).astype(low)


def attend_kernel(shards, *refs):
    norm_ref, bias_ref = refs[:2]
    pieces = refs[2 : 2 + shards]
    joined_ref, out_ref, log_ref, weight_ref, small_ref, att_ref = refs[2 + shards :]
    rows, width = norm_ref.shape
    shard = lax.axis_index("shard")
    part = width // shards
    fill_cols(weight_ref, shard, pieces, 0, part, width)
    fill_small(small_ref, shard, pieces, 3 * part)
    gain, shift = small_ref[0, 0:1, :], small_ref[0, 1:2, :]
    bias_query, bias_value = small_ref[1, 1:2, :], small_ref[1, 2:3, :]
    hidden = (norm_ref[...] * gain + shift).astype(low)
    for block, bias in enumerate((bias_query, None, bias_value)):
        cols = slice(block * width, (block + 1) * width)
        value = dot_nn(hidden, weight_ref[:, cols])
        if bias is not None:
            value = value + bias
        joined_ref[:, cols] = value.astype(low)
    values_t = joined_ref[:, 2 * width :].T
    for head in range(width // HEAD):
        tile = head_tile(head)
        key_tile = joined_ref[:, width + tile.start : width + tile.stop] * head_mask(head)
        feature = slice(head * HEAD, (head + 1) * HEAD)
        for start, stop in query_blocks(rows):
            scores = dot_nt(key_tile[:stop], joined_ref[start:stop, tile])
            scores = scores * (score_scale * log2_e) + bias_ref[:stop, start:stop]
            top = jnp.max(scores, axis=0, keepdims=True)
            exponent = jnp.exp2(scores - top)
            total = jnp.sum(exponent, axis=0, keepdims=True)
            probs = (exponent * (1.0 / total)).astype(low)
            att_ref[feature, start:stop] = dot_nn(values_t[feature, :stop], probs).astype(low)
            log_ref[head : head + 1, start:stop] = top + jnp.log2(total)
    out_ref[...] = att_ref[...].T


def feed_kernel(shards, *refs):
    x_ref, att_ref, seed_ref = refs[:3]
    firsts = refs[3 : 3 + shards]
    pieces = refs[3 + shards : 3 + 2 * shards]
    refs = refs[3 + 2 * shards :]
    out_ref, middle_ref, dattend_ref, sums_ref, keep_ref, send_ref = refs[:6]
    small_ref, out_w, up_w, down_w, grads_ref = refs[6:]
    rows, width = x_ref.shape
    hidden_count = up_w.shape[1]
    shard = lax.axis_index("shard")
    part = width // shards
    blocks = hidden_count // width
    down_part = hidden_count // shards
    fill_small(small_ref, shard, firsts, 3 * part)
    fill_cols(out_w, shard, pieces, 0, part, width)
    fill_cols(up_w, shard, pieces, part, part, width)
    fill_cols(down_w, shard, pieces, part + blocks * part, down_part, width)
    gain, shift = small_ref[0, 2:3, :], small_ref[1, 0:1, :]
    bias_out, bias_down = small_ref[2, 0:1, :], small_ref[2, 1:2, :]
    bias_up = [small_ref[2, 2:3, :]] + [small_ref[3, row : row + 1, :] for row in range(3)]
    seed_low = seed_ref[...]
    seed = seed_low.astype(wide)
    attended = att_ref[...]
    middle = x_ref[...].astype(wide) + (dot_nn(attended, out_w[...]) + bias_out)
    normed, root = standardize(middle)
    hidden = (normed * gain + shift).astype(low)
    hidden_t = hidden.T
    result = middle + bias_down
    dhidden = jnp.zeros((rows, width), wide)
    sums_ref[...] = jnp.zeros(sums_ref.shape, wide)
    for block in range(blocks):
        cols = slice(block * width, (block + 1) * width)
        pre = dot_nn(hidden, up_w[:, cols]) + bias_up[block]
        square = pre * pre
        bend = jnp.tanh(tanh_scale * (pre + cubic * (pre * square)))
        half = 0.5 * (1.0 + bend)
        act = (pre * half).astype(low)
        slope = half + (0.5 * tanh_scale) * pre * (1.0 - bend * bend) * (
            1.0 + (3.0 * cubic) * square
        )
        dpre = (dot_nt(seed_low, down_w[cols, :]) * slope).astype(low)
        result = result + dot_nn(act, down_w[cols, :])
        dhidden = dhidden + dot_nt(dpre, up_w[:, cols])
        grad_down = dot_nn(act.T, seed_low)
        grad_up = dot_nn(hidden_t, dpre)
        for piece in range(width // down_part):
            target = block * (width // down_part) + piece
            at = part + blocks * part
            grads_ref[target, at : at + down_part, :] = grad_down[
                piece * down_part : (piece + 1) * down_part, :
            ]
        for target in range(shards):
            at = part + block * part
            grads_ref[target, at : at + part, :] = grad_up[target * part : (target + 1) * part, :]
        sums_ref[4 + block : 5 + block, :] = jnp.sum(dpre.astype(wide), axis=0, keepdims=True)
    out_ref[...] = result.astype(low)
    through, gain_grad, shift_grad = norm_back(dhidden, normed, root, gain)
    dmiddle = seed + through
    middle_ref[...] = dmiddle
    dmiddle_low = dmiddle.astype(low)
    grad_out = dot_nn(attended.T, dmiddle_low)
    for target in range(shards):
        grads_ref[target, :part, :] = grad_out[target * part : (target + 1) * part, :]
    dattend_ref[...] = dot_nt(dmiddle_low, out_w[...]).astype(low)
    sums_ref[0:1, :] = gain_grad
    sums_ref[1:2, :] = shift_grad
    sums_ref[2:3, :] = jnp.sum(dmiddle_low.astype(wide), axis=0, keepdims=True)
    sums_ref[3:4, :] = jnp.sum(seed, axis=0, keepdims=True)
    part_ways(grads_ref, keep_ref, send_ref, shard % 2)


def part_ways(grads_ref, keep_ref, send_ref, side):
    for pair in range(keep_ref.shape[0]):
        keep_ref[pair] = grads_ref[2 * pair + side]
        send_ref[pair] = grads_ref[2 * pair + 1 - side].astype(low)


def back_tile(tile_index, joined_ref, dattend_ref, log_ref, bias_ref, dquery_t, dkey, dvalue):
    rows = joined_ref.shape[0]
    width = joined_ref.shape[1] // 3
    first = tile_index * LANES
    tile = slice(first, first + LANES)
    keys_t = joined_ref[:, width + first : width + first + LANES].T
    dkey[...] = jnp.zeros(dkey.shape, wide)
    dvalue[...] = jnp.zeros(dvalue.shape, wide)
    per_tile = LANES // HEAD
    for local in range(per_tile):
        head = tile_index * per_tile + local
        mask = head_mask(head)
        key_tile = joined_ref[:, width + first : width + first + LANES] * mask
        value_tile = joined_ref[:, 2 * width + first : 2 * width + first + LANES] * mask
        feature = slice(local * HEAD, (local + 1) * HEAD)
        for start, stop in query_blocks(rows):
            query = joined_ref[start:stop, tile]
            datt = dattend_ref[start:stop, tile]
            scores = dot_nt(key_tile[:stop], query)
            scores = scores * (score_scale * log2_e) + bias_ref[:stop, start:stop]
            probs = jnp.exp2(scores - log_ref[head : head + 1, start:stop])
            dprobs = dot_nt(value_tile[:stop], datt)
            weighted = jnp.sum(probs * dprobs, axis=0, keepdims=True)
            dscores = (probs * (dprobs - weighted)).astype(low)
            dquery_t[feature, start:stop] = (
                dot_nn(keys_t[feature, :stop], dscores) * score_scale
            ).astype(low)
            dvalue[:stop, :] += dot_nn(probs.astype(low), datt * mask)
            dkey[:stop, :] += dot_nn(dscores, query * mask)
    return dquery_t[...].T, (dkey[...] * score_scale).astype(low), dvalue[...].astype(low)


def back_first_kernel(joined_ref, dattend_ref, log_ref, bias_ref, *refs):
    results, scratch = refs[:3], refs[3:]
    values = back_tile(0, joined_ref, dattend_ref, log_ref, bias_ref, *scratch)
    for target, value in zip(results, values):
        target[...] = value


def back_last_kernel(shards, *refs):
    joined_ref, dattend_ref, log_ref, bias_ref = refs[:4]
    earlier = refs[4:7]
    norm_ref, root_ref, middle_ref, sums_in = refs[7:11]
    pieces = refs[11 : 11 + shards]
    refs = refs[11 + shards :]
    dx_ref, keep_ref, send_ref = refs[:3]
    weight_ref, small_ref, dquery_t, dkey, dvalue, djoined, grads_ref = refs[3:]
    rows, width = norm_ref.shape
    shard = lax.axis_index("shard")
    part = width // shards
    fill_cols(weight_ref, shard, pieces, 0, part, width)
    fill_small(small_ref, shard, pieces, 3 * part)
    gain, shift = small_ref[0, 0:1, :], small_ref[0, 1:2, :]
    values = back_tile(1, joined_ref, dattend_ref, log_ref, bias_ref, dquery_t, dkey, dvalue)
    for block in range(3):
        at = block * width
        djoined[:, at : at + LANES] = earlier[block][...]
        djoined[:, at + LANES : at + 2 * LANES] = values[block]
    normed, root = norm_ref[...], root_ref[...]
    hidden_t = (normed * gain + shift).astype(low).T
    dhidden = jnp.zeros((rows, width), wide)
    bias_sums = []
    for block in range(3):
        cols = slice(block * width, (block + 1) * width)
        piece = djoined[:, cols]
        dhidden = dhidden + dot_nt(piece, weight_ref[:, cols])
        grad = dot_nn(hidden_t, piece)
        for target in range(shards):
            grads_ref[target, block * part : (block + 1) * part, :] = grad[
                target * part : (target + 1) * part, :
            ]
        if block != 1:
            bias_sums.append(jnp.sum(piece.astype(wide), axis=0, keepdims=True))
    through, gain_grad, shift_grad = norm_back(dhidden, normed, root, gain)
    dx_ref[...] = middle_ref[...] + through
    sums = [gain_grad, shift_grad, sums_in[0:1, :], sums_in[1:2, :]] + bias_sums
    sums += [sums_in[row : row + 1, :] for row in range(2, 8)]
    per_shard = len(sums) // shards
    for target in range(shards):
        at = 3 * part
        grads_ref[target, at:, :] = jnp.zeros((grads_ref.shape[1] - at, width), wide)
        for row in range(per_shard):
            grads_ref[target, at + row * TILE_ROWS : at + row * TILE_ROWS + 1, :] = sums[
                target * per_shard + row
            ]
    part_ways(grads_ref, keep_ref, send_ref, shard % 2)


def halve_kernel(axis, bit, *refs):
    count = (len(refs) - 2) // 2
    keep_ref, send_ref = refs[-2:]
    side = (lax.axis_index(axis) >> bit) & 1
    for pair in range(keep_ref.shape[0]):
        for target, index in ((keep_ref, 2 * pair + side), (send_ref, 2 * pair + 1 - side)):
            parts = []
            for chunk in range(count):
                kept, arrived = refs[2 * chunk : 2 * chunk + 2]
                parts.append(kept[index] + arrived[index].astype(wide))
            value = parts[0] if count == 1 else jnp.concatenate(parts, axis=0)
            target[pair] = value.astype(target.dtype)


def piece_spans(total, tail, group):
    spans = [((total - tail) // group, 0)]
    if tail:
        spans.append((tail // group, total - tail))
    return spans


def split_kernel(tail, *refs):
    arrived, keep_ref, send_ref, sum_ref = refs[:-3], *refs[-3:]
    group = sum_ref.shape[0]
    total = arrived[0][...]
    for piece in arrived[1:]:
        total = total + piece[...].astype(wide)
    for index in range(group):
        row = 0
        for rows, first in piece_spans(total.shape[0], tail, group):
            at = first + index * rows
            sum_ref[index, row : row + rows, :] = total[at : at + rows, :]
            row += rows
    side = lax.axis_index("dp") & 1
    for pair in range(group // 2):
        keep_ref[pair] = sum_ref[2 * pair + side]
        send_ref[pair] = sum_ref[2 * pair + 1 - side].astype(low)


def add_kernel(mine_ref, other_ref, sum_ref):
    total = mine_ref[...].astype(wide) + other_ref[...].astype(wide)
    sum_ref[...] = total.astype(low).reshape(sum_ref.shape)


def adam_values(weight, grad, first, second, decay_rate):
    first_next = beta_one * first + (1.0 - beta_one) * grad
    second_next = beta_two * second + (1.0 - beta_two) * grad * grad
    first_fix = 1.0 - beta_one**STEP
    second_fix = 1.0 - beta_two**STEP
    update = (first_next * (1.0 / first_fix)) / (
        jnp.sqrt(second_next * (1.0 / second_fix)) + adam_eps
    )
    return first_next, second_next, weight - learn_rate * (update + decay_rate * weight)


def adam_kernel(group, spans, layout, *refs):
    pieces = refs[:group]
    grad_ref = refs[-1]
    count = len(layout)
    states = refs[group : group + 3 * count]
    results = refs[group + 3 * count : -1]
    for offset, piece in enumerate(pieces):
        value = piece[...].astype(wide)
        index = (lax.axis_index("dp") & (group - 1)) ^ offset
        for rows, first, row in spans:
            at = pl.multiple_of(first + index * rows, TILE_ROWS)
            grad_ref[pl.ds(at, rows), :] = value[row : row + rows, :]
    width = grad_ref.shape[1]
    for array, (first_row, stride, decay) in enumerate(layout):
        weight, first, second = states[3 * array : 3 * array + 3]
        new = results[3 * array : 3 * array + 3]
        vector = len(weight.shape) == 1
        rows = 1 if vector else weight.shape[0]
        for block in range(weight.shape[-1] // width):
            cols = slice(block * width, (block + 1) * width)
            where = cols if vector else (slice(None), cols)
            at = first_row + block * stride
            values = adam_values(
                weight[where].reshape(rows, width),
                grad_ref[at : at + rows, :],
                first[where].reshape(rows, width),
                second[where].reshape(rows, width),
                decay,
            )
            for target, value in zip(new, values):
                target[where] = value.reshape(width) if vector else value


def local_call(kernel, outs, operands, scratch=(), flops=0, name=None, fetch=False):
    space = pl.ANY if fetch else pltpu.VMEM
    outs = [jax.ShapeDtypeStruct(*out) for out in outs]
    moved = sum(
        math.prod(item.shape) * item.dtype.itemsize for item in list(operands) + outs
    )
    scratch_shapes = [pltpu.VMEM(*item) for item in scratch]
    if fetch:
        scratch_shapes.append(pltpu.SemaphoreType.DMA((len(operands),)))
    return pl.pallas_call(
        kernel,
        out_shape=outs,
        in_specs=[pl.BlockSpec(memory_space=space)] * len(operands),
        out_specs=[pl.BlockSpec(memory_space=pltpu.VMEM)] * len(outs),
        scratch_shapes=scratch_shapes,
        compiler_params=pltpu.CompilerParams(vmem_limit_bytes=40 * 1024 * 1024),
        cost_estimate=pl.CostEstimate(flops=flops, bytes_accessed=moved, transcendentals=0),
        name=name,
    )(*operands)


def exchange(values, axis, mask):
    count = lax.axis_size(axis)
    return lax.ppermute(values, axis, [(index, index ^ mask) for index in range(count)])


def gather_near(value, axis, count):
    found = {0: value}
    far = count // 2
    while far:
        for offset in sorted(found):
            found[offset ^ far] = exchange(found[offset], axis, far)
        far //= 2
    return [found[offset] for offset in range(count)]


def halve_call(axis, bit, flat, name):
    half, _, width = flat[0].shape
    shape = (half // 2, sum(item.shape[1] for item in flat[::2]), width)
    return local_call(
        functools.partial(halve_kernel, axis, bit), [(shape, wide), (shape, low)], flat, name=name
    )


def split_chunk(chunk, tail, group):
    rows, width = chunk[0].shape
    half = (group // 2, rows // group, width)
    keep, send = local_call(
        functools.partial(split_kernel, tail),
        [(half, wide), (half, low)],
        chunk,
        [((group,) + half[1:], wide)],
        name="split_sum",
    )
    return keep, exchange(send, "dp", 1)


def finish_sum(chunks, group):
    replicas = lax.axis_size("dp")
    half, _, width = chunks[0][0].shape
    rows = sum(chunk[0].shape[1] for chunk in chunks)
    flat = [item for chunk in chunks for item in chunk]
    bit = 1
    while half > 1:
        half //= 2
        keep, send = halve_call("dp", bit, flat, "halve_dp")
        flat = [keep, exchange(send, "dp", 1 << bit)]
        bit += 1
    mask = group
    (piece,) = local_call(add_kernel, [((rows, width), low)], flat, name="piece_sum")
    while mask < replicas:
        other = exchange(piece, "dp", mask)
        (piece,) = local_call(add_kernel, [((rows, width), low)], [piece, other], name="far_sum")
        mask *= 2
    return gather_near(piece, "dp", group)


def adam_call(pieces, counts, tails, states, layout):
    group = len(pieces)
    width = pieces[0].shape[1]
    spans = []
    first = row = 0
    for total, tail in zip(counts, tails):
        for rows, start in piece_spans(total, tail, group):
            spans.append((rows, first + start, row))
            row += rows
        first += total
    return local_call(
        functools.partial(adam_kernel, group, spans, layout),
        [(state[0].shape, wide) for state in states for _ in range(3)],
        pieces + [item for state in states for item in state],
        [((first, width), wide)],
        name="adam",
    )


def shards_program(
    tokens,
    cotangent,
    lengths,
    seq_owner,
    qkv_weight,
    out_weight,
    up_weight,
    down_weight,
    gains_biases,
    qkv_first,
    qkv_second,
    out_first,
    out_second,
    up_first,
    up_second,
    down_first,
    down_second,
    small_first,
    small_second,
):
    rows, width = tokens.shape
    shards = lax.axis_size("shard")
    heads = width // HEAD
    part = qkv_weight.shape[0]
    hidden_count = up_weight.shape[1]
    group = min(GROUP, lax.axis_size("dp"))
    lengths = lengths.reshape(1, -1)
    seq_owner = seq_owner.reshape(1, -1)
    first_rows = 3 * part + SMALL_PAD
    second_rows = part + up_weight.size // width + down_weight.shape[0]
    (first_pack,) = local_call(
        pack_first_kernel,
        [((first_rows, width), low)],
        [qkv_weight, gains_biases],
        [(qkv_weight.shape, wide), (gains_biases.shape, wide)],
        name="pack_first",
        fetch=True,
    )
    firsts = gather_near(first_pack, "shard", shards)
    square = (rows, rows)
    bias, normed, root, seed = local_call(
        functools.partial(prepare_kernel, shards),
        [(square, wide), ((rows, width), wide), ((rows, 1), wide), ((rows, width), low)],
        [tokens, cotangent, lengths, seq_owner],
        name="prepare",
    )
    matrices = [out_weight, up_weight, down_weight]
    (second_pack,) = local_call(
        pack_second_kernel,
        [((second_rows, width), low)],
        matrices,
        [(item.shape, wide) for item in matrices],
        name="pack_second",
        fetch=True,
    )
    firsts[2], second_pack = lax.optimization_barrier((firsts[2], second_pack))
    seconds = {0: second_pack}
    seconds[2] = exchange(second_pack, "shard", 2)
    seconds[1] = exchange(second_pack, "shard", 1)
    joined, attended, log_sums = local_call(
        functools.partial(attend_kernel, shards),
        [((rows, 3 * width), low), ((rows, width), low), ((heads, rows), wide)],
        [normed, bias] + firsts,
        [
            ((width, 3 * width), low),
            ((shards, SMALL_PAD, width), wide),
            ((width, rows), low),
        ],
        flops=heads * rows * rows * 256 * 4,
        name="attend",
    )
    attended, seconds[2] = lax.optimization_barrier((attended, seconds[2]))
    seconds[3] = exchange(seconds[2], "shard", 1)
    seconds = [seconds[offset] for offset in range(shards)]
    pair = (shards // 2, second_rows, width)
    output, middle_grad, attended_grad, sums, kept_ffn, send_ffn = local_call(
        functools.partial(feed_kernel, shards),
        [
            ((rows, width), low),
            ((rows, width), wide),
            ((rows, width), low),
            ((SMALL_PAD, width), wide),
            (pair, wide),
            (pair, low),
        ],
        [tokens, attended, seed] + firsts + seconds,
        [
            ((shards, SMALL_PAD, width), wide),
            ((width, width), low),
            ((width, hidden_count), low),
            ((hidden_count, width), low),
            ((shards, second_rows, width), wide),
        ],
        flops=rows * width * (hidden_count * 12 + width * 6),
        name="feed",
    )
    arrived_ffn = exchange(send_ffn, "shard", 1)
    shared = [joined, attended_grad, log_sums, bias]
    tile_scratch = [((LANES, rows), low), ((rows, LANES), wide), ((rows, LANES), wide)]
    first_query, first_key, first_value = local_call(
        back_first_kernel,
        [((rows, LANES), low)] * 3,
        shared,
        tile_scratch,
        flops=heads * rows * rows * 256 * 5,
        name="back_first",
    )
    first_query, arrived_ffn = lax.optimization_barrier((first_query, arrived_ffn))
    keep_ffn, send_ffn = halve_call("shard", 1, [kept_ffn, arrived_ffn], "halve_ffn")
    first_query, send_ffn = lax.optimization_barrier((first_query, send_ffn))
    arrived_ffn = exchange(send_ffn, "shard", 2)
    tail = GROUP * TILE_ROWS
    att_rows = 3 * part + tail
    pair = (shards // 2, att_rows, width)
    input_grad, kept_att, send_att = local_call(
        functools.partial(back_last_kernel, shards),
        [((rows, width), wide), (pair, wide), (pair, low)],
        shared + [first_query, first_key, first_value, normed, root, middle_grad, sums] + firsts,
        [((width, 3 * width), low), ((shards, SMALL_PAD, width), wide)]
        + tile_scratch
        + [((rows, 3 * width), low), ((shards, att_rows, width), wide)],
        flops=heads * rows * rows * 256 * 6,
        name="back_last",
    )
    arrived_att = exchange(send_att, "shard", 1)
    keep_att, send_att = halve_call("shard", 1, [kept_att, arrived_att], "halve_att")
    send_att, arrived_ffn = lax.optimization_barrier((send_att, arrived_ffn))
    tails = (0, tail)
    arrived_att = exchange(send_att, "shard", 2)
    chunk_ffn = split_chunk([keep_ffn[0], arrived_ffn[0]], 0, group)
    chunk_att = split_chunk([keep_att[0], arrived_att[0]], tail, group)
    pieces = finish_sum([chunk_ffn, chunk_att], group)
    blocks = hidden_count // width
    results = adam_call(
        pieces,
        (second_rows, att_rows),
        tails,
        [
            (qkv_weight, qkv_first, qkv_second),
            (out_weight, out_first, out_second),
            (up_weight, up_first, up_second),
            (down_weight, down_first, down_second),
            (gains_biases, small_first, small_second),
        ],
        [
            (second_rows, part, matrix_decay),
            (0, part, matrix_decay),
            (part, part, matrix_decay),
            (part + blocks * part, 0, matrix_decay),
            (second_rows + 3 * part, TILE_ROWS, 0.0),
        ],
    )
    return (output, input_grad, *results)


def solution(mesh):
    rows = P(("dp", "shard"), None)
    matrix = P("shard", None)
    vector = P("shard")
    return jax.shard_map(
        shards_program,
        mesh=mesh,
        in_specs=(rows, rows, P(), P())
        + (matrix,) * 4
        + (vector,)
        + (matrix,) * 8
        + (vector, vector),
        out_specs=(rows, rows) + (matrix,) * 12 + (vector,) * 3,
        check_vma=False,
    )
```

```python
import functools
import math

import jax
import jax.numpy as jnp
from jax import lax
from jax.experimental import pallas as pl
from jax.experimental.pallas import tpu as pltpu
from jax.sharding import PartitionSpec as P

HEAD = 32
STEP = 10
LANES = 128
GROUP = 8
SMALL_PAD = 16
TILE_ROWS = 8
CHUNK = 64

norm_eps = 1e-05
beta_one = 0.9
beta_two = 0.95
learn_rate = 0.1
adam_eps = 1e-08
matrix_decay = 0.1
masked_score = -1e30
low = jnp.bfloat16
wide = jnp.float32
log2_e = math.log2(math.e)
score_scale = 1.0 / math.sqrt(HEAD)
tanh_scale = math.sqrt(2.0 / math.pi)
cubic = 0.044715


def dot_nn(left, right):
    return jnp.dot(left, right, preferred_element_type=wide)


def dot_nt(left, right):
    return lax.dot_general(left, right, (((1,), (1,)), ((), ())), preferred_element_type=wide)


def standardize(values):
    centered = values - jnp.mean(values, axis=-1, keepdims=True)
    root_inv = lax.rsqrt(jnp.mean(centered * centered, axis=-1, keepdims=True) + norm_eps)
    return centered * root_inv, root_inv


def norm_back(upstream, normed, root_inv, gain):
    scaled = upstream * gain
    inner_mean = jnp.mean(scaled, axis=-1, keepdims=True)
    cross_mean = jnp.mean(scaled * normed, axis=-1, keepdims=True)
    through = root_inv * (scaled - inner_mean - normed * cross_mean)
    return (
        through,
        jnp.sum(upstream * normed, axis=0, keepdims=True),
        jnp.sum(upstream, axis=0, keepdims=True),
    )


def iota(shape, dim):
    return lax.broadcasted_iota(jnp.int32, shape, dim)


def own_row(lengths, owners, device):
    return jnp.where(owners == device, lengths, 0)


def ends_both(own):
    count = own.shape[1]
    shape = (count, count)
    rows, cols = iota(shape, 0), iota(shape, 1)
    spread = jnp.broadcast_to(own, shape)
    ends_col = jnp.sum(jnp.where(cols <= rows, spread, 0), axis=1, keepdims=True)
    own_col = jnp.sum(jnp.where(cols == rows, spread, 0), axis=1, keepdims=True)
    ends_row = jnp.sum(
        jnp.where(rows <= cols, jnp.broadcast_to(own_col, shape), 0), axis=0, keepdims=True
    )
    return ends_col, ends_row


def fill_mask(bias_ref, own, rows):
    ends_col, ends_row = ends_both(own)
    count = own.shape[1]
    seg_row = jnp.sum(
        (ends_col <= iota((count, rows), 1)).astype(jnp.int32), axis=0, keepdims=True
    )
    seg_col = jnp.sum(
        (ends_row <= iota((rows, count), 0)).astype(jnp.int32), axis=1, keepdims=True
    )
    allowed = (seg_row == seg_col) & (iota((rows, rows), 0) <= iota((rows, rows), 1))
    bias_ref[...] = jnp.where(allowed, 0.0, masked_score)


def fill_small(small_ref, shard, pieces, first_row):
    for offset, piece in enumerate(pieces):
        small_ref[shard ^ offset] = piece[first_row:, :].astype(wide)


def fill_cols(full_ref, shard, pieces, first_row, rows, width):
    blocks = full_ref.shape[1] // width
    for offset, piece in enumerate(pieces):
        at = pl.multiple_of((shard ^ offset) * rows, rows)
        for block in range(blocks):
            start = first_row + block * rows
            full_ref[pl.ds(at, rows), block * width : (block + 1) * width] = piece[
                start : start + rows, :
            ]


def head_mask(head):
    lane = iota((1, LANES), 1)
    first = head * HEAD % LANES
    return ((lane >= first) & (lane < first + HEAD)).astype(wide).astype(low)


def head_tile(head):
    first = head * HEAD // LANES * LANES
    return slice(first, first + LANES)


def query_blocks(rows):
    size = min(256, rows)
    return [(at, at + size) for at in range(0, rows, size)]


def put_blocks(target, row, source, width):
    rows = source.shape[0]
    for block in range(source.shape[1] // width):
        cols = slice(block * width, (block + 1) * width)
        target[row : row + rows, :] = source[:, cols].astype(low)
        row += rows
    return row


def fetch_all(sources, buffers, sems):
    copies = [
        pltpu.make_async_copy(source, buffer, sems.at[index])
        for index, (source, buffer) in enumerate(zip(sources, buffers))
    ]
    for copy in copies:
        copy.start()
    return copies


def pack_first_kernel(qkv_ref, small_ref, first_ref, qkv_buf, small_buf, sems):
    width = first_ref.shape[1]
    small_copy, qkv_copy = fetch_all((small_ref, qkv_ref), (small_buf, qkv_buf), sems)
    small_copy.wait()
    parts = [
        small_buf[block * width : (block + 1) * width].reshape(1, width)
        for block in range(small_buf.shape[0] // width)
    ]
    parts.append(jnp.zeros((SMALL_PAD - len(parts), width), wide))
    first_ref[first_ref.shape[0] - SMALL_PAD :, :] = jnp.concatenate(parts, axis=0).astype(low)
    qkv_copy.wait()
    put_blocks(first_ref, 0, qkv_buf, width)


def pack_second_kernel(out_ref, up_ref, down_ref, second_ref, out_buf, up_buf, down_buf, sems):
    width = second_ref.shape[1]
    buffers = (out_buf, up_buf, down_buf)
    copies = fetch_all((out_ref, up_ref, down_ref), buffers, sems)
    row = 0
    for copy, buffer in zip(copies, buffers):
        copy.wait()
        row = put_blocks(second_ref, row, buffer, width)


def prepare_kernel(shards, x_ref, seed_ref, len_ref, owner_ref, bias_ref, norm_ref, root_ref, low_ref):
    rows = x_ref.shape[0]
    device = lax.axis_index("dp") * shards + lax.axis_index("shard")
    own = own_row(len_ref[...], owner_ref[...], device)
    fill_mask(bias_ref, own, rows)
    normed, root = standardize(x_ref[...].astype(wide))
    norm_ref[...] = normed
    root_ref[...] = root
    live = jnp.sum(own, axis=1, keepdims=True)
    live_rows = (iota((rows, 1), 0) < live).astype(wide)
    low_ref[...] = (seed_ref[...].astype(wide) * live_rows).astype(low)


def attend_kernel(shards, *refs):
    norm_ref, bias_ref = refs[:2]
    pieces = refs[2 : 2 + shards]
    joined_ref, out_ref, log_ref, att_ref, weight_ref, small_ref = refs[2 + shards :]
    rows, width = norm_ref.shape
    shard = lax.axis_index("shard")
    part = width // shards
    fill_cols(weight_ref, shard, pieces, 0, part, width)
    fill_small(small_ref, shard, pieces, 3 * part)
    gain, shift = small_ref[0, 0:1, :], small_ref[0, 1:2, :]
    bias_query, bias_value = small_ref[1, 1:2, :], small_ref[1, 2:3, :]
    hidden = (norm_ref[...] * gain + shift).astype(low)
    for block, bias in enumerate((bias_query, None, bias_value)):
        cols = slice(block * width, (block + 1) * width)
        value = dot_nn(hidden, weight_ref[:, cols])
        if bias is not None:
            value = value + bias
        joined_ref[:, cols] = value.astype(low)
    values_t = joined_ref[:, 2 * width :].T
    for head in range(width // HEAD):
        tile = head_tile(head)
        key_tile = joined_ref[:, width + tile.start : width + tile.stop] * head_mask(head)
        feature = slice(head * HEAD, (head + 1) * HEAD)
        for start, stop in query_blocks(rows):
            raw = dot_nt(key_tile[:stop], joined_ref[start:stop, tile])
            scores = []
            top = None
            for at in range(0, stop, CHUNK):
                piece = raw[at : at + CHUNK] * (score_scale * log2_e)
                piece = piece + bias_ref[at : at + CHUNK, start:stop]
                scores.append(piece)
                top = piece if top is None else jnp.maximum(top, piece)
            top = jnp.max(top, axis=0, keepdims=True)
            exponents = []
            total = None
            for piece in scores:
                piece = jnp.exp2(piece - top)
                total = piece if total is None else total + piece
                exponents.append(piece.astype(low))
            total = jnp.sum(total, axis=0, keepdims=True)
            mixed = dot_nn(values_t[feature, :stop], jnp.concatenate(exponents, axis=0))
            att_ref[feature, start:stop] = mixed * (1.0 / total)
            log_ref[head : head + 1, start:stop] = top + jnp.log2(total)
    out_ref[...] = att_ref[...].astype(low).T


def feed_kernel(shards, *refs):
    x_ref, att_ref, seed_ref = refs[:3]
    firsts = refs[3 : 3 + shards]
    pieces = refs[3 + shards : 3 + 2 * shards]
    refs = refs[3 + 2 * shards :]
    out_ref, middle_ref, dattend_ref, sums_ref, keep_ref, send_ref = refs[:6]
    small_ref, out_w, up_w, down_w, grads_ref = refs[6:]
    rows, width = x_ref.shape
    hidden_count = up_w.shape[1]
    shard = lax.axis_index("shard")
    part = width // shards
    blocks = hidden_count // width
    down_part = hidden_count // shards
    fill_small(small_ref, shard, firsts, 3 * part)
    fill_cols(out_w, shard, pieces, 0, part, width)
    fill_cols(up_w, shard, pieces, part, part, width)
    fill_cols(down_w, shard, pieces, part + blocks * part, down_part, width)
    gain, shift = small_ref[0, 2:3, :], small_ref[1, 0:1, :]
    bias_out, bias_down = small_ref[2, 0:1, :], small_ref[2, 1:2, :]
    bias_up = [small_ref[2, 2:3, :]] + [small_ref[3, row : row + 1, :] for row in range(3)]
    seed_low = seed_ref[...]
    seed = seed_low.astype(wide)
    attended = att_ref[...]
    middle = x_ref[...].astype(wide) + (dot_nn(attended, out_w[...]) + bias_out)
    normed, root = standardize(middle)
    hidden = (normed * gain + shift).astype(low)
    hidden_t = hidden.T
    result = middle + bias_down
    dhidden = jnp.zeros((rows, width), wide)
    sums_ref[...] = jnp.zeros(sums_ref.shape, wide)
    for block in range(blocks):
        cols = slice(block * width, (block + 1) * width)
        raw = dot_nn(hidden, up_w[:, cols])
        dact = dot_nt(seed_low, down_w[cols, :])
        act, dpre = [], []
        for at in range(0, rows, CHUNK):
            pre = raw[at : at + CHUNK] + bias_up[block]
            square = pre * pre
            bend = jnp.tanh(pre * (tanh_scale + (tanh_scale * cubic) * square))
            half = 0.5 + 0.5 * bend
            act.append((pre * half).astype(low))
            slope = 0.5 * tanh_scale + (1.5 * tanh_scale * cubic) * square
            slope = half + (pre * slope) * (1.0 - bend * bend)
            dpre.append((dact[at : at + CHUNK] * slope).astype(low))
        act = jnp.concatenate(act, axis=0)
        dpre = jnp.concatenate(dpre, axis=0)
        result = result + dot_nn(act, down_w[cols, :])
        dhidden = dhidden + dot_nt(dpre, up_w[:, cols])
        grad_down = dot_nn(act.T, seed_low)
        grad_up = dot_nn(hidden_t, dpre)
        for piece in range(width // down_part):
            target = block * (width // down_part) + piece
            at = part + blocks * part
            grads_ref[target, at : at + down_part, :] = grad_down[
                piece * down_part : (piece + 1) * down_part, :
            ]
        for target in range(shards):
            at = part + block * part
            grads_ref[target, at : at + part, :] = grad_up[target * part : (target + 1) * part, :]
        sums_ref[4 + block : 5 + block, :] = jnp.sum(dpre.astype(wide), axis=0, keepdims=True)
    out_ref[...] = result.astype(low)
    through, gain_grad, shift_grad = norm_back(dhidden, normed, root, gain)
    dmiddle = seed + through
    middle_ref[...] = dmiddle
    dmiddle_low = dmiddle.astype(low)
    grad_out = dot_nn(attended.T, dmiddle_low)
    for target in range(shards):
        grads_ref[target, :part, :] = grad_out[target * part : (target + 1) * part, :]
    dattend_ref[...] = dot_nt(dmiddle_low, out_w[...]).astype(low)
    sums_ref[0:1, :] = gain_grad
    sums_ref[1:2, :] = shift_grad
    sums_ref[2:3, :] = jnp.sum(dmiddle_low.astype(wide), axis=0, keepdims=True)
    sums_ref[3:4, :] = jnp.sum(seed, axis=0, keepdims=True)
    part_ways(grads_ref, keep_ref, send_ref, shard % 2)


def part_ways(grads_ref, keep_ref, send_ref, side):
    for pair in range(keep_ref.shape[0]):
        keep_ref[pair] = grads_ref[2 * pair + side]
        send_ref[pair] = grads_ref[2 * pair + 1 - side].astype(low)


def back_tile(
    tile_index, joined_ref, dattend_ref, log_ref, bias_ref, mixed_ref, dquery_t, dkey, dvalue
):
    rows = joined_ref.shape[0]
    width = joined_ref.shape[1] // 3
    first = tile_index * LANES
    tile = slice(first, first + LANES)
    keys_t = joined_ref[:, width + first : width + first + LANES].T
    dkey[...] = jnp.zeros(dkey.shape, wide)
    dvalue[...] = jnp.zeros(dvalue.shape, wide)
    per_tile = LANES // HEAD
    inner = dattend_ref[:, tile].T.astype(wide) * mixed_ref[first : first + LANES, :]
    for local in range(per_tile):
        head = tile_index * per_tile + local
        mask = head_mask(head)
        key_tile = joined_ref[:, width + first : width + first + LANES] * mask
        value_tile = joined_ref[:, 2 * width + first : 2 * width + first + LANES] * mask
        feature = slice(local * HEAD, (local + 1) * HEAD)
        weighted = jnp.sum(inner[feature, :], axis=0, keepdims=True)
        for start, stop in query_blocks(rows):
            query = joined_ref[start:stop, tile]
            datt = dattend_ref[start:stop, tile]
            raw = dot_nt(key_tile[:stop], query)
            dprobs = dot_nt(value_tile[:stop], datt)
            logs = log_ref[head : head + 1, start:stop]
            probs, dscores = [], []
            for at in range(0, stop, CHUNK):
                piece = raw[at : at + CHUNK] * (score_scale * log2_e)
                piece = jnp.exp2(piece + bias_ref[at : at + CHUNK, start:stop] - logs)
                probs.append(piece.astype(low))
                piece = piece * (dprobs[at : at + CHUNK] - weighted[:, start:stop])
                dscores.append(piece.astype(low))
            probs = jnp.concatenate(probs, axis=0)
            dscores = jnp.concatenate(dscores, axis=0)
            dquery_t[feature, start:stop] = (
                dot_nn(keys_t[feature, :stop], dscores) * score_scale
            ).astype(low)
            dvalue[:stop, :] += dot_nn(probs, datt * mask)
            dkey[:stop, :] += dot_nn(dscores, query * mask)
    return dquery_t[...].T, (dkey[...] * score_scale).astype(low), dvalue[...].astype(low)


def back_first_kernel(*refs):
    results, scratch = refs[5:8], refs[8:]
    values = back_tile(0, *refs[:5], *scratch)
    for target, value in zip(results, values):
        target[...] = value


def back_last_kernel(shards, *refs):
    shared = refs[:5]
    earlier = refs[5:8]
    norm_ref, root_ref, middle_ref, sums_in = refs[8:12]
    pieces = refs[12 : 12 + shards]
    refs = refs[12 + shards :]
    dx_ref, keep_ref, send_ref = refs[:3]
    weight_ref, small_ref, dquery_t, dkey, dvalue, djoined, grads_ref = refs[3:]
    rows, width = norm_ref.shape
    shard = lax.axis_index("shard")
    part = width // shards
    fill_cols(weight_ref, shard, pieces, 0, part, width)
    fill_small(small_ref, shard, pieces, 3 * part)
    gain, shift = small_ref[0, 0:1, :], small_ref[0, 1:2, :]
    values = back_tile(1, *shared, dquery_t, dkey, dvalue)
    for block in range(3):
        at = block * width
        djoined[:, at : at + LANES] = earlier[block][...]
        djoined[:, at + LANES : at + 2 * LANES] = values[block]
    normed, root = norm_ref[...], root_ref[...]
    hidden_t = (normed * gain + shift).astype(low).T
    dhidden = jnp.zeros((rows, width), wide)
    bias_sums = []
    for block in range(3):
        cols = slice(block * width, (block + 1) * width)
        piece = djoined[:, cols]
        dhidden = dhidden + dot_nt(piece, weight_ref[:, cols])
        grad = dot_nn(hidden_t, piece)
        for target in range(shards):
            grads_ref[target, block * part : (block + 1) * part, :] = grad[
                target * part : (target + 1) * part, :
            ]
        if block != 1:
            bias_sums.append(jnp.sum(piece.astype(wide), axis=0, keepdims=True))
    through, gain_grad, shift_grad = norm_back(dhidden, normed, root, gain)
    dx_ref[...] = middle_ref[...] + through
    sums = [gain_grad, shift_grad, sums_in[0:1, :], sums_in[1:2, :]] + bias_sums
    sums += [sums_in[row : row + 1, :] for row in range(2, 8)]
    per_shard = len(sums) // shards
    for target in range(shards):
        at = 3 * part
        grads_ref[target, at:, :] = jnp.zeros((grads_ref.shape[1] - at, width), wide)
        for row in range(per_shard):
            grads_ref[target, at + row * TILE_ROWS : at + row * TILE_ROWS + 1, :] = sums[
                target * per_shard + row
            ]
    part_ways(grads_ref, keep_ref, send_ref, shard % 2)


def halve_kernel(axis, bit, *refs):
    count = (len(refs) - 2) // 2
    keep_ref, send_ref = refs[-2:]
    side = (lax.axis_index(axis) >> bit) & 1
    for pair in range(keep_ref.shape[0]):
        for target, index in ((keep_ref, 2 * pair + side), (send_ref, 2 * pair + 1 - side)):
            parts = []
            for chunk in range(count):
                kept, arrived = refs[2 * chunk : 2 * chunk + 2]
                parts.append(kept[index] + arrived[index].astype(wide))
            value = parts[0] if count == 1 else jnp.concatenate(parts, axis=0)
            target[pair] = value.astype(target.dtype)


def piece_spans(total, tail, group):
    spans = [((total - tail) // group, 0)]
    if tail:
        spans.append((tail // group, total - tail))
    return spans


def split_kernel(tail, *refs):
    arrived, keep_ref, send_ref, sum_ref = refs[:-3], *refs[-3:]
    group = sum_ref.shape[0]
    total = arrived[0][...]
    for piece in arrived[1:]:
        total = total + piece[...].astype(wide)
    for index in range(group):
        row = 0
        for rows, first in piece_spans(total.shape[0], tail, group):
            at = first + index * rows
            sum_ref[index, row : row + rows, :] = total[at : at + rows, :]
            row += rows
    side = lax.axis_index("dp") & 1
    for pair in range(group // 2):
        keep_ref[pair] = sum_ref[2 * pair + side]
        send_ref[pair] = sum_ref[2 * pair + 1 - side].astype(low)


def add_kernel(mine_ref, other_ref, sum_ref):
    total = mine_ref[...].astype(wide) + other_ref[...].astype(wide)
    sum_ref[...] = total.astype(low).reshape(sum_ref.shape)


def adam_values(weight, grad, first, second, decay_rate):
    first_next = beta_one * first + (1.0 - beta_one) * grad
    second_next = beta_two * second + (1.0 - beta_two) * grad * grad
    first_fix = 1.0 - beta_one**STEP
    second_fix = 1.0 - beta_two**STEP
    update = (first_next * (1.0 / first_fix)) / (
        jnp.sqrt(second_next * (1.0 / second_fix)) + adam_eps
    )
    return first_next, second_next, weight - learn_rate * (update + decay_rate * weight)


def adam_kernel(group, spans, layout, *refs):
    pieces = refs[:group]
    grad_ref = refs[-1]
    count = len(layout)
    states = refs[group : group + 3 * count]
    results = refs[group + 3 * count : -1]
    for offset, piece in enumerate(pieces):
        value = piece[...].astype(wide)
        index = (lax.axis_index("dp") & (group - 1)) ^ offset
        for rows, first, row in spans:
            at = pl.multiple_of(first + index * rows, TILE_ROWS)
            grad_ref[pl.ds(at, rows), :] = value[row : row + rows, :]
    width = grad_ref.shape[1]
    for array, (first_row, stride, decay) in enumerate(layout):
        weight, first, second = states[3 * array : 3 * array + 3]
        new = results[3 * array : 3 * array + 3]
        vector = len(weight.shape) == 1
        rows = 1 if vector else weight.shape[0]
        for block in range(weight.shape[-1] // width):
            cols = slice(block * width, (block + 1) * width)
            where = cols if vector else (slice(None), cols)
            at = first_row + block * stride
            values = adam_values(
                weight[where].reshape(rows, width),
                grad_ref[at : at + rows, :],
                first[where].reshape(rows, width),
                second[where].reshape(rows, width),
                decay,
            )
            for target, value in zip(new, values):
                target[where] = value.reshape(width) if vector else value


def local_call(kernel, outs, operands, scratch=(), flops=0, name=None, fetch=False):
    space = pltpu.HBM if fetch else pltpu.VMEM
    outs = [jax.ShapeDtypeStruct(*out) for out in outs]
    moved = sum(
        math.prod(item.shape) * item.dtype.itemsize for item in list(operands) + outs
    )
    scratch_shapes = [pltpu.VMEM(*item) for item in scratch]
    if fetch:
        scratch_shapes.append(pltpu.SemaphoreType.DMA((len(operands),)))
    return pl.pallas_call(
        kernel,
        out_shape=outs,
        in_specs=[pl.BlockSpec(memory_space=space)] * len(operands),
        out_specs=[pl.BlockSpec(memory_space=pltpu.VMEM)] * len(outs),
        scratch_shapes=scratch_shapes,
        compiler_params=pltpu.CompilerParams(vmem_limit_bytes=(56 if fetch else 40) * 1024 * 1024),
        cost_estimate=pl.CostEstimate(flops=flops, bytes_accessed=moved, transcendentals=0),
        name=name,
    )(*operands)


def exchange(values, axis, mask):
    count = lax.axis_size(axis)
    return lax.ppermute(values, axis, [(index, index ^ mask) for index in range(count)])


def gather_near(value, axis, count):
    found = {0: value}
    far = count // 2
    while far:
        for offset in sorted(found):
            found[offset ^ far] = exchange(found[offset], axis, far)
        far //= 2
    return [found[offset] for offset in range(count)]


def halve_call(axis, bit, flat, name):
    half, _, width = flat[0].shape
    shape = (half // 2, sum(item.shape[1] for item in flat[::2]), width)
    return local_call(
        functools.partial(halve_kernel, axis, bit), [(shape, wide), (shape, low)], flat, name=name
    )


def split_chunk(chunk, tail, group):
    rows, width = chunk[0].shape
    half = (group // 2, rows // group, width)
    keep, send = local_call(
        functools.partial(split_kernel, tail),
        [(half, wide), (half, low)],
        chunk,
        [((group,) + half[1:], wide)],
        name="split_sum",
    )
    return keep, exchange(send, "dp", 1)


def finish_sum(chunks, group):
    replicas = lax.axis_size("dp")
    half, _, width = chunks[0][0].shape
    rows = sum(chunk[0].shape[1] for chunk in chunks)
    flat = [item for chunk in chunks for item in chunk]
    bit = 1
    while half > 1:
        half //= 2
        keep, send = halve_call("dp", bit, flat, "halve_dp")
        flat = [keep, exchange(send, "dp", 1 << bit)]
        bit += 1
    mask = group
    (piece,) = local_call(add_kernel, [((rows, width), low)], flat, name="piece_sum")
    while mask < replicas:
        other = exchange(piece, "dp", mask)
        (piece,) = local_call(add_kernel, [((rows, width), low)], [piece, other], name="far_sum")
        mask *= 2
    return gather_near(piece, "dp", group)


def adam_call(pieces, counts, tails, states, layout):
    group = len(pieces)
    width = pieces[0].shape[1]
    spans = []
    first = row = 0
    for total, tail in zip(counts, tails):
        for rows, start in piece_spans(total, tail, group):
            spans.append((rows, first + start, row))
            row += rows
        first += total
    return local_call(
        functools.partial(adam_kernel, group, spans, layout),
        [(state[0].shape, wide) for state in states for _ in range(3)],
        pieces + [item for state in states for item in state],
        [((first, width), wide)],
        name="adam",
    )


def shards_program(
    tokens,
    cotangent,
    lengths,
    seq_owner,
    qkv_weight,
    out_weight,
    up_weight,
    down_weight,
    gains_biases,
    qkv_first,
    qkv_second,
    out_first,
    out_second,
    up_first,
    up_second,
    down_first,
    down_second,
    small_first,
    small_second,
):
    rows, width = tokens.shape
    shards = lax.axis_size("shard")
    heads = width // HEAD
    part = qkv_weight.shape[0]
    hidden_count = up_weight.shape[1]
    group = min(GROUP, lax.axis_size("dp"))
    lengths = lengths.reshape(1, -1)
    seq_owner = seq_owner.reshape(1, -1)
    first_rows = 3 * part + SMALL_PAD
    second_rows = part + up_weight.size // width + down_weight.shape[0]
    (first_pack,) = local_call(
        pack_first_kernel,
        [((first_rows, width), low)],
        [qkv_weight, gains_biases],
        [(qkv_weight.shape, wide), (gains_biases.shape, wide)],
        name="pack_first",
        fetch=True,
    )
    firsts = {0: first_pack}
    firsts[2] = exchange(first_pack, "shard", 2)
    firsts[1] = exchange(first_pack, "shard", 1)
    square = (rows, rows)
    bias, normed, root, seed = local_call(
        functools.partial(prepare_kernel, shards),
        [(square, wide), ((rows, width), wide), ((rows, 1), wide), ((rows, width), low)],
        [tokens, cotangent, lengths, seq_owner],
        name="prepare",
    )
    matrices = [out_weight, up_weight, down_weight]
    (second_pack,) = local_call(
        pack_second_kernel,
        [((second_rows, width), low)],
        matrices,
        [(item.shape, wide) for item in matrices],
        name="pack_second",
        fetch=True,
    )
    firsts[2], second_pack, bias, normed, root, seed = lax.optimization_barrier(
        (firsts[2], second_pack, bias, normed, root, seed)
    )
    firsts[3] = exchange(firsts[2], "shard", 1)
    firsts = [firsts[offset] for offset in range(shards)]
    seconds = {0: second_pack}
    seconds[2] = exchange(second_pack, "shard", 2)
    seconds[1] = exchange(second_pack, "shard", 1)
    joined, attended, log_sums, mixed = local_call(
        functools.partial(attend_kernel, shards),
        [
            ((rows, 3 * width), low),
            ((rows, width), low),
            ((heads, rows), wide),
            ((width, rows), wide),
        ],
        [normed, bias] + firsts,
        [((width, 3 * width), low), ((shards, SMALL_PAD, width), wide)],
        flops=heads * rows * rows * 256 * 4,
        name="attend",
    )
    attended, seconds[2] = lax.optimization_barrier((attended, seconds[2]))
    seconds[3] = exchange(seconds[2], "shard", 1)
    seconds = [seconds[offset] for offset in range(shards)]
    pair = (shards // 2, second_rows, width)
    output, middle_grad, attended_grad, sums, kept_ffn, send_ffn = local_call(
        functools.partial(feed_kernel, shards),
        [
            ((rows, width), low),
            ((rows, width), wide),
            ((rows, width), low),
            ((SMALL_PAD, width), wide),
            (pair, wide),
            (pair, low),
        ],
        [tokens, attended, seed] + firsts + seconds,
        [
            ((shards, SMALL_PAD, width), wide),
            ((width, width), low),
            ((width, hidden_count), low),
            ((hidden_count, width), low),
            ((shards, second_rows, width), wide),
        ],
        flops=rows * width * (hidden_count * 12 + width * 6),
        name="feed",
    )
    arrived_ffn = exchange(send_ffn, "shard", 1)
    shared = [joined, attended_grad, log_sums, bias, mixed]
    tile_scratch = [((LANES, rows), low), ((rows, LANES), wide), ((rows, LANES), wide)]
    first_query, first_key, first_value = local_call(
        back_first_kernel,
        [((rows, LANES), low)] * 3,
        shared,
        tile_scratch,
        flops=heads * rows * rows * 256 * 5,
        name="back_first",
    )
    first_query, arrived_ffn = lax.optimization_barrier((first_query, arrived_ffn))
    keep_ffn, send_ffn = halve_call("shard", 1, [kept_ffn, arrived_ffn], "halve_ffn")
    first_query, send_ffn = lax.optimization_barrier((first_query, send_ffn))
    arrived_ffn = exchange(send_ffn, "shard", 2)
    tail = GROUP * TILE_ROWS
    att_rows = 3 * part + tail
    pair = (shards // 2, att_rows, width)
    input_grad, kept_att, send_att = local_call(
        functools.partial(back_last_kernel, shards),
        [((rows, width), wide), (pair, wide), (pair, low)],
        shared + [first_query, first_key, first_value, normed, root, middle_grad, sums] + firsts,
        [((width, 3 * width), low), ((shards, SMALL_PAD, width), wide)]
        + tile_scratch
        + [((rows, 3 * width), low), ((shards, att_rows, width), wide)],
        flops=heads * rows * rows * 256 * 6,
        name="back_last",
    )
    arrived_att = exchange(send_att, "shard", 1)
    keep_att, send_att = halve_call("shard", 1, [kept_att, arrived_att], "halve_att")
    send_att, arrived_ffn = lax.optimization_barrier((send_att, arrived_ffn))
    tails = (0, tail)
    arrived_att = exchange(send_att, "shard", 2)
    chunk_ffn = split_chunk([keep_ffn[0], arrived_ffn[0]], 0, group)
    chunk_att = split_chunk([keep_att[0], arrived_att[0]], tail, group)
    pieces = finish_sum([chunk_ffn, chunk_att], group)
    blocks = hidden_count // width
    results = adam_call(
        pieces,
        (second_rows, att_rows),
        tails,
        [
            (qkv_weight, qkv_first, qkv_second),
            (out_weight, out_first, out_second),
            (up_weight, up_first, up_second),
            (down_weight, down_first, down_second),
            (gains_biases, small_first, small_second),
        ],
        [
            (second_rows, part, matrix_decay),
            (0, part, matrix_decay),
            (part, part, matrix_decay),
            (part + blocks * part, 0, matrix_decay),
            (second_rows + 3 * part, TILE_ROWS, 0.0),
        ],
    )
    return (output, input_grad, *results)


def solution(mesh):
    rows = P(("dp", "shard"), None)
    matrix = P("shard", None)
    vector = P("shard")
    return jax.shard_map(
        shards_program,
        mesh=mesh,
        in_specs=(rows, rows, P(), P())
        + (matrix,) * 4
        + (vector,)
        + (matrix,) * 8
        + (vector, vector),
        out_specs=(rows, rows) + (matrix,) * 12 + (vector,) * 3,
        check_vma=False,
    )
```

```python
import functools
import math

import jax
import jax.numpy as jnp
from jax import lax
from jax.experimental import pallas as pl
from jax.experimental.pallas import tpu as pltpu
from jax.sharding import PartitionSpec as P

HEAD = 32
STEP = 10
LANES = 128
GROUP = 8
SMALL_PAD = 16
TILE_ROWS = 8
CHUNK = 64

norm_eps = 1e-05
beta_one = 0.9
beta_two = 0.95
learn_rate = 0.1
adam_eps = 1e-08
matrix_decay = 0.1
masked_score = -1e30
low = jnp.bfloat16
wide = jnp.float32
log2_e = math.log2(math.e)
score_scale = 1.0 / math.sqrt(HEAD)
tanh_scale = math.sqrt(2.0 / math.pi)
cubic = 0.044715


def dot_nn(left, right):
    return jnp.dot(left, right, preferred_element_type=wide)


def dot_nt(left, right):
    return lax.dot_general(left, right, (((1,), (1,)), ((), ())), preferred_element_type=wide)


def standardize(values):
    centered = values - jnp.mean(values, axis=-1, keepdims=True)
    root_inv = lax.rsqrt(jnp.mean(centered * centered, axis=-1, keepdims=True) + norm_eps)
    return centered * root_inv, root_inv


def norm_back(upstream, normed, root_inv, gain):
    scaled = upstream * gain
    inner_mean = jnp.mean(scaled, axis=-1, keepdims=True)
    cross_mean = jnp.mean(scaled * normed, axis=-1, keepdims=True)
    through = root_inv * (scaled - inner_mean - normed * cross_mean)
    return (
        through,
        jnp.sum(upstream * normed, axis=0, keepdims=True),
        jnp.sum(upstream, axis=0, keepdims=True),
    )


def iota(shape, dim):
    return lax.broadcasted_iota(jnp.int32, shape, dim)


def own_row(lengths, owners, device):
    return jnp.where(owners == device, lengths, 0)


def ends_both(own):
    count = own.shape[1]
    shape = (count, count)
    rows, cols = iota(shape, 0), iota(shape, 1)
    spread = jnp.broadcast_to(own, shape)
    ends_col = jnp.sum(jnp.where(cols <= rows, spread, 0), axis=1, keepdims=True)
    own_col = jnp.sum(jnp.where(cols == rows, spread, 0), axis=1, keepdims=True)
    ends_row = jnp.sum(
        jnp.where(rows <= cols, jnp.broadcast_to(own_col, shape), 0), axis=0, keepdims=True
    )
    return ends_col, ends_row


def fill_mask(bias_ref, own, rows):
    ends_col, ends_row = ends_both(own)
    count = own.shape[1]
    seg_row = jnp.sum(
        (ends_col <= iota((count, rows), 1)).astype(jnp.int32), axis=0, keepdims=True
    )
    seg_col = jnp.sum(
        (ends_row <= iota((rows, count), 0)).astype(jnp.int32), axis=1, keepdims=True
    )
    allowed = (seg_row == seg_col) & (iota((rows, rows), 0) <= iota((rows, rows), 1))
    bias_ref[...] = jnp.where(allowed, 0.0, masked_score)


def fill_small(small_ref, shard, pieces, first_row):
    for offset, piece in enumerate(pieces):
        small_ref[shard ^ offset] = piece[first_row:, :].astype(wide)


def fill_cols(full_ref, shard, pieces, first_row, rows, width):
    blocks = full_ref.shape[1] // width
    for offset, piece in enumerate(pieces):
        at = pl.multiple_of((shard ^ offset) * rows, rows)
        for block in range(blocks):
            start = first_row + block * rows
            full_ref[pl.ds(at, rows), block * width : (block + 1) * width] = piece[
                start : start + rows, :
            ]


def head_mask(head):
    lane = iota((1, LANES), 1)
    first = head * HEAD % LANES
    return ((lane >= first) & (lane < first + HEAD)).astype(wide).astype(low)


def head_tile(head):
    first = head * HEAD // LANES * LANES
    return slice(first, first + LANES)


def query_blocks(rows):
    size = min(256, rows)
    return [(at, at + size) for at in range(0, rows, size)]


def put_blocks(target, row, source, width):
    rows = source.shape[0]
    for block in range(source.shape[1] // width):
        cols = slice(block * width, (block + 1) * width)
        target[row : row + rows, :] = source[:, cols].astype(low)
        row += rows
    return row


def fetch_all(sources, buffers, sems):
    copies = [
        pltpu.make_async_copy(source, buffer, sems.at[index])
        for index, (source, buffer) in enumerate(zip(sources, buffers))
    ]
    for copy in copies:
        copy.start()
    return copies


def pack_first_kernel(qkv_ref, small_ref, first_ref, qkv_buf, small_buf, sems):
    width = first_ref.shape[1]
    small_copy, qkv_copy = fetch_all((small_ref, qkv_ref), (small_buf, qkv_buf), sems)
    small_copy.wait()
    parts = [
        small_buf[block * width : (block + 1) * width].reshape(1, width)
        for block in range(small_buf.shape[0] // width)
    ]
    parts.append(jnp.zeros((SMALL_PAD - len(parts), width), wide))
    first_ref[first_ref.shape[0] - SMALL_PAD :, :] = jnp.concatenate(parts, axis=0).astype(low)
    qkv_copy.wait()
    put_blocks(first_ref, 0, qkv_buf, width)


def pack_second_kernel(out_ref, up_ref, down_ref, second_ref, out_buf, up_buf, down_buf, sems):
    width = second_ref.shape[1]
    buffers = (out_buf, up_buf, down_buf)
    copies = fetch_all((out_ref, up_ref, down_ref), buffers, sems)
    row = 0
    for copy, buffer in zip(copies, buffers):
        copy.wait()
        row = put_blocks(second_ref, row, buffer, width)


def prepare_kernel(shards, x_ref, seed_ref, len_ref, owner_ref, bias_ref, norm_ref, root_ref, low_ref):
    rows = x_ref.shape[0]
    device = lax.axis_index("dp") * shards + lax.axis_index("shard")
    own = own_row(len_ref[...], owner_ref[...], device)
    fill_mask(bias_ref, own, rows)
    normed, root = standardize(x_ref[...].astype(wide))
    norm_ref[...] = normed
    root_ref[...] = root
    live = jnp.sum(own, axis=1, keepdims=True)
    live_rows = (iota((rows, 1), 0) < live).astype(wide)
    low_ref[...] = (seed_ref[...].astype(wide) * live_rows).astype(low)


def attend_kernel(shards, *refs):
    norm_ref, bias_ref = refs[:2]
    pieces = refs[2 : 2 + shards]
    joined_ref, out_ref, log_ref, att_ref, weight_ref, small_ref = refs[2 + shards :]
    rows, width = norm_ref.shape
    shard = lax.axis_index("shard")
    part = width // shards
    fill_cols(weight_ref, shard, pieces, 0, part, width)
    fill_small(small_ref, shard, pieces, 3 * part)
    gain, shift = small_ref[0, 0:1, :], small_ref[0, 1:2, :]
    bias_query, bias_value = small_ref[1, 1:2, :], small_ref[1, 2:3, :]
    hidden = (norm_ref[...] * gain + shift).astype(low)
    for block, bias in enumerate((bias_query, None, bias_value)):
        cols = slice(block * width, (block + 1) * width)
        value = dot_nn(hidden, weight_ref[:, cols])
        if bias is not None:
            value = value + bias
        joined_ref[:, cols] = value.astype(low)
    values_t = joined_ref[:, 2 * width :].T
    units = [
        (head, start, stop) for head in range(width // HEAD) for start, stop in query_blocks(rows)
    ]

    def raw_scores(head, start, stop):
        tile = head_tile(head)
        key_tile = joined_ref[:stop, width + tile.start : width + tile.stop] * head_mask(head)
        return dot_nt(key_tile, joined_ref[start:stop, tile])

    ahead = raw_scores(*units[0])
    for index, (head, start, stop) in enumerate(units):
        raw = ahead
        if index + 1 < len(units):
            ahead = raw_scores(*units[index + 1])
        feature = slice(head * HEAD, (head + 1) * HEAD)
        scores = []
        top = None
        for at in range(0, stop, CHUNK):
            piece = raw[at : at + CHUNK] * (score_scale * log2_e)
            piece = piece + bias_ref[at : at + CHUNK, start:stop]
            scores.append(piece)
            top = piece if top is None else jnp.maximum(top, piece)
        top = jnp.max(top, axis=0, keepdims=True)
        exponents = []
        total = None
        for piece in scores:
            piece = jnp.exp2(piece - top)
            total = piece if total is None else total + piece
            exponents.append(piece.astype(low))
        total = jnp.sum(total, axis=0, keepdims=True)
        mixed = dot_nn(values_t[feature, :stop], jnp.concatenate(exponents, axis=0))
        att_ref[feature, start:stop] = mixed * (1.0 / total)
        log_ref[head : head + 1, start:stop] = top + jnp.log2(total)
    out_ref[...] = att_ref[...].astype(low).T


def feed_kernel(shards, *refs):
    x_ref, att_ref, seed_ref = refs[:3]
    firsts = refs[3 : 3 + shards]
    pieces = refs[3 + shards : 3 + 2 * shards]
    refs = refs[3 + 2 * shards :]
    out_ref, middle_ref, dattend_ref, sums_ref, keep_ref, send_ref = refs[:6]
    small_ref, out_w, up_w, down_w, grads_ref = refs[6:]
    rows, width = x_ref.shape
    hidden_count = up_w.shape[1]
    shard = lax.axis_index("shard")
    part = width // shards
    blocks = hidden_count // width
    down_part = hidden_count // shards
    fill_small(small_ref, shard, firsts, 3 * part)
    fill_cols(out_w, shard, pieces, 0, part, width)
    fill_cols(up_w, shard, pieces, part, part, width)
    fill_cols(down_w, shard, pieces, part + blocks * part, down_part, width)
    gain, shift = small_ref[0, 2:3, :], small_ref[1, 0:1, :]
    bias_out, bias_down = small_ref[2, 0:1, :], small_ref[2, 1:2, :]
    bias_up = [small_ref[2, 2:3, :]] + [small_ref[3, row : row + 1, :] for row in range(3)]
    seed_low = seed_ref[...]
    seed = seed_low.astype(wide)
    attended = att_ref[...]
    middle = x_ref[...].astype(wide) + (dot_nn(attended, out_w[...]) + bias_out)
    normed, root = standardize(middle)
    hidden = (normed * gain + shift).astype(low)
    hidden_t = hidden.T
    result = middle + bias_down
    dhidden = jnp.zeros((rows, width), wide)
    sums_ref[...] = jnp.zeros(sums_ref.shape, wide)

    def raw_products(block):
        cols = slice(block * width, (block + 1) * width)
        return dot_nn(hidden, up_w[:, cols]), dot_nt(seed_low, down_w[cols, :])

    ahead = raw_products(0)
    for block in range(blocks):
        cols = slice(block * width, (block + 1) * width)
        raw, dact = ahead
        if block + 1 < blocks:
            ahead = raw_products(block + 1)
        act, dpre = [], []
        for at in range(0, rows, CHUNK):
            pre = raw[at : at + CHUNK] + bias_up[block]
            square = pre * pre
            bend = jnp.tanh(pre * (tanh_scale + (tanh_scale * cubic) * square))
            half = 0.5 + 0.5 * bend
            act.append((pre * half).astype(low))
            slope = 0.5 * tanh_scale + (1.5 * tanh_scale * cubic) * square
            slope = half + (pre * slope) * (1.0 - bend * bend)
            dpre.append((dact[at : at + CHUNK] * slope).astype(low))
        act = jnp.concatenate(act, axis=0)
        dpre = jnp.concatenate(dpre, axis=0)
        result = result + dot_nn(act, down_w[cols, :])
        dhidden = dhidden + dot_nt(dpre, up_w[:, cols])
        grad_down = dot_nn(act.T, seed_low)
        grad_up = dot_nn(hidden_t, dpre)
        for piece in range(width // down_part):
            target = block * (width // down_part) + piece
            at = part + blocks * part
            grads_ref[target, at : at + down_part, :] = grad_down[
                piece * down_part : (piece + 1) * down_part, :
            ]
        for target in range(shards):
            at = part + block * part
            grads_ref[target, at : at + part, :] = grad_up[target * part : (target + 1) * part, :]
        sums_ref[4 + block : 5 + block, :] = jnp.sum(dpre.astype(wide), axis=0, keepdims=True)
    out_ref[...] = result.astype(low)
    through, gain_grad, shift_grad = norm_back(dhidden, normed, root, gain)
    dmiddle = seed + through
    middle_ref[...] = dmiddle
    dmiddle_low = dmiddle.astype(low)
    grad_out = dot_nn(attended.T, dmiddle_low)
    for target in range(shards):
        grads_ref[target, :part, :] = grad_out[target * part : (target + 1) * part, :]
    dattend_ref[...] = dot_nt(dmiddle_low, out_w[...]).astype(low)
    sums_ref[0:1, :] = gain_grad
    sums_ref[1:2, :] = shift_grad
    sums_ref[2:3, :] = jnp.sum(dmiddle_low.astype(wide), axis=0, keepdims=True)
    sums_ref[3:4, :] = jnp.sum(seed, axis=0, keepdims=True)
    part_ways(grads_ref, keep_ref, send_ref, shard % 2)


def part_ways(grads_ref, keep_ref, send_ref, side):
    for pair in range(keep_ref.shape[0]):
        keep_ref[pair] = grads_ref[2 * pair + side]
        send_ref[pair] = grads_ref[2 * pair + 1 - side].astype(low)


def back_heads(
    heads, joined_ref, dattend_ref, log_ref, bias_ref, mixed_ref, dquery_t, dkey, dvalue
):
    rows = joined_ref.shape[0]
    width = joined_ref.shape[1] // 3
    first = heads[0] * HEAD
    count = len(heads) * HEAD
    base = first // LANES * LANES
    tile = slice(base, base + LANES)
    inside = slice(first - base, first - base + count)
    keys_t = joined_ref[:, width + base : width + base + LANES].T
    datt_t = dattend_ref[:, tile].T[inside]
    inner = datt_t.astype(wide) * mixed_ref[first : first + count, :]
    units = [(head, start, stop) for head in heads for start, stop in query_blocks(rows)]

    def raw_products(head, start, stop):
        mask = head_mask(head)
        key_tile = joined_ref[:stop, width + base : width + base + LANES] * mask
        value_tile = joined_ref[:stop, 2 * width + base : 2 * width + base + LANES] * mask
        query = joined_ref[start:stop, tile]
        datt = dattend_ref[start:stop, tile]
        return dot_nt(key_tile, query), dot_nt(value_tile, datt), query * mask, datt * mask

    ahead = raw_products(*units[0])
    for index, (head, start, stop) in enumerate(units):
        raw, dprobs, query, datt = ahead
        if index + 1 < len(units):
            ahead = raw_products(*units[index + 1])
        local = head * HEAD - first
        feature = slice(local, local + HEAD)
        weighted = jnp.sum(inner[feature, start:stop], axis=0, keepdims=True)
        logs = log_ref[head : head + 1, start:stop]
        probs, dscores = [], []
        for at in range(0, stop, CHUNK):
            piece = raw[at : at + CHUNK] * (score_scale * log2_e)
            piece = jnp.exp2(piece + bias_ref[at : at + CHUNK, start:stop] - logs)
            probs.append(piece.astype(low))
            piece = piece * (dprobs[at : at + CHUNK] - weighted)
            dscores.append(piece.astype(low))
        probs = jnp.concatenate(probs, axis=0)
        dscores = jnp.concatenate(dscores, axis=0)
        depth = slice(head * HEAD - base, head * HEAD - base + HEAD)
        dquery_t[depth, start:stop] = (
            dot_nn(keys_t[depth, :stop], dscores) * score_scale
        ).astype(low)
        dvalue[:stop, :] += dot_nn(probs, datt)
        dkey[:stop, :] += dot_nn(dscores, query)


def back_first_kernel(heads, *refs):
    dquery_t, dkey, dvalue = refs[5:8]
    dkey[...] = jnp.zeros(dkey.shape, wide)
    dvalue[...] = jnp.zeros(dvalue.shape, wide)
    dquery_t[...] = jnp.zeros(dquery_t.shape, low)
    back_heads(heads, *refs)


def back_last_kernel(shards, groups, *refs):
    shared = refs[:5]
    earlier = refs[5:8]
    norm_ref, root_ref, middle_ref, sums_in = refs[8:12]
    pieces = refs[12 : 12 + shards]
    refs = refs[12 + shards :]
    dx_ref, keep_ref, send_ref = refs[:3]
    weight_ref, small_ref, dquery_t, dkey, dvalue, djoined, grads_ref = refs[3:]
    rows, width = norm_ref.shape
    shard = lax.axis_index("shard")
    part = width // shards
    fill_cols(weight_ref, shard, pieces, 0, part, width)
    fill_small(small_ref, shard, pieces, 3 * part)
    gain, shift = small_ref[0, 0:1, :], small_ref[0, 1:2, :]
    for target, value in zip((dquery_t, dkey, dvalue), earlier):
        target[...] = value[...]
    for index, heads in enumerate(groups):
        back_heads(heads, *shared, dquery_t, dkey, dvalue)
        if (heads[-1] + 1) * HEAD % LANES == 0:
            first = (heads[-1] + 1) * HEAD - LANES
            values = (dquery_t[...].T, dkey[...] * score_scale, dvalue[...])
            for block, value in enumerate(values):
                at = block * width + first
                djoined[:, at : at + LANES] = value.astype(low)
            dkey[...] = jnp.zeros(dkey.shape, wide)
            dvalue[...] = jnp.zeros(dvalue.shape, wide)
    normed, root = norm_ref[...], root_ref[...]
    hidden_t = (normed * gain + shift).astype(low).T
    dhidden = jnp.zeros((rows, width), wide)
    bias_sums = []
    for block in range(3):
        cols = slice(block * width, (block + 1) * width)
        piece = djoined[:, cols]
        dhidden = dhidden + dot_nt(piece, weight_ref[:, cols])
        grad = dot_nn(hidden_t, piece)
        for target in range(shards):
            grads_ref[target, block * part : (block + 1) * part, :] = grad[
                target * part : (target + 1) * part, :
            ]
        if block != 1:
            bias_sums.append(jnp.sum(piece.astype(wide), axis=0, keepdims=True))
    through, gain_grad, shift_grad = norm_back(dhidden, normed, root, gain)
    dx_ref[...] = middle_ref[...] + through
    sums = [gain_grad, shift_grad, sums_in[0:1, :], sums_in[1:2, :]] + bias_sums
    sums += [sums_in[row : row + 1, :] for row in range(2, 8)]
    per_shard = len(sums) // shards
    for target in range(shards):
        at = 3 * part
        grads_ref[target, at:, :] = jnp.zeros((grads_ref.shape[1] - at, width), wide)
        for row in range(per_shard):
            grads_ref[target, at + row * TILE_ROWS : at + row * TILE_ROWS + 1, :] = sums[
                target * per_shard + row
            ]
    part_ways(grads_ref, keep_ref, send_ref, shard % 2)


def halve_kernel(axis, bit, *refs):
    count = (len(refs) - 2) // 2
    keep_ref, send_ref = refs[-2:]
    side = (lax.axis_index(axis) >> bit) & 1
    for pair in range(keep_ref.shape[0]):
        for target, index in ((keep_ref, 2 * pair + side), (send_ref, 2 * pair + 1 - side)):
            parts = []
            for chunk in range(count):
                kept, arrived = refs[2 * chunk : 2 * chunk + 2]
                parts.append(kept[index] + arrived[index].astype(wide))
            value = parts[0] if count == 1 else jnp.concatenate(parts, axis=0)
            target[pair] = value.astype(target.dtype)


def piece_spans(total, tail, group):
    spans = [((total - tail) // group, 0)]
    if tail:
        spans.append((tail // group, total - tail))
    return spans


def split_kernel(tail, *refs):
    arrived, keep_ref, send_ref, sum_ref = refs[:-3], *refs[-3:]
    group = sum_ref.shape[0]
    total = arrived[0][...]
    for piece in arrived[1:]:
        total = total + piece[...].astype(wide)
    for index in range(group):
        row = 0
        for rows, first in piece_spans(total.shape[0], tail, group):
            at = first + index * rows
            sum_ref[index, row : row + rows, :] = total[at : at + rows, :]
            row += rows
    side = lax.axis_index("dp") & 1
    for pair in range(group // 2):
        keep_ref[pair] = sum_ref[2 * pair + side]
        send_ref[pair] = sum_ref[2 * pair + 1 - side].astype(low)


def add_kernel(mine_ref, other_ref, sum_ref):
    total = mine_ref[...].astype(wide) + other_ref[...].astype(wide)
    sum_ref[...] = total.astype(low).reshape(sum_ref.shape)


def adam_values(weight, grad, first, second, decay_rate):
    first_next = beta_one * first + (1.0 - beta_one) * grad
    second_next = beta_two * second + (1.0 - beta_two) * grad * grad
    first_fix = 1.0 - beta_one**STEP
    second_fix = 1.0 - beta_two**STEP
    update = (first_next * (1.0 / first_fix)) / (
        jnp.sqrt(second_next * (1.0 / second_fix)) + adam_eps
    )
    return first_next, second_next, weight - learn_rate * (update + decay_rate * weight)


def adam_kernel(group, spans, layout, *refs):
    pieces = refs[:group]
    count = len(layout)
    states = refs[group : group + 3 * count]
    results = refs[group + 3 * count : group + 6 * count]
    buffers = refs[group + 6 * count : group + 9 * count]
    grad_ref, sems = refs[-2:]
    copies = []
    for offset, piece in enumerate(pieces):
        value = piece[...].astype(wide)
        index = (lax.axis_index("dp") & (group - 1)) ^ offset
        for rows, first, row in spans:
            at = pl.multiple_of(first + index * rows, TILE_ROWS)
            grad_ref[pl.ds(at, rows), :] = value[row : row + rows, :]
    width = grad_ref.shape[1]
    for array, (first_row, stride, decay) in enumerate(layout):
        weight, first, second = states[3 * array : 3 * array + 3]
        new = buffers[3 * array : 3 * array + 3]
        vector = len(weight.shape) == 1
        rows = 1 if vector else weight.shape[0]
        for block in range(weight.shape[-1] // width):
            cols = slice(block * width, (block + 1) * width)
            where = cols if vector else (slice(None), cols)
            at = first_row + block * stride
            values = adam_values(
                weight[where].reshape(rows, width),
                grad_ref[at : at + rows, :],
                first[where].reshape(rows, width),
                second[where].reshape(rows, width),
                decay,
            )
            for target, value in zip(new, values):
                target[where] = value.reshape(width) if vector else value
        for index in range(3 * array, 3 * array + 3):
            copies.append(
                pltpu.make_async_copy(buffers[index], results[index], sems.at[index])
            )
            copies[-1].start()
    for copy in copies:
        copy.wait()


def local_call(kernel, outs, operands, scratch=(), flops=0, name=None, fetch=False, sems=0):
    in_space = pltpu.HBM if fetch else pltpu.VMEM
    out_space = pltpu.HBM if sems else pltpu.VMEM
    outs = [jax.ShapeDtypeStruct(*out) for out in outs]
    moved = sum(
        math.prod(item.shape) * item.dtype.itemsize for item in list(operands) + outs
    )
    scratch_shapes = [pltpu.VMEM(*item) for item in scratch]
    if fetch or sems:
        scratch_shapes.append(pltpu.SemaphoreType.DMA((sems or len(operands),)))
    limit = 56 if fetch else 40
    return pl.pallas_call(
        kernel,
        out_shape=outs,
        in_specs=[pl.BlockSpec(memory_space=in_space)] * len(operands),
        out_specs=[pl.BlockSpec(memory_space=out_space)] * len(outs),
        scratch_shapes=scratch_shapes,
        compiler_params=pltpu.CompilerParams(vmem_limit_bytes=limit * 1024 * 1024),
        cost_estimate=pl.CostEstimate(flops=flops, bytes_accessed=moved, transcendentals=0),
        name=name,
    )(*operands)


def exchange(values, axis, mask):
    count = lax.axis_size(axis)
    return lax.ppermute(values, axis, [(index, index ^ mask) for index in range(count)])


def gather_near(value, axis, count):
    found = {0: value}
    far = count // 2
    while far:
        for offset in sorted(found):
            found[offset ^ far] = exchange(found[offset], axis, far)
        far //= 2
    return [found[offset] for offset in range(count)]


def halve_call(axis, bit, flat, name):
    half, _, width = flat[0].shape
    shape = (half // 2, sum(item.shape[1] for item in flat[::2]), width)
    return local_call(
        functools.partial(halve_kernel, axis, bit), [(shape, wide), (shape, low)], flat, name=name
    )


def split_chunk(chunk, tail, group):
    rows, width = chunk[0].shape
    half = (group // 2, rows // group, width)
    keep, send = local_call(
        functools.partial(split_kernel, tail),
        [(half, wide), (half, low)],
        chunk,
        [((group,) + half[1:], wide)],
        name="split_sum",
    )
    return keep, exchange(send, "dp", 1)


def finish_sum(chunks, group):
    replicas = lax.axis_size("dp")
    half, _, width = chunks[0][0].shape
    rows = sum(chunk[0].shape[1] for chunk in chunks)
    flat = [item for chunk in chunks for item in chunk]
    bit = 1
    while half > 1:
        half //= 2
        keep, send = halve_call("dp", bit, flat, "halve_dp")
        flat = [keep, exchange(send, "dp", 1 << bit)]
        bit += 1
    mask = group
    (piece,) = local_call(add_kernel, [((rows, width), low)], flat, name="piece_sum")
    while mask < replicas:
        other = exchange(piece, "dp", mask)
        (piece,) = local_call(add_kernel, [((rows, width), low)], [piece, other], name="far_sum")
        mask *= 2
    return gather_near(piece, "dp", group)


def adam_call(pieces, counts, tails, states, layout):
    group = len(pieces)
    width = pieces[0].shape[1]
    spans = []
    first = row = 0
    for total, tail in zip(counts, tails):
        for rows, start in piece_spans(total, tail, group):
            spans.append((rows, first + start, row))
            row += rows
        first += total
    outs = [(state[0].shape, wide) for state in states for _ in range(3)]
    return local_call(
        functools.partial(adam_kernel, group, spans, layout),
        outs,
        pieces + [item for state in states for item in state],
        outs + [((first, width), wide)],
        name="adam",
        sems=len(outs),
    )


def shards_program(
    tokens,
    cotangent,
    lengths,
    seq_owner,
    qkv_weight,
    out_weight,
    up_weight,
    down_weight,
    gains_biases,
    qkv_first,
    qkv_second,
    out_first,
    out_second,
    up_first,
    up_second,
    down_first,
    down_second,
    small_first,
    small_second,
):
    rows, width = tokens.shape
    shards = lax.axis_size("shard")
    heads = width // HEAD
    part = qkv_weight.shape[0]
    hidden_count = up_weight.shape[1]
    group = min(GROUP, lax.axis_size("dp"))
    lengths = lengths.reshape(1, -1)
    seq_owner = seq_owner.reshape(1, -1)
    first_rows = 3 * part + SMALL_PAD
    second_rows = part + up_weight.size // width + down_weight.shape[0]
    (first_pack,) = local_call(
        pack_first_kernel,
        [((first_rows, width), low)],
        [qkv_weight, gains_biases],
        [(qkv_weight.shape, wide), (gains_biases.shape, wide)],
        name="pack_first",
        fetch=True,
    )
    firsts = {0: first_pack}
    firsts[2] = exchange(first_pack, "shard", 2)
    firsts[1] = exchange(first_pack, "shard", 1)
    first_pack, matrices = lax.optimization_barrier(
        (first_pack, [out_weight, up_weight, down_weight])
    )
    (second_pack,) = local_call(
        pack_second_kernel,
        [((second_rows, width), low)],
        matrices,
        [(item.shape, wide) for item in matrices],
        name="pack_second",
        fetch=True,
    )
    early_tokens, second_pack = lax.optimization_barrier((tokens, second_pack))
    square = (rows, rows)
    bias, normed, root, seed = local_call(
        functools.partial(prepare_kernel, shards),
        [(square, wide), ((rows, width), wide), ((rows, 1), wide), ((rows, width), low)],
        [early_tokens, cotangent, lengths, seq_owner],
        name="prepare",
    )
    seconds = {0: second_pack}
    seconds[2] = exchange(second_pack, "shard", 2)
    seconds[1] = exchange(second_pack, "shard", 1)
    firsts[2], bias, normed, root, seed = lax.optimization_barrier(
        (firsts[2], bias, normed, root, seed)
    )
    firsts[3] = exchange(firsts[2], "shard", 1)
    firsts = [firsts[offset] for offset in range(shards)]
    joined, attended, log_sums, mixed = local_call(
        functools.partial(attend_kernel, shards),
        [
            ((rows, 3 * width), low),
            ((rows, width), low),
            ((heads, rows), wide),
            ((width, rows), wide),
        ],
        [normed, bias] + firsts,
        [((width, 3 * width), low), ((shards, SMALL_PAD, width), wide)],
        flops=heads * rows * rows * 640,
        name="attend",
    )
    attended, seconds[2] = lax.optimization_barrier((attended, seconds[2]))
    seconds[3] = exchange(seconds[2], "shard", 1)
    seconds = [seconds[offset] for offset in range(shards)]
    pair = (shards // 2, second_rows, width)
    output, middle_grad, attended_grad, sums, kept_ffn, send_ffn = local_call(
        functools.partial(feed_kernel, shards),
        [
            ((rows, width), low),
            ((rows, width), wide),
            ((rows, width), low),
            ((SMALL_PAD, width), wide),
            (pair, wide),
            (pair, low),
        ],
        [tokens, attended, seed] + firsts + seconds,
        [
            ((shards, SMALL_PAD, width), wide),
            ((width, width), low),
            ((width, hidden_count), low),
            ((hidden_count, width), low),
            ((shards, second_rows, width), wide),
        ],
        flops=rows * width * (hidden_count * 12 + width * 6),
        name="feed",
    )
    arrived_ffn = exchange(send_ffn, "shard", 1)
    shared = [joined, attended_grad, log_sums, bias, mixed]
    tile_scratch = [((LANES, rows), low), ((rows, LANES), wide), ((rows, LANES), wide)]
    per_tile = LANES // HEAD
    groups = [list(range(at, at + per_tile)) for at in range(0, heads, per_tile)]
    groups = [groups[0][:2], groups[0][2:]] + groups[1:]
    first_query, first_key, first_value = local_call(
        functools.partial(back_first_kernel, groups[0]),
        tile_scratch,
        shared,
        flops=heads * rows * rows * 256 * 5 // 2,
        name="back_first",
    )
    first_query, arrived_ffn = lax.optimization_barrier((first_query, arrived_ffn))
    keep_ffn, send_ffn = halve_call("shard", 1, [kept_ffn, arrived_ffn], "halve_ffn")
    first_query, send_ffn = lax.optimization_barrier((first_query, send_ffn))
    arrived_ffn = exchange(send_ffn, "shard", 2)
    tail = GROUP * TILE_ROWS
    att_rows = 3 * part + tail
    pair = (shards // 2, att_rows, width)
    input_grad, kept_att, send_att = local_call(
        functools.partial(back_last_kernel, shards, groups[1:]),
        [((rows, width), wide), (pair, wide), (pair, low)],
        shared + [first_query, first_key, first_value, normed, root, middle_grad, sums] + firsts,
        [((width, 3 * width), low), ((shards, SMALL_PAD, width), wide)]
        + tile_scratch
        + [((rows, 3 * width), low), ((shards, att_rows, width), wide)],
        flops=heads * rows * rows * 256 * 6,
        name="back_last",
    )
    arrived_att = exchange(send_att, "shard", 1)
    keep_att, send_att = halve_call("shard", 1, [kept_att, arrived_att], "halve_att")
    send_att, arrived_ffn = lax.optimization_barrier((send_att, arrived_ffn))
    tails = (0, tail)
    arrived_att = exchange(send_att, "shard", 2)
    chunk_ffn = split_chunk([keep_ffn[0], arrived_ffn[0]], 0, group)
    chunk_att = split_chunk([keep_att[0], arrived_att[0]], tail, group)
    pieces = finish_sum([chunk_ffn, chunk_att], group)
    blocks = hidden_count // width
    results = adam_call(
        pieces,
        (second_rows, att_rows),
        tails,
        [
            (qkv_weight, qkv_first, qkv_second),
            (out_weight, out_first, out_second),
            (up_weight, up_first, up_second),
            (down_weight, down_first, down_second),
            (gains_biases, small_first, small_second),
        ],
        [
            (second_rows, part, matrix_decay),
            (0, part, matrix_decay),
            (part, part, matrix_decay),
            (part + blocks * part, 0, matrix_decay),
            (second_rows + 3 * part, TILE_ROWS, 0.0),
        ],
    )
    return (output, input_grad, *results)


def solution(mesh):
    rows = P(("dp", "shard"), None)
    matrix = P("shard", None)
    vector = P("shard")
    return jax.shard_map(
        shards_program,
        mesh=mesh,
        in_specs=(rows, rows, P(), P())
        + (matrix,) * 4
        + (vector,)
        + (matrix,) * 8
        + (vector, vector),
        out_specs=(rows, rows) + (matrix,) * 12 + (vector,) * 3,
        check_vma=False,
    )
```

```python
import functools
import math

import jax
import jax.numpy as jnp
from jax import lax
from jax.experimental import pallas as pl
from jax.experimental.pallas import tpu as pltpu
from jax.sharding import PartitionSpec as P

HEAD = 32
STEP = 10
LANES = 128
GROUP = 8
SMALL_PAD = 16
TILE_ROWS = 8
CHUNK = 64

norm_eps = 1e-05
beta_one = 0.9
beta_two = 0.95
learn_rate = 0.1
adam_eps = 1e-08
matrix_decay = 0.1
masked_score = -1e30
low = jnp.bfloat16
wide = jnp.float32
log2_e = math.log2(math.e)
score_scale = 1.0 / math.sqrt(HEAD)
tanh_scale = math.sqrt(2.0 / math.pi)
cubic = 0.044715


def dot_nn(left, right):
    return jnp.dot(left, right, preferred_element_type=wide)


def dot_nt(left, right):
    return lax.dot_general(left, right, (((1,), (1,)), ((), ())), preferred_element_type=wide)


def standardize(values):
    centered = values - jnp.mean(values, axis=-1, keepdims=True)
    root_inv = lax.rsqrt(jnp.mean(centered * centered, axis=-1, keepdims=True) + norm_eps)
    return centered * root_inv, root_inv


def norm_back(upstream, normed, root_inv, gain):
    scaled = upstream * gain
    inner_mean = jnp.mean(scaled, axis=-1, keepdims=True)
    cross_mean = jnp.mean(scaled * normed, axis=-1, keepdims=True)
    through = root_inv * (scaled - inner_mean - normed * cross_mean)
    return (
        through,
        jnp.sum(upstream * normed, axis=0, keepdims=True),
        jnp.sum(upstream, axis=0, keepdims=True),
    )


def iota(shape, dim):
    return lax.broadcasted_iota(jnp.int32, shape, dim)


def own_row(lengths, owners, device):
    return jnp.where(owners == device, lengths, 0)


def ends_both(own):
    count = own.shape[1]
    shape = (count, count)
    rows, cols = iota(shape, 0), iota(shape, 1)
    spread = jnp.broadcast_to(own, shape)
    ends_col = jnp.sum(jnp.where(cols <= rows, spread, 0), axis=1, keepdims=True)
    own_col = jnp.sum(jnp.where(cols == rows, spread, 0), axis=1, keepdims=True)
    ends_row = jnp.sum(
        jnp.where(rows <= cols, jnp.broadcast_to(own_col, shape), 0), axis=0, keepdims=True
    )
    return ends_col, ends_row


def fill_mask(bias_ref, own, rows):
    ends_col, ends_row = ends_both(own)
    count = own.shape[1]
    seg_row = jnp.sum(
        (ends_col <= iota((count, rows), 1)).astype(jnp.int32), axis=0, keepdims=True
    )
    seg_col = jnp.sum(
        (ends_row <= iota((rows, count), 0)).astype(jnp.int32), axis=1, keepdims=True
    )
    allowed = (seg_row == seg_col) & (iota((rows, rows), 0) <= iota((rows, rows), 1))
    bias_ref[...] = jnp.where(allowed, 0.0, masked_score)


def fill_small(small_ref, shard, pieces, first_row):
    for offset, piece in enumerate(pieces):
        small_ref[shard ^ offset] = piece[first_row:, :].astype(wide)


def fill_cols(full_ref, shard, pieces, first_row, rows, width):
    blocks = full_ref.shape[1] // width
    for offset, piece in enumerate(pieces):
        at = pl.multiple_of((shard ^ offset) * rows, rows)
        for block in range(blocks):
            start = first_row + block * rows
            full_ref[pl.ds(at, rows), block * width : (block + 1) * width] = piece[
                start : start + rows, :
            ]


def head_mask(head):
    lane = iota((1, LANES), 1)
    first = head * HEAD % LANES
    return ((lane >= first) & (lane < first + HEAD)).astype(wide).astype(low)


def head_tile(head):
    first = head * HEAD // LANES * LANES
    return slice(first, first + LANES)


def query_blocks(rows):
    size = min(256, rows)
    return [(at, at + size) for at in range(0, rows, size)]


def put_blocks(target, row, source, width):
    rows = source.shape[0]
    for block in range(source.shape[1] // width):
        cols = slice(block * width, (block + 1) * width)
        target[row : row + rows, :] = source[:, cols].astype(low)
        row += rows
    return row


def fetch_all(sources, buffers, sems):
    copies = [
        pltpu.make_async_copy(source, buffer, sems.at[index])
        for index, (source, buffer) in enumerate(zip(sources, buffers))
    ]
    for copy in copies:
        copy.start()
    return copies


def pack_first_kernel(qkv_ref, small_ref, first_ref, qkv_buf, small_buf, sems):
    width = first_ref.shape[1]
    small_copy, qkv_copy = fetch_all((small_ref, qkv_ref), (small_buf, qkv_buf), sems)
    small_copy.wait()
    parts = [
        small_buf[block * width : (block + 1) * width].reshape(1, width)
        for block in range(small_buf.shape[0] // width)
    ]
    parts.append(jnp.zeros((SMALL_PAD - len(parts), width), wide))
    first_ref[first_ref.shape[0] - SMALL_PAD :, :] = jnp.concatenate(parts, axis=0).astype(low)
    qkv_copy.wait()
    put_blocks(first_ref, 0, qkv_buf, width)


def pack_second_kernel(out_ref, up_ref, down_ref, second_ref, out_buf, up_buf, down_buf, sems):
    width = second_ref.shape[1]
    buffers = (out_buf, up_buf, down_buf)
    copies = fetch_all((out_ref, up_ref, down_ref), buffers, sems)
    row = 0
    for copy, buffer in zip(copies, buffers):
        copy.wait()
        row = put_blocks(second_ref, row, buffer, width)


def prepare_kernel(shards, x_ref, seed_ref, len_ref, owner_ref, bias_ref, norm_ref, root_ref, low_ref):
    rows = x_ref.shape[0]
    device = lax.axis_index("dp") * shards + lax.axis_index("shard")
    own = own_row(len_ref[...], owner_ref[...], device)
    fill_mask(bias_ref, own, rows)
    normed, root = standardize(x_ref[...].astype(wide))
    norm_ref[...] = normed
    root_ref[...] = root
    live = jnp.sum(own, axis=1, keepdims=True)
    live_rows = (iota((rows, 1), 0) < live).astype(wide)
    low_ref[...] = (seed_ref[...].astype(wide) * live_rows).astype(low)


def attend_kernel(shards, *refs):
    norm_ref, bias_ref = refs[:2]
    pieces = refs[2 : 2 + shards]
    joined_ref, out_ref, log_ref, att_ref, weight_ref, small_ref = refs[2 + shards :]
    rows, width = norm_ref.shape
    shard = lax.axis_index("shard")
    part = width // shards
    fill_cols(weight_ref, shard, pieces, 0, part, width)
    fill_small(small_ref, shard, pieces, 3 * part)
    gain, shift = small_ref[0, 0:1, :], small_ref[0, 1:2, :]
    bias_query, bias_value = small_ref[1, 1:2, :], small_ref[1, 2:3, :]
    hidden = (norm_ref[...] * gain + shift).astype(low)
    for block, bias in enumerate((bias_query, None, bias_value)):
        cols = slice(block * width, (block + 1) * width)
        value = dot_nn(hidden, weight_ref[:, cols])
        if bias is not None:
            value = value + bias
        joined_ref[:, cols] = value.astype(low)
    values_t = joined_ref[:, 2 * width :].T
    units = [
        (head, start, stop) for head in range(width // HEAD) for start, stop in query_blocks(rows)
    ]

    def raw_scores(head, start, stop):
        tile = head_tile(head)
        key_tile = joined_ref[:stop, width + tile.start : width + tile.stop] * head_mask(head)
        return dot_nt(key_tile, joined_ref[start:stop, tile])

    ahead = raw_scores(*units[0])
    for index, (head, start, stop) in enumerate(units):
        raw = ahead
        if index + 1 < len(units):
            ahead = raw_scores(*units[index + 1])
        feature = slice(head * HEAD, (head + 1) * HEAD)
        scores = []
        top = None
        for at in range(0, stop, CHUNK):
            piece = raw[at : at + CHUNK] * (score_scale * log2_e)
            piece = piece + bias_ref[at : at + CHUNK, start:stop]
            scores.append(piece)
            top = piece if top is None else jnp.maximum(top, piece)
        top = jnp.max(top, axis=0, keepdims=True)
        exponents = []
        total = None
        for piece in scores:
            piece = jnp.exp2(piece - top)
            total = piece if total is None else total + piece
            exponents.append(piece.astype(low))
        total = jnp.sum(total, axis=0, keepdims=True)
        mixed = dot_nn(values_t[feature, :stop], jnp.concatenate(exponents, axis=0))
        att_ref[feature, start:stop] = mixed * (1.0 / total)
        log_ref[head : head + 1, start:stop] = top + jnp.log2(total)
    out_ref[...] = att_ref[...].astype(low).T


def feed_kernel(shards, group, *refs):
    x_ref, att_ref, seed_ref = refs[:3]
    firsts = refs[3 : 3 + shards]
    pieces = refs[3 + shards : 3 + 2 * shards]
    refs = refs[3 + 2 * shards :]
    out_ref, middle_ref, dattend_ref, sums_ref, keep_ref, send_ref = refs[:6]
    small_ref, out_w, up_w, down_w, grads_ref = refs[6:]
    rows, width = x_ref.shape
    hidden_count = up_w.shape[1]
    shard = lax.axis_index("shard")
    part = width // shards
    blocks = hidden_count // width
    down_part = hidden_count // shards
    fill_small(small_ref, shard, firsts, 3 * part)
    fill_cols(out_w, shard, pieces, 0, part, width)
    fill_cols(up_w, shard, pieces, part, part, width)
    fill_cols(down_w, shard, pieces, part + blocks * part, down_part, width)
    gain, shift = small_ref[0, 2:3, :], small_ref[1, 0:1, :]
    bias_out, bias_down = small_ref[2, 0:1, :], small_ref[2, 1:2, :]
    bias_up = [small_ref[2, 2:3, :]] + [small_ref[3, row : row + 1, :] for row in range(3)]
    seed_low = seed_ref[...]
    seed = seed_low.astype(wide)
    attended = att_ref[...]
    middle = x_ref[...].astype(wide) + (dot_nn(attended, out_w[...]) + bias_out)
    normed, root = standardize(middle)
    hidden = (normed * gain + shift).astype(low)
    hidden_t = hidden.T
    result = middle + bias_down
    dhidden = jnp.zeros((rows, width), wide)
    sums_ref[...] = jnp.zeros(sums_ref.shape, wide)

    def raw_products(block):
        cols = slice(block * width, (block + 1) * width)
        return dot_nn(hidden, up_w[:, cols]), dot_nt(seed_low, down_w[cols, :])

    ahead = raw_products(0)
    for block in range(blocks):
        cols = slice(block * width, (block + 1) * width)
        raw, dact = ahead
        if block + 1 < blocks:
            ahead = raw_products(block + 1)
        act, dpre = [], []
        for at in range(0, rows, CHUNK):
            pre = raw[at : at + CHUNK] + bias_up[block]
            square = pre * pre
            bend = jnp.tanh(pre * (tanh_scale + (tanh_scale * cubic) * square))
            half = 0.5 + 0.5 * bend
            act.append((pre * half).astype(low))
            slope = 0.5 * tanh_scale + (1.5 * tanh_scale * cubic) * square
            slope = half + (pre * slope) * (1.0 - bend * bend)
            dpre.append((dact[at : at + CHUNK] * slope).astype(low))
        act = jnp.concatenate(act, axis=0)
        dpre = jnp.concatenate(dpre, axis=0)
        result = result + dot_nn(act, down_w[cols, :])
        dhidden = dhidden + dot_nt(dpre, up_w[:, cols])
        grad_down = dot_nn(act.T, seed_low)
        grad_up = dot_nn(hidden_t, dpre)
        for piece in range(width // down_part):
            target = block * (width // down_part) + piece
            at = part + blocks * part
            grads_ref[target, at : at + down_part, :] = grad_down[
                piece * down_part : (piece + 1) * down_part, :
            ]
        for target in range(shards):
            at = part + block * part
            grads_ref[target, at : at + part, :] = grad_up[target * part : (target + 1) * part, :]
        sums_ref[4 + block : 5 + block, :] = jnp.sum(dpre.astype(wide), axis=0, keepdims=True)
    out_ref[...] = result.astype(low)
    through, gain_grad, shift_grad = norm_back(dhidden, normed, root, gain)
    dmiddle = seed + through
    middle_ref[...] = dmiddle
    dmiddle_low = dmiddle.astype(low)
    grad_out = dot_nn(attended.T, dmiddle_low)
    for target in range(shards):
        grads_ref[target, :part, :] = grad_out[target * part : (target + 1) * part, :]
    dattend_ref[...] = dot_nt(dmiddle_low, out_w[...]).astype(low)
    sums_ref[0:1, :] = gain_grad
    sums_ref[1:2, :] = shift_grad
    sums_ref[2:3, :] = jnp.sum(dmiddle_low.astype(wide), axis=0, keepdims=True)
    sums_ref[3:4, :] = jnp.sum(seed, axis=0, keepdims=True)
    side = (shard ^ parity(lax.axis_index("dp"), group)) & 1
    part_ways(grads_ref, keep_ref, send_ref, side)


def part_ways(grads_ref, keep_ref, send_ref, side):
    for pair in range(keep_ref.shape[0]):
        keep_ref[pair] = grads_ref[2 * pair + side]
        send_ref[pair] = grads_ref[2 * pair + 1 - side].astype(low)


def back_heads(
    heads, joined_ref, dattend_ref, log_ref, bias_ref, mixed_ref, dquery_t, dkey, dvalue
):
    rows = joined_ref.shape[0]
    width = joined_ref.shape[1] // 3
    first = heads[0] * HEAD
    count = len(heads) * HEAD
    base = first // LANES * LANES
    tile = slice(base, base + LANES)
    inside = slice(first - base, first - base + count)
    keys_t = joined_ref[:, width + base : width + base + LANES].T
    datt_t = dattend_ref[:, tile].T[inside]
    inner = datt_t.astype(wide) * mixed_ref[first : first + count, :]
    units = [(head, start, stop) for head in heads for start, stop in query_blocks(rows)]

    def raw_products(head, start, stop):
        mask = head_mask(head)
        key_tile = joined_ref[:stop, width + base : width + base + LANES] * mask
        value_tile = joined_ref[:stop, 2 * width + base : 2 * width + base + LANES] * mask
        query = joined_ref[start:stop, tile]
        datt = dattend_ref[start:stop, tile]
        return dot_nt(key_tile, query), dot_nt(value_tile, datt), query * mask, datt * mask

    ahead = raw_products(*units[0])
    for index, (head, start, stop) in enumerate(units):
        raw, dprobs, query, datt = ahead
        if index + 1 < len(units):
            ahead = raw_products(*units[index + 1])
        local = head * HEAD - first
        feature = slice(local, local + HEAD)
        weighted = jnp.sum(inner[feature, start:stop], axis=0, keepdims=True)
        logs = log_ref[head : head + 1, start:stop]
        probs, dscores = [], []
        for at in range(0, stop, CHUNK):
            piece = raw[at : at + CHUNK] * (score_scale * log2_e)
            piece = jnp.exp2(piece + bias_ref[at : at + CHUNK, start:stop] - logs)
            probs.append(piece.astype(low))
            piece = piece * (dprobs[at : at + CHUNK] - weighted)
            dscores.append(piece.astype(low))
        probs = jnp.concatenate(probs, axis=0)
        dscores = jnp.concatenate(dscores, axis=0)
        depth = slice(head * HEAD - base, head * HEAD - base + HEAD)
        dquery_t[depth, start:stop] = (
            dot_nn(keys_t[depth, :stop], dscores) * score_scale
        ).astype(low)
        dvalue[:stop, :] += dot_nn(probs, datt)
        dkey[:stop, :] += dot_nn(dscores, query)


def back_first_kernel(heads, *refs):
    dquery_t, dkey, dvalue = refs[5:8]
    dkey[...] = jnp.zeros(dkey.shape, wide)
    dvalue[...] = jnp.zeros(dvalue.shape, wide)
    dquery_t[...] = jnp.zeros(dquery_t.shape, low)
    back_heads(heads, *refs)


def back_last_kernel(shards, group, head_groups, *refs):
    shared = refs[:5]
    earlier = refs[5:8]
    norm_ref, root_ref, middle_ref, sums_in = refs[8:12]
    pieces = refs[12 : 12 + shards]
    refs = refs[12 + shards :]
    dx_ref, keep_ref, send_ref = refs[:3]
    weight_ref, small_ref, dquery_t, dkey, dvalue, djoined, grads_ref = refs[3:]
    rows, width = norm_ref.shape
    shard = lax.axis_index("shard")
    part = width // shards
    fill_cols(weight_ref, shard, pieces, 0, part, width)
    fill_small(small_ref, shard, pieces, 3 * part)
    gain, shift = small_ref[0, 0:1, :], small_ref[0, 1:2, :]
    for target, value in zip((dquery_t, dkey, dvalue), earlier):
        target[...] = value[...]
    for heads in head_groups:
        back_heads(heads, *shared, dquery_t, dkey, dvalue)
        if (heads[-1] + 1) * HEAD % LANES == 0:
            first = (heads[-1] + 1) * HEAD - LANES
            values = (dquery_t[...].T, dkey[...] * score_scale, dvalue[...])
            for block, value in enumerate(values):
                at = block * width + first
                djoined[:, at : at + LANES] = value.astype(low)
            dkey[...] = jnp.zeros(dkey.shape, wide)
            dvalue[...] = jnp.zeros(dvalue.shape, wide)
    normed, root = norm_ref[...], root_ref[...]
    hidden_t = (normed * gain + shift).astype(low).T
    dhidden = jnp.zeros((rows, width), wide)
    bias_sums = []
    for block in range(3):
        cols = slice(block * width, (block + 1) * width)
        piece = djoined[:, cols]
        dhidden = dhidden + dot_nt(piece, weight_ref[:, cols])
        grad = dot_nn(hidden_t, piece)
        for target in range(shards):
            grads_ref[target, block * part : (block + 1) * part, :] = grad[
                target * part : (target + 1) * part, :
            ]
        if block != 1:
            bias_sums.append(jnp.sum(piece.astype(wide), axis=0, keepdims=True))
    through, gain_grad, shift_grad = norm_back(dhidden, normed, root, gain)
    dx_ref[...] = middle_ref[...] + through
    sums = [gain_grad, shift_grad, sums_in[0:1, :], sums_in[1:2, :]] + bias_sums
    sums += [sums_in[row : row + 1, :] for row in range(2, 8)]
    per_shard = len(sums) // shards
    empty = [jnp.zeros((grads_ref.shape[1] - 3 * part - per_shard, width), wide)]
    for target in range(shards):
        rows_here = sums[target * per_shard : (target + 1) * per_shard]
        grads_ref[target, 3 * part :, :] = jnp.concatenate(rows_here + empty, axis=0)
    side = (shard ^ parity(lax.axis_index("dp"), group)) & 1
    part_ways(grads_ref, keep_ref, send_ref, side)


def halve_kernel(axis, bit, *refs):
    count = (len(refs) - 2) // 2
    keep_ref, send_ref = refs[-2:]
    side = (lax.axis_index(axis) >> bit) & 1
    for pair in range(keep_ref.shape[0]):
        for target, index in ((keep_ref, 2 * pair + side), (send_ref, 2 * pair + 1 - side)):
            parts = []
            for chunk in range(count):
                kept, arrived = refs[2 * chunk : 2 * chunk + 2]
                parts.append(kept[index] + arrived[index].astype(wide))
            value = parts[0] if count == 1 else jnp.concatenate(parts, axis=0)
            target[pair] = value.astype(target.dtype)


def piece_spans(total, tail, group):
    spans = [((total - tail) // group, 0, True)]
    if tail:
        spans.append((tail, total - tail, False))
    return spans


def split_kernel(tail, *refs):
    arrived, keep_ref, send_ref, sum_ref = refs[:-3], *refs[-3:]
    group = sum_ref.shape[0]
    total = arrived[0][...]
    for piece in arrived[1:]:
        total = total + piece[...].astype(wide)
    for index in range(group):
        row = 0
        for rows, first, moves in piece_spans(total.shape[0], tail, group):
            at = first + index * rows if moves else first
            sum_ref[index, row : row + rows, :] = total[at : at + rows, :]
            row += rows
    side = lax.axis_index("dp") & 1
    for pair in range(group // 2):
        keep_ref[pair] = sum_ref[2 * pair + side]
        send_ref[pair] = sum_ref[2 * pair + 1 - side].astype(low)


def add_kernel(mine_ref, other_ref, sum_ref):
    total = mine_ref[...].astype(wide) + other_ref[...].astype(wide)
    sum_ref[...] = total.astype(low).reshape(sum_ref.shape)


def adam_values(weight, grad, first, second, decay_rate):
    first_next = beta_one * first + (1.0 - beta_one) * grad
    second_next = beta_two * second + (1.0 - beta_two) * grad * grad
    first_fix = 1.0 - beta_one**STEP
    second_fix = 1.0 - beta_two**STEP
    update = (first_next * (1.0 / first_fix)) / (
        jnp.sqrt(second_next * (1.0 / second_fix)) + adam_eps
    )
    return first_next, second_next, weight - learn_rate * (update + decay_rate * weight)


def adam_kernel(group, spans, layout, *refs):
    pieces = refs[:group]
    count = len(layout)
    states = refs[group : group + 3 * count]
    results = refs[group + 3 * count : group + 6 * count]
    buffers = refs[group + 6 * count : group + 9 * count]
    grad_ref, sems = refs[-2:]
    copies = []
    for offset, piece in enumerate(pieces):
        value = piece[...].astype(wide)
        index = (lax.axis_index("dp") & (group - 1)) ^ offset
        for rows, first, row in spans:
            at = pl.multiple_of(first + index * rows, TILE_ROWS)
            grad_ref[pl.ds(at, rows), :] = value[row : row + rows, :]
    width = grad_ref.shape[1]
    for array, (first_row, stride, decay) in enumerate(layout):
        weight, first, second = states[3 * array : 3 * array + 3]
        new = buffers[3 * array : 3 * array + 3]
        vector = len(weight.shape) == 1
        rows = 1 if vector else weight.shape[0]
        for block in range(weight.shape[-1] // width):
            cols = slice(block * width, (block + 1) * width)
            where = cols if vector else (slice(None), cols)
            at = first_row + block * stride
            values = adam_values(
                weight[where].reshape(rows, width),
                grad_ref[at : at + rows, :],
                first[where].reshape(rows, width),
                second[where].reshape(rows, width),
                decay,
            )
            for target, value in zip(new, values):
                target[where] = value.reshape(width) if vector else value
        for index in range(3 * array, 3 * array + 3):
            copies.append(
                pltpu.make_async_copy(buffers[index], results[index], sems.at[index])
            )
            copies[-1].start()
    for copy in copies:
        copy.wait()


def local_call(kernel, outs, operands, scratch=(), flops=0, name=None, fetch=False, sems=0):
    in_space = pltpu.HBM if fetch else pltpu.VMEM
    out_space = pltpu.HBM if sems else pltpu.VMEM
    outs = [jax.ShapeDtypeStruct(*out) for out in outs]
    moved = sum(
        math.prod(item.shape) * item.dtype.itemsize for item in list(operands) + outs
    )
    scratch_shapes = [pltpu.VMEM(*item) for item in scratch]
    if fetch or sems:
        scratch_shapes.append(pltpu.SemaphoreType.DMA((sems or len(operands),)))
    limit = 56 if fetch else 40
    return pl.pallas_call(
        kernel,
        out_shape=outs,
        in_specs=[pl.BlockSpec(memory_space=in_space)] * len(operands),
        out_specs=[pl.BlockSpec(memory_space=out_space)] * len(outs),
        scratch_shapes=scratch_shapes,
        compiler_params=pltpu.CompilerParams(vmem_limit_bytes=limit * 1024 * 1024),
        cost_estimate=pl.CostEstimate(flops=flops, bytes_accessed=moved, transcendentals=0),
        name=name,
    )(*operands)


def exchange(values, axis, mask):
    count = lax.axis_size(axis)
    return lax.ppermute(values, axis, [(index, index ^ mask) for index in range(count)])


def parity(index, group):
    result = index & 1
    bit = 1
    while (1 << bit) < group:
        result = result ^ ((index >> bit) & 1)
        bit += 1
    return result


def cross(values, mask, group, settle=False):
    replicas, shards = lax.axis_size("dp"), lax.axis_size("shard")
    pairs = []
    for replica in range(replicas):
        flip = parity(replica, group) if settle else 1
        for shard in range(shards):
            target = (replica ^ mask) * shards + (shard ^ flip)
            pairs.append((replica * shards + shard, target))
    return lax.ppermute(values, ("dp", "shard"), pairs)


def gather_pieces(value, group):
    held = {0: value}
    far = group // 2
    while far > 1:
        for offset in sorted(held):
            held[offset ^ far] = cross(held[offset], far, group)
        far //= 2
    found = {}
    for offset in sorted(held):
        found[offset ^ 1] = cross(held[offset], 1, group, settle=True)
        found[offset] = cross(held[offset], 0, group, settle=True)
    return [found[offset] for offset in range(group)]


def halve_call(axis, bit, flat, name):
    half, _, width = flat[0].shape
    shape = (half // 2, sum(item.shape[1] for item in flat[::2]), width)
    return local_call(
        functools.partial(halve_kernel, axis, bit), [(shape, wide), (shape, low)], flat, name=name
    )


def split_chunk(chunk, tail, group):
    rows, width = chunk[0].shape
    half = (group // 2, (rows - tail) // group + tail, width)
    keep, send = local_call(
        functools.partial(split_kernel, tail),
        [(half, wide), (half, low)],
        chunk,
        [((group,) + half[1:], wide)],
        name="split_sum",
    )
    return keep, cross(send, 1, group)


def finish_sum(chunks, group):
    replicas = lax.axis_size("dp")
    half, _, width = chunks[0][0].shape
    rows = sum(chunk[0].shape[1] for chunk in chunks)
    flat = [item for chunk in chunks for item in chunk]
    bit = 1
    while half > 1:
        half //= 2
        keep, send = halve_call("dp", bit, flat, "halve_dp")
        flat = [keep, cross(send, 1 << bit, group)]
        bit += 1
    mask = group
    (piece,) = local_call(add_kernel, [((rows, width), low)], flat, name="piece_sum")
    while mask < replicas:
        other = exchange(piece, "dp", mask)
        (piece,) = local_call(add_kernel, [((rows, width), low)], [piece, other], name="far_sum")
        mask *= 2
    return gather_pieces(piece, group)


def adam_call(pieces, counts, tails, states, layout):
    group = len(pieces)
    width = pieces[0].shape[1]
    spans = []
    first = row = 0
    for total, tail in zip(counts, tails):
        for rows, start, moves in piece_spans(total, tail, group):
            spans.append((rows, first + start, row))
            row += rows
            first += rows * (group - 1) * (not moves)
        first += total
    outs = [(state[0].shape, wide) for state in states for _ in range(3)]
    return local_call(
        functools.partial(adam_kernel, group, spans, layout),
        outs,
        pieces + [item for state in states for item in state],
        outs + [((first, width), wide)],
        name="adam",
        sems=len(outs),
    )


def shards_program(
    tokens,
    cotangent,
    lengths,
    seq_owner,
    qkv_weight,
    out_weight,
    up_weight,
    down_weight,
    gains_biases,
    qkv_first,
    qkv_second,
    out_first,
    out_second,
    up_first,
    up_second,
    down_first,
    down_second,
    small_first,
    small_second,
):
    rows, width = tokens.shape
    shards = lax.axis_size("shard")
    heads = width // HEAD
    part = qkv_weight.shape[0]
    hidden_count = up_weight.shape[1]
    group = min(GROUP, lax.axis_size("dp"))
    lengths = lengths.reshape(1, -1)
    seq_owner = seq_owner.reshape(1, -1)
    first_rows = 3 * part + SMALL_PAD
    second_rows = part + up_weight.size // width + down_weight.shape[0]
    (first_pack,) = local_call(
        pack_first_kernel,
        [((first_rows, width), low)],
        [qkv_weight, gains_biases],
        [(qkv_weight.shape, wide), (gains_biases.shape, wide)],
        name="pack_first",
        fetch=True,
    )
    firsts = {0: first_pack}
    firsts[2] = exchange(first_pack, "shard", 2)
    firsts[1] = exchange(first_pack, "shard", 1)
    first_pack, matrices = lax.optimization_barrier(
        (first_pack, [out_weight, up_weight, down_weight])
    )
    (second_pack,) = local_call(
        pack_second_kernel,
        [((second_rows, width), low)],
        matrices,
        [(item.shape, wide) for item in matrices],
        name="pack_second",
        fetch=True,
    )
    early_tokens, second_pack = lax.optimization_barrier((tokens, second_pack))
    square = (rows, rows)
    bias, normed, root, seed = local_call(
        functools.partial(prepare_kernel, shards),
        [(square, wide), ((rows, width), wide), ((rows, 1), wide), ((rows, width), low)],
        [early_tokens, cotangent, lengths, seq_owner],
        name="prepare",
    )
    seconds = {0: second_pack}
    seconds[2] = exchange(second_pack, "shard", 2)
    seconds[1] = exchange(second_pack, "shard", 1)
    firsts[2], bias, normed, root, seed = lax.optimization_barrier(
        (firsts[2], bias, normed, root, seed)
    )
    firsts[3] = exchange(firsts[2], "shard", 1)
    firsts = [firsts[offset] for offset in range(shards)]
    joined, attended, log_sums, mixed = local_call(
        functools.partial(attend_kernel, shards),
        [
            ((rows, 3 * width), low),
            ((rows, width), low),
            ((heads, rows), wide),
            ((width, rows), wide),
        ],
        [normed, bias] + firsts,
        [((width, 3 * width), low), ((shards, SMALL_PAD, width), wide)],
        flops=heads * rows * rows * 640,
        name="attend",
    )
    attended, seconds[2] = lax.optimization_barrier((attended, seconds[2]))
    seconds[3] = exchange(seconds[2], "shard", 1)
    seconds = [seconds[offset] for offset in range(shards)]
    pair = (shards // 2, second_rows, width)
    output, middle_grad, attended_grad, sums, kept_ffn, send_ffn = local_call(
        functools.partial(feed_kernel, shards, group),
        [
            ((rows, width), low),
            ((rows, width), wide),
            ((rows, width), low),
            ((SMALL_PAD, width), wide),
            (pair, wide),
            (pair, low),
        ],
        [tokens, attended, seed] + firsts + seconds,
        [
            ((shards, SMALL_PAD, width), wide),
            ((width, width), low),
            ((width, hidden_count), low),
            ((hidden_count, width), low),
            ((shards, second_rows, width), wide),
        ],
        flops=rows * width * (hidden_count * 12 + width * 6),
        name="feed",
    )
    arrived_ffn = exchange(send_ffn, "shard", 1)
    shared = [joined, attended_grad, log_sums, bias, mixed]
    tile_scratch = [((LANES, rows), low), ((rows, LANES), wide), ((rows, LANES), wide)]
    per_tile = LANES // HEAD
    groups = [list(range(at, at + per_tile)) for at in range(0, heads, per_tile)]
    groups = [groups[0][:2], groups[0][2:]] + groups[1:]
    first_query, first_key, first_value = local_call(
        functools.partial(back_first_kernel, groups[0]),
        tile_scratch,
        shared,
        flops=heads * rows * rows * 256 * 5 // 2,
        name="back_first",
    )
    first_query, arrived_ffn = lax.optimization_barrier((first_query, arrived_ffn))
    keep_ffn, send_ffn = halve_call("shard", 1, [kept_ffn, arrived_ffn], "halve_ffn")
    first_query, send_ffn = lax.optimization_barrier((first_query, send_ffn))
    arrived_ffn = exchange(send_ffn, "shard", 2)
    tail = TILE_ROWS
    att_rows = 3 * part + tail
    pair = (shards // 2, att_rows, width)
    input_grad, kept_att, send_att = local_call(
        functools.partial(back_last_kernel, shards, group, groups[1:]),
        [((rows, width), wide), (pair, wide), (pair, low)],
        shared + [first_query, first_key, first_value, normed, root, middle_grad, sums] + firsts,
        [((width, 3 * width), low), ((shards, SMALL_PAD, width), wide)]
        + tile_scratch
        + [((rows, 3 * width), low), ((shards, att_rows, width), wide)],
        flops=heads * rows * rows * 256 * 6,
        name="back_last",
    )
    arrived_att = exchange(send_att, "shard", 1)
    keep_att, send_att = halve_call("shard", 1, [kept_att, arrived_att], "halve_att")
    send_att, arrived_ffn = lax.optimization_barrier((send_att, arrived_ffn))
    tails = (0, tail)
    arrived_att = exchange(send_att, "shard", 2)
    chunk_ffn = split_chunk([keep_ffn[0], arrived_ffn[0]], 0, group)
    chunk_att = split_chunk([keep_att[0], arrived_att[0]], tail, group)
    pieces = finish_sum([chunk_ffn, chunk_att], group)
    blocks = hidden_count // width
    results = adam_call(
        pieces,
        (second_rows, att_rows),
        tails,
        [
            (qkv_weight, qkv_first, qkv_second),
            (out_weight, out_first, out_second),
            (up_weight, up_first, up_second),
            (down_weight, down_first, down_second),
            (gains_biases, small_first, small_second),
        ],
        [
            (second_rows, part, matrix_decay),
            (0, part, matrix_decay),
            (part, part, matrix_decay),
            (part + blocks * part, 0, matrix_decay),
            (second_rows + 3 * part, 1, 0.0),
        ],
    )
    return (output, input_grad, *results)


def solution(mesh):
    rows = P(("dp", "shard"), None)
    matrix = P("shard", None)
    vector = P("shard")
    return jax.shard_map(
        shards_program,
        mesh=mesh,
        in_specs=(rows, rows, P(), P())
        + (matrix,) * 4
        + (vector,)
        + (matrix,) * 8
        + (vector, vector),
        out_specs=(rows, rows) + (matrix,) * 12 + (vector,) * 3,
        check_vma=False,
    )
```

```python
import functools
import math

import jax
import jax.numpy as jnp
from jax import lax
from jax.experimental import pallas as pl
from jax.experimental.pallas import tpu as pltpu
from jax.sharding import PartitionSpec as P

HEAD = 32
STEP = 10
LANES = 128
GROUP = 8
SMALL_PAD = 16
TILE_ROWS = 8
CHUNK = 64

norm_eps = 1e-05
beta_one = 0.9
beta_two = 0.95
learn_rate = 0.1
adam_eps = 1e-08
matrix_decay = 0.1
masked_score = -1e30
low = jnp.bfloat16
wide = jnp.float32
log2_e = math.log2(math.e)
score_scale = 1.0 / math.sqrt(HEAD)
tanh_scale = math.sqrt(2.0 / math.pi)
cubic = 0.044715


def dot_nn(left, right):
    return jnp.dot(left, right, preferred_element_type=wide)


def dot_nt(left, right):
    return lax.dot_general(left, right, (((1,), (1,)), ((), ())), preferred_element_type=wide)


def standardize(values):
    centered = values - jnp.mean(values, axis=-1, keepdims=True)
    root_inv = lax.rsqrt(jnp.mean(centered * centered, axis=-1, keepdims=True) + norm_eps)
    return centered * root_inv, root_inv


def norm_back(upstream, normed, root_inv, gain):
    scaled = upstream * gain
    inner_mean = jnp.mean(scaled, axis=-1, keepdims=True)
    cross_mean = jnp.mean(scaled * normed, axis=-1, keepdims=True)
    through = root_inv * (scaled - inner_mean - normed * cross_mean)
    return (
        through,
        jnp.sum(upstream * normed, axis=0, keepdims=True),
        jnp.sum(upstream, axis=0, keepdims=True),
    )


def iota(shape, dim):
    return lax.broadcasted_iota(jnp.int32, shape, dim)


def own_row(lengths, owners, device):
    return jnp.where(owners == device, lengths, 0)


def ends_both(own):
    count = own.shape[1]
    shape = (count, count)
    rows, cols = iota(shape, 0), iota(shape, 1)
    spread = jnp.broadcast_to(own, shape)
    ends_col = jnp.sum(jnp.where(cols <= rows, spread, 0), axis=1, keepdims=True)
    own_col = jnp.sum(jnp.where(cols == rows, spread, 0), axis=1, keepdims=True)
    ends_row = jnp.sum(
        jnp.where(rows <= cols, jnp.broadcast_to(own_col, shape), 0), axis=0, keepdims=True
    )
    return ends_col, ends_row


def fill_mask(bias_ref, own, rows):
    ends_col, ends_row = ends_both(own)
    count = own.shape[1]
    seg_row = jnp.sum(
        (ends_col <= iota((count, rows), 1)).astype(jnp.int32), axis=0, keepdims=True
    )
    seg_col = jnp.sum(
        (ends_row <= iota((rows, count), 0)).astype(jnp.int32), axis=1, keepdims=True
    )
    allowed = (seg_row == seg_col) & (iota((rows, rows), 0) <= iota((rows, rows), 1))
    bias_ref[...] = jnp.where(allowed, 0.0, masked_score)


def fill_small(small_ref, shard, pieces, first_row):
    for offset, piece in enumerate(pieces):
        small_ref[shard ^ offset] = piece[first_row:, :].astype(wide)


def fill_cols(full_ref, shard, pieces, first_row, rows, width):
    blocks = full_ref.shape[1] // width
    for offset, piece in enumerate(pieces):
        at = pl.multiple_of((shard ^ offset) * rows, rows)
        for block in range(blocks):
            start = first_row + block * rows
            full_ref[pl.ds(at, rows), block * width : (block + 1) * width] = piece[
                start : start + rows, :
            ]


def head_mask(head):
    lane = iota((1, LANES), 1)
    first = head * HEAD % LANES
    return ((lane >= first) & (lane < first + HEAD)).astype(wide).astype(low)


def head_tile(head):
    first = head * HEAD // LANES * LANES
    return slice(first, first + LANES)


def query_blocks(rows):
    size = min(256, rows)
    return [(at, at + size) for at in range(0, rows, size)]


def put_blocks(target, row, source, width):
    rows = source.shape[0]
    for block in range(source.shape[1] // width):
        cols = slice(block * width, (block + 1) * width)
        target[row : row + rows, :] = source[:, cols].astype(low)
        row += rows
    return row


def fetch_all(sources, buffers, sems):
    copies = [
        pltpu.make_async_copy(source, buffer, sems.at[index])
        for index, (source, buffer) in enumerate(zip(sources, buffers))
    ]
    for copy in copies:
        copy.start()
    return copies


def pack_first_kernel(qkv_ref, small_ref, first_ref, qkv_buf, small_buf, sems):
    width = first_ref.shape[1]
    small_copy, qkv_copy = fetch_all((small_ref, qkv_ref), (small_buf, qkv_buf), sems)
    small_copy.wait()
    parts = [
        small_buf[block * width : (block + 1) * width].reshape(1, width)
        for block in range(small_buf.shape[0] // width)
    ]
    parts.append(jnp.zeros((SMALL_PAD - len(parts), width), wide))
    first_ref[first_ref.shape[0] - SMALL_PAD :, :] = jnp.concatenate(parts, axis=0).astype(low)
    qkv_copy.wait()
    put_blocks(first_ref, 0, qkv_buf, width)


def pack_second_kernel(out_ref, up_ref, down_ref, second_ref, out_buf, up_buf, down_buf, sems):
    width = second_ref.shape[1]
    buffers = (out_buf, up_buf, down_buf)
    copies = fetch_all((out_ref, up_ref, down_ref), buffers, sems)
    row = 0
    for copy, buffer in zip(copies, buffers):
        copy.wait()
        row = put_blocks(second_ref, row, buffer, width)


def prepare_kernel(shards, x_ref, seed_ref, len_ref, owner_ref, bias_ref, norm_ref, root_ref, low_ref):
    rows = x_ref.shape[0]
    device = lax.axis_index("dp") * shards + lax.axis_index("shard")
    own = own_row(len_ref[...], owner_ref[...], device)
    fill_mask(bias_ref, own, rows)
    normed, root = standardize(x_ref[...].astype(wide))
    norm_ref[...] = normed
    root_ref[...] = root
    live = jnp.sum(own, axis=1, keepdims=True)
    live_rows = (iota((rows, 1), 0) < live).astype(wide)
    low_ref[...] = (seed_ref[...].astype(wide) * live_rows).astype(low)


def attend_kernel(shards, *refs):
    norm_ref, bias_ref = refs[:2]
    pieces = refs[2 : 2 + shards]
    joined_ref, out_ref, log_ref, att_ref, weight_ref, small_ref = refs[2 + shards :]
    rows, width = norm_ref.shape
    shard = lax.axis_index("shard")
    part = width // shards
    fill_cols(weight_ref, shard, pieces, 0, part, width)
    fill_small(small_ref, shard, pieces, 3 * part)
    gain, shift = small_ref[0, 0:1, :], small_ref[0, 1:2, :]
    bias_query, bias_value = small_ref[1, 1:2, :], small_ref[1, 2:3, :]
    hidden = (norm_ref[...] * gain + shift).astype(low)
    for block, bias in enumerate((bias_query, None, bias_value)):
        cols = slice(block * width, (block + 1) * width)
        value = dot_nn(hidden, weight_ref[:, cols])
        if bias is not None:
            value = value + bias
        joined_ref[:, cols] = value.astype(low)
    values_t = joined_ref[:, 2 * width :].T
    units = [
        (head, start, stop) for head in range(width // HEAD) for start, stop in query_blocks(rows)
    ]

    def raw_scores(head, start, stop):
        tile = head_tile(head)
        key_tile = joined_ref[:stop, width + tile.start : width + tile.stop] * head_mask(head)
        return dot_nt(key_tile, joined_ref[start:stop, tile])

    ahead = raw_scores(*units[0])
    for index, (head, start, stop) in enumerate(units):
        raw = ahead
        if index + 1 < len(units):
            ahead = raw_scores(*units[index + 1])
        feature = slice(head * HEAD, (head + 1) * HEAD)
        scores = []
        top = None
        for at in range(0, stop, CHUNK):
            piece = raw[at : at + CHUNK] * (score_scale * log2_e)
            piece = piece + bias_ref[at : at + CHUNK, start:stop]
            scores.append(piece)
            top = piece if top is None else jnp.maximum(top, piece)
        top = jnp.max(top, axis=0, keepdims=True)
        exponents = []
        total = None
        for piece in scores:
            piece = jnp.exp2(piece - top)
            total = piece if total is None else total + piece
            exponents.append(piece.astype(low))
        total = jnp.sum(total, axis=0, keepdims=True)
        mixed = dot_nn(values_t[feature, :stop], jnp.concatenate(exponents, axis=0))
        att_ref[feature, start:stop] = mixed * (1.0 / total)
        log_ref[head : head + 1, start:stop] = top + jnp.log2(total)
    out_ref[...] = att_ref[...].astype(low).T


def feed_kernel(shards, *refs):
    x_ref, att_ref, seed_ref = refs[:3]
    firsts = refs[3 : 3 + shards]
    pieces = refs[3 + shards : 3 + 2 * shards]
    refs = refs[3 + 2 * shards :]
    out_ref, middle_ref, dattend_ref, sums_ref, keep_ref, send_ref = refs[:6]
    small_ref, out_w, up_w, down_w, grads_ref = refs[6:]
    rows, width = x_ref.shape
    hidden_count = up_w.shape[1]
    shard = lax.axis_index("shard")
    part = width // shards
    blocks = hidden_count // width
    down_part = hidden_count // shards
    fill_small(small_ref, shard, firsts, 3 * part)
    fill_cols(out_w, shard, pieces, 0, part, width)
    fill_cols(up_w, shard, pieces, part, part, width)
    fill_cols(down_w, shard, pieces, part + blocks * part, down_part, width)
    gain, shift = small_ref[0, 2:3, :], small_ref[1, 0:1, :]
    bias_out, bias_down = small_ref[2, 0:1, :], small_ref[2, 1:2, :]
    bias_up = [small_ref[2, 2:3, :]] + [small_ref[3, row : row + 1, :] for row in range(3)]
    seed_low = seed_ref[...]
    seed = seed_low.astype(wide)
    attended = att_ref[...]
    middle = x_ref[...].astype(wide) + (dot_nn(attended, out_w[...]) + bias_out)
    normed, root = standardize(middle)
    hidden = (normed * gain + shift).astype(low)
    hidden_t = hidden.T
    result = middle + bias_down
    dhidden = jnp.zeros((rows, width), wide)
    sums_ref[...] = jnp.zeros(sums_ref.shape, wide)

    def raw_products(block):
        cols = slice(block * width, (block + 1) * width)
        return dot_nn(hidden, up_w[:, cols]), dot_nt(seed_low, down_w[cols, :])

    ahead = raw_products(0)
    for block in range(blocks):
        cols = slice(block * width, (block + 1) * width)
        raw, dact = ahead
        if block + 1 < blocks:
            ahead = raw_products(block + 1)
        act, dpre = [], []
        for at in range(0, rows, CHUNK):
            pre = raw[at : at + CHUNK] + bias_up[block]
            square = pre * pre
            bend = jnp.tanh(pre * (tanh_scale + (tanh_scale * cubic) * square))
            half = 0.5 + 0.5 * bend
            act.append((pre * half).astype(low))
            slope = 0.5 * tanh_scale + (1.5 * tanh_scale * cubic) * square
            slope = half + (pre * slope) * (1.0 - bend * bend)
            dpre.append((dact[at : at + CHUNK] * slope).astype(low))
        act = jnp.concatenate(act, axis=0)
        dpre = jnp.concatenate(dpre, axis=0)
        result = result + dot_nn(act, down_w[cols, :])
        dhidden = dhidden + dot_nt(dpre, up_w[:, cols])
        grad_down = dot_nn(act.T, seed_low)
        grad_up = dot_nn(hidden_t, dpre)
        for piece in range(width // down_part):
            target = block * (width // down_part) + piece
            at = part + blocks * part
            grads_ref[target, at : at + down_part, :] = grad_down[
                piece * down_part : (piece + 1) * down_part, :
            ]
        for target in range(shards):
            at = part + block * part
            grads_ref[target, at : at + part, :] = grad_up[target * part : (target + 1) * part, :]
        sums_ref[4 + block : 5 + block, :] = jnp.sum(dpre.astype(wide), axis=0, keepdims=True)
    out_ref[...] = result.astype(low)
    through, gain_grad, shift_grad = norm_back(dhidden, normed, root, gain)
    dmiddle = seed + through
    middle_ref[...] = dmiddle
    dmiddle_low = dmiddle.astype(low)
    grad_out = dot_nn(attended.T, dmiddle_low)
    for target in range(shards):
        grads_ref[target, :part, :] = grad_out[target * part : (target + 1) * part, :]
    dattend_ref[...] = dot_nt(dmiddle_low, out_w[...]).astype(low)
    sums_ref[0:1, :] = gain_grad
    sums_ref[1:2, :] = shift_grad
    sums_ref[2:3, :] = jnp.sum(dmiddle_low.astype(wide), axis=0, keepdims=True)
    sums_ref[3:4, :] = jnp.sum(seed, axis=0, keepdims=True)
    part_ways(grads_ref, keep_ref, send_ref, shard & 1)


def part_ways(grads_ref, keep_ref, send_ref, side):
    for pair in range(keep_ref.shape[0]):
        keep_ref[pair] = grads_ref[2 * pair + side]
        send_ref[pair] = grads_ref[2 * pair + 1 - side].astype(low)


def back_heads(
    heads, joined_ref, dattend_ref, log_ref, bias_ref, mixed_ref, dquery_t, dkey, dvalue
):
    rows = joined_ref.shape[0]
    width = joined_ref.shape[1] // 3
    first = heads[0] * HEAD
    count = len(heads) * HEAD
    base = first // LANES * LANES
    tile = slice(base, base + LANES)
    inside = slice(first - base, first - base + count)
    keys_t = joined_ref[:, width + base : width + base + LANES].T
    datt_t = dattend_ref[:, tile].T[inside]
    inner = datt_t.astype(wide) * mixed_ref[first : first + count, :]
    units = [(head, start, stop) for head in heads for start, stop in query_blocks(rows)]

    def raw_products(head, start, stop):
        mask = head_mask(head)
        key_tile = joined_ref[:stop, width + base : width + base + LANES] * mask
        value_tile = joined_ref[:stop, 2 * width + base : 2 * width + base + LANES] * mask
        query = joined_ref[start:stop, tile]
        datt = dattend_ref[start:stop, tile]
        return dot_nt(key_tile, query), dot_nt(value_tile, datt), query * mask, datt * mask

    ahead = raw_products(*units[0])
    for index, (head, start, stop) in enumerate(units):
        raw, dprobs, query, datt = ahead
        if index + 1 < len(units):
            ahead = raw_products(*units[index + 1])
        local = head * HEAD - first
        feature = slice(local, local + HEAD)
        weighted = jnp.sum(inner[feature, start:stop], axis=0, keepdims=True)
        logs = log_ref[head : head + 1, start:stop]
        probs, dscores = [], []
        for at in range(0, stop, CHUNK):
            piece = raw[at : at + CHUNK] * (score_scale * log2_e)
            piece = jnp.exp2(piece + bias_ref[at : at + CHUNK, start:stop] - logs)
            probs.append(piece.astype(low))
            piece = piece * (dprobs[at : at + CHUNK] - weighted)
            dscores.append(piece.astype(low))
        probs = jnp.concatenate(probs, axis=0)
        dscores = jnp.concatenate(dscores, axis=0)
        depth = slice(head * HEAD - base, head * HEAD - base + HEAD)
        dquery_t[depth, start:stop] = (
            dot_nn(keys_t[depth, :stop], dscores) * score_scale
        ).astype(low)
        dvalue[:stop, :] += dot_nn(probs, datt)
        dkey[:stop, :] += dot_nn(dscores, query)


def back_first_kernel(heads, *refs):
    dquery_t, dkey, dvalue = refs[5:8]
    dkey[...] = jnp.zeros(dkey.shape, wide)
    dvalue[...] = jnp.zeros(dvalue.shape, wide)
    dquery_t[...] = jnp.zeros(dquery_t.shape, low)
    back_heads(heads, *refs)


def back_last_kernel(shards, head_groups, *refs):
    shared = refs[:5]
    earlier = refs[5:8]
    norm_ref, root_ref, middle_ref, sums_in = refs[8:12]
    pieces = refs[12 : 12 + shards]
    refs = refs[12 + shards :]
    dx_ref, keep_ref, send_ref = refs[:3]
    weight_ref, small_ref, dquery_t, dkey, dvalue, djoined, grads_ref = refs[3:]
    rows, width = norm_ref.shape
    shard = lax.axis_index("shard")
    part = width // shards
    fill_cols(weight_ref, shard, pieces, 0, part, width)
    fill_small(small_ref, shard, pieces, 3 * part)
    gain, shift = small_ref[0, 0:1, :], small_ref[0, 1:2, :]
    for target, value in zip((dquery_t, dkey, dvalue), earlier):
        target[...] = value[...]
    for heads in head_groups:
        back_heads(heads, *shared, dquery_t, dkey, dvalue)
        if (heads[-1] + 1) * HEAD % LANES == 0:
            first = (heads[-1] + 1) * HEAD - LANES
            values = (dquery_t[...].T, dkey[...] * score_scale, dvalue[...])
            for block, value in enumerate(values):
                at = block * width + first
                djoined[:, at : at + LANES] = value.astype(low)
            dkey[...] = jnp.zeros(dkey.shape, wide)
            dvalue[...] = jnp.zeros(dvalue.shape, wide)
    normed, root = norm_ref[...], root_ref[...]
    hidden_t = (normed * gain + shift).astype(low).T
    dhidden = jnp.zeros((rows, width), wide)
    bias_sums = []
    for block in range(3):
        cols = slice(block * width, (block + 1) * width)
        piece = djoined[:, cols]
        dhidden = dhidden + dot_nt(piece, weight_ref[:, cols])
        grad = dot_nn(hidden_t, piece)
        for target in range(shards):
            grads_ref[target, block * part : (block + 1) * part, :] = grad[
                target * part : (target + 1) * part, :
            ]
        if block != 1:
            bias_sums.append(jnp.sum(piece.astype(wide), axis=0, keepdims=True))
    through, gain_grad, shift_grad = norm_back(dhidden, normed, root, gain)
    dx_ref[...] = middle_ref[...] + through
    sums = [gain_grad, shift_grad, sums_in[0:1, :], sums_in[1:2, :]] + bias_sums
    sums += [sums_in[row : row + 1, :] for row in range(2, 8)]
    per_shard = len(sums) // shards
    empty = [jnp.zeros((grads_ref.shape[1] - 3 * part - per_shard, width), wide)]
    for target in range(shards):
        rows_here = sums[target * per_shard : (target + 1) * per_shard]
        grads_ref[target, 3 * part :, :] = jnp.concatenate(rows_here + empty, axis=0)
    part_ways(grads_ref, keep_ref, send_ref, shard & 1)


def halve_kernel(axis, bit, *refs):
    count = (len(refs) - 2) // 2
    keep_ref, send_ref = refs[-2:]
    side = (lax.axis_index(axis) >> bit) & 1
    for pair in range(keep_ref.shape[0]):
        for target, index in ((keep_ref, 2 * pair + side), (send_ref, 2 * pair + 1 - side)):
            parts = []
            for chunk in range(count):
                kept, arrived = refs[2 * chunk : 2 * chunk + 2]
                parts.append(kept[index] + arrived[index].astype(wide))
            value = parts[0] if count == 1 else jnp.concatenate(parts, axis=0)
            target[pair] = value.astype(target.dtype)


def piece_spans(total, tail, group):
    spans = [((total - tail) // group, 0, True)]
    if tail:
        spans.append((tail, total - tail, False))
    return spans


def split_kernel(tail, *refs):
    arrived, keep_ref, send_ref, sum_ref = refs[:-3], *refs[-3:]
    group = sum_ref.shape[0]
    total = arrived[0][...]
    for piece in arrived[1:]:
        total = total + piece[...].astype(wide)
    for index in range(group):
        row = 0
        for rows, first, moves in piece_spans(total.shape[0], tail, group):
            at = first + index * rows if moves else first
            sum_ref[index, row : row + rows, :] = total[at : at + rows, :]
            row += rows
    side = lax.axis_index("dp") & 1
    for pair in range(group // 2):
        keep_ref[pair] = sum_ref[2 * pair + side]
        send_ref[pair] = sum_ref[2 * pair + 1 - side].astype(low)


def piece_kernel(*refs):
    parts = [
        mine[...].reshape(mine.shape[-2:]).astype(wide)
        + other[...].reshape(other.shape[-2:]).astype(wide)
        for mine, other in zip(refs[:-1:2], refs[1:-1:2])
    ]
    refs[-1][...] = jnp.concatenate(parts, axis=0).astype(low)


def adam_values(weight, grad, first, second, decay_rate):
    first_next = beta_one * first + (1.0 - beta_one) * grad
    second_next = beta_two * second + (1.0 - beta_two) * grad * grad
    first_fix = 1.0 - beta_one**STEP
    second_fix = 1.0 - beta_two**STEP
    update = (first_next * (1.0 / first_fix)) / (
        jnp.sqrt(second_next * (1.0 / second_fix)) + adam_eps
    )
    return first_next, second_next, weight - learn_rate * (update + decay_rate * weight)


def adam_kernel(group, spans, layout, *refs):
    pieces = refs[:group]
    count = len(layout)
    states = refs[group : group + 3 * count]
    results = refs[group + 3 * count : group + 6 * count]
    buffers = refs[group + 6 * count : group + 9 * count]
    grad_ref, sems = refs[-2:]
    copies = []
    for offset, piece in enumerate(pieces):
        value = piece[...].astype(wide)
        index = (lax.axis_index("dp") & (group - 1)) ^ offset
        for rows, first, row in spans:
            at = pl.multiple_of(first + index * rows, TILE_ROWS)
            grad_ref[pl.ds(at, rows), :] = value[row : row + rows, :]
    width = grad_ref.shape[1]
    for array, (first_row, stride, decay) in enumerate(layout):
        weight, first, second = states[3 * array : 3 * array + 3]
        new = buffers[3 * array : 3 * array + 3]
        vector = len(weight.shape) == 1
        rows = 1 if vector else weight.shape[0]
        for block in range(weight.shape[-1] // width):
            cols = slice(block * width, (block + 1) * width)
            where = cols if vector else (slice(None), cols)
            at = first_row + block * stride
            values = adam_values(
                weight[where].reshape(rows, width),
                grad_ref[at : at + rows, :],
                first[where].reshape(rows, width),
                second[where].reshape(rows, width),
                decay,
            )
            for target, value in zip(new, values):
                target[where] = value.reshape(width) if vector else value
        for index in range(3 * array, 3 * array + 3):
            copies.append(
                pltpu.make_async_copy(buffers[index], results[index], sems.at[index])
            )
            copies[-1].start()
    for copy in copies:
        copy.wait()


def local_call(kernel, outs, operands, scratch=(), flops=0, name=None, fetch=False, sems=0):
    in_space = pltpu.HBM if fetch else pltpu.VMEM
    out_space = pltpu.HBM if sems else pltpu.VMEM
    outs = [jax.ShapeDtypeStruct(*out) for out in outs]
    moved = sum(
        math.prod(item.shape) * item.dtype.itemsize for item in list(operands) + outs
    )
    scratch_shapes = [pltpu.VMEM(*item) for item in scratch]
    if fetch or sems:
        scratch_shapes.append(pltpu.SemaphoreType.DMA((sems or len(operands),)))
    limit = 56 if fetch else 40
    return pl.pallas_call(
        kernel,
        out_shape=outs,
        in_specs=[pl.BlockSpec(memory_space=in_space)] * len(operands),
        out_specs=[pl.BlockSpec(memory_space=out_space)] * len(outs),
        scratch_shapes=scratch_shapes,
        compiler_params=pltpu.CompilerParams(vmem_limit_bytes=limit * 1024 * 1024),
        cost_estimate=pl.CostEstimate(flops=flops, bytes_accessed=moved, transcendentals=0),
        name=name,
    )(*operands)


def exchange(values, axis, mask):
    count = lax.axis_size(axis)
    return lax.ppermute(values, axis, [(index, index ^ mask) for index in range(count)])


def gather_pieces(value, group):
    found = {0: value}
    found[1] = exchange(value, "dp", 1)
    far = group // 2
    while far > 1:
        for offset in sorted(found):
            if offset & 1 == 0:
                found[offset ^ far] = exchange(found[offset], "dp", far)
        if far == group // 2:
            found[far], found[1] = lax.optimization_barrier((found[far], found[1]))
        far //= 2
    for offset in range(2, group, 2):
        found[offset ^ 1] = exchange(found[offset], "dp", 1)
    return [found[offset] for offset in range(group)]


def halve_call(axis, bit, flat, name):
    half, _, width = flat[0].shape
    shape = (half // 2, sum(item.shape[1] for item in flat[::2]), width)
    return local_call(
        functools.partial(halve_kernel, axis, bit), [(shape, wide), (shape, low)], flat, name=name
    )


def split_chunk(chunk, tail, group):
    rows, width = chunk[0].shape
    half = (group // 2, (rows - tail) // group + tail, width)
    keep, send = local_call(
        functools.partial(split_kernel, tail),
        [(half, wide), (half, low)],
        chunk,
        [((group,) + half[1:], wide)],
        name="split_sum",
    )
    return keep, exchange(send, "dp", 1)


def near_sum(flat):
    half = flat[0].shape[0]
    bit = 1
    while half > 1:
        half //= 2
        keep, send = halve_call("dp", bit, flat, "halve_dp")
        flat = [keep, exchange(send, "dp", 1 << bit)]
        bit += 1
    return flat


def finish_sum(chunks, group):
    replicas = lax.axis_size("dp")
    flat = [item for chunk in chunks for item in near_sum(chunk)]
    width = flat[0].shape[-1]
    rows = sum(item.shape[1] for item in flat[::2])
    (piece,) = local_call(piece_kernel, [((rows, width), low)], flat, name="piece_sum")
    mask = group
    while mask < replicas:
        other = exchange(piece, "dp", mask)
        (piece,) = local_call(piece_kernel, [((rows, width), low)], [piece, other], name="far_sum")
        mask *= 2
    return gather_pieces(piece, group)


def adam_call(pieces, counts, tails, states, layout):
    group = len(pieces)
    width = pieces[0].shape[1]
    spans = []
    first = row = 0
    for total, tail in zip(counts, tails):
        for rows, start, moves in piece_spans(total, tail, group):
            spans.append((rows, first + start, row))
            row += rows
            first += rows * (group - 1) * (not moves)
        first += total
    outs = [(state[0].shape, wide) for state in states for _ in range(3)]
    return local_call(
        functools.partial(adam_kernel, group, spans, layout),
        outs,
        pieces + [item for state in states for item in state],
        outs + [((first, width), wide)],
        name="adam",
        sems=len(outs),
    )


def shards_program(
    tokens,
    cotangent,
    lengths,
    seq_owner,
    qkv_weight,
    out_weight,
    up_weight,
    down_weight,
    gains_biases,
    qkv_first,
    qkv_second,
    out_first,
    out_second,
    up_first,
    up_second,
    down_first,
    down_second,
    small_first,
    small_second,
):
    rows, width = tokens.shape
    shards = lax.axis_size("shard")
    heads = width // HEAD
    part = qkv_weight.shape[0]
    hidden_count = up_weight.shape[1]
    group = min(GROUP, lax.axis_size("dp"))
    lengths = lengths.reshape(1, -1)
    seq_owner = seq_owner.reshape(1, -1)
    first_rows = 3 * part + SMALL_PAD
    second_rows = part + up_weight.size // width + down_weight.shape[0]
    (first_pack,) = local_call(
        pack_first_kernel,
        [((first_rows, width), low)],
        [qkv_weight, gains_biases],
        [(qkv_weight.shape, wide), (gains_biases.shape, wide)],
        name="pack_first",
        fetch=True,
    )
    firsts = {0: first_pack}
    firsts[2] = exchange(first_pack, "shard", 2)
    firsts[1] = exchange(first_pack, "shard", 1)
    first_pack, matrices = lax.optimization_barrier(
        (first_pack, [out_weight, up_weight, down_weight])
    )
    (second_pack,) = local_call(
        pack_second_kernel,
        [((second_rows, width), low)],
        matrices,
        [(item.shape, wide) for item in matrices],
        name="pack_second",
        fetch=True,
    )
    early_tokens, second_pack = lax.optimization_barrier((tokens, second_pack))
    square = (rows, rows)
    bias, normed, root, seed = local_call(
        functools.partial(prepare_kernel, shards),
        [(square, wide), ((rows, width), wide), ((rows, 1), wide), ((rows, width), low)],
        [early_tokens, cotangent, lengths, seq_owner],
        name="prepare",
    )
    seconds = {0: second_pack}
    seconds[2] = exchange(second_pack, "shard", 2)
    seconds[1] = exchange(second_pack, "shard", 1)
    firsts[2], bias, normed, root, seed = lax.optimization_barrier(
        (firsts[2], bias, normed, root, seed)
    )
    firsts[3] = exchange(firsts[2], "shard", 1)
    firsts = [firsts[offset] for offset in range(shards)]
    joined, attended, log_sums, mixed = local_call(
        functools.partial(attend_kernel, shards),
        [
            ((rows, 3 * width), low),
            ((rows, width), low),
            ((heads, rows), wide),
            ((width, rows), wide),
        ],
        [normed, bias] + firsts,
        [((width, 3 * width), low), ((shards, SMALL_PAD, width), wide)],
        flops=heads * rows * rows * 640,
        name="attend",
    )
    attended, seconds[2] = lax.optimization_barrier((attended, seconds[2]))
    seconds[3] = exchange(seconds[2], "shard", 1)
    seconds = [seconds[offset] for offset in range(shards)]
    pair = (shards // 2, second_rows, width)
    output, middle_grad, attended_grad, sums, kept_ffn, send_ffn = local_call(
        functools.partial(feed_kernel, shards),
        [
            ((rows, width), low),
            ((rows, width), wide),
            ((rows, width), low),
            ((SMALL_PAD, width), wide),
            (pair, wide),
            (pair, low),
        ],
        [tokens, attended, seed] + firsts + seconds,
        [
            ((shards, SMALL_PAD, width), wide),
            ((width, width), low),
            ((width, hidden_count), low),
            ((hidden_count, width), low),
            ((shards, second_rows, width), wide),
        ],
        flops=rows * width * (hidden_count * 12 + width * 6),
        name="feed",
    )
    arrived_ffn = exchange(send_ffn, "shard", 1)
    shared = [joined, attended_grad, log_sums, bias, mixed]
    tile_scratch = [((LANES, rows), low), ((rows, LANES), wide), ((rows, LANES), wide)]
    per_tile = LANES // HEAD
    groups = [list(range(at, at + per_tile)) for at in range(0, heads, per_tile)]
    groups = [groups[0][:3], groups[0][3:]] + groups[1:]
    first_query, first_key, first_value = local_call(
        functools.partial(back_first_kernel, groups[0]),
        tile_scratch,
        shared,
        flops=heads * rows * rows * 256 * 5 // 2,
        name="back_first",
    )
    first_query, arrived_ffn = lax.optimization_barrier((first_query, arrived_ffn))
    keep_ffn, send_ffn = halve_call("shard", 1, [kept_ffn, arrived_ffn], "halve_ffn")
    first_query, send_ffn = lax.optimization_barrier((first_query, send_ffn))
    arrived_ffn = exchange(send_ffn, "shard", 2)
    tail = TILE_ROWS
    att_rows = 3 * part + tail
    pair = (shards // 2, att_rows, width)
    input_grad, kept_att, send_att = local_call(
        functools.partial(back_last_kernel, shards, groups[1:]),
        [((rows, width), wide), (pair, wide), (pair, low)],
        shared + [first_query, first_key, first_value, normed, root, middle_grad, sums] + firsts,
        [((width, 3 * width), low), ((shards, SMALL_PAD, width), wide)]
        + tile_scratch
        + [((rows, 3 * width), low), ((shards, att_rows, width), wide)],
        flops=heads * rows * rows * 256 * 6,
        name="back_last",
    )
    arrived_att = exchange(send_att, "shard", 1)
    keep_att, send_att = halve_call("shard", 1, [kept_att, arrived_att], "halve_att")
    send_att, arrived_ffn = lax.optimization_barrier((send_att, arrived_ffn))
    tails = (0, tail)
    arrived_att = exchange(send_att, "shard", 2)
    chunk_ffn = split_chunk([keep_ffn[0], arrived_ffn[0]], 0, group)
    chunk_att = split_chunk([keep_att[0], arrived_att[0]], tail, group)
    pieces = finish_sum([chunk_ffn, chunk_att], group)
    blocks = hidden_count // width
    results = adam_call(
        pieces,
        (second_rows, att_rows),
        tails,
        [
            (qkv_weight, qkv_first, qkv_second),
            (out_weight, out_first, out_second),
            (up_weight, up_first, up_second),
            (down_weight, down_first, down_second),
            (gains_biases, small_first, small_second),
        ],
        [
            (second_rows, part, matrix_decay),
            (0, part, matrix_decay),
            (part, part, matrix_decay),
            (part + blocks * part, 0, matrix_decay),
            (second_rows + 3 * part, 1, 0.0),
        ],
    )
    return (output, input_grad, *results)


def solution(mesh):
    rows = P(("dp", "shard"), None)
    matrix = P("shard", None)
    vector = P("shard")
    return jax.shard_map(
        shards_program,
        mesh=mesh,
        in_specs=(rows, rows, P(), P())
        + (matrix,) * 4
        + (vector,)
        + (matrix,) * 8
        + (vector, vector),
        out_specs=(rows, rows) + (matrix,) * 12 + (vector,) * 3,
        check_vma=False,
    )
```

```python
import functools
import math

import jax
import jax.numpy as jnp
from jax import lax
from jax.experimental import pallas as pl
from jax.experimental.pallas import tpu as pltpu
from jax.sharding import PartitionSpec as P

HEAD = 32
STEP = 10
LANES = 128
GROUP = 8
SMALL_PAD = 16
TILE_ROWS = 8
CHUNK = 64

norm_eps = 1e-05
beta_one = 0.9
beta_two = 0.95
learn_rate = 0.1
adam_eps = 1e-08
matrix_decay = 0.1
masked_score = -1e30
low = jnp.bfloat16
wide = jnp.float32
log2_e = math.log2(math.e)
score_scale = 1.0 / math.sqrt(HEAD)
tanh_scale = math.sqrt(2.0 / math.pi)
cubic = 0.044715


def dot_nn(left, right):
    return jnp.dot(left, right, preferred_element_type=wide)


def dot_nt(left, right):
    return lax.dot_general(left, right, (((1,), (1,)), ((), ())), preferred_element_type=wide)


def standardize(values):
    centered = values - jnp.mean(values, axis=-1, keepdims=True)
    root_inv = lax.rsqrt(jnp.mean(centered * centered, axis=-1, keepdims=True) + norm_eps)
    return centered * root_inv, root_inv


def norm_back(upstream, normed, root_inv, gain):
    scaled = upstream * gain
    inner_mean = jnp.mean(scaled, axis=-1, keepdims=True)
    cross_mean = jnp.mean(scaled * normed, axis=-1, keepdims=True)
    through = root_inv * (scaled - inner_mean - normed * cross_mean)
    return (
        through,
        jnp.sum(upstream * normed, axis=0, keepdims=True),
        jnp.sum(upstream, axis=0, keepdims=True),
    )


def iota(shape, dim):
    return lax.broadcasted_iota(jnp.int32, shape, dim)


def own_row(lengths, owners, device):
    return jnp.where(owners == device, lengths, 0)


def ends_both(own):
    count = own.shape[1]
    shape = (count, count)
    rows, cols = iota(shape, 0), iota(shape, 1)
    spread = jnp.broadcast_to(own, shape)
    ends_col = jnp.sum(jnp.where(cols <= rows, spread, 0), axis=1, keepdims=True)
    own_col = jnp.sum(jnp.where(cols == rows, spread, 0), axis=1, keepdims=True)
    ends_row = jnp.sum(
        jnp.where(rows <= cols, jnp.broadcast_to(own_col, shape), 0), axis=0, keepdims=True
    )
    return ends_col, ends_row


def fill_mask(bias_ref, own, rows):
    ends_col, ends_row = ends_both(own)
    count = own.shape[1]
    seg_row = jnp.sum(
        (ends_col <= iota((count, rows), 1)).astype(jnp.int32), axis=0, keepdims=True
    )
    seg_col = jnp.sum(
        (ends_row <= iota((rows, count), 0)).astype(jnp.int32), axis=1, keepdims=True
    )
    allowed = (seg_row == seg_col) & (iota((rows, rows), 0) <= iota((rows, rows), 1))
    bias_ref[...] = jnp.where(allowed, 0.0, masked_score)


def fill_small(small_ref, shard, pieces, first_row):
    for offset, piece in enumerate(pieces):
        small_ref[shard ^ offset] = piece[first_row:, :].astype(wide)


def fill_cols(full_ref, shard, pieces, first_row, rows, width):
    blocks = full_ref.shape[1] // width
    for offset, piece in enumerate(pieces):
        at = pl.multiple_of((shard ^ offset) * rows, rows)
        for block in range(blocks):
            start = first_row + block * rows
            full_ref[pl.ds(at, rows), block * width : (block + 1) * width] = piece[
                start : start + rows, :
            ]


def head_mask(head):
    lane = iota((1, LANES), 1)
    first = head * HEAD % LANES
    return ((lane >= first) & (lane < first + HEAD)).astype(wide).astype(low)


def head_tile(head):
    first = head * HEAD // LANES * LANES
    return slice(first, first + LANES)


def query_blocks(rows):
    size = min(256, rows)
    return [(at, at + size) for at in range(0, rows, size)]


def put_blocks(target, row, source, width):
    rows = source.shape[0]
    for block in range(source.shape[1] // width):
        cols = slice(block * width, (block + 1) * width)
        target[row : row + rows, :] = source[:, cols].astype(low)
        row += rows
    return row


def fetch_all(sources, buffers, sems):
    copies = [
        pltpu.make_async_copy(source, buffer, sems.at[index])
        for index, (source, buffer) in enumerate(zip(sources, buffers))
    ]
    for copy in copies:
        copy.start()
    return copies


def pack_first_kernel(qkv_ref, small_ref, first_ref, qkv_buf, small_buf, sems):
    width = first_ref.shape[1]
    small_copy, qkv_copy = fetch_all((small_ref, qkv_ref), (small_buf, qkv_buf), sems)
    small_copy.wait()
    parts = [
        small_buf[block * width : (block + 1) * width].reshape(1, width)
        for block in range(small_buf.shape[0] // width)
    ]
    parts.append(jnp.zeros((SMALL_PAD - len(parts), width), wide))
    first_ref[first_ref.shape[0] - SMALL_PAD :, :] = jnp.concatenate(parts, axis=0).astype(low)
    qkv_copy.wait()
    put_blocks(first_ref, 0, qkv_buf, width)


def pack_second_kernel(out_ref, up_ref, down_ref, second_ref, out_buf, up_buf, down_buf, sems):
    width = second_ref.shape[1]
    buffers = (out_buf, up_buf, down_buf)
    copies = fetch_all((out_ref, up_ref, down_ref), buffers, sems)
    row = 0
    for copy, buffer in zip(copies, buffers):
        copy.wait()
        row = put_blocks(second_ref, row, buffer, width)


def prepare_kernel(shards, x_ref, seed_ref, len_ref, owner_ref, bias_ref, norm_ref, root_ref, low_ref):
    rows = x_ref.shape[0]
    device = lax.axis_index("dp") * shards + lax.axis_index("shard")
    own = own_row(len_ref[...], owner_ref[...], device)
    fill_mask(bias_ref, own, rows)
    normed, root = standardize(x_ref[...].astype(wide))
    norm_ref[...] = normed
    root_ref[...] = root
    live = jnp.sum(own, axis=1, keepdims=True)
    live_rows = (iota((rows, 1), 0) < live).astype(wide)
    low_ref[...] = (seed_ref[...].astype(wide) * live_rows).astype(low)


def attend_kernel(shards, *refs):
    norm_ref, bias_ref = refs[:2]
    pieces = refs[2 : 2 + shards]
    joined_ref, out_ref, log_ref, att_ref, weight_ref, small_ref = refs[2 + shards :]
    rows, width = norm_ref.shape
    shard = lax.axis_index("shard")
    part = width // shards
    fill_cols(weight_ref, shard, pieces, 0, part, width)
    fill_small(small_ref, shard, pieces, 3 * part)
    gain, shift = small_ref[0, 0:1, :], small_ref[0, 1:2, :]
    bias_query, bias_value = small_ref[1, 1:2, :], small_ref[1, 2:3, :]
    hidden = (norm_ref[...] * gain + shift).astype(low)
    for block, bias in enumerate((bias_query, None, bias_value)):
        cols = slice(block * width, (block + 1) * width)
        value = dot_nn(hidden, weight_ref[:, cols])
        if bias is not None:
            value = value + bias
        joined_ref[:, cols] = value.astype(low)
    values_t = joined_ref[:, 2 * width :].T
    units = [
        (head, start, stop) for head in range(width // HEAD) for start, stop in query_blocks(rows)
    ]

    def raw_scores(head, start, stop):
        tile = head_tile(head)
        key_tile = joined_ref[:stop, width + tile.start : width + tile.stop] * head_mask(head)
        return dot_nt(key_tile, joined_ref[start:stop, tile])

    ahead = raw_scores(*units[0])
    for index, (head, start, stop) in enumerate(units):
        raw = ahead
        if index + 1 < len(units):
            ahead = raw_scores(*units[index + 1])
        feature = slice(head * HEAD, (head + 1) * HEAD)
        scores = []
        top = None
        for at in range(0, stop, CHUNK):
            piece = raw[at : at + CHUNK] * (score_scale * log2_e)
            piece = piece + bias_ref[at : at + CHUNK, start:stop]
            scores.append(piece)
            top = piece if top is None else jnp.maximum(top, piece)
        top = jnp.max(top, axis=0, keepdims=True)
        exponents = []
        total = None
        for piece in scores:
            piece = jnp.exp2(piece - top)
            total = piece if total is None else total + piece
            exponents.append(piece.astype(low))
        total = jnp.sum(total, axis=0, keepdims=True)
        mixed = dot_nn(values_t[feature, :stop], jnp.concatenate(exponents, axis=0))
        att_ref[feature, start:stop] = mixed * (1.0 / total)
        log_ref[head : head + 1, start:stop] = top + jnp.log2(total)
    out_ref[...] = att_ref[...].astype(low).T


def feed_first_kernel(shards, *refs):
    x_ref, att_ref, seed_ref = refs[:3]
    firsts = refs[3 : 3 + shards]
    pieces = refs[3 + shards : 3 + 2 * shards]
    refs = refs[3 + 2 * shards :]
    act_ref, base_ref, dhidden_ref, norm_ref, root_ref, out_w, down_w, sums_ref = refs[:8]
    keep_ref, send_ref, small_ref, up_w, grads_ref = refs[8:]
    rows, width = x_ref.shape
    hidden_count = up_w.shape[1]
    shard = lax.axis_index("shard")
    part = width // shards
    blocks = hidden_count // width
    down_part = hidden_count // shards
    fill_small(small_ref, shard, firsts, 3 * part)
    fill_cols(out_w, shard, pieces, 0, part, width)
    fill_cols(up_w, shard, pieces, part, part, width)
    fill_cols(down_w, shard, pieces, part + blocks * part, down_part, width)
    gain, shift = small_ref[0, 2:3, :], small_ref[1, 0:1, :]
    bias_out, bias_down = small_ref[2, 0:1, :], small_ref[2, 1:2, :]
    bias_up = [small_ref[2, 2:3, :]] + [small_ref[3, row : row + 1, :] for row in range(3)]
    seed_low = seed_ref[...]
    middle = x_ref[...].astype(wide) + (dot_nn(att_ref[...], out_w[...]) + bias_out)
    base_ref[...] = middle + bias_down
    normed, root = standardize(middle)
    norm_ref[...] = normed
    root_ref[...] = root
    hidden = (normed * gain + shift).astype(low)
    hidden_t = hidden.T
    dhidden = jnp.zeros((rows, width), wide)
    sums_ref[...] = jnp.zeros(sums_ref.shape, wide)

    def raw_products(block):
        cols = slice(block * width, (block + 1) * width)
        return dot_nn(hidden, up_w[:, cols]), dot_nt(seed_low, down_w[cols, :])

    ahead = raw_products(0)
    for block in range(blocks):
        cols = slice(block * width, (block + 1) * width)
        raw, dact = ahead
        if block + 1 < blocks:
            ahead = raw_products(block + 1)
        act, dpre = [], []
        for at in range(0, rows, CHUNK):
            pre = raw[at : at + CHUNK] + bias_up[block]
            square = pre * pre
            bend = jnp.tanh(pre * (tanh_scale + (tanh_scale * cubic) * square))
            half = 0.5 + 0.5 * bend
            act.append((pre * half).astype(low))
            slope = 0.5 * tanh_scale + (1.5 * tanh_scale * cubic) * square
            slope = half + (pre * slope) * (1.0 - bend * bend)
            dpre.append((dact[at : at + CHUNK] * slope).astype(low))
        act = jnp.concatenate(act, axis=0)
        dpre = jnp.concatenate(dpre, axis=0)
        act_ref[:, cols] = act
        dhidden = dhidden + dot_nt(dpre, up_w[:, cols])
        grad_down = dot_nn(act.T, seed_low)
        grad_up = dot_nn(hidden_t, dpre)
        for piece in range(width // down_part):
            target = block * (width // down_part) + piece
            grads_ref[target, :down_part, :] = grad_down[
                piece * down_part : (piece + 1) * down_part, :
            ]
        for target in range(shards):
            at = down_part + block * part
            grads_ref[target, at : at + part, :] = grad_up[target * part : (target + 1) * part, :]
        sums_ref[4 + block : 5 + block, :] = jnp.sum(dpre.astype(wide), axis=0, keepdims=True)
    dhidden_ref[...] = dhidden
    part_ways(grads_ref, keep_ref, send_ref, shard & 1)


def output_kernel(base_ref, act_ref, down_w, out_ref):
    out_ref[...] = (base_ref[...] + dot_nn(act_ref[...], down_w[...])).astype(low)


def feed_last_kernel(shards, *refs):
    att_ref, seed_ref, dhidden_ref, norm_ref, root_ref, out_w, sums_in = refs[:7]
    firsts = refs[7 : 7 + shards]
    middle_ref, dattend_ref, grad_ref, sums_ref, small_ref = refs[7 + shards :]
    rows, width = norm_ref.shape
    shard = lax.axis_index("shard")
    fill_small(small_ref, shard, firsts, 3 * (width // shards))
    seed = seed_ref[...].astype(wide)
    through, gain_grad, shift_grad = norm_back(
        dhidden_ref[...], norm_ref[...], root_ref[...], small_ref[0, 2:3, :]
    )
    dmiddle = seed + through
    middle_ref[...] = dmiddle
    dmiddle_low = dmiddle.astype(low)
    dattend_ref[...] = dot_nt(dmiddle_low, out_w[...]).astype(low)
    grad_ref[...] = dot_nn(att_ref[...].T, dmiddle_low)
    sums_ref[...] = sums_in[...]
    sums_ref[0:1, :] = gain_grad
    sums_ref[1:2, :] = shift_grad
    sums_ref[2:3, :] = jnp.sum(dmiddle_low.astype(wide), axis=0, keepdims=True)
    sums_ref[3:4, :] = jnp.sum(seed, axis=0, keepdims=True)


def part_ways(grads_ref, keep_ref, send_ref, side):
    for pair in range(keep_ref.shape[0]):
        keep_ref[pair] = grads_ref[2 * pair + side]
        send_ref[pair] = grads_ref[2 * pair + 1 - side].astype(low)


def back_heads(
    heads, joined_ref, dattend_ref, log_ref, bias_ref, mixed_ref, dquery_t, dkey, dvalue
):
    rows = joined_ref.shape[0]
    width = joined_ref.shape[1] // 3
    first = heads[0] * HEAD
    count = len(heads) * HEAD
    base = first // LANES * LANES
    tile = slice(base, base + LANES)
    inside = slice(first - base, first - base + count)
    keys_t = joined_ref[:, width + base : width + base + LANES].T
    datt_t = dattend_ref[:, tile].T[inside]
    inner = datt_t.astype(wide) * mixed_ref[first : first + count, :]
    units = [(head, start, stop) for head in heads for start, stop in query_blocks(rows)]

    def raw_products(head, start, stop):
        mask = head_mask(head)
        key_tile = joined_ref[:stop, width + base : width + base + LANES] * mask
        value_tile = joined_ref[:stop, 2 * width + base : 2 * width + base + LANES] * mask
        query = joined_ref[start:stop, tile]
        datt = dattend_ref[start:stop, tile]
        return dot_nt(key_tile, query), dot_nt(value_tile, datt), query * mask, datt * mask

    ahead = raw_products(*units[0])
    for index, (head, start, stop) in enumerate(units):
        raw, dprobs, query, datt = ahead
        if index + 1 < len(units):
            ahead = raw_products(*units[index + 1])
        local = head * HEAD - first
        feature = slice(local, local + HEAD)
        weighted = jnp.sum(inner[feature, start:stop], axis=0, keepdims=True)
        logs = log_ref[head : head + 1, start:stop]
        probs, dscores = [], []
        for at in range(0, stop, CHUNK):
            piece = raw[at : at + CHUNK] * (score_scale * log2_e)
            piece = jnp.exp2(piece + bias_ref[at : at + CHUNK, start:stop] - logs)
            probs.append(piece.astype(low))
            piece = piece * (dprobs[at : at + CHUNK] - weighted)
            dscores.append(piece.astype(low))
        probs = jnp.concatenate(probs, axis=0)
        dscores = jnp.concatenate(dscores, axis=0)
        depth = slice(head * HEAD - base, head * HEAD - base + HEAD)
        dquery_t[depth, start:stop] = (
            dot_nn(keys_t[depth, :stop], dscores) * score_scale
        ).astype(low)
        dvalue[:stop, :] += dot_nn(probs, datt)
        dkey[:stop, :] += dot_nn(dscores, query)


def back_kernel(shards, *refs):
    shared = refs[:5]
    norm_ref, root_ref, middle_ref, sums_in, grad_out = refs[5:10]
    pieces = refs[10 : 10 + shards]
    refs = refs[10 + shards :]
    dx_ref, keep_ref, send_ref = refs[:3]
    weight_ref, small_ref, dquery_t, dkey, dvalue, djoined, grads_ref = refs[3:]
    rows, width = norm_ref.shape
    shard = lax.axis_index("shard")
    part = width // shards
    fill_cols(weight_ref, shard, pieces, 0, part, width)
    fill_small(small_ref, shard, pieces, 3 * part)
    gain, shift = small_ref[0, 0:1, :], small_ref[0, 1:2, :]
    per_tile = LANES // HEAD
    for first in range(0, width, LANES):
        dkey[...] = jnp.zeros(dkey.shape, wide)
        dvalue[...] = jnp.zeros(dvalue.shape, wide)
        heads = range(first // HEAD, first // HEAD + per_tile)
        back_heads(heads, *shared, dquery_t, dkey, dvalue)
        values = (dquery_t[...].T, dkey[...] * score_scale, dvalue[...])
        for block, value in enumerate(values):
            at = block * width + first
            djoined[:, at : at + LANES] = value.astype(low)
    normed, root = norm_ref[...], root_ref[...]
    hidden_t = (normed * gain + shift).astype(low).T
    dhidden = jnp.zeros((rows, width), wide)
    bias_sums = []
    for block in range(3):
        cols = slice(block * width, (block + 1) * width)
        piece = djoined[:, cols]
        dhidden = dhidden + dot_nt(piece, weight_ref[:, cols])
        grad = dot_nn(hidden_t, piece)
        for target in range(shards):
            grads_ref[target, block * part : (block + 1) * part, :] = grad[
                target * part : (target + 1) * part, :
            ]
        if block != 1:
            bias_sums.append(jnp.sum(piece.astype(wide), axis=0, keepdims=True))
    through, gain_grad, shift_grad = norm_back(dhidden, normed, root, gain)
    dx_ref[...] = middle_ref[...] + through
    sums = [gain_grad, shift_grad, sums_in[0:1, :], sums_in[1:2, :]] + bias_sums
    sums += [sums_in[row : row + 1, :] for row in range(2, 8)]
    per_shard = len(sums) // shards
    body = 4 * part
    empty = [jnp.zeros((grads_ref.shape[1] - body - per_shard, width), wide)]
    for target in range(shards):
        rows_here = sums[target * per_shard : (target + 1) * per_shard]
        grads_ref[target, 3 * part : body, :] = grad_out[target * part : (target + 1) * part, :]
        grads_ref[target, body:, :] = jnp.concatenate(rows_here + empty, axis=0)
    part_ways(grads_ref, keep_ref, send_ref, shard & 1)


def halve_kernel(axis, bit, counts, kept, arrived, *outs):
    side = (lax.axis_index(axis) >> bit) & 1
    for pair in range(outs[0].shape[0]):
        mine = kept[2 * pair + side] + arrived[2 * pair + side].astype(wide)
        other = kept[2 * pair + 1 - side] + arrived[2 * pair + 1 - side].astype(wide)
        row = 0
        for chunk, count in enumerate(counts):
            outs[2 * chunk][pair] = mine[row : row + count]
            outs[2 * chunk + 1][pair] = other[row : row + count].astype(low)
            row += count


def piece_spans(total, tail, group):
    spans = [((total - tail) // group, 0, True)]
    if tail:
        spans.append((tail, total - tail, False))
    return spans


def split_kernel(tail, *refs):
    arrived, keep_ref, send_ref, sum_ref = refs[:-3], *refs[-3:]
    group = sum_ref.shape[0]
    total = arrived[0][...]
    for piece in arrived[1:]:
        total = total + piece[...].astype(wide)
    for index in range(group):
        row = 0
        for rows, first, moves in piece_spans(total.shape[0], tail, group):
            at = first + index * rows if moves else first
            sum_ref[index, row : row + rows, :] = total[at : at + rows, :]
            row += rows
    side = lax.axis_index("dp") & 1
    for pair in range(group // 2):
        keep_ref[pair] = sum_ref[2 * pair + side]
        send_ref[pair] = sum_ref[2 * pair + 1 - side].astype(low)


def piece_kernel(*refs):
    parts = [
        mine[...].reshape(mine.shape[-2:]).astype(wide)
        + other[...].reshape(other.shape[-2:]).astype(wide)
        for mine, other in zip(refs[:-1:2], refs[1:-1:2])
    ]
    refs[-1][...] = jnp.concatenate(parts, axis=0).astype(low)


def adam_values(weight, grad, first, second, decay_rate):
    first_next = beta_one * first + (1.0 - beta_one) * grad
    second_next = beta_two * second + (1.0 - beta_two) * grad * grad
    first_fix = 1.0 - beta_one**STEP
    second_fix = 1.0 - beta_two**STEP
    update = (first_next * (1.0 / first_fix)) / (
        jnp.sqrt(second_next * (1.0 / second_fix)) + adam_eps
    )
    return first_next, second_next, weight - learn_rate * (update + decay_rate * weight)


def adam_kernel(group, spans, layout, *refs):
    pieces = refs[:group]
    count = len(layout)
    states = refs[group : group + 3 * count]
    results = refs[group + 3 * count : group + 6 * count]
    buffers = refs[group + 6 * count : group + 9 * count]
    grad_ref, sems = refs[-2:]
    copies = []
    for offset, piece in enumerate(pieces):
        value = piece[...].astype(wide)
        index = (lax.axis_index("dp") & (group - 1)) ^ offset
        for rows, first, row in spans:
            at = pl.multiple_of(first + index * rows, TILE_ROWS)
            grad_ref[pl.ds(at, rows), :] = value[row : row + rows, :]
    width = grad_ref.shape[1]
    for array, (first_row, stride, decay) in enumerate(layout):
        weight, first, second = states[3 * array : 3 * array + 3]
        new = buffers[3 * array : 3 * array + 3]
        vector = len(weight.shape) == 1
        rows = 1 if vector else weight.shape[0]
        for block in range(weight.shape[-1] // width):
            cols = slice(block * width, (block + 1) * width)
            where = cols if vector else (slice(None), cols)
            at = first_row + block * stride
            values = adam_values(
                weight[where].reshape(rows, width),
                grad_ref[at : at + rows, :],
                first[where].reshape(rows, width),
                second[where].reshape(rows, width),
                decay,
            )
            for target, value in zip(new, values):
                target[where] = value.reshape(width) if vector else value
        for index in range(3 * array, 3 * array + 3):
            copies.append(
                pltpu.make_async_copy(buffers[index], results[index], sems.at[index])
            )
            copies[-1].start()
    for copy in copies:
        copy.wait()


def local_call(kernel, outs, operands, scratch=(), flops=0, name=None, fetch=False, sems=0):
    in_space = pltpu.HBM if fetch else pltpu.VMEM
    out_space = pltpu.HBM if sems else pltpu.VMEM
    outs = [jax.ShapeDtypeStruct(*out) for out in outs]
    moved = sum(
        math.prod(item.shape) * item.dtype.itemsize for item in list(operands) + outs
    )
    scratch_shapes = [pltpu.VMEM(*item) for item in scratch]
    if fetch or sems:
        scratch_shapes.append(pltpu.SemaphoreType.DMA((sems or len(operands),)))
    limit = 56 if fetch else 40
    return pl.pallas_call(
        kernel,
        out_shape=outs,
        in_specs=[pl.BlockSpec(memory_space=in_space)] * len(operands),
        out_specs=[pl.BlockSpec(memory_space=out_space)] * len(outs),
        scratch_shapes=scratch_shapes,
        compiler_params=pltpu.CompilerParams(vmem_limit_bytes=limit * 1024 * 1024),
        cost_estimate=pl.CostEstimate(flops=flops, bytes_accessed=moved, transcendentals=0),
        name=name,
    )(*operands)


def exchange(values, axis, mask):
    count = lax.axis_size(axis)
    return lax.ppermute(values, axis, [(index, index ^ mask) for index in range(count)])


def gather_pieces(value, group):
    found = {0: value}
    found[1] = exchange(value, "dp", 1)
    far = group // 2
    while far > 1:
        for offset in sorted(found):
            if offset & 1 == 0:
                found[offset ^ far] = exchange(found[offset], "dp", far)
        if far == group // 2:
            found[far], found[1] = lax.optimization_barrier((found[far], found[1]))
        far //= 2
    for offset in range(2, group, 2):
        found[offset ^ 1] = exchange(found[offset], "dp", 1)
    return [found[offset] for offset in range(group)]


def halve_call(axis, bit, kept, arrived, name, counts=None):
    half, rows, width = kept.shape
    counts = counts or [rows]
    outs = []
    for count in counts:
        shape = (half // 2, count, width)
        outs += [(shape, wide), (shape, low)]
    kernel = functools.partial(halve_kernel, axis, bit, counts)
    return local_call(kernel, outs, [kept, arrived], name=name)


def split_chunk(chunk, tail, group):
    rows, width = chunk[0].shape
    half = (group // 2, (rows - tail) // group + tail, width)
    keep, send = local_call(
        functools.partial(split_kernel, tail),
        [(half, wide), (half, low)],
        chunk,
        [((group,) + half[1:], wide)],
        name="split_sum",
    )
    return keep, exchange(send, "dp", 1)


def after_arrivals(early, arrival):
    ready, arrival = lax.optimization_barrier(([flat[1] for flat in early], arrival))
    return [[flat[0], item] for flat, item in zip(early, ready)], arrival


def next_sum(flat, bit):
    keep, send = halve_call("dp", bit, *flat, "halve_dp")
    return [keep, exchange(send, "dp", 1 << bit)]


def finish_sum(early, late, group):
    replicas = lax.axis_size("dp")
    bit = 1
    while (1 << bit) < group:
        early = [next_sum(flat, bit) for flat in early]
        last = (2 << bit) >= group
        waited, ready = after_arrivals(early[:1] if last else early, late[1])
        early = waited + early[len(waited) :]
        late = [late[0], ready]
        late = next_sum(late, bit)
        bit += 1
    flat = [item for chunk in early + [late] for item in chunk]
    width = flat[0].shape[-1]
    rows = sum(item.shape[1] for item in flat[::2])
    (piece,) = local_call(piece_kernel, [((rows, width), low)], flat, name="piece_sum")
    mask = group
    while mask < replicas:
        other = exchange(piece, "dp", mask)
        (piece,) = local_call(piece_kernel, [((rows, width), low)], [piece, other], name="far_sum")
        mask *= 2
    return gather_pieces(piece, group)


def adam_call(pieces, counts, tails, states, layout):
    group = len(pieces)
    width = pieces[0].shape[1]
    spans = []
    first = row = 0
    for total, tail in zip(counts, tails):
        for rows, start, moves in piece_spans(total, tail, group):
            spans.append((rows, first + start, row))
            row += rows
            first += rows * (group - 1) * (not moves)
        first += total
    outs = [(state[0].shape, wide) for state in states for _ in range(3)]
    return local_call(
        functools.partial(adam_kernel, group, spans, layout),
        outs,
        pieces + [item for state in states for item in state],
        outs + [((first, width), wide)],
        name="adam",
        sems=len(outs),
    )


def shards_program(
    tokens,
    cotangent,
    lengths,
    seq_owner,
    qkv_weight,
    out_weight,
    up_weight,
    down_weight,
    gains_biases,
    qkv_first,
    qkv_second,
    out_first,
    out_second,
    up_first,
    up_second,
    down_first,
    down_second,
    small_first,
    small_second,
):
    rows, width = tokens.shape
    shards = lax.axis_size("shard")
    heads = width // HEAD
    part = qkv_weight.shape[0]
    hidden_count = up_weight.shape[1]
    group = min(GROUP, lax.axis_size("dp"))
    lengths = lengths.reshape(1, -1)
    seq_owner = seq_owner.reshape(1, -1)
    first_rows = 3 * part + SMALL_PAD
    second_rows = part + up_weight.size // width + down_weight.shape[0]
    (first_pack,) = local_call(
        pack_first_kernel,
        [((first_rows, width), low)],
        [qkv_weight, gains_biases],
        [(qkv_weight.shape, wide), (gains_biases.shape, wide)],
        name="pack_first",
        fetch=True,
    )
    firsts = {0: first_pack}
    firsts[2] = exchange(first_pack, "shard", 2)
    firsts[1] = exchange(first_pack, "shard", 1)
    first_pack, matrices = lax.optimization_barrier(
        (first_pack, [out_weight, up_weight, down_weight])
    )
    (second_pack,) = local_call(
        pack_second_kernel,
        [((second_rows, width), low)],
        matrices,
        [(item.shape, wide) for item in matrices],
        name="pack_second",
        fetch=True,
    )
    early_tokens, second_pack = lax.optimization_barrier((tokens, second_pack))
    square = (rows, rows)
    bias, normed, root, seed = local_call(
        functools.partial(prepare_kernel, shards),
        [(square, wide), ((rows, width), wide), ((rows, 1), wide), ((rows, width), low)],
        [early_tokens, cotangent, lengths, seq_owner],
        name="prepare",
    )
    seconds = {0: second_pack}
    seconds[2] = exchange(second_pack, "shard", 2)
    seconds[1] = exchange(second_pack, "shard", 1)
    firsts[2], bias, normed, root, seed = lax.optimization_barrier(
        (firsts[2], bias, normed, root, seed)
    )
    firsts[3] = exchange(firsts[2], "shard", 1)
    firsts = [firsts[offset] for offset in range(shards)]
    joined, attended, log_sums, mixed = local_call(
        functools.partial(attend_kernel, shards),
        [
            ((rows, 3 * width), low),
            ((rows, width), low),
            ((heads, rows), wide),
            ((width, rows), wide),
        ],
        [normed, bias] + firsts,
        [((width, 3 * width), low), ((shards, SMALL_PAD, width), wide)],
        flops=heads * rows * rows * 640,
        name="attend",
    )
    attended, seconds[2] = lax.optimization_barrier((attended, seconds[2]))
    seconds[3] = exchange(seconds[2], "shard", 1)
    seconds = [seconds[offset] for offset in range(shards)]
    down_rows, up_rows = down_weight.shape[0], up_weight.size // width
    blocks = hidden_count // width
    square = (width, width)
    pair = (shards // 2, down_rows + up_rows, width)
    act, base, dhidden, norm_two, root_two, out_full, down_full, sums, kept_ffn, send_ffn = (
        local_call(
            functools.partial(feed_first_kernel, shards),
            [
                ((rows, hidden_count), low),
                ((rows, width), wide),
                ((rows, width), wide),
                ((rows, width), wide),
                ((rows, 1), wide),
                (square, low),
                ((hidden_count, width), low),
                ((SMALL_PAD, width), wide),
                (pair, wide),
                (pair, low),
            ],
            [tokens, attended, seed] + firsts + seconds,
            [
                ((shards, SMALL_PAD, width), wide),
                ((width, hidden_count), low),
                ((shards, down_rows + up_rows, width), wide),
            ],
            flops=rows * width * hidden_count * 10,
            name="feed_first",
        )
    )
    arrived_ffn = exchange(send_ffn, "shard", 1)
    (output,) = local_call(
        output_kernel,
        [((rows, width), low)],
        [base, act, down_full],
        flops=rows * width * hidden_count * 2,
        name="output",
    )
    middle_grad, attended_grad, grad_out, sums = local_call(
        functools.partial(feed_last_kernel, shards),
        [((rows, width), wide), ((rows, width), low), (square, wide), ((SMALL_PAD, width), wide)],
        [attended, seed, dhidden, norm_two, root_two, out_full, sums] + firsts,
        [((shards, SMALL_PAD, width), wide)],
        flops=rows * width * width * 4,
        name="feed_last",
    )
    attended_grad, arrived_ffn = lax.optimization_barrier((attended_grad, arrived_ffn))
    keep_down, send_down, keep_up, send_up = halve_call(
        "shard", 1, kept_ffn, arrived_ffn, "halve_ffn", [down_rows, up_rows]
    )
    attended_grad, send_down, send_up = lax.optimization_barrier(
        (attended_grad, send_down, send_up)
    )
    arrived_down = exchange(send_down, "shard", 2)
    arrived_up = exchange(send_up, "shard", 2)
    tail = TILE_ROWS
    att_rows = 4 * part + tail
    pair = (shards // 2, att_rows, width)
    input_grad, kept_att, send_att = local_call(
        functools.partial(back_kernel, shards),
        [((rows, width), wide), (pair, wide), (pair, low)],
        [joined, attended_grad, log_sums, bias, mixed]
        + [normed, root, middle_grad, sums, grad_out]
        + firsts,
        [
            ((width, 3 * width), low),
            ((shards, SMALL_PAD, width), wide),
            ((LANES, rows), low),
            ((rows, LANES), wide),
            ((rows, LANES), wide),
            ((rows, 3 * width), low),
            ((shards, att_rows, width), wide),
        ],
        flops=heads * rows * rows * 256 * 10,
        name="back",
    )
    send_att, arrived_down, arrived_up = lax.optimization_barrier(
        (send_att, arrived_down, arrived_up)
    )
    arrived_att = exchange(send_att, "shard", 1)
    keep_att, send_att = halve_call("shard", 1, kept_att, arrived_att, "halve_att")
    arrived_att = exchange(send_att, "shard", 2)
    early = [
        split_chunk([keep_down[0], arrived_down[0]], 0, group),
        split_chunk([keep_up[0], arrived_up[0]], 0, group),
    ]
    early, arrived_att = after_arrivals(early, arrived_att)
    late = split_chunk([keep_att[0], arrived_att[0]], tail, group)
    pieces = finish_sum(early, late, group)
    second_at = down_rows + up_rows
    results = adam_call(
        pieces,
        (down_rows, up_rows, att_rows),
        (0, 0, tail),
        [
            (qkv_weight, qkv_first, qkv_second),
            (out_weight, out_first, out_second),
            (up_weight, up_first, up_second),
            (down_weight, down_first, down_second),
            (gains_biases, small_first, small_second),
        ],
        [
            (second_at, part, matrix_decay),
            (second_at + 3 * part, part, matrix_decay),
            (down_rows, part, matrix_decay),
            (0, 0, matrix_decay),
            (second_at + 4 * part, 1, 0.0),
        ],
    )
    return (output, input_grad, *results)


def solution(mesh):
    rows = P(("dp", "shard"), None)
    matrix = P("shard", None)
    vector = P("shard")
    return jax.shard_map(
        shards_program,
        mesh=mesh,
        in_specs=(rows, rows, P(), P())
        + (matrix,) * 4
        + (vector,)
        + (matrix,) * 8
        + (vector, vector),
        out_specs=(rows, rows) + (matrix,) * 12 + (vector,) * 3,
        check_vma=False,
    )
```

```python
import functools
import math

import jax
import jax.numpy as jnp
from jax import lax
from jax.experimental import pallas as pl
from jax.experimental.pallas import tpu as pltpu
from jax.sharding import PartitionSpec as P

HEAD = 32
STEP = 10
LANES = 128
GROUP = 8
SMALL_PAD = 16
TILE_ROWS = 8
CHUNK = 64

norm_eps = 1e-05
beta_one = 0.9
beta_two = 0.95
learn_rate = 0.1
adam_eps = 1e-08
matrix_decay = 0.1
masked_score = -1e30
low = jnp.bfloat16
wide = jnp.float32
log2_e = math.log2(math.e)
score_scale = 1.0 / math.sqrt(HEAD)
tanh_scale = math.sqrt(2.0 / math.pi)
cubic = 0.044715


def dot_nn(left, right):
    return jnp.dot(left, right, preferred_element_type=wide)


def dot_nt(left, right):
    return lax.dot_general(left, right, (((1,), (1,)), ((), ())), preferred_element_type=wide)


def standardize(values):
    centered = values - jnp.mean(values, axis=-1, keepdims=True)
    root_inv = lax.rsqrt(jnp.mean(centered * centered, axis=-1, keepdims=True) + norm_eps)
    return centered * root_inv, root_inv


def norm_back(upstream, normed, root_inv, gain):
    scaled = upstream * gain
    inner_mean = jnp.mean(scaled, axis=-1, keepdims=True)
    cross_mean = jnp.mean(scaled * normed, axis=-1, keepdims=True)
    through = root_inv * (scaled - inner_mean - normed * cross_mean)
    return (
        through,
        jnp.sum(upstream * normed, axis=0, keepdims=True),
        jnp.sum(upstream, axis=0, keepdims=True),
    )


def iota(shape, dim):
    return lax.broadcasted_iota(jnp.int32, shape, dim)


def own_row(lengths, owners, device):
    return jnp.where(owners == device, lengths, 0)


def ends_both(own):
    count = own.shape[1]
    shape = (count, count)
    rows, cols = iota(shape, 0), iota(shape, 1)
    spread = jnp.broadcast_to(own, shape)
    ends_col = jnp.sum(jnp.where(cols <= rows, spread, 0), axis=1, keepdims=True)
    own_col = jnp.sum(jnp.where(cols == rows, spread, 0), axis=1, keepdims=True)
    ends_row = jnp.sum(
        jnp.where(rows <= cols, jnp.broadcast_to(own_col, shape), 0), axis=0, keepdims=True
    )
    return ends_col, ends_row


def fill_mask(bias_ref, own, rows):
    ends_col, ends_row = ends_both(own)
    count = own.shape[1]
    seg_row = jnp.sum(
        (ends_col <= iota((count, rows), 1)).astype(jnp.int32), axis=0, keepdims=True
    )
    seg_col = jnp.sum(
        (ends_row <= iota((rows, count), 0)).astype(jnp.int32), axis=1, keepdims=True
    )
    allowed = (seg_row == seg_col) & (iota((rows, rows), 0) <= iota((rows, rows), 1))
    bias_ref[...] = jnp.where(allowed, 0.0, masked_score)


def fill_small(small_ref, shard, pieces, first_row):
    for offset, piece in enumerate(pieces):
        small_ref[shard ^ offset] = piece[first_row:, :].astype(wide)


def fill_cols(full_ref, shard, pieces, first_row, rows, width):
    blocks = full_ref.shape[1] // width
    for offset, piece in enumerate(pieces):
        at = pl.multiple_of((shard ^ offset) * rows, rows)
        for block in range(blocks):
            start = first_row + block * rows
            full_ref[pl.ds(at, rows), block * width : (block + 1) * width] = piece[
                start : start + rows, :
            ]


def head_mask(head):
    lane = iota((1, LANES), 1)
    first = head * HEAD % LANES
    return ((lane >= first) & (lane < first + HEAD)).astype(wide).astype(low)


def head_tile(head):
    first = head * HEAD // LANES * LANES
    return slice(first, first + LANES)


def query_blocks(rows):
    size = min(256, rows)
    return [(at, at + size) for at in range(0, rows, size)]


def put_blocks(target, row, source, width):
    rows = source.shape[0]
    for block in range(source.shape[1] // width):
        cols = slice(block * width, (block + 1) * width)
        target[row : row + rows, :] = source[:, cols].astype(low)
        row += rows
    return row


def fetch_all(sources, buffers, sems):
    copies = [
        pltpu.make_async_copy(source, buffer, sems.at[index])
        for index, (source, buffer) in enumerate(zip(sources, buffers))
    ]
    for copy in copies:
        copy.start()
    return copies


def pack_first_kernel(qkv_ref, small_ref, first_ref, qkv_buf, small_buf, sems):
    width = first_ref.shape[1]
    small_copy, qkv_copy = fetch_all((small_ref, qkv_ref), (small_buf, qkv_buf), sems)
    small_copy.wait()
    parts = [
        small_buf[block * width : (block + 1) * width].reshape(1, width)
        for block in range(small_buf.shape[0] // width)
    ]
    parts.append(jnp.zeros((SMALL_PAD - len(parts), width), wide))
    first_ref[first_ref.shape[0] - SMALL_PAD :, :] = jnp.concatenate(parts, axis=0).astype(low)
    qkv_copy.wait()
    put_blocks(first_ref, 0, qkv_buf, width)


def pack_second_kernel(out_ref, up_ref, down_ref, second_ref, out_buf, up_buf, down_buf, sems):
    width = second_ref.shape[1]
    buffers = (out_buf, up_buf, down_buf)
    copies = fetch_all((out_ref, up_ref, down_ref), buffers, sems)
    row = 0
    for copy, buffer in zip(copies, buffers):
        copy.wait()
        row = put_blocks(second_ref, row, buffer, width)


def prepare_kernel(shards, x_ref, seed_ref, len_ref, owner_ref, bias_ref, norm_ref, root_ref, low_ref):
    rows = x_ref.shape[0]
    device = lax.axis_index("dp") * shards + lax.axis_index("shard")
    own = own_row(len_ref[...], owner_ref[...], device)
    fill_mask(bias_ref, own, rows)
    normed, root = standardize(x_ref[...].astype(wide))
    norm_ref[...] = normed
    root_ref[...] = root
    live = jnp.sum(own, axis=1, keepdims=True)
    live_rows = (iota((rows, 1), 0) < live).astype(wide)
    low_ref[...] = (seed_ref[...].astype(wide) * live_rows).astype(low)


def attend_kernel(shards, *refs):
    norm_ref, bias_ref = refs[:2]
    pieces = refs[2 : 2 + shards]
    joined_ref, out_ref, log_ref, att_ref, weight_ref, small_ref = refs[2 + shards :]
    rows, width = norm_ref.shape
    shard = lax.axis_index("shard")
    part = width // shards
    fill_cols(weight_ref, shard, pieces, 0, part, width)
    fill_small(small_ref, shard, pieces, 3 * part)
    gain, shift = small_ref[0, 0:1, :], small_ref[0, 1:2, :]
    bias_query, bias_value = small_ref[1, 1:2, :], small_ref[1, 2:3, :]
    hidden = (norm_ref[...] * gain + shift).astype(low)
    for block, bias in enumerate((bias_query, None, bias_value)):
        cols = slice(block * width, (block + 1) * width)
        value = dot_nn(hidden, weight_ref[:, cols])
        if bias is not None:
            value = value + bias
        joined_ref[:, cols] = value.astype(low)
    values_t = joined_ref[:, 2 * width :].T
    units = [
        (head, start, stop) for head in range(width // HEAD) for start, stop in query_blocks(rows)
    ]

    def raw_scores(head, start, stop):
        tile = head_tile(head)
        key_tile = joined_ref[:stop, width + tile.start : width + tile.stop] * head_mask(head)
        return dot_nt(key_tile, joined_ref[start:stop, tile])

    ahead = raw_scores(*units[0])
    for index, (head, start, stop) in enumerate(units):
        raw = ahead
        if index + 1 < len(units):
            ahead = raw_scores(*units[index + 1])
        feature = slice(head * HEAD, (head + 1) * HEAD)
        scores = []
        top = None
        for at in range(0, stop, CHUNK):
            piece = raw[at : at + CHUNK] * (score_scale * log2_e)
            piece = piece + bias_ref[at : at + CHUNK, start:stop]
            scores.append(piece)
            top = piece if top is None else jnp.maximum(top, piece)
        top = jnp.max(top, axis=0, keepdims=True)
        exponents = []
        total = None
        for piece in scores:
            piece = jnp.exp2(piece - top)
            total = piece if total is None else total + piece
            exponents.append(piece.astype(low))
        total = jnp.sum(total, axis=0, keepdims=True)
        mixed = dot_nn(values_t[feature, :stop], jnp.concatenate(exponents, axis=0))
        att_ref[feature, start:stop] = mixed * (1.0 / total)
        log_ref[head : head + 1, start:stop] = top + jnp.log2(total)
    out_ref[...] = att_ref[...].astype(low).T


def feed_first_kernel(shards, *refs):
    x_ref, att_ref, seed_ref = refs[:3]
    firsts = refs[3 : 3 + shards]
    pieces = refs[3 + shards : 3 + 2 * shards]
    refs = refs[3 + 2 * shards :]
    act_ref, base_ref, dhidden_ref, norm_ref, root_ref, out_w, down_w, sums_ref = refs[:8]
    keep_ref, send_ref, small_ref, up_w, grads_ref = refs[8:]
    rows, width = x_ref.shape
    hidden_count = up_w.shape[1]
    shard = lax.axis_index("shard")
    part = width // shards
    blocks = hidden_count // width
    down_part = hidden_count // shards
    fill_small(small_ref, shard, firsts, 3 * part)
    fill_cols(out_w, shard, pieces, 0, part, width)
    fill_cols(up_w, shard, pieces, part, part, width)
    fill_cols(down_w, shard, pieces, part + blocks * part, down_part, width)
    gain, shift = small_ref[0, 2:3, :], small_ref[1, 0:1, :]
    bias_out, bias_down = small_ref[2, 0:1, :], small_ref[2, 1:2, :]
    bias_up = [small_ref[2, 2:3, :]] + [small_ref[3, row : row + 1, :] for row in range(3)]
    seed_low = seed_ref[...]
    middle = x_ref[...].astype(wide) + (dot_nn(att_ref[...], out_w[...]) + bias_out)
    base_ref[...] = middle + bias_down
    normed, root = standardize(middle)
    norm_ref[...] = normed
    root_ref[...] = root
    hidden = (normed * gain + shift).astype(low)
    hidden_t = hidden.T
    dhidden = jnp.zeros((rows, width), wide)
    sums_ref[...] = jnp.zeros(sums_ref.shape, wide)

    def raw_products(block):
        cols = slice(block * width, (block + 1) * width)
        return dot_nn(hidden, up_w[:, cols]), dot_nt(seed_low, down_w[cols, :])

    ahead = raw_products(0)
    for block in range(blocks):
        cols = slice(block * width, (block + 1) * width)
        raw, dact = ahead
        if block + 1 < blocks:
            ahead = raw_products(block + 1)
        act, dpre = [], []
        for at in range(0, rows, CHUNK):
            pre = raw[at : at + CHUNK] + bias_up[block]
            square = pre * pre
            bend = jnp.tanh(pre * (tanh_scale + (tanh_scale * cubic) * square))
            half = 0.5 + 0.5 * bend
            act.append((pre * half).astype(low))
            slope = 0.5 * tanh_scale + (1.5 * tanh_scale * cubic) * square
            slope = half + (pre * slope) * (1.0 - bend * bend)
            dpre.append((dact[at : at + CHUNK] * slope).astype(low))
        act = jnp.concatenate(act, axis=0)
        dpre = jnp.concatenate(dpre, axis=0)
        act_ref[:, cols] = act
        dhidden = dhidden + dot_nt(dpre, up_w[:, cols])
        grad_down = dot_nn(act.T, seed_low)
        grad_up = dot_nn(hidden_t, dpre)
        for piece in range(width // down_part):
            target = block * (width // down_part) + piece
            grads_ref[target, :down_part, :] = grad_down[
                piece * down_part : (piece + 1) * down_part, :
            ]
        for target in range(shards):
            at = down_part + block * part
            grads_ref[target, at : at + part, :] = grad_up[target * part : (target + 1) * part, :]
        sums_ref[4 + block : 5 + block, :] = jnp.sum(dpre.astype(wide), axis=0, keepdims=True)
    dhidden_ref[...] = dhidden
    part_ways(grads_ref, keep_ref, send_ref, shard & 1)


def output_kernel(base_ref, act_ref, down_w, out_ref):
    out_ref[...] = (base_ref[...] + dot_nn(act_ref[...], down_w[...])).astype(low)


def feed_last_kernel(shards, *refs):
    att_ref, seed_ref, dhidden_ref, norm_ref, root_ref, out_w, sums_in = refs[:7]
    firsts = refs[7 : 7 + shards]
    middle_ref, dattend_ref, grad_ref, sums_ref, small_ref = refs[7 + shards :]
    rows, width = norm_ref.shape
    shard = lax.axis_index("shard")
    fill_small(small_ref, shard, firsts, 3 * (width // shards))
    seed = seed_ref[...].astype(wide)
    through, gain_grad, shift_grad = norm_back(
        dhidden_ref[...], norm_ref[...], root_ref[...], small_ref[0, 2:3, :]
    )
    dmiddle = seed + through
    middle_ref[...] = dmiddle
    dmiddle_low = dmiddle.astype(low)
    dattend_ref[...] = dot_nt(dmiddle_low, out_w[...]).astype(low)
    grad_ref[...] = dot_nn(att_ref[...].T, dmiddle_low)
    sums_ref[...] = sums_in[...]
    sums_ref[0:1, :] = gain_grad
    sums_ref[1:2, :] = shift_grad
    sums_ref[2:3, :] = jnp.sum(dmiddle_low.astype(wide), axis=0, keepdims=True)
    sums_ref[3:4, :] = jnp.sum(seed, axis=0, keepdims=True)


def part_ways(grads_ref, keep_ref, send_ref, side):
    for pair in range(keep_ref.shape[0]):
        keep_ref[pair] = grads_ref[2 * pair + side]
        send_ref[pair] = grads_ref[2 * pair + 1 - side].astype(low)


def back_heads(
    heads, joined_ref, dattend_ref, log_ref, bias_ref, mixed_ref, dquery_t, dkey, dvalue
):
    rows = joined_ref.shape[0]
    width = joined_ref.shape[1] // 3
    first = heads[0] * HEAD
    count = len(heads) * HEAD
    base = first // LANES * LANES
    tile = slice(base, base + LANES)
    inside = slice(first - base, first - base + count)
    keys_t = joined_ref[:, width + base : width + base + LANES].T
    datt_t = dattend_ref[:, tile].T[inside]
    inner = datt_t.astype(wide) * mixed_ref[first : first + count, :]
    units = [(head, start, stop) for head in heads for start, stop in query_blocks(rows)]

    def raw_products(head, start, stop):
        mask = head_mask(head)
        key_tile = joined_ref[:stop, width + base : width + base + LANES] * mask
        value_tile = joined_ref[:stop, 2 * width + base : 2 * width + base + LANES] * mask
        query = joined_ref[start:stop, tile]
        datt = dattend_ref[start:stop, tile]
        return dot_nt(key_tile, query), dot_nt(value_tile, datt), query * mask, datt * mask

    ahead = raw_products(*units[0])
    for index, (head, start, stop) in enumerate(units):
        raw, dprobs, query, datt = ahead
        if index + 1 < len(units):
            ahead = raw_products(*units[index + 1])
        local = head * HEAD - first
        feature = slice(local, local + HEAD)
        weighted = jnp.sum(inner[feature, start:stop], axis=0, keepdims=True)
        logs = log_ref[head : head + 1, start:stop]
        probs, dscores = [], []
        for at in range(0, stop, CHUNK):
            piece = raw[at : at + CHUNK] * (score_scale * log2_e)
            piece = jnp.exp2(piece + bias_ref[at : at + CHUNK, start:stop] - logs)
            probs.append(piece.astype(low))
            piece = piece * (dprobs[at : at + CHUNK] - weighted)
            dscores.append(piece.astype(low))
        probs = jnp.concatenate(probs, axis=0)
        dscores = jnp.concatenate(dscores, axis=0)
        depth = slice(head * HEAD - base, head * HEAD - base + HEAD)
        dquery_t[depth, start:stop] = (
            dot_nn(keys_t[depth, :stop], dscores) * score_scale
        ).astype(low)
        dvalue[:stop, :] += dot_nn(probs, datt)
        dkey[:stop, :] += dot_nn(dscores, query)


def back_kernel(shards, *refs):
    shared = refs[:5]
    norm_ref, root_ref, middle_ref, sums_in, grad_out = refs[5:10]
    pieces = refs[10 : 10 + shards]
    refs = refs[10 + shards :]
    dx_ref, keep_ref, send_ref = refs[:3]
    weight_ref, small_ref, dquery_t, dkey, dvalue, djoined, grads_ref = refs[3:]
    rows, width = norm_ref.shape
    shard = lax.axis_index("shard")
    part = width // shards
    fill_cols(weight_ref, shard, pieces, 0, part, width)
    fill_small(small_ref, shard, pieces, 3 * part)
    gain, shift = small_ref[0, 0:1, :], small_ref[0, 1:2, :]
    per_tile = LANES // HEAD
    for first in range(0, width, LANES):
        dkey[...] = jnp.zeros(dkey.shape, wide)
        dvalue[...] = jnp.zeros(dvalue.shape, wide)
        heads = range(first // HEAD, first // HEAD + per_tile)
        back_heads(heads, *shared, dquery_t, dkey, dvalue)
        values = (dquery_t[...].T, dkey[...] * score_scale, dvalue[...])
        for block, value in enumerate(values):
            at = block * width + first
            djoined[:, at : at + LANES] = value.astype(low)
    normed, root = norm_ref[...], root_ref[...]
    hidden_t = (normed * gain + shift).astype(low).T
    dhidden = jnp.zeros((rows, width), wide)
    bias_sums = []
    for block in range(3):
        cols = slice(block * width, (block + 1) * width)
        piece = djoined[:, cols]
        dhidden = dhidden + dot_nt(piece, weight_ref[:, cols])
        grad = dot_nn(hidden_t, piece)
        for target in range(shards):
            grads_ref[target, block * part : (block + 1) * part, :] = grad[
                target * part : (target + 1) * part, :
            ]
        if block != 1:
            bias_sums.append(jnp.sum(piece.astype(wide), axis=0, keepdims=True))
    through, gain_grad, shift_grad = norm_back(dhidden, normed, root, gain)
    dx_ref[...] = middle_ref[...] + through
    sums = [gain_grad, shift_grad, sums_in[0:1, :], sums_in[1:2, :]] + bias_sums
    sums += [sums_in[row : row + 1, :] for row in range(2, 8)]
    per_shard = len(sums) // shards
    body = 4 * part
    empty = [jnp.zeros((grads_ref.shape[1] - body - per_shard, width), wide)]
    for target in range(shards):
        rows_here = sums[target * per_shard : (target + 1) * per_shard]
        grads_ref[target, 3 * part : body, :] = grad_out[target * part : (target + 1) * part, :]
        grads_ref[target, body:, :] = jnp.concatenate(rows_here + empty, axis=0)
    part_ways(grads_ref, keep_ref, send_ref, shard & 1)


def halve_kernel(axis, bit, counts, kept, arrived, *outs):
    side = (lax.axis_index(axis) >> bit) & 1
    for pair in range(outs[0].shape[0]):
        mine = kept[2 * pair + side] + arrived[2 * pair + side].astype(wide)
        other = kept[2 * pair + 1 - side] + arrived[2 * pair + 1 - side].astype(wide)
        row = 0
        for chunk, count in enumerate(counts):
            outs[2 * chunk][pair] = mine[row : row + count]
            outs[2 * chunk + 1][pair] = other[row : row + count].astype(low)
            row += count


def piece_spans(total, tail, group):
    spans = [((total - tail) // group, 0, True)]
    if tail:
        spans.append((tail, total - tail, False))
    return spans


def split_kernel(tail, *refs):
    arrived, keep_ref, send_ref, sum_ref = refs[:-3], *refs[-3:]
    group = sum_ref.shape[0]
    total = arrived[0][...]
    for piece in arrived[1:]:
        total = total + piece[...].astype(wide)
    for index in range(group):
        row = 0
        for rows, first, moves in piece_spans(total.shape[0], tail, group):
            at = first + index * rows if moves else first
            sum_ref[index, row : row + rows, :] = total[at : at + rows, :]
            row += rows
    side = lax.axis_index("dp") & 1
    for pair in range(group // 2):
        keep_ref[pair] = sum_ref[2 * pair + side]
        send_ref[pair] = sum_ref[2 * pair + 1 - side].astype(low)


def merge_kernel(*refs):
    target = refs[-1]
    for index in range(target.shape[0]):
        parts = [
            kept[index] + arrived[index].astype(wide)
            for kept, arrived in zip(refs[:-1:2], refs[1:-1:2])
        ]
        target[index] = jnp.concatenate(parts, axis=0).astype(low)


def piece_kernel(arrived_ref, piece_ref):
    total = arrived_ref[0].astype(wide)
    for index in range(1, arrived_ref.shape[0]):
        total = total + arrived_ref[index].astype(wide)
    piece_ref[...] = total.astype(low)


def adam_values(weight, grad, first, second, decay_rate):
    first_next = beta_one * first + (1.0 - beta_one) * grad
    second_next = beta_two * second + (1.0 - beta_two) * grad * grad
    first_fix = 1.0 - beta_one**STEP
    second_fix = 1.0 - beta_two**STEP
    update = (first_next * (1.0 / first_fix)) / (
        jnp.sqrt(second_next * (1.0 / second_fix)) + adam_eps
    )
    return first_next, second_next, weight - learn_rate * (update + decay_rate * weight)


def adam_kernel(group, spans, layout, *refs):
    pieces = refs[:group]
    count = len(layout)
    states = refs[group : group + 3 * count]
    results = refs[group + 3 * count : group + 6 * count]
    buffers = refs[group + 6 * count : group + 9 * count]
    grad_ref, sems = refs[-2:]
    copies = []
    for offset, piece in enumerate(pieces):
        value = piece[...].astype(wide)
        index = (lax.axis_index("dp") & (group - 1)) ^ offset
        for rows, first, row in spans:
            at = pl.multiple_of(first + index * rows, TILE_ROWS)
            grad_ref[pl.ds(at, rows), :] = value[row : row + rows, :]
    width = grad_ref.shape[1]
    for array, (first_row, stride, decay) in enumerate(layout):
        weight, first, second = states[3 * array : 3 * array + 3]
        new = buffers[3 * array : 3 * array + 3]
        vector = len(weight.shape) == 1
        rows = 1 if vector else weight.shape[0]
        for block in range(weight.shape[-1] // width):
            cols = slice(block * width, (block + 1) * width)
            where = cols if vector else (slice(None), cols)
            at = first_row + block * stride
            values = adam_values(
                weight[where].reshape(rows, width),
                grad_ref[at : at + rows, :],
                first[where].reshape(rows, width),
                second[where].reshape(rows, width),
                decay,
            )
            for target, value in zip(new, values):
                target[where] = value.reshape(width) if vector else value
        for index in range(3 * array, 3 * array + 3):
            copies.append(
                pltpu.make_async_copy(buffers[index], results[index], sems.at[index])
            )
            copies[-1].start()
    for copy in copies:
        copy.wait()


def local_call(kernel, outs, operands, scratch=(), flops=0, name=None, fetch=False, sems=0):
    in_space = pltpu.HBM if fetch else pltpu.VMEM
    out_space = pltpu.HBM if sems else pltpu.VMEM
    outs = [jax.ShapeDtypeStruct(*out) for out in outs]
    moved = sum(
        math.prod(item.shape) * item.dtype.itemsize for item in list(operands) + outs
    )
    scratch_shapes = [pltpu.VMEM(*item) for item in scratch]
    if fetch or sems:
        scratch_shapes.append(pltpu.SemaphoreType.DMA((sems or len(operands),)))
    limit = 56 if fetch else 40
    return pl.pallas_call(
        kernel,
        out_shape=outs,
        in_specs=[pl.BlockSpec(memory_space=in_space)] * len(operands),
        out_specs=[pl.BlockSpec(memory_space=out_space)] * len(outs),
        scratch_shapes=scratch_shapes,
        compiler_params=pltpu.CompilerParams(vmem_limit_bytes=limit * 1024 * 1024),
        cost_estimate=pl.CostEstimate(flops=flops, bytes_accessed=moved, transcendentals=0),
        name=name,
    )(*operands)


def exchange(values, axis, mask):
    count = lax.axis_size(axis)
    return lax.ppermute(values, axis, [(index, index ^ mask) for index in range(count)])


def gather_pieces(value, group):
    found = {0: value}
    found[1] = exchange(value, "dp", 1)
    far = group // 2
    while far > 1:
        for offset in sorted(found):
            if offset & 1 == 0:
                found[offset ^ far] = exchange(found[offset], "dp", far)
        if far == group // 2:
            found[far], found[1] = lax.optimization_barrier((found[far], found[1]))
        far //= 2
    for offset in range(2, group, 2):
        found[offset ^ 1] = exchange(found[offset], "dp", 1)
    return [found[offset] for offset in range(group)]


def halve_call(axis, bit, kept, arrived, name, counts=None):
    half, rows, width = kept.shape
    counts = counts or [rows]
    outs = []
    for count in counts:
        shape = (half // 2, count, width)
        outs += [(shape, wide), (shape, low)]
    kernel = functools.partial(halve_kernel, axis, bit, counts)
    return local_call(kernel, outs, [kept, arrived], name=name)


def split_chunk(chunk, tail, group):
    rows, width = chunk[0].shape
    half = (group // 2, (rows - tail) // group + tail, width)
    keep, send = local_call(
        functools.partial(split_kernel, tail),
        [(half, wide), (half, low)],
        chunk,
        [((group,) + half[1:], wide)],
        name="split_sum",
    )
    return keep, exchange(send, "dp", 1)


def swap_far(pieces, group):
    replicas = lax.axis_size("dp")
    groups = [
        list(range(base + side, base + group, 2))
        for base in range(0, replicas, group)
        for side in range(2)
    ]
    return lax.all_to_all(pieces, "dp", 0, 0, axis_index_groups=groups, tiled=True)


def finish_sum(chunks, group):
    replicas = lax.axis_size("dp")
    width = chunks[0][0].shape[-1]
    rows = sum(chunk[0].shape[1] for chunk in chunks)
    flat = [item for chunk in chunks for item in chunk]
    (pieces,) = local_call(
        merge_kernel, [((group // 2, rows, width), low)], flat, name="merge_chunks"
    )
    arrived = swap_far(pieces, group)
    (piece,) = local_call(piece_kernel, [((rows, width), low)], [arrived], name="piece_sum")
    mask = group
    while mask < replicas:
        other = exchange(piece, "dp", mask)
        (piece,) = local_call(
            piece_kernel, [((rows, width), low)], [jnp.stack([piece, other])], name="far_sum"
        )
        mask *= 2
    return gather_pieces(piece, group)


def adam_call(pieces, counts, tails, states, layout):
    group = len(pieces)
    width = pieces[0].shape[1]
    spans = []
    first = row = 0
    for total, tail in zip(counts, tails):
        for rows, start, moves in piece_spans(total, tail, group):
            spans.append((rows, first + start, row))
            row += rows
            first += rows * (group - 1) * (not moves)
        first += total
    outs = [(state[0].shape, wide) for state in states for _ in range(3)]
    return local_call(
        functools.partial(adam_kernel, group, spans, layout),
        outs,
        pieces + [item for state in states for item in state],
        outs + [((first, width), wide)],
        name="adam",
        sems=len(outs),
    )


def shards_program(
    tokens,
    cotangent,
    lengths,
    seq_owner,
    qkv_weight,
    out_weight,
    up_weight,
    down_weight,
    gains_biases,
    qkv_first,
    qkv_second,
    out_first,
    out_second,
    up_first,
    up_second,
    down_first,
    down_second,
    small_first,
    small_second,
):
    rows, width = tokens.shape
    shards = lax.axis_size("shard")
    heads = width // HEAD
    part = qkv_weight.shape[0]
    hidden_count = up_weight.shape[1]
    group = min(GROUP, lax.axis_size("dp"))
    lengths = lengths.reshape(1, -1)
    seq_owner = seq_owner.reshape(1, -1)
    first_rows = 3 * part + SMALL_PAD
    second_rows = part + up_weight.size // width + down_weight.shape[0]
    (first_pack,) = local_call(
        pack_first_kernel,
        [((first_rows, width), low)],
        [qkv_weight, gains_biases],
        [(qkv_weight.shape, wide), (gains_biases.shape, wide)],
        name="pack_first",
        fetch=True,
    )
    firsts = {0: first_pack}
    firsts[2] = exchange(first_pack, "shard", 2)
    firsts[1] = exchange(first_pack, "shard", 1)
    first_pack, matrices = lax.optimization_barrier(
        (first_pack, [out_weight, up_weight, down_weight])
    )
    (second_pack,) = local_call(
        pack_second_kernel,
        [((second_rows, width), low)],
        matrices,
        [(item.shape, wide) for item in matrices],
        name="pack_second",
        fetch=True,
    )
    early_tokens, second_pack = lax.optimization_barrier((tokens, second_pack))
    square = (rows, rows)
    bias, normed, root, seed = local_call(
        functools.partial(prepare_kernel, shards),
        [(square, wide), ((rows, width), wide), ((rows, 1), wide), ((rows, width), low)],
        [early_tokens, cotangent, lengths, seq_owner],
        name="prepare",
    )
    seconds = {0: second_pack}
    seconds[2] = exchange(second_pack, "shard", 2)
    seconds[1] = exchange(second_pack, "shard", 1)
    firsts[2], bias, normed, root, seed = lax.optimization_barrier(
        (firsts[2], bias, normed, root, seed)
    )
    firsts[3] = exchange(firsts[2], "shard", 1)
    firsts = [firsts[offset] for offset in range(shards)]
    joined, attended, log_sums, mixed = local_call(
        functools.partial(attend_kernel, shards),
        [
            ((rows, 3 * width), low),
            ((rows, width), low),
            ((heads, rows), wide),
            ((width, rows), wide),
        ],
        [normed, bias] + firsts,
        [((width, 3 * width), low), ((shards, SMALL_PAD, width), wide)],
        flops=heads * rows * rows * 640,
        name="attend",
    )
    attended, seconds[2] = lax.optimization_barrier((attended, seconds[2]))
    seconds[3] = exchange(seconds[2], "shard", 1)
    seconds = [seconds[offset] for offset in range(shards)]
    down_rows, up_rows = down_weight.shape[0], up_weight.size // width
    blocks = hidden_count // width
    square = (width, width)
    pair = (shards // 2, down_rows + up_rows, width)
    act, base, dhidden, norm_two, root_two, out_full, down_full, sums, kept_ffn, send_ffn = (
        local_call(
            functools.partial(feed_first_kernel, shards),
            [
                ((rows, hidden_count), low),
                ((rows, width), wide),
                ((rows, width), wide),
                ((rows, width), wide),
                ((rows, 1), wide),
                (square, low),
                ((hidden_count, width), low),
                ((SMALL_PAD, width), wide),
                (pair, wide),
                (pair, low),
            ],
            [tokens, attended, seed] + firsts + seconds,
            [
                ((shards, SMALL_PAD, width), wide),
                ((width, hidden_count), low),
                ((shards, down_rows + up_rows, width), wide),
            ],
            flops=rows * width * hidden_count * 10,
            name="feed_first",
        )
    )
    arrived_ffn = exchange(send_ffn, "shard", 1)
    (output,) = local_call(
        output_kernel,
        [((rows, width), low)],
        [base, act, down_full],
        flops=rows * width * hidden_count * 2,
        name="output",
    )
    middle_grad, attended_grad, grad_out, sums = local_call(
        functools.partial(feed_last_kernel, shards),
        [((rows, width), wide), ((rows, width), low), (square, wide), ((SMALL_PAD, width), wide)],
        [attended, seed, dhidden, norm_two, root_two, out_full, sums] + firsts,
        [((shards, SMALL_PAD, width), wide)],
        flops=rows * width * width * 4,
        name="feed_last",
    )
    attended_grad, arrived_ffn = lax.optimization_barrier((attended_grad, arrived_ffn))
    keep_ffn, send_ffn = halve_call("shard", 1, kept_ffn, arrived_ffn, "halve_ffn")
    attended_grad, send_ffn = lax.optimization_barrier((attended_grad, send_ffn))
    arrived_ffn = exchange(send_ffn, "shard", 2)
    tail = TILE_ROWS
    att_rows = 4 * part + tail
    pair = (shards // 2, att_rows, width)
    input_grad, kept_att, send_att = local_call(
        functools.partial(back_kernel, shards),
        [((rows, width), wide), (pair, wide), (pair, low)],
        [joined, attended_grad, log_sums, bias, mixed]
        + [normed, root, middle_grad, sums, grad_out]
        + firsts,
        [
            ((width, 3 * width), low),
            ((shards, SMALL_PAD, width), wide),
            ((LANES, rows), low),
            ((rows, LANES), wide),
            ((rows, LANES), wide),
            ((rows, 3 * width), low),
            ((shards, att_rows, width), wide),
        ],
        flops=heads * rows * rows * 256 * 10,
        name="back",
    )
    send_att, arrived_ffn = lax.optimization_barrier((send_att, arrived_ffn))
    arrived_att = exchange(send_att, "shard", 1)
    keep_att, send_att = halve_call("shard", 1, kept_att, arrived_att, "halve_att")
    send_att, arrived_ffn = lax.optimization_barrier((send_att, arrived_ffn))
    arrived_att = exchange(send_att, "shard", 2)
    chunks = [
        split_chunk([keep_ffn[0], arrived_ffn[0]], 0, group),
        split_chunk([keep_att[0], arrived_att[0]], tail, group),
    ]
    pieces = finish_sum(chunks, group)
    second_at = down_rows + up_rows
    results = adam_call(
        pieces,
        (second_at, att_rows),
        (0, tail),
        [
            (qkv_weight, qkv_first, qkv_second),
            (out_weight, out_first, out_second),
            (up_weight, up_first, up_second),
            (down_weight, down_first, down_second),
            (gains_biases, small_first, small_second),
        ],
        [
            (second_at, part, matrix_decay),
            (second_at + 3 * part, part, matrix_decay),
            (down_rows, part, matrix_decay),
            (0, 0, matrix_decay),
            (second_at + 4 * part, 1, 0.0),
        ],
    )
    return (output, input_grad, *results)


def solution(mesh):
    rows = P(("dp", "shard"), None)
    matrix = P("shard", None)
    vector = P("shard")
    return jax.shard_map(
        shards_program,
        mesh=mesh,
        in_specs=(rows, rows, P(), P())
        + (matrix,) * 4
        + (vector,)
        + (matrix,) * 8
        + (vector, vector),
        out_specs=(rows, rows) + (matrix,) * 12 + (vector,) * 3,
        check_vma=False,
    )
```

```python
import functools
import math

import jax
import jax.numpy as jnp
from jax import lax
from jax.experimental import pallas as pl
from jax.experimental.pallas import tpu as pltpu
from jax.sharding import PartitionSpec as P

HEAD = 32
STEP = 10
LANES = 128
GROUP = 8
SMALL_PAD = 16
TILE_ROWS = 8
CHUNK = 64

norm_eps = 1e-05
beta_one = 0.9
beta_two = 0.95
learn_rate = 0.1
adam_eps = 1e-08
matrix_decay = 0.1
masked_score = -1e30
low = jnp.bfloat16
wide = jnp.float32
log2_e = math.log2(math.e)
score_scale = 1.0 / math.sqrt(HEAD)
tanh_scale = math.sqrt(2.0 / math.pi)
cubic = 0.044715


def dot_nn(left, right):
    return jnp.dot(left, right, preferred_element_type=wide)


def dot_nt(left, right):
    return lax.dot_general(left, right, (((1,), (1,)), ((), ())), preferred_element_type=wide)


def standardize(values):
    centered = values - jnp.mean(values, axis=-1, keepdims=True)
    root_inv = lax.rsqrt(jnp.mean(centered * centered, axis=-1, keepdims=True) + norm_eps)
    return centered * root_inv, root_inv


def norm_back(upstream, normed, root_inv, gain):
    scaled = upstream * gain
    inner_mean = jnp.mean(scaled, axis=-1, keepdims=True)
    cross_mean = jnp.mean(scaled * normed, axis=-1, keepdims=True)
    through = root_inv * (scaled - inner_mean - normed * cross_mean)
    return (
        through,
        jnp.sum(upstream * normed, axis=0, keepdims=True),
        jnp.sum(upstream, axis=0, keepdims=True),
    )


def iota(shape, dim):
    return lax.broadcasted_iota(jnp.int32, shape, dim)


def own_row(lengths, owners, device):
    return jnp.where(owners == device, lengths, 0)


def ends_both(own):
    count = own.shape[1]
    shape = (count, count)
    rows, cols = iota(shape, 0), iota(shape, 1)
    spread = jnp.broadcast_to(own, shape)
    ends_col = jnp.sum(jnp.where(cols <= rows, spread, 0), axis=1, keepdims=True)
    own_col = jnp.sum(jnp.where(cols == rows, spread, 0), axis=1, keepdims=True)
    ends_row = jnp.sum(
        jnp.where(rows <= cols, jnp.broadcast_to(own_col, shape), 0), axis=0, keepdims=True
    )
    return ends_col, ends_row


def fill_mask(bias_ref, own, rows):
    ends_col, ends_row = ends_both(own)
    count = own.shape[1]
    seg_row = jnp.sum(
        (ends_col <= iota((count, rows), 1)).astype(jnp.int32), axis=0, keepdims=True
    )
    seg_col = jnp.sum(
        (ends_row <= iota((rows, count), 0)).astype(jnp.int32), axis=1, keepdims=True
    )
    allowed = (seg_row == seg_col) & (iota((rows, rows), 0) <= iota((rows, rows), 1))
    bias_ref[...] = jnp.where(allowed, 0.0, masked_score)


def fill_small(small_ref, shard, pieces, first_row):
    for offset, piece in enumerate(pieces):
        small_ref[shard ^ offset] = piece[first_row:, :].astype(wide)


def fill_cols(full_ref, shard, pieces, first_row, rows, width):
    blocks = full_ref.shape[1] // width
    for offset, piece in enumerate(pieces):
        at = pl.multiple_of((shard ^ offset) * rows, rows)
        for block in range(blocks):
            start = first_row + block * rows
            full_ref[pl.ds(at, rows), block * width : (block + 1) * width] = piece[
                start : start + rows, :
            ]


def head_mask(head):
    lane = iota((1, LANES), 1)
    first = head * HEAD % LANES
    return ((lane >= first) & (lane < first + HEAD)).astype(wide).astype(low)


def head_tile(head):
    first = head * HEAD // LANES * LANES
    return slice(first, first + LANES)


def query_blocks(rows):
    size = min(256, rows)
    return [(at, at + size) for at in range(0, rows, size)]


def put_blocks(target, row, source, width):
    rows = source.shape[0]
    for block in range(source.shape[1] // width):
        cols = slice(block * width, (block + 1) * width)
        target[row : row + rows, :] = source[:, cols].astype(low)
        row += rows
    return row


def fetch_all(sources, buffers, sems):
    copies = [
        pltpu.make_async_copy(source, buffer, sems.at[index])
        for index, (source, buffer) in enumerate(zip(sources, buffers))
    ]
    for copy in copies:
        copy.start()
    return copies


def pack_first_kernel(qkv_ref, small_ref, first_ref, qkv_buf, small_buf, sems):
    width = first_ref.shape[1]
    small_copy, qkv_copy = fetch_all((small_ref, qkv_ref), (small_buf, qkv_buf), sems)
    small_copy.wait()
    parts = [
        small_buf[block * width : (block + 1) * width].reshape(1, width)
        for block in range(small_buf.shape[0] // width)
    ]
    parts.append(jnp.zeros((SMALL_PAD - len(parts), width), wide))
    first_ref[first_ref.shape[0] - SMALL_PAD :, :] = jnp.concatenate(parts, axis=0).astype(low)
    qkv_copy.wait()
    put_blocks(first_ref, 0, qkv_buf, width)


def pack_second_kernel(out_ref, up_ref, down_ref, second_ref, out_buf, up_buf, down_buf, sems):
    width = second_ref.shape[1]
    buffers = (out_buf, up_buf, down_buf)
    copies = fetch_all((out_ref, up_ref, down_ref), buffers, sems)
    row = 0
    for copy, buffer in zip(copies, buffers):
        copy.wait()
        row = put_blocks(second_ref, row, buffer, width)


def prepare_kernel(shards, x_ref, seed_ref, len_ref, owner_ref, bias_ref, norm_ref, root_ref, low_ref):
    rows = x_ref.shape[0]
    device = lax.axis_index("dp") * shards + lax.axis_index("shard")
    own = own_row(len_ref[...], owner_ref[...], device)
    fill_mask(bias_ref, own, rows)
    normed, root = standardize(x_ref[...].astype(wide))
    norm_ref[...] = normed
    root_ref[...] = root
    live = jnp.sum(own, axis=1, keepdims=True)
    live_rows = (iota((rows, 1), 0) < live).astype(wide)
    low_ref[...] = (seed_ref[...].astype(wide) * live_rows).astype(low)


def attend_kernel(shards, *refs):
    norm_ref, bias_ref = refs[:2]
    pieces = refs[2 : 2 + shards]
    joined_ref, out_ref, log_ref, att_ref, weight_ref, small_ref = refs[2 + shards :]
    rows, width = norm_ref.shape
    shard = lax.axis_index("shard")
    part = width // shards
    fill_cols(weight_ref, shard, pieces, 0, part, width)
    fill_small(small_ref, shard, pieces, 3 * part)
    gain, shift = small_ref[0, 0:1, :], small_ref[0, 1:2, :]
    bias_query, bias_value = small_ref[1, 1:2, :], small_ref[1, 2:3, :]
    hidden = (norm_ref[...] * gain + shift).astype(low)
    for block, bias in enumerate((bias_query, None, bias_value)):
        cols = slice(block * width, (block + 1) * width)
        value = dot_nn(hidden, weight_ref[:, cols])
        if bias is not None:
            value = value + bias
        joined_ref[:, cols] = value.astype(low)
    values_t = joined_ref[:, 2 * width :].T
    units = [
        (head, start, stop) for head in range(width // HEAD) for start, stop in query_blocks(rows)
    ]

    def raw_scores(head, start, stop):
        tile = head_tile(head)
        key_tile = joined_ref[:stop, width + tile.start : width + tile.stop] * head_mask(head)
        return dot_nt(key_tile, joined_ref[start:stop, tile])

    ahead = raw_scores(*units[0])
    for index, (head, start, stop) in enumerate(units):
        raw = ahead
        if index + 1 < len(units):
            ahead = raw_scores(*units[index + 1])
        feature = slice(head * HEAD, (head + 1) * HEAD)
        scores = []
        top = None
        for at in range(0, stop, CHUNK):
            piece = raw[at : at + CHUNK] * (score_scale * log2_e)
            piece = piece + bias_ref[at : at + CHUNK, start:stop]
            scores.append(piece)
            top = piece if top is None else jnp.maximum(top, piece)
        top = jnp.max(top, axis=0, keepdims=True)
        exponents = []
        total = None
        for piece in scores:
            piece = jnp.exp2(piece - top)
            total = piece if total is None else total + piece
            exponents.append(piece.astype(low))
        total = jnp.sum(total, axis=0, keepdims=True)
        mixed = dot_nn(values_t[feature, :stop], jnp.concatenate(exponents, axis=0))
        att_ref[feature, start:stop] = mixed * (1.0 / total)
        log_ref[head : head + 1, start:stop] = top + jnp.log2(total)
    out_ref[...] = att_ref[...].astype(low).T


def feed_kernel(shards, *refs):
    x_ref, att_ref, seed_ref = refs[:3]
    firsts = refs[3 : 3 + shards]
    pieces = refs[3 + shards : 3 + 2 * shards]
    refs = refs[3 + 2 * shards :]
    out_ref, middle_ref, dattend_ref, sums_ref, keep_ref, send_ref = refs[:6]
    small_ref, out_w, up_w, down_w, grads_ref = refs[6:]
    rows, width = x_ref.shape
    hidden_count = up_w.shape[1]
    shard = lax.axis_index("shard")
    part = width // shards
    blocks = hidden_count // width
    down_part = hidden_count // shards
    fill_small(small_ref, shard, firsts, 3 * part)
    fill_cols(out_w, shard, pieces, 0, part, width)
    fill_cols(up_w, shard, pieces, part, part, width)
    fill_cols(down_w, shard, pieces, part + blocks * part, down_part, width)
    gain, shift = small_ref[0, 2:3, :], small_ref[1, 0:1, :]
    bias_out, bias_down = small_ref[2, 0:1, :], small_ref[2, 1:2, :]
    bias_up = [small_ref[2, 2:3, :]] + [small_ref[3, row : row + 1, :] for row in range(3)]
    seed_low = seed_ref[...]
    seed = seed_low.astype(wide)
    attended = att_ref[...]
    middle = x_ref[...].astype(wide) + (dot_nn(attended, out_w[...]) + bias_out)
    normed, root = standardize(middle)
    hidden = (normed * gain + shift).astype(low)
    hidden_t = hidden.T
    result = middle + bias_down
    dhidden = jnp.zeros((rows, width), wide)
    sums_ref[...] = jnp.zeros(sums_ref.shape, wide)

    def raw_products(block):
        cols = slice(block * width, (block + 1) * width)
        return dot_nn(hidden, up_w[:, cols]), dot_nt(seed_low, down_w[cols, :])

    ahead = raw_products(0)
    for block in range(blocks):
        cols = slice(block * width, (block + 1) * width)
        raw, dact = ahead
        if block + 1 < blocks:
            ahead = raw_products(block + 1)
        act, dpre = [], []
        for at in range(0, rows, CHUNK):
            pre = raw[at : at + CHUNK] + bias_up[block]
            square = pre * pre
            bend = jnp.tanh(pre * (tanh_scale + (tanh_scale * cubic) * square))
            half = 0.5 + 0.5 * bend
            act.append((pre * half).astype(low))
            slope = 0.5 * tanh_scale + (1.5 * tanh_scale * cubic) * square
            slope = half + (pre * slope) * (1.0 - bend * bend)
            dpre.append((dact[at : at + CHUNK] * slope).astype(low))
        act = jnp.concatenate(act, axis=0)
        dpre = jnp.concatenate(dpre, axis=0)
        result = result + dot_nn(act, down_w[cols, :])
        dhidden = dhidden + dot_nt(dpre, up_w[:, cols])
        grad_down = dot_nn(act.T, seed_low)
        grad_up = dot_nn(hidden_t, dpre)
        for piece in range(width // down_part):
            target = block * (width // down_part) + piece
            at = part + blocks * part
            grads_ref[target, at : at + down_part, :] = grad_down[
                piece * down_part : (piece + 1) * down_part, :
            ]
        for target in range(shards):
            at = part + block * part
            grads_ref[target, at : at + part, :] = grad_up[target * part : (target + 1) * part, :]
        sums_ref[4 + block : 5 + block, :] = jnp.sum(dpre.astype(wide), axis=0, keepdims=True)
    out_ref[...] = result.astype(low)
    through, gain_grad, shift_grad = norm_back(dhidden, normed, root, gain)
    dmiddle = seed + through
    middle_ref[...] = dmiddle
    dmiddle_low = dmiddle.astype(low)
    grad_out = dot_nn(attended.T, dmiddle_low)
    for target in range(shards):
        grads_ref[target, :part, :] = grad_out[target * part : (target + 1) * part, :]
    dattend_ref[...] = dot_nt(dmiddle_low, out_w[...]).astype(low)
    sums_ref[0:1, :] = gain_grad
    sums_ref[1:2, :] = shift_grad
    sums_ref[2:3, :] = jnp.sum(dmiddle_low.astype(wide), axis=0, keepdims=True)
    sums_ref[3:4, :] = jnp.sum(seed, axis=0, keepdims=True)
    part_ways(grads_ref, keep_ref, send_ref, shard & 1)


def part_ways(grads_ref, keep_ref, send_ref, side):
    for pair in range(keep_ref.shape[0]):
        keep_ref[pair] = grads_ref[2 * pair + side]
        send_ref[pair] = grads_ref[2 * pair + 1 - side].astype(low)


def back_heads(
    heads, joined_ref, dattend_ref, log_ref, bias_ref, mixed_ref, dquery_t, dkey, dvalue
):
    rows = joined_ref.shape[0]
    width = joined_ref.shape[1] // 3
    first = heads[0] * HEAD
    count = len(heads) * HEAD
    base = first // LANES * LANES
    tile = slice(base, base + LANES)
    inside = slice(first - base, first - base + count)
    keys_t = joined_ref[:, width + base : width + base + LANES].T
    datt_t = dattend_ref[:, tile].T[inside]
    inner = datt_t.astype(wide) * mixed_ref[first : first + count, :]
    units = [(head, start, stop) for head in heads for start, stop in query_blocks(rows)]

    def raw_products(head, start, stop):
        mask = head_mask(head)
        key_tile = joined_ref[:stop, width + base : width + base + LANES] * mask
        value_tile = joined_ref[:stop, 2 * width + base : 2 * width + base + LANES] * mask
        query = joined_ref[start:stop, tile]
        datt = dattend_ref[start:stop, tile]
        return dot_nt(key_tile, query), dot_nt(value_tile, datt), query * mask, datt * mask

    ahead = raw_products(*units[0])
    for index, (head, start, stop) in enumerate(units):
        raw, dprobs, query, datt = ahead
        if index + 1 < len(units):
            ahead = raw_products(*units[index + 1])
        local = head * HEAD - first
        feature = slice(local, local + HEAD)
        weighted = jnp.sum(inner[feature, start:stop], axis=0, keepdims=True)
        logs = log_ref[head : head + 1, start:stop]
        probs, dscores = [], []
        for at in range(0, stop, CHUNK):
            piece = raw[at : at + CHUNK] * (score_scale * log2_e)
            piece = jnp.exp2(piece + bias_ref[at : at + CHUNK, start:stop] - logs)
            probs.append(piece.astype(low))
            piece = piece * (dprobs[at : at + CHUNK] - weighted)
            dscores.append(piece.astype(low))
        probs = jnp.concatenate(probs, axis=0)
        dscores = jnp.concatenate(dscores, axis=0)
        depth = slice(head * HEAD - base, head * HEAD - base + HEAD)
        dquery_t[depth, start:stop] = (
            dot_nn(keys_t[depth, :stop], dscores) * score_scale
        ).astype(low)
        dvalue[:stop, :] += dot_nn(probs, datt)
        dkey[:stop, :] += dot_nn(dscores, query)


def back_first_kernel(heads, *refs):
    dquery_t, dkey, dvalue = refs[5:8]
    dkey[...] = jnp.zeros(dkey.shape, wide)
    dvalue[...] = jnp.zeros(dvalue.shape, wide)
    dquery_t[...] = jnp.zeros(dquery_t.shape, low)
    back_heads(heads, *refs)


def back_last_kernel(shards, head_groups, *refs):
    shared = refs[:5]
    earlier = refs[5:8]
    norm_ref, root_ref, middle_ref, sums_in = refs[8:12]
    pieces = refs[12 : 12 + shards]
    refs = refs[12 + shards :]
    dx_ref, keep_ref, send_ref = refs[:3]
    weight_ref, small_ref, dquery_t, dkey, dvalue, djoined, grads_ref = refs[3:]
    rows, width = norm_ref.shape
    shard = lax.axis_index("shard")
    part = width // shards
    fill_cols(weight_ref, shard, pieces, 0, part, width)
    fill_small(small_ref, shard, pieces, 3 * part)
    gain, shift = small_ref[0, 0:1, :], small_ref[0, 1:2, :]
    for target, value in zip((dquery_t, dkey, dvalue), earlier):
        target[...] = value[...]
    for heads in head_groups:
        back_heads(heads, *shared, dquery_t, dkey, dvalue)
        if (heads[-1] + 1) * HEAD % LANES == 0:
            first = (heads[-1] + 1) * HEAD - LANES
            values = (dquery_t[...].T, dkey[...] * score_scale, dvalue[...])
            for block, value in enumerate(values):
                at = block * width + first
                djoined[:, at : at + LANES] = value.astype(low)
            dkey[...] = jnp.zeros(dkey.shape, wide)
            dvalue[...] = jnp.zeros(dvalue.shape, wide)
    normed, root = norm_ref[...], root_ref[...]
    hidden_t = (normed * gain + shift).astype(low).T
    dhidden = jnp.zeros((rows, width), wide)
    bias_sums = []
    for block in range(3):
        cols = slice(block * width, (block + 1) * width)
        piece = djoined[:, cols]
        dhidden = dhidden + dot_nt(piece, weight_ref[:, cols])
        grad = dot_nn(hidden_t, piece)
        for target in range(shards):
            grads_ref[target, block * part : (block + 1) * part, :] = grad[
                target * part : (target + 1) * part, :
            ]
        if block != 1:
            bias_sums.append(jnp.sum(piece.astype(wide), axis=0, keepdims=True))
    through, gain_grad, shift_grad = norm_back(dhidden, normed, root, gain)
    dx_ref[...] = middle_ref[...] + through
    sums = [gain_grad, shift_grad, sums_in[0:1, :], sums_in[1:2, :]] + bias_sums
    sums += [sums_in[row : row + 1, :] for row in range(2, 8)]
    per_shard = len(sums) // shards
    empty = [jnp.zeros((grads_ref.shape[1] - 3 * part - per_shard, width), wide)]
    for target in range(shards):
        rows_here = sums[target * per_shard : (target + 1) * per_shard]
        grads_ref[target, 3 * part :, :] = jnp.concatenate(rows_here + empty, axis=0)
    part_ways(grads_ref, keep_ref, send_ref, shard & 1)


def halve_kernel(bit, kept, *refs):
    arrived, (keep_ref, send_ref) = refs[:-2], refs[-2:]
    side = (lax.axis_index("dp") >> bit) & 1

    def total(index):
        value = kept[index]
        for piece in arrived:
            value = value + piece[index].astype(wide)
        return value

    for pair in range(keep_ref.shape[0]):
        keep_ref[pair] = total(2 * pair + side)
        send_ref[pair] = total(2 * pair + 1 - side).astype(low)


def piece_spans(total, tail, group):
    spans = [((total - tail) // group, 0, True)]
    if tail:
        spans.append((tail, total - tail, False))
    return spans


def quarter_kernel(tail, kept, arrived, keep_ref, beside_ref, across_ref, corner_ref, sum_ref):
    group = sum_ref.shape[1]
    for half in range(2):
        total = kept[half] + arrived[half].astype(wide)
        for index in range(group):
            row = 0
            for rows, first, moves in piece_spans(total.shape[0], tail, group):
                at = first + index * rows if moves else first
                sum_ref[half, index, row : row + rows, :] = total[at : at + rows, :]
                row += rows
    mine = (lax.axis_index("shard") >> 1) & 1
    side = lax.axis_index("dp") & 1
    for pair in range(group // 2):
        keep_ref[pair] = sum_ref[mine, 2 * pair + side]
        beside_ref[pair] = sum_ref[1 - mine, 2 * pair + side].astype(low)
        across_ref[pair] = sum_ref[mine, 2 * pair + 1 - side].astype(low)
        corner_ref[pair] = sum_ref[1 - mine, 2 * pair + 1 - side].astype(low)


def piece_kernel(*refs):
    parts = [
        mine[...].reshape(mine.shape[-2:]).astype(wide)
        + other[...].reshape(other.shape[-2:]).astype(wide)
        for mine, other in zip(refs[:-1:2], refs[1:-1:2])
    ]
    refs[-1][...] = jnp.concatenate(parts, axis=0).astype(low)


def adam_values(weight, grad, first, second, decay_rate):
    first_next = beta_one * first + (1.0 - beta_one) * grad
    second_next = beta_two * second + (1.0 - beta_two) * grad * grad
    first_fix = 1.0 - beta_one**STEP
    second_fix = 1.0 - beta_two**STEP
    update = (first_next * (1.0 / first_fix)) / (
        jnp.sqrt(second_next * (1.0 / second_fix)) + adam_eps
    )
    return first_next, second_next, weight - learn_rate * (update + decay_rate * weight)


def adam_kernel(group, spans, layout, *refs):
    pieces = refs[:group]
    count = len(layout)
    states = refs[group : group + 3 * count]
    results = refs[group + 3 * count : group + 6 * count]
    buffers = refs[group + 6 * count : group + 9 * count]
    grad_ref, sems = refs[-2:]
    copies = []
    for offset, piece in enumerate(pieces):
        value = piece[...].astype(wide)
        index = (lax.axis_index("dp") & (group - 1)) ^ offset
        for rows, first, row in spans:
            at = pl.multiple_of(first + index * rows, TILE_ROWS)
            grad_ref[pl.ds(at, rows), :] = value[row : row + rows, :]
    width = grad_ref.shape[1]
    for array, (first_row, stride, decay) in enumerate(layout):
        weight, first, second = states[3 * array : 3 * array + 3]
        new = buffers[3 * array : 3 * array + 3]
        vector = len(weight.shape) == 1
        rows = 1 if vector else weight.shape[0]
        for block in range(weight.shape[-1] // width):
            cols = slice(block * width, (block + 1) * width)
            where = cols if vector else (slice(None), cols)
            at = first_row + block * stride
            values = adam_values(
                weight[where].reshape(rows, width),
                grad_ref[at : at + rows, :],
                first[where].reshape(rows, width),
                second[where].reshape(rows, width),
                decay,
            )
            for target, value in zip(new, values):
                target[where] = value.reshape(width) if vector else value
        for index in range(3 * array, 3 * array + 3):
            copies.append(
                pltpu.make_async_copy(buffers[index], results[index], sems.at[index])
            )
            copies[-1].start()
    for copy in copies:
        copy.wait()


def local_call(kernel, outs, operands, scratch=(), flops=0, name=None, fetch=False, sems=0):
    in_space = pltpu.HBM if fetch else pltpu.VMEM
    out_space = pltpu.HBM if sems else pltpu.VMEM
    outs = [jax.ShapeDtypeStruct(*out) for out in outs]
    moved = sum(
        math.prod(item.shape) * item.dtype.itemsize for item in list(operands) + outs
    )
    scratch_shapes = [pltpu.VMEM(*item) for item in scratch]
    if fetch or sems:
        scratch_shapes.append(pltpu.SemaphoreType.DMA((sems or len(operands),)))
    limit = 56 if fetch else 40
    return pl.pallas_call(
        kernel,
        out_shape=outs,
        in_specs=[pl.BlockSpec(memory_space=in_space)] * len(operands),
        out_specs=[pl.BlockSpec(memory_space=out_space)] * len(outs),
        scratch_shapes=scratch_shapes,
        compiler_params=pltpu.CompilerParams(vmem_limit_bytes=limit * 1024 * 1024),
        cost_estimate=pl.CostEstimate(flops=flops, bytes_accessed=moved, transcendentals=0),
        name=name,
    )(*operands)


def exchange(values, axis, mask):
    count = lax.axis_size(axis)
    return lax.ppermute(values, axis, [(index, index ^ mask) for index in range(count)])


def gather_pieces(value, group):
    found = {0: value}
    found[1] = exchange(value, "dp", 1)
    far = group // 2
    while far > 1:
        for offset in sorted(found):
            if offset & 1 == 0:
                found[offset ^ far] = exchange(found[offset], "dp", far)
        if far == group // 2:
            found[far], found[1] = lax.optimization_barrier((found[far], found[1]))
        far //= 2
    for offset in range(2, group, 2):
        found[offset ^ 1] = exchange(found[offset], "dp", 1)
    return [found[offset] for offset in range(group)]


def corner(values):
    replicas, shards = lax.axis_size("dp"), lax.axis_size("shard")
    pairs = [
        (replica * shards + shard, (replica ^ 1) * shards + (shard ^ 2))
        for replica in range(replicas)
        for shard in range(shards)
    ]
    return lax.ppermute(values, ("dp", "shard"), pairs)


def quarter_call(kept, arrived, tail, group, name):
    _, rows, width = kept.shape
    shape = (group // 2, (rows - tail) // group + tail, width)
    return local_call(
        functools.partial(quarter_kernel, tail),
        [(shape, wide)] + [(shape, low)] * 3,
        [kept, arrived],
        [((2, group) + shape[1:], wide)],
        name=name,
    )


def spread(beside, across, far):
    return [exchange(beside, "shard", 2), exchange(across, "dp", 1), corner(far)]


def near_sum(flat):
    half = flat[0].shape[0]
    bit = 1
    while half > 1:
        half //= 2
        shape = (half,) + flat[0].shape[1:]
        keep, send = local_call(
            functools.partial(halve_kernel, bit),
            [(shape, wide), (shape, low)],
            flat,
            name="halve_dp",
        )
        flat = [keep, exchange(send, "dp", 1 << bit)]
        bit += 1
    return flat


def finish_sum(chunks, group):
    replicas = lax.axis_size("dp")
    flat = [item for chunk in chunks for item in near_sum(chunk)]
    width = flat[0].shape[-1]
    rows = sum(item.shape[1] for item in flat[::2])
    (piece,) = local_call(piece_kernel, [((rows, width), low)], flat, name="piece_sum")
    mask = group
    while mask < replicas:
        other = exchange(piece, "dp", mask)
        (piece,) = local_call(piece_kernel, [((rows, width), low)], [piece, other], name="far_sum")
        mask *= 2
    return gather_pieces(piece, group)


def adam_call(pieces, counts, tails, states, layout):
    group = len(pieces)
    width = pieces[0].shape[1]
    spans = []
    first = row = 0
    for total, tail in zip(counts, tails):
        for rows, start, moves in piece_spans(total, tail, group):
            spans.append((rows, first + start, row))
            row += rows
            first += rows * (group - 1) * (not moves)
        first += total
    outs = [(state[0].shape, wide) for state in states for _ in range(3)]
    return local_call(
        functools.partial(adam_kernel, group, spans, layout),
        outs,
        pieces + [item for state in states for item in state],
        outs + [((first, width), wide)],
        name="adam",
        sems=len(outs),
    )


def shards_program(
    tokens,
    cotangent,
    lengths,
    seq_owner,
    qkv_weight,
    out_weight,
    up_weight,
    down_weight,
    gains_biases,
    qkv_first,
    qkv_second,
    out_first,
    out_second,
    up_first,
    up_second,
    down_first,
    down_second,
    small_first,
    small_second,
):
    rows, width = tokens.shape
    shards = lax.axis_size("shard")
    heads = width // HEAD
    part = qkv_weight.shape[0]
    hidden_count = up_weight.shape[1]
    group = min(GROUP, lax.axis_size("dp"))
    lengths = lengths.reshape(1, -1)
    seq_owner = seq_owner.reshape(1, -1)
    first_rows = 3 * part + SMALL_PAD
    second_rows = part + up_weight.size // width + down_weight.shape[0]
    (first_pack,) = local_call(
        pack_first_kernel,
        [((first_rows, width), low)],
        [qkv_weight, gains_biases],
        [(qkv_weight.shape, wide), (gains_biases.shape, wide)],
        name="pack_first",
        fetch=True,
    )
    firsts = {0: first_pack}
    firsts[2] = exchange(first_pack, "shard", 2)
    firsts[1] = exchange(first_pack, "shard", 1)
    first_pack, matrices = lax.optimization_barrier(
        (first_pack, [out_weight, up_weight, down_weight])
    )
    (second_pack,) = local_call(
        pack_second_kernel,
        [((second_rows, width), low)],
        matrices,
        [(item.shape, wide) for item in matrices],
        name="pack_second",
        fetch=True,
    )
    early_tokens, second_pack = lax.optimization_barrier((tokens, second_pack))
    square = (rows, rows)
    bias, normed, root, seed = local_call(
        functools.partial(prepare_kernel, shards),
        [(square, wide), ((rows, width), wide), ((rows, 1), wide), ((rows, width), low)],
        [early_tokens, cotangent, lengths, seq_owner],
        name="prepare",
    )
    seconds = {0: second_pack}
    seconds[2] = exchange(second_pack, "shard", 2)
    seconds[1] = exchange(second_pack, "shard", 1)
    firsts[2], bias, normed, root, seed = lax.optimization_barrier(
        (firsts[2], bias, normed, root, seed)
    )
    firsts[3] = exchange(firsts[2], "shard", 1)
    firsts = [firsts[offset] for offset in range(shards)]
    joined, attended, log_sums, mixed = local_call(
        functools.partial(attend_kernel, shards),
        [
            ((rows, 3 * width), low),
            ((rows, width), low),
            ((heads, rows), wide),
            ((width, rows), wide),
        ],
        [normed, bias] + firsts,
        [((width, 3 * width), low), ((shards, SMALL_PAD, width), wide)],
        flops=heads * rows * rows * 640,
        name="attend",
    )
    attended, seconds[2] = lax.optimization_barrier((attended, seconds[2]))
    seconds[3] = exchange(seconds[2], "shard", 1)
    seconds = [seconds[offset] for offset in range(shards)]
    pair = (shards // 2, second_rows, width)
    output, middle_grad, attended_grad, sums, kept_ffn, send_ffn = local_call(
        functools.partial(feed_kernel, shards),
        [
            ((rows, width), low),
            ((rows, width), wide),
            ((rows, width), low),
            ((SMALL_PAD, width), wide),
            (pair, wide),
            (pair, low),
        ],
        [tokens, attended, seed] + firsts + seconds,
        [
            ((shards, SMALL_PAD, width), wide),
            ((width, width), low),
            ((width, hidden_count), low),
            ((hidden_count, width), low),
            ((shards, second_rows, width), wide),
        ],
        flops=rows * width * (hidden_count * 12 + width * 6),
        name="feed",
    )
    arrived_ffn = exchange(send_ffn, "shard", 1)
    shared = [joined, attended_grad, log_sums, bias, mixed]
    tile_scratch = [((LANES, rows), low), ((rows, LANES), wide), ((rows, LANES), wide)]
    per_tile = LANES // HEAD
    groups = [list(range(at, at + per_tile)) for at in range(0, heads, per_tile)]
    groups = [groups[0][:3], groups[0][3:]] + groups[1:]
    first_query, first_key, first_value = local_call(
        functools.partial(back_first_kernel, groups[0]),
        tile_scratch,
        shared,
        flops=heads * rows * rows * 256 * 5 // 2,
        name="back_first",
    )
    first_query, arrived_ffn = lax.optimization_barrier((first_query, arrived_ffn))
    tail = TILE_ROWS
    keep_ffn, *sends_ffn = quarter_call(kept_ffn, arrived_ffn, 0, group, "quarter_ffn")
    first_query, sends_ffn = lax.optimization_barrier((first_query, sends_ffn))
    arrived_ffn = spread(*sends_ffn)
    att_rows = 3 * part + tail
    pair = (shards // 2, att_rows, width)
    input_grad, kept_att, send_att = local_call(
        functools.partial(back_last_kernel, shards, groups[1:]),
        [((rows, width), wide), (pair, wide), (pair, low)],
        shared + [first_query, first_key, first_value, normed, root, middle_grad, sums] + firsts,
        [((width, 3 * width), low), ((shards, SMALL_PAD, width), wide)]
        + tile_scratch
        + [((rows, 3 * width), low), ((shards, att_rows, width), wide)],
        flops=heads * rows * rows * 256 * 6,
        name="back_last",
    )
    send_att, arrived_ffn[0], arrived_ffn[1] = lax.optimization_barrier(
        (send_att, arrived_ffn[0], arrived_ffn[1])
    )
    arrived_att = exchange(send_att, "shard", 1)
    keep_att, *sends_att = quarter_call(kept_att, arrived_att, tail, group, "quarter_att")
    arrived_att = spread(*sends_att)
    tails = (0, tail)
    pieces = finish_sum([[keep_ffn] + arrived_ffn, [keep_att] + arrived_att], group)
    blocks = hidden_count // width
    results = adam_call(
        pieces,
        (second_rows, att_rows),
        tails,
        [
            (qkv_weight, qkv_first, qkv_second),
            (out_weight, out_first, out_second),
            (up_weight, up_first, up_second),
            (down_weight, down_first, down_second),
            (gains_biases, small_first, small_second),
        ],
        [
            (second_rows, part, matrix_decay),
            (0, part, matrix_decay),
            (part, part, matrix_decay),
            (part + blocks * part, 0, matrix_decay),
            (second_rows + 3 * part, 1, 0.0),
        ],
    )
    return (output, input_grad, *results)


def solution(mesh):
    rows = P(("dp", "shard"), None)
    matrix = P("shard", None)
    vector = P("shard")
    return jax.shard_map(
        shards_program,
        mesh=mesh,
        in_specs=(rows, rows, P(), P())
        + (matrix,) * 4
        + (vector,)
        + (matrix,) * 8
        + (vector, vector),
        out_specs=(rows, rows) + (matrix,) * 12 + (vector,) * 3,
        check_vma=False,
    )
```

```python
import functools
import math

import jax
import jax.numpy as jnp
from jax import lax
from jax.experimental import pallas as pl
from jax.experimental.pallas import tpu as pltpu
from jax.sharding import PartitionSpec as P

HEAD = 32
STEP = 10
LANES = 128
GROUP = 8
SMALL_PAD = 16
TILE_ROWS = 8
CHUNK = 64

norm_eps = 1e-05
beta_one = 0.9
beta_two = 0.95
learn_rate = 0.1
adam_eps = 1e-08
matrix_decay = 0.1
masked_score = -1e30
low = jnp.bfloat16
wide = jnp.float32
log2_e = math.log2(math.e)
score_scale = 1.0 / math.sqrt(HEAD)
tanh_scale = math.sqrt(2.0 / math.pi)
cubic = 0.044715


def dot_nn(left, right):
    return jnp.dot(left, right, preferred_element_type=wide)


def dot_nt(left, right):
    return lax.dot_general(left, right, (((1,), (1,)), ((), ())), preferred_element_type=wide)


def standardize(values):
    centered = values - jnp.mean(values, axis=-1, keepdims=True)
    root_inv = lax.rsqrt(jnp.mean(centered * centered, axis=-1, keepdims=True) + norm_eps)
    return centered * root_inv, root_inv


def norm_back(upstream, normed, root_inv, gain):
    scaled = upstream * gain
    inner_mean = jnp.mean(scaled, axis=-1, keepdims=True)
    cross_mean = jnp.mean(scaled * normed, axis=-1, keepdims=True)
    through = root_inv * (scaled - inner_mean - normed * cross_mean)
    return (
        through,
        jnp.sum(upstream * normed, axis=0, keepdims=True),
        jnp.sum(upstream, axis=0, keepdims=True),
    )


def iota(shape, dim):
    return lax.broadcasted_iota(jnp.int32, shape, dim)


def own_row(lengths, owners, device):
    return jnp.where(owners == device, lengths, 0)


def ends_both(own):
    count = own.shape[1]
    shape = (count, count)
    rows, cols = iota(shape, 0), iota(shape, 1)
    spread = jnp.broadcast_to(own, shape)
    ends_col = jnp.sum(jnp.where(cols <= rows, spread, 0), axis=1, keepdims=True)
    own_col = jnp.sum(jnp.where(cols == rows, spread, 0), axis=1, keepdims=True)
    ends_row = jnp.sum(
        jnp.where(rows <= cols, jnp.broadcast_to(own_col, shape), 0), axis=0, keepdims=True
    )
    return ends_col, ends_row


def fill_mask(bias_ref, own, rows):
    ends_col, ends_row = ends_both(own)
    count = own.shape[1]
    seg_row = jnp.sum(
        (ends_col <= iota((count, rows), 1)).astype(jnp.int32), axis=0, keepdims=True
    )
    seg_col = jnp.sum(
        (ends_row <= iota((rows, count), 0)).astype(jnp.int32), axis=1, keepdims=True
    )
    allowed = (seg_row == seg_col) & (iota((rows, rows), 0) <= iota((rows, rows), 1))
    bias_ref[...] = jnp.where(allowed, 0.0, masked_score)


def fill_small(small_ref, shard, pieces, first_row):
    for offset, piece in enumerate(pieces):
        small_ref[shard ^ offset] = piece[first_row:, :].astype(wide)


def fill_cols(full_ref, shard, pieces, first_row, rows, width):
    blocks = full_ref.shape[1] // width
    for offset, piece in enumerate(pieces):
        at = pl.multiple_of((shard ^ offset) * rows, rows)
        for block in range(blocks):
            start = first_row + block * rows
            full_ref[pl.ds(at, rows), block * width : (block + 1) * width] = piece[
                start : start + rows, :
            ]


def head_mask(head):
    lane = iota((1, LANES), 1)
    first = head * HEAD % LANES
    return ((lane >= first) & (lane < first + HEAD)).astype(wide).astype(low)


def head_tile(head):
    first = head * HEAD // LANES * LANES
    return slice(first, first + LANES)


def query_blocks(rows):
    size = min(256, rows)
    return [(at, at + size) for at in range(0, rows, size)]


def put_blocks(target, row, source, width):
    rows = source.shape[0]
    for block in range(source.shape[1] // width):
        cols = slice(block * width, (block + 1) * width)
        target[row : row + rows, :] = source[:, cols].astype(low)
        row += rows
    return row


def fetch_all(sources, buffers, sems):
    copies = [
        pltpu.make_async_copy(source, buffer, sems.at[index])
        for index, (source, buffer) in enumerate(zip(sources, buffers))
    ]
    for copy in copies:
        copy.start()
    return copies


def pack_first_kernel(qkv_ref, small_ref, first_ref, qkv_buf, small_buf, sems):
    width = first_ref.shape[1]
    small_copy, qkv_copy = fetch_all((small_ref, qkv_ref), (small_buf, qkv_buf), sems)
    small_copy.wait()
    parts = [
        small_buf[block * width : (block + 1) * width].reshape(1, width)
        for block in range(small_buf.shape[0] // width)
    ]
    parts.append(jnp.zeros((SMALL_PAD - len(parts), width), wide))
    first_ref[first_ref.shape[0] - SMALL_PAD :, :] = jnp.concatenate(parts, axis=0).astype(low)
    qkv_copy.wait()
    put_blocks(first_ref, 0, qkv_buf, width)


def pack_second_kernel(out_ref, up_ref, down_ref, second_ref, out_buf, up_buf, down_buf, sems):
    width = second_ref.shape[1]
    buffers = (out_buf, up_buf, down_buf)
    copies = fetch_all((out_ref, up_ref, down_ref), buffers, sems)
    row = 0
    for copy, buffer in zip(copies, buffers):
        copy.wait()
        row = put_blocks(second_ref, row, buffer, width)


def prepare_kernel(shards, x_ref, seed_ref, len_ref, owner_ref, bias_ref, norm_ref, root_ref, low_ref):
    rows = x_ref.shape[0]
    device = lax.axis_index("dp") * shards + lax.axis_index("shard")
    own = own_row(len_ref[...], owner_ref[...], device)
    fill_mask(bias_ref, own, rows)
    normed, root = standardize(x_ref[...].astype(wide))
    norm_ref[...] = normed
    root_ref[...] = root
    live = jnp.sum(own, axis=1, keepdims=True)
    live_rows = (iota((rows, 1), 0) < live).astype(wide)
    low_ref[...] = (seed_ref[...].astype(wide) * live_rows).astype(low)


def attend_kernel(shards, *refs):
    norm_ref, bias_ref = refs[:2]
    pieces = refs[2 : 2 + shards]
    joined_ref, out_ref, log_ref, att_ref, weight_ref, small_ref = refs[2 + shards :]
    rows, width = norm_ref.shape
    shard = lax.axis_index("shard")
    part = width // shards
    fill_cols(weight_ref, shard, pieces, 0, part, width)
    fill_small(small_ref, shard, pieces, 3 * part)
    gain, shift = small_ref[0, 0:1, :], small_ref[0, 1:2, :]
    bias_query, bias_value = small_ref[1, 1:2, :], small_ref[1, 2:3, :]
    hidden = (norm_ref[...] * gain + shift).astype(low)
    for block, bias in enumerate((bias_query, None, bias_value)):
        cols = slice(block * width, (block + 1) * width)
        value = dot_nn(hidden, weight_ref[:, cols])
        if bias is not None:
            value = value + bias
        joined_ref[:, cols] = value.astype(low)
    values_t = joined_ref[:, 2 * width :].T
    units = [
        (head, start, stop) for head in range(width // HEAD) for start, stop in query_blocks(rows)
    ]

    def raw_scores(head, start, stop):
        tile = head_tile(head)
        key_tile = joined_ref[:stop, width + tile.start : width + tile.stop] * head_mask(head)
        return dot_nt(key_tile, joined_ref[start:stop, tile])

    ahead = raw_scores(*units[0])
    for index, (head, start, stop) in enumerate(units):
        raw = ahead
        if index + 1 < len(units):
            ahead = raw_scores(*units[index + 1])
        feature = slice(head * HEAD, (head + 1) * HEAD)
        scores = []
        top = None
        for at in range(0, stop, CHUNK):
            piece = raw[at : at + CHUNK] * (score_scale * log2_e)
            piece = piece + bias_ref[at : at + CHUNK, start:stop]
            scores.append(piece)
            top = piece if top is None else jnp.maximum(top, piece)
        top = jnp.max(top, axis=0, keepdims=True)
        exponents = []
        total = None
        for piece in scores:
            piece = jnp.exp2(piece - top)
            total = piece if total is None else total + piece
            exponents.append(piece.astype(low))
        total = jnp.sum(total, axis=0, keepdims=True)
        mixed = dot_nn(values_t[feature, :stop], jnp.concatenate(exponents, axis=0))
        att_ref[feature, start:stop] = mixed * (1.0 / total)
        log_ref[head : head + 1, start:stop] = top + jnp.log2(total)
    out_ref[...] = att_ref[...].astype(low).T


def feed_kernel(shards, *refs):
    x_ref, att_ref, seed_ref = refs[:3]
    firsts = refs[3 : 3 + shards]
    pieces = refs[3 + shards : 3 + 2 * shards]
    refs = refs[3 + 2 * shards :]
    out_ref, middle_ref, dattend_ref, sums_ref, keep_ref, send_ref = refs[:6]
    small_ref, out_w, up_w, down_w, grads_ref = refs[6:]
    rows, width = x_ref.shape
    hidden_count = up_w.shape[1]
    shard = lax.axis_index("shard")
    part = width // shards
    blocks = hidden_count // width
    down_part = hidden_count // shards
    fill_small(small_ref, shard, firsts, 3 * part)
    fill_cols(out_w, shard, pieces, 0, part, width)
    fill_cols(up_w, shard, pieces, part, part, width)
    fill_cols(down_w, shard, pieces, part + blocks * part, down_part, width)
    gain, shift = small_ref[0, 2:3, :], small_ref[1, 0:1, :]
    bias_out, bias_down = small_ref[2, 0:1, :], small_ref[2, 1:2, :]
    bias_up = [small_ref[2, 2:3, :]] + [small_ref[3, row : row + 1, :] for row in range(3)]
    seed_low = seed_ref[...]
    seed = seed_low.astype(wide)
    attended = att_ref[...]
    middle = x_ref[...].astype(wide) + (dot_nn(attended, out_w[...]) + bias_out)
    normed, root = standardize(middle)
    hidden = (normed * gain + shift).astype(low)
    hidden_t = hidden.T
    result = middle + bias_down
    dhidden = jnp.zeros((rows, width), wide)
    sums_ref[...] = jnp.zeros(sums_ref.shape, wide)

    def raw_products(block):
        cols = slice(block * width, (block + 1) * width)
        return dot_nn(hidden, up_w[:, cols]), dot_nt(seed_low, down_w[cols, :])

    ahead = raw_products(0)
    for block in range(blocks):
        cols = slice(block * width, (block + 1) * width)
        raw, dact = ahead
        if block + 1 < blocks:
            ahead = raw_products(block + 1)
        act, dpre = [], []
        for at in range(0, rows, CHUNK):
            pre = raw[at : at + CHUNK] + bias_up[block]
            square = pre * pre
            bend = jnp.tanh(pre * (tanh_scale + (tanh_scale * cubic) * square))
            half = 0.5 + 0.5 * bend
            act.append((pre * half).astype(low))
            slope = 0.5 * tanh_scale + (1.5 * tanh_scale * cubic) * square
            slope = half + (pre * slope) * (1.0 - bend * bend)
            dpre.append((dact[at : at + CHUNK] * slope).astype(low))
        act = jnp.concatenate(act, axis=0)
        dpre = jnp.concatenate(dpre, axis=0)
        result = result + dot_nn(act, down_w[cols, :])
        dhidden = dhidden + dot_nt(dpre, up_w[:, cols])
        grad_down = dot_nn(act.T, seed_low)
        grad_up = dot_nn(hidden_t, dpre)
        for piece in range(width // down_part):
            target = block * (width // down_part) + piece
            at = part + blocks * part
            grads_ref[target, at : at + down_part, :] = grad_down[
                piece * down_part : (piece + 1) * down_part, :
            ]
        for target in range(shards):
            at = part + block * part
            grads_ref[target, at : at + part, :] = grad_up[target * part : (target + 1) * part, :]
        sums_ref[4 + block : 5 + block, :] = jnp.sum(dpre.astype(wide), axis=0, keepdims=True)
    out_ref[...] = result.astype(low)
    through, gain_grad, shift_grad = norm_back(dhidden, normed, root, gain)
    dmiddle = seed + through
    middle_ref[...] = dmiddle
    dmiddle_low = dmiddle.astype(low)
    grad_out = dot_nn(attended.T, dmiddle_low)
    for target in range(shards):
        grads_ref[target, :part, :] = grad_out[target * part : (target + 1) * part, :]
    dattend_ref[...] = dot_nt(dmiddle_low, out_w[...]).astype(low)
    sums_ref[0:1, :] = gain_grad
    sums_ref[1:2, :] = shift_grad
    sums_ref[2:3, :] = jnp.sum(dmiddle_low.astype(wide), axis=0, keepdims=True)
    sums_ref[3:4, :] = jnp.sum(seed, axis=0, keepdims=True)
    part_ways(grads_ref, keep_ref, send_ref, shard & 1)


def part_ways(grads_ref, keep_ref, send_ref, side):
    for pair in range(keep_ref.shape[0]):
        keep_ref[pair] = grads_ref[2 * pair + side]
        send_ref[pair] = grads_ref[2 * pair + 1 - side].astype(low)


def back_heads(
    heads, joined_ref, dattend_ref, log_ref, bias_ref, mixed_ref, dquery_t, dkey, dvalue
):
    rows = joined_ref.shape[0]
    width = joined_ref.shape[1] // 3
    first = heads[0] * HEAD
    count = len(heads) * HEAD
    base = first // LANES * LANES
    tile = slice(base, base + LANES)
    inside = slice(first - base, first - base + count)
    keys_t = joined_ref[:, width + base : width + base + LANES].T
    datt_t = dattend_ref[:, tile].T[inside]
    inner = datt_t.astype(wide) * mixed_ref[first : first + count, :]
    units = [(head, start, stop) for head in heads for start, stop in query_blocks(rows)]

    def raw_products(head, start, stop):
        mask = head_mask(head)
        key_tile = joined_ref[:stop, width + base : width + base + LANES] * mask
        value_tile = joined_ref[:stop, 2 * width + base : 2 * width + base + LANES] * mask
        query = joined_ref[start:stop, tile]
        datt = dattend_ref[start:stop, tile]
        return dot_nt(key_tile, query), dot_nt(value_tile, datt), query * mask, datt * mask

    ahead = raw_products(*units[0])
    for index, (head, start, stop) in enumerate(units):
        raw, dprobs, query, datt = ahead
        if index + 1 < len(units):
            ahead = raw_products(*units[index + 1])
        local = head * HEAD - first
        feature = slice(local, local + HEAD)
        weighted = jnp.sum(inner[feature, start:stop], axis=0, keepdims=True)
        logs = log_ref[head : head + 1, start:stop]
        probs, dscores = [], []
        for at in range(0, stop, CHUNK):
            piece = raw[at : at + CHUNK] * (score_scale * log2_e)
            piece = jnp.exp2(piece + bias_ref[at : at + CHUNK, start:stop] - logs)
            probs.append(piece.astype(low))
            piece = piece * (dprobs[at : at + CHUNK] - weighted)
            dscores.append(piece.astype(low))
        probs = jnp.concatenate(probs, axis=0)
        dscores = jnp.concatenate(dscores, axis=0)
        depth = slice(head * HEAD - base, head * HEAD - base + HEAD)
        dquery_t[depth, start:stop] = (
            dot_nn(keys_t[depth, :stop], dscores) * score_scale
        ).astype(low)
        dvalue[:stop, :] += dot_nn(probs, datt)
        dkey[:stop, :] += dot_nn(dscores, query)


def back_first_kernel(heads, *refs):
    dquery_t, dkey, dvalue = refs[5:8]
    dkey[...] = jnp.zeros(dkey.shape, wide)
    dvalue[...] = jnp.zeros(dvalue.shape, wide)
    dquery_t[...] = jnp.zeros(dquery_t.shape, low)
    back_heads(heads, *refs)


def back_last_kernel(shards, head_groups, *refs):
    shared = refs[:5]
    earlier = refs[5:8]
    norm_ref, root_ref, middle_ref, sums_in = refs[8:12]
    pieces = refs[12 : 12 + shards]
    refs = refs[12 + shards :]
    dx_ref, keep_ref, send_ref = refs[:3]
    weight_ref, small_ref, dquery_t, dkey, dvalue, djoined, grads_ref = refs[3:]
    rows, width = norm_ref.shape
    shard = lax.axis_index("shard")
    part = width // shards
    fill_cols(weight_ref, shard, pieces, 0, part, width)
    fill_small(small_ref, shard, pieces, 3 * part)
    gain, shift = small_ref[0, 0:1, :], small_ref[0, 1:2, :]
    for target, value in zip((dquery_t, dkey, dvalue), earlier):
        target[...] = value[...]
    for heads in head_groups:
        back_heads(heads, *shared, dquery_t, dkey, dvalue)
        if (heads[-1] + 1) * HEAD % LANES == 0:
            first = (heads[-1] + 1) * HEAD - LANES
            values = (dquery_t[...].T, dkey[...] * score_scale, dvalue[...])
            for block, value in enumerate(values):
                at = block * width + first
                djoined[:, at : at + LANES] = value.astype(low)
            dkey[...] = jnp.zeros(dkey.shape, wide)
            dvalue[...] = jnp.zeros(dvalue.shape, wide)
    normed, root = norm_ref[...], root_ref[...]
    hidden_t = (normed * gain + shift).astype(low).T
    dhidden = jnp.zeros((rows, width), wide)
    bias_sums = []
    for block in range(3):
        cols = slice(block * width, (block + 1) * width)
        piece = djoined[:, cols]
        dhidden = dhidden + dot_nt(piece, weight_ref[:, cols])
        grad = dot_nn(hidden_t, piece)
        for target in range(shards):
            grads_ref[target, block * part : (block + 1) * part, :] = grad[
                target * part : (target + 1) * part, :
            ]
        if block != 1:
            bias_sums.append(jnp.sum(piece.astype(wide), axis=0, keepdims=True))
    through, gain_grad, shift_grad = norm_back(dhidden, normed, root, gain)
    dx_ref[...] = middle_ref[...] + through
    sums = [gain_grad, shift_grad, sums_in[0:1, :], sums_in[1:2, :]] + bias_sums
    sums += [sums_in[row : row + 1, :] for row in range(2, 8)]
    per_shard = len(sums) // shards
    empty = [jnp.zeros((grads_ref.shape[1] - 3 * part - per_shard, width), wide)]
    for target in range(shards):
        rows_here = sums[target * per_shard : (target + 1) * per_shard]
        grads_ref[target, 3 * part :, :] = jnp.concatenate(rows_here + empty, axis=0)
    part_ways(grads_ref, keep_ref, send_ref, shard & 1)


def halve_kernel(bit, kept, *refs):
    arrived, (keep_ref, send_ref) = refs[:-2], refs[-2:]
    side = (lax.axis_index("dp") >> bit) & 1

    def total(index):
        value = kept[index]
        for piece in arrived:
            value = value + piece[index].astype(wide)
        return value

    for pair in range(keep_ref.shape[0]):
        keep_ref[pair] = total(2 * pair + side)
        send_ref[pair] = total(2 * pair + 1 - side).astype(low)


def piece_spans(total, tail, group):
    spans = [((total - tail) // group, 0, True)]
    if tail:
        spans.append((tail, total - tail, False))
    return spans


def quarter_kernel(tail, kept, arrived, keep_ref, beside_ref, across_ref, corner_ref, sum_ref):
    group = sum_ref.shape[1]
    for half in range(2):
        total = kept[half] + arrived[half].astype(wide)
        for index in range(group):
            row = 0
            for rows, first, moves in piece_spans(total.shape[0], tail, group):
                at = first + index * rows if moves else first
                sum_ref[half, index, row : row + rows, :] = total[at : at + rows, :]
                row += rows
    mine = (lax.axis_index("shard") >> 1) & 1
    side = lax.axis_index("dp") & 1
    for pair in range(group // 2):
        keep_ref[pair] = sum_ref[mine, 2 * pair + side]
        beside_ref[pair] = sum_ref[1 - mine, 2 * pair + side].astype(low)
        across_ref[pair] = sum_ref[mine, 2 * pair + 1 - side].astype(low)
        corner_ref[pair] = sum_ref[1 - mine, 2 * pair + 1 - side].astype(low)


def piece_kernel(*refs):
    parts = [
        mine[...].reshape(mine.shape[-2:]).astype(wide)
        + other[...].reshape(other.shape[-2:]).astype(wide)
        for mine, other in zip(refs[:-1:2], refs[1:-1:2])
    ]
    refs[-1][...] = jnp.concatenate(parts, axis=0).astype(low)


def adam_values(weight, grad, first, second, decay_rate):
    first_next = beta_one * first + (1.0 - beta_one) * grad
    second_next = beta_two * second + (1.0 - beta_two) * grad * grad
    first_fix = 1.0 - beta_one**STEP
    second_fix = 1.0 - beta_two**STEP
    update = (first_next * (1.0 / first_fix)) / (
        jnp.sqrt(second_next * (1.0 / second_fix)) + adam_eps
    )
    return first_next, second_next, weight - learn_rate * (update + decay_rate * weight)


def adam_kernel(group, spans, layout, *refs):
    pieces = refs[:group]
    count = len(layout)
    states = refs[group : group + 3 * count]
    results = refs[group + 3 * count : group + 6 * count]
    buffers = refs[group + 6 * count : group + 9 * count]
    grad_ref, sems = refs[-2:]
    copies = []
    for offset, piece in enumerate(pieces):
        value = piece[...].astype(wide)
        index = (lax.axis_index("dp") & (group - 1)) ^ offset
        for rows, first, row in spans:
            at = pl.multiple_of(first + index * rows, TILE_ROWS)
            grad_ref[pl.ds(at, rows), :] = value[row : row + rows, :]
    width = grad_ref.shape[1]
    for array, (first_row, stride, decay) in enumerate(layout):
        weight, first, second = states[3 * array : 3 * array + 3]
        new = buffers[3 * array : 3 * array + 3]
        vector = len(weight.shape) == 1
        rows = 1 if vector else weight.shape[0]
        for block in range(weight.shape[-1] // width):
            cols = slice(block * width, (block + 1) * width)
            where = cols if vector else (slice(None), cols)
            at = first_row + block * stride
            values = adam_values(
                weight[where].reshape(rows, width),
                grad_ref[at : at + rows, :],
                first[where].reshape(rows, width),
                second[where].reshape(rows, width),
                decay,
            )
            for target, value in zip(new, values):
                target[where] = value.reshape(width) if vector else value
        for index in range(3 * array, 3 * array + 3):
            copies.append(
                pltpu.make_async_copy(buffers[index], results[index], sems.at[index])
            )
            copies[-1].start()
    for copy in copies:
        copy.wait()


def local_call(kernel, outs, operands, scratch=(), flops=0, name=None, fetch=False, sems=0):
    in_space = pltpu.HBM if fetch else pltpu.VMEM
    out_space = pltpu.HBM if sems else pltpu.VMEM
    outs = [jax.ShapeDtypeStruct(*out) for out in outs]
    moved = sum(
        math.prod(item.shape) * item.dtype.itemsize for item in list(operands) + outs
    )
    scratch_shapes = [pltpu.VMEM(*item) for item in scratch]
    if fetch or sems:
        scratch_shapes.append(pltpu.SemaphoreType.DMA((sems or len(operands),)))
    limit = 56 if fetch else 40
    return pl.pallas_call(
        kernel,
        out_shape=outs,
        in_specs=[pl.BlockSpec(memory_space=in_space)] * len(operands),
        out_specs=[pl.BlockSpec(memory_space=out_space)] * len(outs),
        scratch_shapes=scratch_shapes,
        compiler_params=pltpu.CompilerParams(vmem_limit_bytes=limit * 1024 * 1024),
        cost_estimate=pl.CostEstimate(flops=flops, bytes_accessed=moved, transcendentals=0),
        name=name,
    )(*operands)


def exchange(values, axis, mask):
    count = lax.axis_size(axis)
    return lax.ppermute(values, axis, [(index, index ^ mask) for index in range(count)])


def gather_pieces(value, group):
    found = {0: value}
    near = min(group, 4)
    far = near
    while far < group:
        for offset in sorted(found):
            found[offset ^ far] = exchange(found[offset], "dp", far)
        far *= 2
    for offset in range(1, near):
        found[offset] = exchange(value, "dp", offset)
    if near < group:
        found[near], found[1] = lax.optimization_barrier((found[near], found[1]))
    for base in range(near, group, near):
        for offset in range(near - 1, 0, -1):
            found[base ^ offset] = exchange(found[base], "dp", offset)
    return [found[offset] for offset in range(group)]


def corner(values):
    replicas, shards = lax.axis_size("dp"), lax.axis_size("shard")
    pairs = [
        (replica * shards + shard, (replica ^ 1) * shards + (shard ^ 2))
        for replica in range(replicas)
        for shard in range(shards)
    ]
    return lax.ppermute(values, ("dp", "shard"), pairs)


def quarter_call(kept, arrived, tail, group, name):
    _, rows, width = kept.shape
    shape = (group // 2, (rows - tail) // group + tail, width)
    return local_call(
        functools.partial(quarter_kernel, tail),
        [(shape, wide)] + [(shape, low)] * 3,
        [kept, arrived],
        [((2, group) + shape[1:], wide)],
        name=name,
    )


def spread(beside, across, far):
    return [exchange(beside, "shard", 2), exchange(across, "dp", 1), corner(far)]


def near_sum(flat):
    half = flat[0].shape[0]
    bit = 1
    while half > 1:
        half //= 2
        shape = (half,) + flat[0].shape[1:]
        keep, send = local_call(
            functools.partial(halve_kernel, bit),
            [(shape, wide), (shape, low)],
            flat,
            name="halve_dp",
        )
        flat = [keep, exchange(send, "dp", 1 << bit)]
        bit += 1
    return flat


def finish_sum(chunks, group):
    replicas = lax.axis_size("dp")
    flat = [item for chunk in chunks for item in near_sum(chunk)]
    width = flat[0].shape[-1]
    rows = sum(item.shape[1] for item in flat[::2])
    (piece,) = local_call(piece_kernel, [((rows, width), low)], flat, name="piece_sum")
    mask = group
    while mask < replicas:
        other = exchange(piece, "dp", mask)
        (piece,) = local_call(piece_kernel, [((rows, width), low)], [piece, other], name="far_sum")
        mask *= 2
    return gather_pieces(piece, group)


def adam_call(pieces, counts, tails, states, layout):
    group = len(pieces)
    width = pieces[0].shape[1]
    spans = []
    first = row = 0
    for total, tail in zip(counts, tails):
        for rows, start, moves in piece_spans(total, tail, group):
            spans.append((rows, first + start, row))
            row += rows
            first += rows * (group - 1) * (not moves)
        first += total
    outs = [(state[0].shape, wide) for state in states for _ in range(3)]
    return local_call(
        functools.partial(adam_kernel, group, spans, layout),
        outs,
        pieces + [item for state in states for item in state],
        outs + [((first, width), wide)],
        name="adam",
        sems=len(outs),
    )


def shards_program(
    tokens,
    cotangent,
    lengths,
    seq_owner,
    qkv_weight,
    out_weight,
    up_weight,
    down_weight,
    gains_biases,
    qkv_first,
    qkv_second,
    out_first,
    out_second,
    up_first,
    up_second,
    down_first,
    down_second,
    small_first,
    small_second,
):
    rows, width = tokens.shape
    shards = lax.axis_size("shard")
    heads = width // HEAD
    part = qkv_weight.shape[0]
    hidden_count = up_weight.shape[1]
    group = min(GROUP, lax.axis_size("dp"))
    lengths = lengths.reshape(1, -1)
    seq_owner = seq_owner.reshape(1, -1)
    first_rows = 3 * part + SMALL_PAD
    second_rows = part + up_weight.size // width + down_weight.shape[0]
    (first_pack,) = local_call(
        pack_first_kernel,
        [((first_rows, width), low)],
        [qkv_weight, gains_biases],
        [(qkv_weight.shape, wide), (gains_biases.shape, wide)],
        name="pack_first",
        fetch=True,
    )
    firsts = {0: first_pack}
    firsts[2] = exchange(first_pack, "shard", 2)
    firsts[1] = exchange(first_pack, "shard", 1)
    first_pack, matrices = lax.optimization_barrier(
        (first_pack, [out_weight, up_weight, down_weight])
    )
    (second_pack,) = local_call(
        pack_second_kernel,
        [((second_rows, width), low)],
        matrices,
        [(item.shape, wide) for item in matrices],
        name="pack_second",
        fetch=True,
    )
    early_tokens, second_pack = lax.optimization_barrier((tokens, second_pack))
    square = (rows, rows)
    bias, normed, root, seed = local_call(
        functools.partial(prepare_kernel, shards),
        [(square, wide), ((rows, width), wide), ((rows, 1), wide), ((rows, width), low)],
        [early_tokens, cotangent, lengths, seq_owner],
        name="prepare",
    )
    seconds = {0: second_pack}
    seconds[2] = exchange(second_pack, "shard", 2)
    seconds[1] = exchange(second_pack, "shard", 1)
    firsts[2], bias, normed, root, seed = lax.optimization_barrier(
        (firsts[2], bias, normed, root, seed)
    )
    firsts[3] = exchange(firsts[2], "shard", 1)
    firsts = [firsts[offset] for offset in range(shards)]
    joined, attended, log_sums, mixed = local_call(
        functools.partial(attend_kernel, shards),
        [
            ((rows, 3 * width), low),
            ((rows, width), low),
            ((heads, rows), wide),
            ((width, rows), wide),
        ],
        [normed, bias] + firsts,
        [((width, 3 * width), low), ((shards, SMALL_PAD, width), wide)],
        flops=heads * rows * rows * 640,
        name="attend",
    )
    attended, seconds[2] = lax.optimization_barrier((attended, seconds[2]))
    seconds[3] = exchange(seconds[2], "shard", 1)
    seconds = [seconds[offset] for offset in range(shards)]
    pair = (shards // 2, second_rows, width)
    output, middle_grad, attended_grad, sums, kept_ffn, send_ffn = local_call(
        functools.partial(feed_kernel, shards),
        [
            ((rows, width), low),
            ((rows, width), wide),
            ((rows, width), low),
            ((SMALL_PAD, width), wide),
            (pair, wide),
            (pair, low),
        ],
        [tokens, attended, seed] + firsts + seconds,
        [
            ((shards, SMALL_PAD, width), wide),
            ((width, width), low),
            ((width, hidden_count), low),
            ((hidden_count, width), low),
            ((shards, second_rows, width), wide),
        ],
        flops=rows * width * (hidden_count * 12 + width * 6),
        name="feed",
    )
    arrived_ffn = exchange(send_ffn, "shard", 1)
    shared = [joined, attended_grad, log_sums, bias, mixed]
    tile_scratch = [((LANES, rows), low), ((rows, LANES), wide), ((rows, LANES), wide)]
    per_tile = LANES // HEAD
    groups = [list(range(at, at + per_tile)) for at in range(0, heads, per_tile)]
    groups = [groups[0][:3], groups[0][3:]] + groups[1:]
    first_query, first_key, first_value = local_call(
        functools.partial(back_first_kernel, groups[0]),
        tile_scratch,
        shared,
        flops=heads * rows * rows * 256 * 5 // 2,
        name="back_first",
    )
    first_query, arrived_ffn = lax.optimization_barrier((first_query, arrived_ffn))
    tail = TILE_ROWS
    keep_ffn, *sends_ffn = quarter_call(kept_ffn, arrived_ffn, 0, group, "quarter_ffn")
    first_query, sends_ffn = lax.optimization_barrier((first_query, sends_ffn))
    arrived_ffn = spread(*sends_ffn)
    att_rows = 3 * part + tail
    pair = (shards // 2, att_rows, width)
    input_grad, kept_att, send_att = local_call(
        functools.partial(back_last_kernel, shards, groups[1:]),
        [((rows, width), wide), (pair, wide), (pair, low)],
        shared + [first_query, first_key, first_value, normed, root, middle_grad, sums] + firsts,
        [((width, 3 * width), low), ((shards, SMALL_PAD, width), wide)]
        + tile_scratch
        + [((rows, 3 * width), low), ((shards, att_rows, width), wide)],
        flops=heads * rows * rows * 256 * 6,
        name="back_last",
    )
    send_att, arrived_ffn = lax.optimization_barrier((send_att, arrived_ffn))
    arrived_att = exchange(send_att, "shard", 1)
    keep_att, *sends_att = quarter_call(kept_att, arrived_att, tail, group, "quarter_att")
    arrived_att = spread(*sends_att)
    tails = (0, tail)
    pieces = finish_sum([[keep_ffn] + arrived_ffn, [keep_att] + arrived_att], group)
    blocks = hidden_count // width
    results = adam_call(
        pieces,
        (second_rows, att_rows),
        tails,
        [
            (qkv_weight, qkv_first, qkv_second),
            (out_weight, out_first, out_second),
            (up_weight, up_first, up_second),
            (down_weight, down_first, down_second),
            (gains_biases, small_first, small_second),
        ],
        [
            (second_rows, part, matrix_decay),
            (0, part, matrix_decay),
            (part, part, matrix_decay),
            (part + blocks * part, 0, matrix_decay),
            (second_rows + 3 * part, 1, 0.0),
        ],
    )
    return (output, input_grad, *results)


def solution(mesh):
    rows = P(("dp", "shard"), None)
    matrix = P("shard", None)
    vector = P("shard")
    return jax.shard_map(
        shards_program,
        mesh=mesh,
        in_specs=(rows, rows, P(), P())
        + (matrix,) * 4
        + (vector,)
        + (matrix,) * 8
        + (vector, vector),
        out_specs=(rows, rows) + (matrix,) * 12 + (vector,) * 3,
        check_vma=False,
    )
```

```python
import functools
import math

import jax
import jax.numpy as jnp
from jax import lax
from jax.experimental import pallas as pl
from jax.experimental.pallas import tpu as pltpu
from jax.sharding import PartitionSpec as P

HEAD = 32
STEP = 10
LANES = 128
GROUP = 8
SMALL_PAD = 16
TILE_ROWS = 8
CHUNK = 64

norm_eps = 1e-05
beta_one = 0.9
beta_two = 0.95
learn_rate = 0.1
adam_eps = 1e-08
matrix_decay = 0.1
masked_score = -1e30
low = jnp.bfloat16
wide = jnp.float32
log2_e = math.log2(math.e)
score_scale = 1.0 / math.sqrt(HEAD)
tanh_scale = math.sqrt(2.0 / math.pi)
cubic = 0.044715


def dot_nn(left, right):
    return jnp.dot(left, right, preferred_element_type=wide)


def dot_nt(left, right):
    return lax.dot_general(left, right, (((1,), (1,)), ((), ())), preferred_element_type=wide)


def standardize(values):
    centered = values - jnp.mean(values, axis=-1, keepdims=True)
    root_inv = lax.rsqrt(jnp.mean(centered * centered, axis=-1, keepdims=True) + norm_eps)
    return centered * root_inv, root_inv


def norm_back(upstream, normed, root_inv, gain):
    scaled = upstream * gain
    inner_mean = jnp.mean(scaled, axis=-1, keepdims=True)
    cross_mean = jnp.mean(scaled * normed, axis=-1, keepdims=True)
    through = root_inv * (scaled - inner_mean - normed * cross_mean)
    return (
        through,
        jnp.sum(upstream * normed, axis=0, keepdims=True),
        jnp.sum(upstream, axis=0, keepdims=True),
    )


def iota(shape, dim):
    return lax.broadcasted_iota(jnp.int32, shape, dim)


def own_row(lengths, owners, device):
    return jnp.where(owners == device, lengths, 0)


def ends_both(own):
    count = own.shape[1]
    shape = (count, count)
    rows, cols = iota(shape, 0), iota(shape, 1)
    spread = jnp.broadcast_to(own, shape)
    ends_col = jnp.sum(jnp.where(cols <= rows, spread, 0), axis=1, keepdims=True)
    own_col = jnp.sum(jnp.where(cols == rows, spread, 0), axis=1, keepdims=True)
    ends_row = jnp.sum(
        jnp.where(rows <= cols, jnp.broadcast_to(own_col, shape), 0), axis=0, keepdims=True
    )
    return ends_col, ends_row


def fill_mask(bias_ref, own, rows):
    ends_col, ends_row = ends_both(own)
    count = own.shape[1]
    seg_row = jnp.sum(
        (ends_col <= iota((count, rows), 1)).astype(jnp.int32), axis=0, keepdims=True
    )
    seg_col = jnp.sum(
        (ends_row <= iota((rows, count), 0)).astype(jnp.int32), axis=1, keepdims=True
    )
    allowed = (seg_row == seg_col) & (iota((rows, rows), 0) <= iota((rows, rows), 1))
    bias_ref[...] = jnp.where(allowed, 0.0, masked_score)


def fill_small(small_ref, shard, pieces, first_row):
    for offset, piece in enumerate(pieces):
        small_ref[shard ^ offset] = piece[first_row:, :].astype(wide)


def fill_cols(full_ref, shard, pieces, first_row, rows, width):
    blocks = full_ref.shape[1] // width
    for offset, piece in enumerate(pieces):
        at = pl.multiple_of((shard ^ offset) * rows, rows)
        for block in range(blocks):
            start = first_row + block * rows
            full_ref[pl.ds(at, rows), block * width : (block + 1) * width] = piece[
                start : start + rows, :
            ]


def head_mask(head):
    lane = iota((1, LANES), 1)
    first = head * HEAD % LANES
    return ((lane >= first) & (lane < first + HEAD)).astype(wide).astype(low)


def head_tile(head):
    first = head * HEAD // LANES * LANES
    return slice(first, first + LANES)


def query_blocks(rows):
    size = min(256, rows)
    return [(at, at + size) for at in range(0, rows, size)]


def put_blocks(target, row, source, width):
    rows = source.shape[0]
    for block in range(source.shape[1] // width):
        cols = slice(block * width, (block + 1) * width)
        target[row : row + rows, :] = source[:, cols].astype(low)
        row += rows
    return row


def fetch_all(sources, buffers, sems):
    copies = [
        pltpu.make_async_copy(source, buffer, sems.at[index])
        for index, (source, buffer) in enumerate(zip(sources, buffers))
    ]
    for copy in copies:
        copy.start()
    return copies


def pack_first_kernel(qkv_ref, small_ref, first_ref, qkv_buf, small_buf, sems):
    width = first_ref.shape[1]
    small_copy, qkv_copy = fetch_all((small_ref, qkv_ref), (small_buf, qkv_buf), sems)
    small_copy.wait()
    parts = [
        small_buf[block * width : (block + 1) * width].reshape(1, width)
        for block in range(small_buf.shape[0] // width)
    ]
    parts.append(jnp.zeros((SMALL_PAD - len(parts), width), wide))
    first_ref[first_ref.shape[0] - SMALL_PAD :, :] = jnp.concatenate(parts, axis=0).astype(low)
    qkv_copy.wait()
    put_blocks(first_ref, 0, qkv_buf, width)


def pack_second_kernel(out_ref, up_ref, down_ref, second_ref, out_buf, up_buf, down_buf, sems):
    width = second_ref.shape[1]
    buffers = (out_buf, up_buf, down_buf)
    copies = fetch_all((out_ref, up_ref, down_ref), buffers, sems)
    row = 0
    for copy, buffer in zip(copies, buffers):
        copy.wait()
        row = put_blocks(second_ref, row, buffer, width)


def prepare_kernel(shards, x_ref, seed_ref, len_ref, owner_ref, bias_ref, norm_ref, root_ref, low_ref):
    rows = x_ref.shape[0]
    device = lax.axis_index("dp") * shards + lax.axis_index("shard")
    own = own_row(len_ref[...], owner_ref[...], device)
    fill_mask(bias_ref, own, rows)
    normed, root = standardize(x_ref[...].astype(wide))
    norm_ref[...] = normed
    root_ref[...] = root
    live = jnp.sum(own, axis=1, keepdims=True)
    live_rows = (iota((rows, 1), 0) < live).astype(wide)
    low_ref[...] = (seed_ref[...].astype(wide) * live_rows).astype(low)


def attend_kernel(shards, *refs):
    norm_ref, bias_ref = refs[:2]
    pieces = refs[2 : 2 + shards]
    joined_ref, out_ref, log_ref, att_ref, weight_ref, small_ref = refs[2 + shards :]
    rows, width = norm_ref.shape
    shard = lax.axis_index("shard")
    part = width // shards
    fill_cols(weight_ref, shard, pieces, 0, part, width)
    fill_small(small_ref, shard, pieces, 3 * part)
    gain, shift = small_ref[0, 0:1, :], small_ref[0, 1:2, :]
    bias_query, bias_value = small_ref[1, 1:2, :], small_ref[1, 2:3, :]
    hidden = (norm_ref[...] * gain + shift).astype(low)
    for block, bias in enumerate((bias_query, None, bias_value)):
        cols = slice(block * width, (block + 1) * width)
        value = dot_nn(hidden, weight_ref[:, cols])
        if bias is not None:
            value = value + bias
        joined_ref[:, cols] = value.astype(low)
    values_t = joined_ref[:, 2 * width :].T
    units = [
        (head, start, stop) for head in range(width // HEAD) for start, stop in query_blocks(rows)
    ]

    def raw_scores(head, start, stop):
        tile = head_tile(head)
        key_tile = joined_ref[:stop, width + tile.start : width + tile.stop] * head_mask(head)
        return dot_nt(key_tile, joined_ref[start:stop, tile])

    ahead = raw_scores(*units[0])
    for index, (head, start, stop) in enumerate(units):
        raw = ahead
        if index + 1 < len(units):
            ahead = raw_scores(*units[index + 1])
        feature = slice(head * HEAD, (head + 1) * HEAD)
        scores = []
        top = None
        for at in range(0, stop, CHUNK):
            piece = raw[at : at + CHUNK] * (score_scale * log2_e)
            piece = piece + bias_ref[at : at + CHUNK, start:stop]
            scores.append(piece)
            top = piece if top is None else jnp.maximum(top, piece)
        top = jnp.max(top, axis=0, keepdims=True)
        exponents = []
        total = None
        for piece in scores:
            piece = jnp.exp2(piece - top)
            total = piece if total is None else total + piece
            exponents.append(piece.astype(low))
        total = jnp.sum(total, axis=0, keepdims=True)
        mixed = dot_nn(values_t[feature, :stop], jnp.concatenate(exponents, axis=0))
        att_ref[feature, start:stop] = mixed * (1.0 / total)
        log_ref[head : head + 1, start:stop] = top + jnp.log2(total)
    out_ref[...] = att_ref[...].astype(low).T


def feed_kernel(shards, *refs):
    x_ref, att_ref, seed_ref = refs[:3]
    firsts = refs[3 : 3 + shards]
    pieces = refs[3 + shards : 3 + 2 * shards]
    refs = refs[3 + 2 * shards :]
    out_ref, middle_ref, dattend_ref, sums_ref, keep_ref, send_ref = refs[:6]
    small_ref, out_w, up_w, down_w, grads_ref = refs[6:]
    rows, width = x_ref.shape
    hidden_count = up_w.shape[1]
    shard = lax.axis_index("shard")
    part = width // shards
    blocks = hidden_count // width
    down_part = hidden_count // shards
    fill_small(small_ref, shard, firsts, 3 * part)
    fill_cols(out_w, shard, pieces, 0, part, width)
    fill_cols(up_w, shard, pieces, part, part, width)
    fill_cols(down_w, shard, pieces, part + blocks * part, down_part, width)
    gain, shift = small_ref[0, 2:3, :], small_ref[1, 0:1, :]
    bias_out, bias_down = small_ref[2, 0:1, :], small_ref[2, 1:2, :]
    bias_up = [small_ref[2, 2:3, :]] + [small_ref[3, row : row + 1, :] for row in range(3)]
    seed_low = seed_ref[...]
    seed = seed_low.astype(wide)
    attended = att_ref[...]
    middle = x_ref[...].astype(wide) + (dot_nn(attended, out_w[...]) + bias_out)
    normed, root = standardize(middle)
    hidden = (normed * gain + shift).astype(low)
    hidden_t = hidden.T
    result = middle + bias_down
    dhidden = jnp.zeros((rows, width), wide)
    sums_ref[...] = jnp.zeros(sums_ref.shape, wide)

    def raw_products(block):
        cols = slice(block * width, (block + 1) * width)
        return dot_nn(hidden, up_w[:, cols]), dot_nt(seed_low, down_w[cols, :])

    ahead = raw_products(0)
    for block in range(blocks):
        cols = slice(block * width, (block + 1) * width)
        raw, dact = ahead
        if block + 1 < blocks:
            ahead = raw_products(block + 1)
        act, dpre = [], []
        for at in range(0, rows, CHUNK):
            pre = raw[at : at + CHUNK] + bias_up[block]
            square = pre * pre
            bend = jnp.tanh(pre * (tanh_scale + (tanh_scale * cubic) * square))
            half = 0.5 + 0.5 * bend
            act.append((pre * half).astype(low))
            slope = 0.5 * tanh_scale + (1.5 * tanh_scale * cubic) * square
            slope = half + (pre * slope) * (1.0 - bend * bend)
            dpre.append((dact[at : at + CHUNK] * slope).astype(low))
        act = jnp.concatenate(act, axis=0)
        dpre = jnp.concatenate(dpre, axis=0)
        result = result + dot_nn(act, down_w[cols, :])
        dhidden = dhidden + dot_nt(dpre, up_w[:, cols])
        grad_down = dot_nn(act.T, seed_low)
        grad_up = dot_nn(hidden_t, dpre)
        for piece in range(width // down_part):
            target = block * (width // down_part) + piece
            at = part + blocks * part
            grads_ref[target, at : at + down_part, :] = grad_down[
                piece * down_part : (piece + 1) * down_part, :
            ]
        for target in range(shards):
            at = part + block * part
            grads_ref[target, at : at + part, :] = grad_up[target * part : (target + 1) * part, :]
        sums_ref[4 + block : 5 + block, :] = jnp.sum(dpre.astype(wide), axis=0, keepdims=True)
    out_ref[...] = result.astype(low)
    through, gain_grad, shift_grad = norm_back(dhidden, normed, root, gain)
    dmiddle = seed + through
    middle_ref[...] = dmiddle
    dmiddle_low = dmiddle.astype(low)
    grad_out = dot_nn(attended.T, dmiddle_low)
    for target in range(shards):
        grads_ref[target, :part, :] = grad_out[target * part : (target + 1) * part, :]
    dattend_ref[...] = dot_nt(dmiddle_low, out_w[...]).astype(low)
    sums_ref[0:1, :] = gain_grad
    sums_ref[1:2, :] = shift_grad
    sums_ref[2:3, :] = jnp.sum(dmiddle_low.astype(wide), axis=0, keepdims=True)
    sums_ref[3:4, :] = jnp.sum(seed, axis=0, keepdims=True)
    part_ways(grads_ref, keep_ref, send_ref, shard & 1)


def part_ways(grads_ref, keep_ref, send_ref, side):
    for pair in range(keep_ref.shape[0]):
        keep_ref[pair] = grads_ref[2 * pair + side]
        send_ref[pair] = grads_ref[2 * pair + 1 - side].astype(low)


def back_heads(
    heads, joined_ref, dattend_ref, log_ref, bias_ref, mixed_ref, dquery_t, dkey, dvalue
):
    rows = joined_ref.shape[0]
    width = joined_ref.shape[1] // 3
    first = heads[0] * HEAD
    count = len(heads) * HEAD
    base = first // LANES * LANES
    tile = slice(base, base + LANES)
    inside = slice(first - base, first - base + count)
    keys_t = joined_ref[:, width + base : width + base + LANES].T
    datt_t = dattend_ref[:, tile].T[inside]
    inner = datt_t.astype(wide) * mixed_ref[first : first + count, :]
    units = [(head, start, stop) for head in heads for start, stop in query_blocks(rows)]

    def raw_products(head, start, stop):
        mask = head_mask(head)
        key_tile = joined_ref[:stop, width + base : width + base + LANES] * mask
        value_tile = joined_ref[:stop, 2 * width + base : 2 * width + base + LANES] * mask
        query = joined_ref[start:stop, tile]
        datt = dattend_ref[start:stop, tile]
        return dot_nt(key_tile, query), dot_nt(value_tile, datt), query * mask, datt * mask

    ahead = raw_products(*units[0])
    for index, (head, start, stop) in enumerate(units):
        raw, dprobs, query, datt = ahead
        if index + 1 < len(units):
            ahead = raw_products(*units[index + 1])
        local = head * HEAD - first
        feature = slice(local, local + HEAD)
        weighted = jnp.sum(inner[feature, start:stop], axis=0, keepdims=True)
        logs = log_ref[head : head + 1, start:stop]
        probs, dscores = [], []
        for at in range(0, stop, CHUNK):
            piece = raw[at : at + CHUNK] * (score_scale * log2_e)
            piece = jnp.exp2(piece + bias_ref[at : at + CHUNK, start:stop] - logs)
            probs.append(piece.astype(low))
            piece = piece * (dprobs[at : at + CHUNK] - weighted)
            dscores.append(piece.astype(low))
        probs = jnp.concatenate(probs, axis=0)
        dscores = jnp.concatenate(dscores, axis=0)
        depth = slice(head * HEAD - base, head * HEAD - base + HEAD)
        dquery_t[depth, start:stop] = (
            dot_nn(keys_t[depth, :stop], dscores) * score_scale
        ).astype(low)
        dvalue[:stop, :] += dot_nn(probs, datt)
        dkey[:stop, :] += dot_nn(dscores, query)


def back_first_kernel(heads, *refs):
    dquery_t, dkey, dvalue = refs[5:8]
    dkey[...] = jnp.zeros(dkey.shape, wide)
    dvalue[...] = jnp.zeros(dvalue.shape, wide)
    dquery_t[...] = jnp.zeros(dquery_t.shape, low)
    back_heads(heads, *refs)


def back_last_kernel(shards, head_groups, *refs):
    shared = refs[:5]
    earlier = refs[5:8]
    norm_ref, root_ref, middle_ref, sums_in = refs[8:12]
    pieces = refs[12 : 12 + shards]
    refs = refs[12 + shards :]
    dx_ref, keep_ref, send_ref = refs[:3]
    weight_ref, small_ref, dquery_t, dkey, dvalue, djoined, grads_ref = refs[3:]
    rows, width = norm_ref.shape
    shard = lax.axis_index("shard")
    part = width // shards
    fill_cols(weight_ref, shard, pieces, 0, part, width)
    fill_small(small_ref, shard, pieces, 3 * part)
    gain, shift = small_ref[0, 0:1, :], small_ref[0, 1:2, :]
    for target, value in zip((dquery_t, dkey, dvalue), earlier):
        target[...] = value[...]
    for heads in head_groups:
        back_heads(heads, *shared, dquery_t, dkey, dvalue)
        if (heads[-1] + 1) * HEAD % LANES == 0:
            first = (heads[-1] + 1) * HEAD - LANES
            values = (dquery_t[...].T, dkey[...] * score_scale, dvalue[...])
            for block, value in enumerate(values):
                at = block * width + first
                djoined[:, at : at + LANES] = value.astype(low)
            dkey[...] = jnp.zeros(dkey.shape, wide)
            dvalue[...] = jnp.zeros(dvalue.shape, wide)
    normed, root = norm_ref[...], root_ref[...]
    hidden_t = (normed * gain + shift).astype(low).T
    dhidden = jnp.zeros((rows, width), wide)
    bias_sums = []
    for block in range(3):
        cols = slice(block * width, (block + 1) * width)
        piece = djoined[:, cols]
        dhidden = dhidden + dot_nt(piece, weight_ref[:, cols])
        grad = dot_nn(hidden_t, piece)
        for target in range(shards):
            grads_ref[target, block * part : (block + 1) * part, :] = grad[
                target * part : (target + 1) * part, :
            ]
        if block != 1:
            bias_sums.append(jnp.sum(piece.astype(wide), axis=0, keepdims=True))
    through, gain_grad, shift_grad = norm_back(dhidden, normed, root, gain)
    dx_ref[...] = middle_ref[...] + through
    sums = [gain_grad, shift_grad, sums_in[0:1, :], sums_in[1:2, :]] + bias_sums
    sums += [sums_in[row : row + 1, :] for row in range(2, 8)]
    per_shard = len(sums) // shards
    empty = [jnp.zeros((grads_ref.shape[1] - 3 * part - per_shard, width), wide)]
    for target in range(shards):
        rows_here = sums[target * per_shard : (target + 1) * per_shard]
        grads_ref[target, 3 * part :, :] = jnp.concatenate(rows_here + empty, axis=0)
    part_ways(grads_ref, keep_ref, send_ref, shard & 1)


def halve_kernel(bit, kept, *refs):
    arrived, (keep_ref, send_ref) = refs[:-2], refs[-2:]
    side = (lax.axis_index("dp") >> bit) & 1

    def total(index):
        value = kept[index]
        for piece in arrived:
            value = value + piece[index].astype(wide)
        return value

    for pair in range(keep_ref.shape[0]):
        keep_ref[pair] = total(2 * pair + side)
        send_ref[pair] = total(2 * pair + 1 - side).astype(low)


def piece_spans(total, tail, group):
    spans = [((total - tail) // group, 0, True)]
    if tail:
        spans.append((tail, total - tail, False))
    return spans


def quarter_kernel(tail, kept, arrived, keep_ref, beside_ref, across_ref, corner_ref, sum_ref):
    group = sum_ref.shape[1]
    for half in range(2):
        total = kept[half] + arrived[half].astype(wide)
        for index in range(group):
            row = 0
            for rows, first, moves in piece_spans(total.shape[0], tail, group):
                at = first + index * rows if moves else first
                sum_ref[half, index, row : row + rows, :] = total[at : at + rows, :]
                row += rows
    mine = (lax.axis_index("shard") >> 1) & 1
    side = lax.axis_index("dp") & 1
    for pair in range(group // 2):
        keep_ref[pair] = sum_ref[mine, 2 * pair + side]
        beside_ref[pair] = sum_ref[1 - mine, 2 * pair + side].astype(low)
        across_ref[pair] = sum_ref[mine, 2 * pair + 1 - side].astype(low)
        corner_ref[pair] = sum_ref[1 - mine, 2 * pair + 1 - side].astype(low)


def piece_kernel(*refs):
    parts = [
        mine[...].reshape(mine.shape[-2:]).astype(wide)
        + other[...].reshape(other.shape[-2:]).astype(wide)
        for mine, other in zip(refs[:-1:2], refs[1:-1:2])
    ]
    refs[-1][...] = jnp.concatenate(parts, axis=0).astype(low)


def adam_values(weight, grad, first, second, decay_rate):
    first_next = beta_one * first + (1.0 - beta_one) * grad
    second_next = beta_two * second + (1.0 - beta_two) * grad * grad
    first_fix = 1.0 - beta_one**STEP
    second_fix = 1.0 - beta_two**STEP
    update = (first_next * (1.0 / first_fix)) / (
        jnp.sqrt(second_next * (1.0 / second_fix)) + adam_eps
    )
    return first_next, second_next, weight - learn_rate * (update + decay_rate * weight)


def adam_kernel(group, spans, layout, *refs):
    pieces = refs[:group]
    count = len(layout)
    states = refs[group : group + 3 * count]
    results = refs[group + 3 * count : group + 6 * count]
    buffers = refs[group + 6 * count : group + 9 * count]
    grad_ref, sems = refs[-2:]
    copies = []
    for offset, piece in enumerate(pieces):
        value = piece[...].astype(wide)
        index = (lax.axis_index("dp") & (group - 1)) ^ offset
        for rows, first, row in spans:
            at = pl.multiple_of(first + index * rows, TILE_ROWS)
            grad_ref[pl.ds(at, rows), :] = value[row : row + rows, :]
    width = grad_ref.shape[1]
    for array, (first_row, stride, decay) in enumerate(layout):
        weight, first, second = states[3 * array : 3 * array + 3]
        new = buffers[3 * array : 3 * array + 3]
        vector = len(weight.shape) == 1
        rows = 1 if vector else weight.shape[0]
        for block in range(weight.shape[-1] // width):
            cols = slice(block * width, (block + 1) * width)
            where = cols if vector else (slice(None), cols)
            at = first_row + block * stride
            values = adam_values(
                weight[where].reshape(rows, width),
                grad_ref[at : at + rows, :],
                first[where].reshape(rows, width),
                second[where].reshape(rows, width),
                decay,
            )
            for target, value in zip(new, values):
                target[where] = value.reshape(width) if vector else value
        for index in range(3 * array, 3 * array + 3):
            copies.append(
                pltpu.make_async_copy(buffers[index], results[index], sems.at[index])
            )
            copies[-1].start()
    for copy in copies:
        copy.wait()


def local_call(kernel, outs, operands, scratch=(), flops=0, name=None, fetch=False, sems=0):
    in_space = pltpu.HBM if fetch else pltpu.VMEM
    out_space = pltpu.HBM if sems else pltpu.VMEM
    outs = [jax.ShapeDtypeStruct(*out) for out in outs]
    moved = sum(
        math.prod(item.shape) * item.dtype.itemsize for item in list(operands) + outs
    )
    scratch_shapes = [pltpu.VMEM(*item) for item in scratch]
    if fetch or sems:
        scratch_shapes.append(pltpu.SemaphoreType.DMA((sems or len(operands),)))
    limit = 56 if fetch else 40
    return pl.pallas_call(
        kernel,
        out_shape=outs,
        in_specs=[pl.BlockSpec(memory_space=in_space)] * len(operands),
        out_specs=[pl.BlockSpec(memory_space=out_space)] * len(outs),
        scratch_shapes=scratch_shapes,
        compiler_params=pltpu.CompilerParams(vmem_limit_bytes=limit * 1024 * 1024),
        cost_estimate=pl.CostEstimate(flops=flops, bytes_accessed=moved, transcendentals=0),
        name=name,
    )(*operands)


def exchange(values, axis, mask):
    count = lax.axis_size(axis)
    return lax.ppermute(values, axis, [(index, index ^ mask) for index in range(count)])


def gather_pieces(value, group):
    found = {0: value}
    near = min(group, 4)
    far = near
    while far < group:
        for offset in sorted(found):
            found[offset ^ far] = exchange(found[offset], "dp", far)
        far *= 2
    for offset in range(1, near):
        found[offset] = exchange(value, "dp", offset)
    if near < group:
        found[near], found[1] = lax.optimization_barrier((found[near], found[1]))
    for base in range(near, group, near):
        for offset in range(near - 1, 0, -1):
            found[base ^ offset] = exchange(found[base], "dp", offset)
    return [found[offset] for offset in range(group)]


def corner(values):
    replicas, shards = lax.axis_size("dp"), lax.axis_size("shard")
    pairs = [
        (replica * shards + shard, (replica ^ 1) * shards + (shard ^ 2))
        for replica in range(replicas)
        for shard in range(shards)
    ]
    return lax.ppermute(values, ("dp", "shard"), pairs)


def quarter_call(kept, arrived, tail, group, name):
    _, rows, width = kept.shape
    shape = (group // 2, (rows - tail) // group + tail, width)
    return local_call(
        functools.partial(quarter_kernel, tail),
        [(shape, wide)] + [(shape, low)] * 3,
        [kept, arrived],
        [((2, group) + shape[1:], wide)],
        name=name,
    )


def spread(beside, across, far):
    return [exchange(beside, "shard", 2), exchange(across, "dp", 1), corner(far)]


def near_sum(flat):
    half = flat[0].shape[0]
    bit = 1
    while half > 1:
        half //= 2
        shape = (half,) + flat[0].shape[1:]
        keep, send = local_call(
            functools.partial(halve_kernel, bit),
            [(shape, wide), (shape, low)],
            flat,
            name="halve_dp",
        )
        flat = [keep, exchange(send, "dp", 1 << bit)]
        bit += 1
    return flat


def finish_sum(chunks, group):
    replicas = lax.axis_size("dp")
    flat = [item for chunk in chunks for item in near_sum(chunk)]
    width = flat[0].shape[-1]
    rows = sum(item.shape[1] for item in flat[::2])
    (piece,) = local_call(piece_kernel, [((rows, width), low)], flat, name="piece_sum")
    mask = group
    while mask < replicas:
        other = exchange(piece, "dp", mask)
        (piece,) = local_call(piece_kernel, [((rows, width), low)], [piece, other], name="far_sum")
        mask *= 2
    return gather_pieces(piece, group)


def adam_call(pieces, counts, tails, states, layout):
    group = len(pieces)
    width = pieces[0].shape[1]
    spans = []
    first = row = 0
    for total, tail in zip(counts, tails):
        for rows, start, moves in piece_spans(total, tail, group):
            spans.append((rows, first + start, row))
            row += rows
            first += rows * (group - 1) * (not moves)
        first += total
    outs = [(state[0].shape, wide) for state in states for _ in range(3)]
    return local_call(
        functools.partial(adam_kernel, group, spans, layout),
        outs,
        pieces + [item for state in states for item in state],
        outs + [((first, width), wide)],
        name="adam",
        sems=len(outs),
    )


def shards_program(
    tokens,
    cotangent,
    lengths,
    seq_owner,
    qkv_weight,
    out_weight,
    up_weight,
    down_weight,
    gains_biases,
    qkv_first,
    qkv_second,
    out_first,
    out_second,
    up_first,
    up_second,
    down_first,
    down_second,
    small_first,
    small_second,
):
    rows, width = tokens.shape
    shards = lax.axis_size("shard")
    heads = width // HEAD
    part = qkv_weight.shape[0]
    hidden_count = up_weight.shape[1]
    group = min(GROUP, lax.axis_size("dp"))
    lengths = lengths.reshape(1, -1)
    seq_owner = seq_owner.reshape(1, -1)
    first_rows = 3 * part + SMALL_PAD
    second_rows = part + up_weight.size // width + down_weight.shape[0]
    (first_pack,) = local_call(
        pack_first_kernel,
        [((first_rows, width), low)],
        [qkv_weight, gains_biases],
        [(qkv_weight.shape, wide), (gains_biases.shape, wide)],
        name="pack_first",
        fetch=True,
    )
    firsts = {0: first_pack}
    firsts[2] = exchange(first_pack, "shard", 2)
    firsts[1] = exchange(first_pack, "shard", 1)
    first_pack, matrices = lax.optimization_barrier(
        (first_pack, [out_weight, up_weight, down_weight])
    )
    (second_pack,) = local_call(
        pack_second_kernel,
        [((second_rows, width), low)],
        matrices,
        [(item.shape, wide) for item in matrices],
        name="pack_second",
        fetch=True,
    )
    early_tokens, second_pack = lax.optimization_barrier((tokens, second_pack))
    square = (rows, rows)
    bias, normed, root, seed = local_call(
        functools.partial(prepare_kernel, shards),
        [(square, wide), ((rows, width), wide), ((rows, 1), wide), ((rows, width), low)],
        [early_tokens, cotangent, lengths, seq_owner],
        name="prepare",
    )
    seconds = {0: second_pack}
    seconds[2] = exchange(second_pack, "shard", 2)
    seconds[1] = exchange(second_pack, "shard", 1)
    firsts[2], bias, normed, root, seed = lax.optimization_barrier(
        (firsts[2], bias, normed, root, seed)
    )
    firsts[3] = exchange(firsts[2], "shard", 1)
    firsts = [firsts[offset] for offset in range(shards)]
    joined, attended, log_sums, mixed = local_call(
        functools.partial(attend_kernel, shards),
        [
            ((rows, 3 * width), low),
            ((rows, width), low),
            ((heads, rows), wide),
            ((width, rows), wide),
        ],
        [normed, bias] + firsts,
        [((width, 3 * width), low), ((shards, SMALL_PAD, width), wide)],
        flops=heads * rows * rows * 640,
        name="attend",
    )
    attended, seconds[2] = lax.optimization_barrier((attended, seconds[2]))
    seconds[3] = exchange(seconds[2], "shard", 1)
    seconds = [seconds[offset] for offset in range(shards)]
    pair = (shards // 2, second_rows, width)
    output, middle_grad, attended_grad, sums, kept_ffn, send_ffn = local_call(
        functools.partial(feed_kernel, shards),
        [
            ((rows, width), low),
            ((rows, width), wide),
            ((rows, width), low),
            ((SMALL_PAD, width), wide),
            (pair, wide),
            (pair, low),
        ],
        [tokens, attended, seed] + firsts + seconds,
        [
            ((shards, SMALL_PAD, width), wide),
            ((width, width), low),
            ((width, hidden_count), low),
            ((hidden_count, width), low),
            ((shards, second_rows, width), wide),
        ],
        flops=rows * width * (hidden_count * 12 + width * 6),
        name="feed",
    )
    arrived_ffn = exchange(send_ffn, "shard", 1)
    shared = [joined, attended_grad, log_sums, bias, mixed]
    tile_scratch = [((LANES, rows), low), ((rows, LANES), wide), ((rows, LANES), wide)]
    per_tile = LANES // HEAD
    groups = [list(range(at, at + per_tile)) for at in range(0, heads, per_tile)]
    groups = [groups[0][:3], groups[0][3:]] + groups[1:]
    first_query, first_key, first_value = local_call(
        functools.partial(back_first_kernel, groups[0]),
        tile_scratch,
        shared,
        flops=heads * rows * rows * 256 * 5 // 2,
        name="back_first",
    )
    first_query, arrived_ffn = lax.optimization_barrier((first_query, arrived_ffn))
    tail = TILE_ROWS
    keep_ffn, *sends_ffn = quarter_call(kept_ffn, arrived_ffn, 0, group, "quarter_ffn")
    first_query, sends_ffn = lax.optimization_barrier((first_query, sends_ffn))
    arrived_ffn = spread(*sends_ffn)
    att_rows = 3 * part + tail
    pair = (shards // 2, att_rows, width)
    input_grad, kept_att, send_att = local_call(
        functools.partial(back_last_kernel, shards, groups[1:]),
        [((rows, width), wide), (pair, wide), (pair, low)],
        shared + [first_query, first_key, first_value, normed, root, middle_grad, sums] + firsts,
        [((width, 3 * width), low), ((shards, SMALL_PAD, width), wide)]
        + tile_scratch
        + [((rows, 3 * width), low), ((shards, att_rows, width), wide)],
        flops=heads * rows * rows * 256 * 6,
        name="back_last",
    )
    send_att, arrived_ffn[0], arrived_ffn[1] = lax.optimization_barrier(
        (send_att, arrived_ffn[0], arrived_ffn[1])
    )
    arrived_att = exchange(send_att, "shard", 1)
    keep_att, *sends_att = quarter_call(kept_att, arrived_att, tail, group, "quarter_att")
    arrived_att = spread(*sends_att)
    tails = (0, tail)
    pieces = finish_sum([[keep_ffn] + arrived_ffn, [keep_att] + arrived_att], group)
    blocks = hidden_count // width
    results = adam_call(
        pieces,
        (second_rows, att_rows),
        tails,
        [
            (qkv_weight, qkv_first, qkv_second),
            (out_weight, out_first, out_second),
            (up_weight, up_first, up_second),
            (down_weight, down_first, down_second),
            (gains_biases, small_first, small_second),
        ],
        [
            (second_rows, part, matrix_decay),
            (0, part, matrix_decay),
            (part, part, matrix_decay),
            (part + blocks * part, 0, matrix_decay),
            (second_rows + 3 * part, 1, 0.0),
        ],
    )
    return (output, input_grad, *results)


def solution(mesh):
    rows = P(("dp", "shard"), None)
    matrix = P("shard", None)
    vector = P("shard")
    return jax.shard_map(
        shards_program,
        mesh=mesh,
        in_specs=(rows, rows, P(), P())
        + (matrix,) * 4
        + (vector,)
        + (matrix,) * 8
        + (vector, vector),
        out_specs=(rows, rows) + (matrix,) * 12 + (vector,) * 3,
        check_vma=False,
    )
```

```python
import functools
import math

import jax
import jax.numpy as jnp
from jax import lax
from jax.experimental import pallas as pl
from jax.experimental.pallas import tpu as pltpu
from jax.sharding import PartitionSpec as P

HEAD = 32
STEP = 10
LANES = 128
GROUP = 8
SMALL_PAD = 16
TILE_ROWS = 8
CHUNK = 64

norm_eps = 1e-05
beta_one = 0.9
beta_two = 0.95
learn_rate = 0.1
adam_eps = 1e-08
matrix_decay = 0.1
masked_score = -1e30
low = jnp.bfloat16
wide = jnp.float32
log2_e = math.log2(math.e)
score_scale = 1.0 / math.sqrt(HEAD)
tanh_scale = math.sqrt(2.0 / math.pi)
cubic = 0.044715


def dot_nn(left, right):
    return jnp.dot(left, right, preferred_element_type=wide)


def dot_nt(left, right):
    return lax.dot_general(left, right, (((1,), (1,)), ((), ())), preferred_element_type=wide)


def standardize(values):
    centered = values - jnp.mean(values, axis=-1, keepdims=True)
    root_inv = lax.rsqrt(jnp.mean(centered * centered, axis=-1, keepdims=True) + norm_eps)
    return centered * root_inv, root_inv


def norm_back(upstream, normed, root_inv, gain):
    scaled = upstream * gain
    inner_mean = jnp.mean(scaled, axis=-1, keepdims=True)
    cross_mean = jnp.mean(scaled * normed, axis=-1, keepdims=True)
    through = root_inv * (scaled - inner_mean - normed * cross_mean)
    return (
        through,
        jnp.sum(upstream * normed, axis=0, keepdims=True),
        jnp.sum(upstream, axis=0, keepdims=True),
    )


def iota(shape, dim):
    return lax.broadcasted_iota(jnp.int32, shape, dim)


def own_row(lengths, owners, device):
    return jnp.where(owners == device, lengths, 0)


def ends_both(own):
    count = own.shape[1]
    shape = (count, count)
    rows, cols = iota(shape, 0), iota(shape, 1)
    spread = jnp.broadcast_to(own, shape)
    ends_col = jnp.sum(jnp.where(cols <= rows, spread, 0), axis=1, keepdims=True)
    own_col = jnp.sum(jnp.where(cols == rows, spread, 0), axis=1, keepdims=True)
    ends_row = jnp.sum(
        jnp.where(rows <= cols, jnp.broadcast_to(own_col, shape), 0), axis=0, keepdims=True
    )
    return ends_col, ends_row


def fill_mask(bias_ref, own, rows):
    ends_col, ends_row = ends_both(own)
    count = own.shape[1]
    seg_row = jnp.sum(
        (ends_col <= iota((count, rows), 1)).astype(jnp.int32), axis=0, keepdims=True
    )
    seg_col = jnp.sum(
        (ends_row <= iota((rows, count), 0)).astype(jnp.int32), axis=1, keepdims=True
    )
    allowed = (seg_row == seg_col) & (iota((rows, rows), 0) <= iota((rows, rows), 1))
    bias_ref[...] = jnp.where(allowed, 0.0, masked_score)


def fill_small(small_ref, shard, pieces, first_row):
    for offset, piece in enumerate(pieces):
        small_ref[shard ^ offset] = piece[first_row:, :].astype(wide)


def fill_cols(full_ref, shard, pieces, first_row, rows, width):
    blocks = full_ref.shape[1] // width
    for offset, piece in enumerate(pieces):
        at = pl.multiple_of((shard ^ offset) * rows, rows)
        for block in range(blocks):
            start = first_row + block * rows
            full_ref[pl.ds(at, rows), block * width : (block + 1) * width] = piece[
                start : start + rows, :
            ]


def head_mask(head):
    lane = iota((1, LANES), 1)
    first = head * HEAD % LANES
    return ((lane >= first) & (lane < first + HEAD)).astype(wide).astype(low)


def head_tile(head):
    first = head * HEAD // LANES * LANES
    return slice(first, first + LANES)


def query_blocks(rows):
    size = min(256, rows)
    return [(at, at + size) for at in range(0, rows, size)]


def put_blocks(target, row, source, width):
    rows = source.shape[0]
    for block in range(source.shape[1] // width):
        cols = slice(block * width, (block + 1) * width)
        target[row : row + rows, :] = source[:, cols].astype(low)
        row += rows
    return row


def fetch_all(sources, buffers, sems):
    copies = [
        pltpu.make_async_copy(source, buffer, sems.at[index])
        for index, (source, buffer) in enumerate(zip(sources, buffers))
    ]
    for copy in copies:
        copy.start()
    return copies


def pack_first_kernel(qkv_ref, small_ref, first_ref, qkv_buf, small_buf, sems):
    width = first_ref.shape[1]
    small_copy, qkv_copy = fetch_all((small_ref, qkv_ref), (small_buf, qkv_buf), sems)
    small_copy.wait()
    parts = [
        small_buf[block * width : (block + 1) * width].reshape(1, width)
        for block in range(small_buf.shape[0] // width)
    ]
    parts.append(jnp.zeros((SMALL_PAD - len(parts), width), wide))
    first_ref[first_ref.shape[0] - SMALL_PAD :, :] = jnp.concatenate(parts, axis=0).astype(low)
    qkv_copy.wait()
    put_blocks(first_ref, 0, qkv_buf, width)


def pack_second_kernel(out_ref, up_ref, down_ref, second_ref, out_buf, up_buf, down_buf, sems):
    width = second_ref.shape[1]
    buffers = (out_buf, up_buf, down_buf)
    copies = fetch_all((out_ref, up_ref, down_ref), buffers, sems)
    row = 0
    for copy, buffer in zip(copies, buffers):
        copy.wait()
        row = put_blocks(second_ref, row, buffer, width)


def prepare_kernel(shards, x_ref, seed_ref, len_ref, owner_ref, bias_ref, norm_ref, root_ref, low_ref):
    rows = x_ref.shape[0]
    device = lax.axis_index("dp") * shards + lax.axis_index("shard")
    own = own_row(len_ref[...], owner_ref[...], device)
    fill_mask(bias_ref, own, rows)
    normed, root = standardize(x_ref[...].astype(wide))
    norm_ref[...] = normed
    root_ref[...] = root
    live = jnp.sum(own, axis=1, keepdims=True)
    live_rows = (iota((rows, 1), 0) < live).astype(wide)
    low_ref[...] = (seed_ref[...].astype(wide) * live_rows).astype(low)


def attend_kernel(shards, *refs):
    norm_ref, bias_ref = refs[:2]
    pieces = refs[2 : 2 + shards]
    joined_ref, out_ref, log_ref, att_ref, weight_ref, small_ref = refs[2 + shards :]
    rows, width = norm_ref.shape
    shard = lax.axis_index("shard")
    part = width // shards
    fill_cols(weight_ref, shard, pieces, 0, part, width)
    fill_small(small_ref, shard, pieces, 3 * part)
    gain, shift = small_ref[0, 0:1, :], small_ref[0, 1:2, :]
    bias_query, bias_value = small_ref[1, 1:2, :], small_ref[1, 2:3, :]
    hidden = (norm_ref[...] * gain + shift).astype(low)
    for block, bias in enumerate((bias_query, None, bias_value)):
        cols = slice(block * width, (block + 1) * width)
        value = dot_nn(hidden, weight_ref[:, cols])
        if bias is not None:
            value = value + bias
        joined_ref[:, cols] = value.astype(low)
    values_t = joined_ref[:, 2 * width :].T
    units = [
        (head, start, stop) for head in range(width // HEAD) for start, stop in query_blocks(rows)
    ]

    def raw_scores(head, start, stop):
        tile = head_tile(head)
        key_tile = joined_ref[:stop, width + tile.start : width + tile.stop] * head_mask(head)
        return dot_nt(key_tile, joined_ref[start:stop, tile])

    ahead = raw_scores(*units[0])
    for index, (head, start, stop) in enumerate(units):
        raw = ahead
        if index + 1 < len(units):
            ahead = raw_scores(*units[index + 1])
        feature = slice(head * HEAD, (head + 1) * HEAD)
        scores = []
        top = None
        for at in range(0, stop, CHUNK):
            piece = raw[at : at + CHUNK] * (score_scale * log2_e)
            piece = piece + bias_ref[at : at + CHUNK, start:stop]
            scores.append(piece)
            top = piece if top is None else jnp.maximum(top, piece)
        top = jnp.max(top, axis=0, keepdims=True)
        exponents = []
        total = None
        for piece in scores:
            piece = jnp.exp2(piece - top)
            total = piece if total is None else total + piece
            exponents.append(piece.astype(low))
        total = jnp.sum(total, axis=0, keepdims=True)
        mixed = dot_nn(values_t[feature, :stop], jnp.concatenate(exponents, axis=0))
        att_ref[feature, start:stop] = mixed * (1.0 / total)
        log_ref[head : head + 1, start:stop] = top + jnp.log2(total)
    out_ref[...] = att_ref[...].astype(low).T


def feed_kernel(shards, *refs):
    x_ref, att_ref, seed_ref = refs[:3]
    firsts = refs[3 : 3 + shards]
    pieces = refs[3 + shards : 3 + 2 * shards]
    refs = refs[3 + 2 * shards :]
    out_ref, middle_ref, dattend_ref, sums_ref, keep_ref, send_ref = refs[:6]
    small_ref, out_w, up_w, down_w, grads_ref = refs[6:]
    rows, width = x_ref.shape
    hidden_count = up_w.shape[1]
    shard = lax.axis_index("shard")
    part = width // shards
    blocks = hidden_count // width
    down_part = hidden_count // shards
    fill_small(small_ref, shard, firsts, 3 * part)
    fill_cols(out_w, shard, pieces, 0, part, width)
    fill_cols(up_w, shard, pieces, part, part, width)
    fill_cols(down_w, shard, pieces, part + blocks * part, down_part, width)
    gain, shift = small_ref[0, 2:3, :], small_ref[1, 0:1, :]
    bias_out, bias_down = small_ref[2, 0:1, :], small_ref[2, 1:2, :]
    bias_up = [small_ref[2, 2:3, :]] + [small_ref[3, row : row + 1, :] for row in range(3)]
    seed_low = seed_ref[...]
    seed = seed_low.astype(wide)
    attended = att_ref[...]
    middle = x_ref[...].astype(wide) + (dot_nn(attended, out_w[...]) + bias_out)
    normed, root = standardize(middle)
    hidden = (normed * gain + shift).astype(low)
    hidden_t = hidden.T
    result = middle + bias_down
    dhidden = jnp.zeros((rows, width), wide)
    sums_ref[...] = jnp.zeros(sums_ref.shape, wide)

    def raw_products(block):
        cols = slice(block * width, (block + 1) * width)
        return dot_nn(hidden, up_w[:, cols]), dot_nt(seed_low, down_w[cols, :])

    ahead = raw_products(0)
    for block in range(blocks):
        cols = slice(block * width, (block + 1) * width)
        raw, dact = ahead
        if block + 1 < blocks:
            ahead = raw_products(block + 1)
        act, dpre = [], []
        for at in range(0, rows, CHUNK):
            pre = raw[at : at + CHUNK] + bias_up[block]
            square = pre * pre
            bend = jnp.tanh(pre * (tanh_scale + (tanh_scale * cubic) * square))
            half = 0.5 + 0.5 * bend
            act.append((pre * half).astype(low))
            slope = 0.5 * tanh_scale + (1.5 * tanh_scale * cubic) * square
            slope = half + (pre * slope) * (1.0 - bend * bend)
            dpre.append((dact[at : at + CHUNK] * slope).astype(low))
        act = jnp.concatenate(act, axis=0)
        dpre = jnp.concatenate(dpre, axis=0)
        result = result + dot_nn(act, down_w[cols, :])
        dhidden = dhidden + dot_nt(dpre, up_w[:, cols])
        grad_down = dot_nn(act.T, seed_low)
        grad_up = dot_nn(hidden_t, dpre)
        for piece in range(width // down_part):
            target = block * (width // down_part) + piece
            at = part + blocks * part
            grads_ref[target, at : at + down_part, :] = grad_down[
                piece * down_part : (piece + 1) * down_part, :
            ]
        for target in range(shards):
            at = part + block * part
            grads_ref[target, at : at + part, :] = grad_up[target * part : (target + 1) * part, :]
        sums_ref[4 + block : 5 + block, :] = jnp.sum(dpre.astype(wide), axis=0, keepdims=True)
    out_ref[...] = result
    through, gain_grad, shift_grad = norm_back(dhidden, normed, root, gain)
    dmiddle = seed + through
    middle_ref[...] = dmiddle
    dmiddle_low = dmiddle.astype(low)
    grad_out = dot_nn(attended.T, dmiddle_low)
    for target in range(shards):
        grads_ref[target, :part, :] = grad_out[target * part : (target + 1) * part, :]
    dattend_ref[...] = dot_nt(dmiddle_low, out_w[...]).astype(low)
    sums_ref[0:1, :] = gain_grad
    sums_ref[1:2, :] = shift_grad
    sums_ref[2:3, :] = jnp.sum(dmiddle_low.astype(wide), axis=0, keepdims=True)
    sums_ref[3:4, :] = jnp.sum(seed, axis=0, keepdims=True)
    part_ways(grads_ref, keep_ref, send_ref, shard & 1)


def part_ways(grads_ref, keep_ref, send_ref, side):
    for pair in range(keep_ref.shape[0]):
        keep_ref[pair] = grads_ref[2 * pair + side]
        send_ref[pair] = grads_ref[2 * pair + 1 - side].astype(low)


def back_heads(
    heads, joined_ref, dattend_ref, log_ref, bias_ref, mixed_ref, dquery_t, dkey, dvalue
):
    rows = joined_ref.shape[0]
    width = joined_ref.shape[1] // 3
    first = heads[0] * HEAD
    count = len(heads) * HEAD
    base = first // LANES * LANES
    tile = slice(base, base + LANES)
    inside = slice(first - base, first - base + count)
    keys_t = joined_ref[:, width + base : width + base + LANES].T
    datt_t = dattend_ref[:, tile].T[inside]
    inner = datt_t.astype(wide) * mixed_ref[first : first + count, :]
    units = [(head, start, stop) for head in heads for start, stop in query_blocks(rows)]

    def raw_products(head, start, stop):
        mask = head_mask(head)
        key_tile = joined_ref[:stop, width + base : width + base + LANES] * mask
        value_tile = joined_ref[:stop, 2 * width + base : 2 * width + base + LANES] * mask
        query = joined_ref[start:stop, tile]
        datt = dattend_ref[start:stop, tile]
        return dot_nt(key_tile, query), dot_nt(value_tile, datt), query * mask, datt * mask

    ahead = raw_products(*units[0])
    for index, (head, start, stop) in enumerate(units):
        raw, dprobs, query, datt = ahead
        if index + 1 < len(units):
            ahead = raw_products(*units[index + 1])
        local = head * HEAD - first
        feature = slice(local, local + HEAD)
        weighted = jnp.sum(inner[feature, start:stop], axis=0, keepdims=True)
        logs = log_ref[head : head + 1, start:stop]
        probs, dscores = [], []
        for at in range(0, stop, CHUNK):
            piece = raw[at : at + CHUNK] * (score_scale * log2_e)
            piece = jnp.exp2(piece + bias_ref[at : at + CHUNK, start:stop] - logs)
            probs.append(piece.astype(low))
            piece = piece * (dprobs[at : at + CHUNK] - weighted)
            dscores.append(piece.astype(low))
        probs = jnp.concatenate(probs, axis=0)
        dscores = jnp.concatenate(dscores, axis=0)
        depth = slice(head * HEAD - base, head * HEAD - base + HEAD)
        dquery_t[depth, start:stop] = (
            dot_nn(keys_t[depth, :stop], dscores) * score_scale
        ).astype(low)
        dvalue[:stop, :] += dot_nn(probs, datt)
        dkey[:stop, :] += dot_nn(dscores, query)


def back_first_kernel(heads, *refs):
    dquery_t, dkey, dvalue = refs[5:8]
    dkey[...] = jnp.zeros(dkey.shape, wide)
    dvalue[...] = jnp.zeros(dvalue.shape, wide)
    dquery_t[...] = jnp.zeros(dquery_t.shape, low)
    back_heads(heads, *refs)


def back_last_kernel(shards, head_groups, *refs):
    shared = refs[:5]
    earlier = refs[5:8]
    norm_ref, root_ref, middle_ref, sums_in = refs[8:12]
    pieces = refs[12 : 12 + shards]
    refs = refs[12 + shards :]
    dx_ref, keep_ref, send_ref = refs[:3]
    weight_ref, small_ref, dquery_t, dkey, dvalue, djoined, grads_ref = refs[3:]
    rows, width = norm_ref.shape
    shard = lax.axis_index("shard")
    part = width // shards
    fill_cols(weight_ref, shard, pieces, 0, part, width)
    fill_small(small_ref, shard, pieces, 3 * part)
    gain, shift = small_ref[0, 0:1, :], small_ref[0, 1:2, :]
    for target, value in zip((dquery_t, dkey, dvalue), earlier):
        target[...] = value[...]
    for heads in head_groups:
        back_heads(heads, *shared, dquery_t, dkey, dvalue)
        if (heads[-1] + 1) * HEAD % LANES == 0:
            first = (heads[-1] + 1) * HEAD - LANES
            values = (dquery_t[...].T, dkey[...] * score_scale, dvalue[...])
            for block, value in enumerate(values):
                at = block * width + first
                djoined[:, at : at + LANES] = value.astype(low)
            dkey[...] = jnp.zeros(dkey.shape, wide)
            dvalue[...] = jnp.zeros(dvalue.shape, wide)
    normed, root = norm_ref[...], root_ref[...]
    hidden_t = (normed * gain + shift).astype(low).T
    dhidden = jnp.zeros((rows, width), wide)
    bias_sums = []
    for block in range(3):
        cols = slice(block * width, (block + 1) * width)
        piece = djoined[:, cols]
        dhidden = dhidden + dot_nt(piece, weight_ref[:, cols])
        grad = dot_nn(hidden_t, piece)
        for target in range(shards):
            grads_ref[target, block * part : (block + 1) * part, :] = grad[
                target * part : (target + 1) * part, :
            ]
        if block != 1:
            bias_sums.append(jnp.sum(piece.astype(wide), axis=0, keepdims=True))
    through, gain_grad, shift_grad = norm_back(dhidden, normed, root, gain)
    dx_ref[...] = through
    sums = [gain_grad, shift_grad, sums_in[0:1, :], sums_in[1:2, :]] + bias_sums
    sums += [sums_in[row : row + 1, :] for row in range(2, 8)]
    per_shard = len(sums) // shards
    empty = [jnp.zeros((grads_ref.shape[1] - 3 * part - per_shard, width), wide)]
    for target in range(shards):
        rows_here = sums[target * per_shard : (target + 1) * per_shard]
        grads_ref[target, 3 * part :, :] = jnp.concatenate(rows_here + empty, axis=0)
    part_ways(grads_ref, keep_ref, send_ref, shard & 1)


def halve_kernel(bit, kept, *refs):
    arrived, (keep_ref, send_ref) = refs[:-2], refs[-2:]
    side = (lax.axis_index("dp") >> bit) & 1

    def total(index):
        value = kept[index]
        for piece in arrived:
            value = value + piece[index].astype(wide)
        return value

    for pair in range(keep_ref.shape[0]):
        keep_ref[pair] = total(2 * pair + side)
        send_ref[pair] = total(2 * pair + 1 - side).astype(low)


def piece_spans(total, tail, group):
    spans = [((total - tail) // group, 0, True)]
    if tail:
        spans.append((tail, total - tail, False))
    return spans


def quarter_kernel(tail, kept, arrived, keep_ref, beside_ref, across_ref, corner_ref, sum_ref):
    group = sum_ref.shape[1]
    for half in range(2):
        total = kept[half] + arrived[half].astype(wide)
        for index in range(group):
            row = 0
            for rows, first, moves in piece_spans(total.shape[0], tail, group):
                at = first + index * rows if moves else first
                sum_ref[half, index, row : row + rows, :] = total[at : at + rows, :]
                row += rows
    mine = (lax.axis_index("shard") >> 1) & 1
    side = lax.axis_index("dp") & 1
    for pair in range(group // 2):
        keep_ref[pair] = sum_ref[mine, 2 * pair + side]
        beside_ref[pair] = sum_ref[1 - mine, 2 * pair + side].astype(low)
        across_ref[pair] = sum_ref[mine, 2 * pair + 1 - side].astype(low)
        corner_ref[pair] = sum_ref[1 - mine, 2 * pair + 1 - side].astype(low)


def piece_kernel(*refs):
    parts = [
        mine[...].reshape(mine.shape[-2:]).astype(wide)
        + other[...].reshape(other.shape[-2:]).astype(wide)
        for mine, other in zip(refs[:-1:2], refs[1:-1:2])
    ]
    refs[-1][...] = jnp.concatenate(parts, axis=0).astype(low)


def adam_values(weight, grad, first, second, decay_rate):
    first_next = beta_one * first + (1.0 - beta_one) * grad
    second_next = beta_two * second + (1.0 - beta_two) * grad * grad
    first_fix = 1.0 - beta_one**STEP
    second_fix = 1.0 - beta_two**STEP
    update = (first_next * (1.0 / first_fix)) / (
        jnp.sqrt(second_next * (1.0 / second_fix)) + adam_eps
    )
    return first_next, second_next, weight - learn_rate * (update + decay_rate * weight)


def adam_kernel(group, spans, layout, *refs):
    pieces = refs[:group]
    count = len(layout)
    states = refs[group : group + 3 * count]
    results = refs[group + 3 * count : group + 6 * count]
    buffers = refs[group + 6 * count : group + 9 * count]
    grad_ref, sems = refs[-2:]
    copies = []
    for offset, piece in enumerate(pieces):
        value = piece[...].astype(wide)
        index = (lax.axis_index("dp") & (group - 1)) ^ offset
        for rows, first, row in spans:
            at = pl.multiple_of(first + index * rows, TILE_ROWS)
            grad_ref[pl.ds(at, rows), :] = value[row : row + rows, :]
    width = grad_ref.shape[1]
    for array, (first_row, stride, decay) in enumerate(layout):
        weight, first, second = states[3 * array : 3 * array + 3]
        new = buffers[3 * array : 3 * array + 3]
        vector = len(weight.shape) == 1
        rows = 1 if vector else weight.shape[0]
        for block in range(weight.shape[-1] // width):
            cols = slice(block * width, (block + 1) * width)
            where = cols if vector else (slice(None), cols)
            at = first_row + block * stride
            values = adam_values(
                weight[where].reshape(rows, width),
                grad_ref[at : at + rows, :],
                first[where].reshape(rows, width),
                second[where].reshape(rows, width),
                decay,
            )
            for target, value in zip(new, values):
                target[where] = value.reshape(width) if vector else value
        for index in range(3 * array, 3 * array + 3):
            copies.append(
                pltpu.make_async_copy(buffers[index], results[index], sems.at[index])
            )
            copies[-1].start()
    for copy in copies:
        copy.wait()


def local_call(kernel, outs, operands, scratch=(), flops=0, name=None, fetch=False, sems=0):
    in_space = pltpu.HBM if fetch else pltpu.VMEM
    out_space = pltpu.HBM if sems else pltpu.VMEM
    outs = [jax.ShapeDtypeStruct(*out) for out in outs]
    moved = sum(
        math.prod(item.shape) * item.dtype.itemsize for item in list(operands) + outs
    )
    scratch_shapes = [pltpu.VMEM(*item) for item in scratch]
    if fetch or sems:
        scratch_shapes.append(pltpu.SemaphoreType.DMA((sems or len(operands),)))
    limit = 56 if fetch else 40
    return pl.pallas_call(
        kernel,
        out_shape=outs,
        in_specs=[pl.BlockSpec(memory_space=in_space)] * len(operands),
        out_specs=[pl.BlockSpec(memory_space=out_space)] * len(outs),
        scratch_shapes=scratch_shapes,
        compiler_params=pltpu.CompilerParams(vmem_limit_bytes=limit * 1024 * 1024),
        cost_estimate=pl.CostEstimate(flops=flops, bytes_accessed=moved, transcendentals=0),
        name=name,
    )(*operands)


def exchange(values, axis, mask):
    count = lax.axis_size(axis)
    return lax.ppermute(values, axis, [(index, index ^ mask) for index in range(count)])


def gather_pieces(value, group):
    found = {0: value}
    near = min(group, 4)
    far = near
    while far < group:
        for offset in sorted(found):
            found[offset ^ far] = exchange(found[offset], "dp", far)
        far *= 2
    for offset in range(1, near):
        found[offset] = exchange(value, "dp", offset)
    if near < group:
        found[near], found[1] = lax.optimization_barrier((found[near], found[1]))
    for base in range(near, group, near):
        for offset in range(near - 1, 0, -1):
            found[base ^ offset] = exchange(found[base], "dp", offset)
    return [found[offset] for offset in range(group)]


def corner(values):
    replicas, shards = lax.axis_size("dp"), lax.axis_size("shard")
    pairs = [
        (replica * shards + shard, (replica ^ 1) * shards + (shard ^ 2))
        for replica in range(replicas)
        for shard in range(shards)
    ]
    return lax.ppermute(values, ("dp", "shard"), pairs)


def quarter_call(kept, arrived, tail, group, name):
    _, rows, width = kept.shape
    shape = (group // 2, (rows - tail) // group + tail, width)
    return local_call(
        functools.partial(quarter_kernel, tail),
        [(shape, wide)] + [(shape, low)] * 3,
        [kept, arrived],
        [((2, group) + shape[1:], wide)],
        name=name,
    )


def spread(beside, across, far):
    return [exchange(beside, "shard", 2), exchange(across, "dp", 1), corner(far)]


def near_sum(flat):
    half = flat[0].shape[0]
    bit = 1
    while half > 1:
        half //= 2
        shape = (half,) + flat[0].shape[1:]
        keep, send = local_call(
            functools.partial(halve_kernel, bit),
            [(shape, wide), (shape, low)],
            flat,
            name="halve_dp",
        )
        flat = [keep, exchange(send, "dp", 1 << bit)]
        bit += 1
    return flat


def finish_sum(chunks, group):
    replicas = lax.axis_size("dp")
    flat = [item for chunk in chunks for item in near_sum(chunk)]
    width = flat[0].shape[-1]
    rows = sum(item.shape[1] for item in flat[::2])
    (piece,) = local_call(piece_kernel, [((rows, width), low)], flat, name="piece_sum")
    mask = group
    while mask < replicas:
        other = exchange(piece, "dp", mask)
        (piece,) = local_call(piece_kernel, [((rows, width), low)], [piece, other], name="far_sum")
        mask *= 2
    return gather_pieces(piece, group)


def adam_call(pieces, counts, tails, states, layout):
    group = len(pieces)
    width = pieces[0].shape[1]
    spans = []
    first = row = 0
    for total, tail in zip(counts, tails):
        for rows, start, moves in piece_spans(total, tail, group):
            spans.append((rows, first + start, row))
            row += rows
            first += rows * (group - 1) * (not moves)
        first += total
    outs = [(state[0].shape, wide) for state in states for _ in range(3)]
    return local_call(
        functools.partial(adam_kernel, group, spans, layout),
        outs,
        pieces + [item for state in states for item in state],
        outs + [((first, width), wide)],
        name="adam",
        sems=len(outs),
    )


def shards_program(
    tokens,
    cotangent,
    lengths,
    seq_owner,
    qkv_weight,
    out_weight,
    up_weight,
    down_weight,
    gains_biases,
    qkv_first,
    qkv_second,
    out_first,
    out_second,
    up_first,
    up_second,
    down_first,
    down_second,
    small_first,
    small_second,
):
    rows, width = tokens.shape
    shards = lax.axis_size("shard")
    heads = width // HEAD
    part = qkv_weight.shape[0]
    hidden_count = up_weight.shape[1]
    group = min(GROUP, lax.axis_size("dp"))
    lengths = lengths.reshape(1, -1)
    seq_owner = seq_owner.reshape(1, -1)
    first_rows = 3 * part + SMALL_PAD
    second_rows = part + up_weight.size // width + down_weight.shape[0]
    (first_pack,) = local_call(
        pack_first_kernel,
        [((first_rows, width), low)],
        [qkv_weight, gains_biases],
        [(qkv_weight.shape, wide), (gains_biases.shape, wide)],
        name="pack_first",
        fetch=True,
    )
    firsts = {0: first_pack}
    firsts[2] = exchange(first_pack, "shard", 2)
    firsts[1] = exchange(first_pack, "shard", 1)
    first_pack, matrices = lax.optimization_barrier(
        (first_pack, [out_weight, up_weight, down_weight])
    )
    (second_pack,) = local_call(
        pack_second_kernel,
        [((second_rows, width), low)],
        matrices,
        [(item.shape, wide) for item in matrices],
        name="pack_second",
        fetch=True,
    )
    early_tokens, second_pack = lax.optimization_barrier((tokens, second_pack))
    square = (rows, rows)
    bias, normed, root, seed = local_call(
        functools.partial(prepare_kernel, shards),
        [(square, wide), ((rows, width), wide), ((rows, 1), wide), ((rows, width), low)],
        [early_tokens, cotangent, lengths, seq_owner],
        name="prepare",
    )
    seconds = {0: second_pack}
    seconds[2] = exchange(second_pack, "shard", 2)
    seconds[1] = exchange(second_pack, "shard", 1)
    firsts[2], bias, normed, root, seed = lax.optimization_barrier(
        (firsts[2], bias, normed, root, seed)
    )
    firsts[3] = exchange(firsts[2], "shard", 1)
    firsts = [firsts[offset] for offset in range(shards)]
    joined, attended, log_sums, mixed = local_call(
        functools.partial(attend_kernel, shards),
        [
            ((rows, 3 * width), low),
            ((rows, width), low),
            ((heads, rows), wide),
            ((width, rows), wide),
        ],
        [normed, bias] + firsts,
        [((width, 3 * width), low), ((shards, SMALL_PAD, width), wide)],
        flops=heads * rows * rows * 640,
        name="attend",
    )
    attended, seconds[2] = lax.optimization_barrier((attended, seconds[2]))
    seconds[3] = exchange(seconds[2], "shard", 1)
    seconds = [seconds[offset] for offset in range(shards)]
    pair = (shards // 2, second_rows, width)
    result, middle_grad, attended_grad, sums, kept_ffn, send_ffn = local_call(
        functools.partial(feed_kernel, shards),
        [
            ((rows, width), wide),
            ((rows, width), wide),
            ((rows, width), low),
            ((SMALL_PAD, width), wide),
            (pair, wide),
            (pair, low),
        ],
        [tokens, attended, seed] + firsts + seconds,
        [
            ((shards, SMALL_PAD, width), wide),
            ((width, width), low),
            ((width, hidden_count), low),
            ((hidden_count, width), low),
            ((shards, second_rows, width), wide),
        ],
        flops=rows * width * (hidden_count * 12 + width * 6),
        name="feed",
    )
    arrived_ffn = exchange(send_ffn, "shard", 1)
    shared = [joined, attended_grad, log_sums, bias, mixed]
    tile_scratch = [((LANES, rows), low), ((rows, LANES), wide), ((rows, LANES), wide)]
    per_tile = LANES // HEAD
    groups = [list(range(at, at + per_tile)) for at in range(0, heads, per_tile)]
    groups = [groups[0][:3], groups[0][3:]] + groups[1:]
    first_query, first_key, first_value = local_call(
        functools.partial(back_first_kernel, groups[0]),
        tile_scratch,
        shared,
        flops=heads * rows * rows * 256 * 5 // 2,
        name="back_first",
    )
    first_query, arrived_ffn = lax.optimization_barrier((first_query, arrived_ffn))
    tail = TILE_ROWS
    keep_ffn, *sends_ffn = quarter_call(kept_ffn, arrived_ffn, 0, group, "quarter_ffn")
    first_query, sends_ffn = lax.optimization_barrier((first_query, sends_ffn))
    arrived_ffn = spread(*sends_ffn)
    att_rows = 3 * part + tail
    pair = (shards // 2, att_rows, width)
    through, kept_att, send_att = local_call(
        functools.partial(back_last_kernel, shards, groups[1:]),
        [((rows, width), wide), (pair, wide), (pair, low)],
        shared + [first_query, first_key, first_value, normed, root, middle_grad, sums] + firsts,
        [((width, 3 * width), low), ((shards, SMALL_PAD, width), wide)]
        + tile_scratch
        + [((rows, 3 * width), low), ((shards, att_rows, width), wide)],
        flops=heads * rows * rows * 256 * 6,
        name="back_last",
    )
    send_att, arrived_ffn[0], arrived_ffn[1] = lax.optimization_barrier(
        (send_att, arrived_ffn[0], arrived_ffn[1])
    )
    arrived_att = exchange(send_att, "shard", 1)
    keep_att, *sends_att = quarter_call(kept_att, arrived_att, tail, group, "quarter_att")
    arrived_att = spread(*sends_att)
    tails = (0, tail)
    pieces = finish_sum([[keep_ffn] + arrived_ffn, [keep_att] + arrived_att], group)
    blocks = hidden_count // width
    results = adam_call(
        pieces,
        (second_rows, att_rows),
        tails,
        [
            (qkv_weight, qkv_first, qkv_second),
            (out_weight, out_first, out_second),
            (up_weight, up_first, up_second),
            (down_weight, down_first, down_second),
            (gains_biases, small_first, small_second),
        ],
        [
            (second_rows, part, matrix_decay),
            (0, part, matrix_decay),
            (part, part, matrix_decay),
            (part + blocks * part, 0, matrix_decay),
            (second_rows + 3 * part, 1, 0.0),
        ],
    )
    return (result.astype(low), middle_grad + through, *results)


def solution(mesh):
    rows = P(("dp", "shard"), None)
    matrix = P("shard", None)
    vector = P("shard")
    return jax.shard_map(
        shards_program,
        mesh=mesh,
        in_specs=(rows, rows, P(), P())
        + (matrix,) * 4
        + (vector,)
        + (matrix,) * 8
        + (vector, vector),
        out_specs=(rows, rows) + (matrix,) * 12 + (vector,) * 3,
        check_vma=False,
    )
```

```python
import functools
import math

import jax
import jax.numpy as jnp
from jax import lax
from jax.experimental import pallas as pl
from jax.experimental.pallas import tpu as pltpu
from jax.sharding import PartitionSpec as P

HEAD = 32
STEP = 10
LANES = 128
GROUP = 8
SMALL_PAD = 16
TILE_ROWS = 8
CHUNK = 64

norm_eps = 1e-05
beta_one = 0.9
beta_two = 0.95
learn_rate = 0.1
adam_eps = 1e-08
matrix_decay = 0.1
masked_score = -1e30
low = jnp.bfloat16
wide = jnp.float32
log2_e = math.log2(math.e)
score_scale = 1.0 / math.sqrt(HEAD)
tanh_scale = math.sqrt(2.0 / math.pi)
cubic = 0.044715


def dot_nn(left, right):
    return jnp.dot(left, right, preferred_element_type=wide)


def dot_nt(left, right):
    return lax.dot_general(left, right, (((1,), (1,)), ((), ())), preferred_element_type=wide)


def standardize(values):
    centered = values - jnp.mean(values, axis=-1, keepdims=True)
    root_inv = lax.rsqrt(jnp.mean(centered * centered, axis=-1, keepdims=True) + norm_eps)
    return centered * root_inv, root_inv


def norm_back(upstream, normed, root_inv, gain):
    scaled = upstream * gain
    inner_mean = jnp.mean(scaled, axis=-1, keepdims=True)
    cross_mean = jnp.mean(scaled * normed, axis=-1, keepdims=True)
    through = root_inv * (scaled - inner_mean - normed * cross_mean)
    return (
        through,
        jnp.sum(upstream * normed, axis=0, keepdims=True),
        jnp.sum(upstream, axis=0, keepdims=True),
    )


def iota(shape, dim):
    return lax.broadcasted_iota(jnp.int32, shape, dim)


def own_row(lengths, owners, device):
    return jnp.where(owners == device, lengths, 0)


def ends_both(own):
    count = own.shape[1]
    shape = (count, count)
    rows, cols = iota(shape, 0), iota(shape, 1)
    spread = jnp.broadcast_to(own, shape)
    ends_col = jnp.sum(jnp.where(cols <= rows, spread, 0), axis=1, keepdims=True)
    own_col = jnp.sum(jnp.where(cols == rows, spread, 0), axis=1, keepdims=True)
    ends_row = jnp.sum(
        jnp.where(rows <= cols, jnp.broadcast_to(own_col, shape), 0), axis=0, keepdims=True
    )
    return ends_col, ends_row


def fill_mask(bias_ref, own, rows):
    ends_col, ends_row = ends_both(own)
    count = own.shape[1]
    seg_row = jnp.sum(
        (ends_col <= iota((count, rows), 1)).astype(jnp.int32), axis=0, keepdims=True
    )
    seg_col = jnp.sum(
        (ends_row <= iota((rows, count), 0)).astype(jnp.int32), axis=1, keepdims=True
    )
    allowed = (seg_row == seg_col) & (iota((rows, rows), 0) <= iota((rows, rows), 1))
    bias_ref[...] = jnp.where(allowed, 0.0, masked_score)


def fill_small(small_ref, shard, pieces, first_row):
    for offset, piece in enumerate(pieces):
        small_ref[shard ^ offset] = piece[first_row:, :].astype(wide)


def fill_cols(full_ref, shard, pieces, first_row, rows, width):
    blocks = full_ref.shape[1] // width
    for offset, piece in enumerate(pieces):
        at = pl.multiple_of((shard ^ offset) * rows, rows)
        for block in range(blocks):
            start = first_row + block * rows
            full_ref[pl.ds(at, rows), block * width : (block + 1) * width] = piece[
                start : start + rows, :
            ]


def head_mask(head):
    lane = iota((1, LANES), 1)
    first = head * HEAD % LANES
    return ((lane >= first) & (lane < first + HEAD)).astype(wide).astype(low)


def head_tile(head):
    first = head * HEAD // LANES * LANES
    return slice(first, first + LANES)


def query_blocks(rows):
    size = min(256, rows)
    return [(at, at + size) for at in range(0, rows, size)]


def put_blocks(target, row, source, width):
    rows = source.shape[0]
    for block in range(source.shape[1] // width):
        cols = slice(block * width, (block + 1) * width)
        target[row : row + rows, :] = source[:, cols].astype(low)
        row += rows
    return row


def fetch_all(sources, buffers, sems):
    copies = [
        pltpu.make_async_copy(source, buffer, sems.at[index])
        for index, (source, buffer) in enumerate(zip(sources, buffers))
    ]
    for copy in copies:
        copy.start()
    return copies


def pack_first_kernel(qkv_ref, small_ref, first_ref, qkv_buf, small_buf, sems):
    width = first_ref.shape[1]
    small_copy, qkv_copy = fetch_all((small_ref, qkv_ref), (small_buf, qkv_buf), sems)
    small_copy.wait()
    parts = [
        small_buf[block * width : (block + 1) * width].reshape(1, width)
        for block in range(small_buf.shape[0] // width)
    ]
    parts.append(jnp.zeros((SMALL_PAD - len(parts), width), wide))
    first_ref[first_ref.shape[0] - SMALL_PAD :, :] = jnp.concatenate(parts, axis=0).astype(low)
    qkv_copy.wait()
    put_blocks(first_ref, 0, qkv_buf, width)


def pack_second_kernel(out_ref, up_ref, down_ref, second_ref, out_buf, up_buf, down_buf, sems):
    width = second_ref.shape[1]
    buffers = (out_buf, up_buf, down_buf)
    copies = fetch_all((out_ref, up_ref, down_ref), buffers, sems)
    row = 0
    for copy, buffer in zip(copies, buffers):
        copy.wait()
        row = put_blocks(second_ref, row, buffer, width)


def prepare_kernel(shards, x_ref, seed_ref, len_ref, owner_ref, bias_ref, norm_ref, root_ref, low_ref):
    rows = x_ref.shape[0]
    device = lax.axis_index("dp") * shards + lax.axis_index("shard")
    own = own_row(len_ref[...], owner_ref[...], device)
    fill_mask(bias_ref, own, rows)
    normed, root = standardize(x_ref[...].astype(wide))
    norm_ref[...] = normed
    root_ref[...] = root
    live = jnp.sum(own, axis=1, keepdims=True)
    live_rows = (iota((rows, 1), 0) < live).astype(wide)
    low_ref[...] = (seed_ref[...].astype(wide) * live_rows).astype(low)


def attend_kernel(shards, *refs):
    norm_ref, bias_ref = refs[:2]
    pieces = refs[2 : 2 + shards]
    joined_ref, out_ref, log_ref, att_ref, weight_ref, small_ref = refs[2 + shards :]
    rows, width = norm_ref.shape
    shard = lax.axis_index("shard")
    part = width // shards
    fill_cols(weight_ref, shard, pieces, 0, part, width)
    fill_small(small_ref, shard, pieces, 3 * part)
    gain, shift = small_ref[0, 0:1, :], small_ref[0, 1:2, :]
    bias_query, bias_value = small_ref[1, 1:2, :], small_ref[1, 2:3, :]
    hidden = (norm_ref[...] * gain + shift).astype(low)
    for block, bias in enumerate((bias_query, None, bias_value)):
        cols = slice(block * width, (block + 1) * width)
        value = dot_nn(hidden, weight_ref[:, cols])
        if bias is not None:
            value = value + bias
        joined_ref[:, cols] = value.astype(low)
    values_t = joined_ref[:, 2 * width :].T
    units = [
        (head, start, stop) for head in range(width // HEAD) for start, stop in query_blocks(rows)
    ]

    def raw_scores(head, start, stop):
        tile = head_tile(head)
        key_tile = joined_ref[:stop, width + tile.start : width + tile.stop] * head_mask(head)
        return dot_nt(key_tile, joined_ref[start:stop, tile])

    ahead = raw_scores(*units[0])
    for index, (head, start, stop) in enumerate(units):
        raw = ahead
        if index + 1 < len(units):
            ahead = raw_scores(*units[index + 1])
        feature = slice(head * HEAD, (head + 1) * HEAD)
        scores = []
        top = None
        for at in range(0, stop, CHUNK):
            piece = raw[at : at + CHUNK] * (score_scale * log2_e)
            piece = piece + bias_ref[at : at + CHUNK, start:stop]
            scores.append(piece)
            top = piece if top is None else jnp.maximum(top, piece)
        top = jnp.max(top, axis=0, keepdims=True)
        exponents = []
        total = None
        for piece in scores:
            piece = jnp.exp2(piece - top)
            total = piece if total is None else total + piece
            exponents.append(piece.astype(low))
        total = jnp.sum(total, axis=0, keepdims=True)
        mixed = dot_nn(values_t[feature, :stop], jnp.concatenate(exponents, axis=0))
        att_ref[feature, start:stop] = mixed * (1.0 / total)
        log_ref[head : head + 1, start:stop] = top + jnp.log2(total)
    out_ref[...] = att_ref[...].astype(low).T


def feed_kernel(shards, *refs):
    x_ref, att_ref, seed_ref = refs[:3]
    firsts = refs[3 : 3 + shards]
    pieces = refs[3 + shards : 3 + 2 * shards]
    refs = refs[3 + 2 * shards :]
    out_ref, middle_ref, dattend_ref, sums_ref, keep_ref, send_ref = refs[:6]
    small_ref, out_w, up_w, down_w, grads_ref = refs[6:]
    rows, width = x_ref.shape
    hidden_count = up_w.shape[1]
    shard = lax.axis_index("shard")
    part = width // shards
    blocks = hidden_count // width
    down_part = hidden_count // shards
    fill_small(small_ref, shard, firsts, 3 * part)
    fill_cols(out_w, shard, pieces, 0, part, width)
    fill_cols(up_w, shard, pieces, part, part, width)
    fill_cols(down_w, shard, pieces, part + blocks * part, down_part, width)
    gain, shift = small_ref[0, 2:3, :], small_ref[1, 0:1, :]
    bias_out, bias_down = small_ref[2, 0:1, :], small_ref[2, 1:2, :]
    bias_up = [small_ref[2, 2:3, :]] + [small_ref[3, row : row + 1, :] for row in range(3)]
    seed_low = seed_ref[...]
    seed = seed_low.astype(wide)
    attended = att_ref[...]
    middle = x_ref[...].astype(wide) + (dot_nn(attended, out_w[...]) + bias_out)
    normed, root = standardize(middle)
    hidden = (normed * gain + shift).astype(low)
    hidden_t = hidden.T
    result = middle + bias_down
    dhidden = jnp.zeros((rows, width), wide)
    sums_ref[...] = jnp.zeros(sums_ref.shape, wide)

    def raw_products(block):
        cols = slice(block * width, (block + 1) * width)
        return dot_nn(hidden, up_w[:, cols]), dot_nt(seed_low, down_w[cols, :])

    ahead = raw_products(0)
    for block in range(blocks):
        cols = slice(block * width, (block + 1) * width)
        raw, dact = ahead
        if block + 1 < blocks:
            ahead = raw_products(block + 1)
        act, dpre = [], []
        for at in range(0, rows, CHUNK):
            pre = raw[at : at + CHUNK] + bias_up[block]
            square = pre * pre
            bend = jnp.tanh(pre * (tanh_scale + (tanh_scale * cubic) * square))
            half = 0.5 + 0.5 * bend
            act.append((pre * half).astype(low))
            slope = 0.5 * tanh_scale + (1.5 * tanh_scale * cubic) * square
            slope = half + (pre * slope) * (1.0 - bend * bend)
            dpre.append((dact[at : at + CHUNK] * slope).astype(low))
        act = jnp.concatenate(act, axis=0)
        dpre = jnp.concatenate(dpre, axis=0)
        result = result + dot_nn(act, down_w[cols, :])
        dhidden = dhidden + dot_nt(dpre, up_w[:, cols])
        grad_down = dot_nn(act.T, seed_low)
        grad_up = dot_nn(hidden_t, dpre)
        for piece in range(width // down_part):
            target = block * (width // down_part) + piece
            at = part + blocks * part
            grads_ref[target, at : at + down_part, :] = grad_down[
                piece * down_part : (piece + 1) * down_part, :
            ]
        for target in range(shards):
            at = part + block * part
            grads_ref[target, at : at + part, :] = grad_up[target * part : (target + 1) * part, :]
        sums_ref[4 + block : 5 + block, :] = jnp.sum(dpre.astype(wide), axis=0, keepdims=True)
    out_ref[...] = result
    through, gain_grad, shift_grad = norm_back(dhidden, normed, root, gain)
    dmiddle = seed + through
    middle_ref[...] = dmiddle
    dmiddle_low = dmiddle.astype(low)
    grad_out = dot_nn(attended.T, dmiddle_low)
    for target in range(shards):
        grads_ref[target, :part, :] = grad_out[target * part : (target + 1) * part, :]
    dattend_ref[...] = dot_nt(dmiddle_low, out_w[...]).astype(low)
    sums_ref[0:1, :] = gain_grad
    sums_ref[1:2, :] = shift_grad
    sums_ref[2:3, :] = jnp.sum(dmiddle_low.astype(wide), axis=0, keepdims=True)
    sums_ref[3:4, :] = jnp.sum(seed, axis=0, keepdims=True)
    part_ways(grads_ref, keep_ref, send_ref, shard & 1)


def part_ways(grads_ref, keep_ref, send_ref, side):
    for pair in range(keep_ref.shape[0]):
        keep_ref[pair] = grads_ref[2 * pair + side]
        send_ref[pair] = grads_ref[2 * pair + 1 - side].astype(low)


def back_heads(
    heads, joined_ref, dattend_ref, log_ref, bias_ref, mixed_ref, dquery_t, dkey, dvalue
):
    rows = joined_ref.shape[0]
    width = joined_ref.shape[1] // 3
    first = heads[0] * HEAD
    count = len(heads) * HEAD
    base = first // LANES * LANES
    tile = slice(base, base + LANES)
    inside = slice(first - base, first - base + count)
    keys_t = joined_ref[:, width + base : width + base + LANES].T
    datt_t = dattend_ref[:, tile].T[inside]
    inner = datt_t.astype(wide) * mixed_ref[first : first + count, :]
    units = [(head, start, stop) for head in heads for start, stop in query_blocks(rows)]

    def raw_products(head, start, stop):
        mask = head_mask(head)
        key_tile = joined_ref[:stop, width + base : width + base + LANES] * mask
        value_tile = joined_ref[:stop, 2 * width + base : 2 * width + base + LANES] * mask
        query = joined_ref[start:stop, tile]
        datt = dattend_ref[start:stop, tile]
        return dot_nt(key_tile, query), dot_nt(value_tile, datt), query * mask, datt * mask

    ahead = raw_products(*units[0])
    for index, (head, start, stop) in enumerate(units):
        raw, dprobs, query, datt = ahead
        if index + 1 < len(units):
            ahead = raw_products(*units[index + 1])
        local = head * HEAD - first
        feature = slice(local, local + HEAD)
        weighted = jnp.sum(inner[feature, start:stop], axis=0, keepdims=True)
        logs = log_ref[head : head + 1, start:stop]
        probs, dscores = [], []
        for at in range(0, stop, CHUNK):
            piece = raw[at : at + CHUNK] * (score_scale * log2_e)
            piece = jnp.exp2(piece + bias_ref[at : at + CHUNK, start:stop] - logs)
            probs.append(piece.astype(low))
            piece = piece * (dprobs[at : at + CHUNK] - weighted)
            dscores.append(piece.astype(low))
        probs = jnp.concatenate(probs, axis=0)
        dscores = jnp.concatenate(dscores, axis=0)
        depth = slice(head * HEAD - base, head * HEAD - base + HEAD)
        dquery_t[depth, start:stop] = (
            dot_nn(keys_t[depth, :stop], dscores) * score_scale
        ).astype(low)
        dvalue[:stop, :] += dot_nn(probs, datt)
        dkey[:stop, :] += dot_nn(dscores, query)


def back_first_kernel(heads, *refs):
    dquery_t, dkey, dvalue = refs[5:8]
    dkey[...] = jnp.zeros(dkey.shape, wide)
    dvalue[...] = jnp.zeros(dvalue.shape, wide)
    dquery_t[...] = jnp.zeros(dquery_t.shape, low)
    back_heads(heads, *refs)


def back_last_kernel(shards, head_groups, *refs):
    shared = refs[:5]
    earlier = refs[5:8]
    norm_ref, root_ref, middle_ref, sums_in = refs[8:12]
    pieces = refs[12 : 12 + shards]
    refs = refs[12 + shards :]
    dx_ref, keep_ref, send_ref = refs[:3]
    weight_ref, small_ref, dquery_t, dkey, dvalue, djoined, grads_ref = refs[3:]
    rows, width = norm_ref.shape
    shard = lax.axis_index("shard")
    part = width // shards
    fill_cols(weight_ref, shard, pieces, 0, part, width)
    fill_small(small_ref, shard, pieces, 3 * part)
    gain, shift = small_ref[0, 0:1, :], small_ref[0, 1:2, :]
    for target, value in zip((dquery_t, dkey, dvalue), earlier):
        target[...] = value[...]
    for heads in head_groups:
        back_heads(heads, *shared, dquery_t, dkey, dvalue)
        if (heads[-1] + 1) * HEAD % LANES == 0:
            first = (heads[-1] + 1) * HEAD - LANES
            values = (dquery_t[...].T, dkey[...] * score_scale, dvalue[...])
            for block, value in enumerate(values):
                at = block * width + first
                djoined[:, at : at + LANES] = value.astype(low)
            dkey[...] = jnp.zeros(dkey.shape, wide)
            dvalue[...] = jnp.zeros(dvalue.shape, wide)
    normed, root = norm_ref[...], root_ref[...]
    hidden_t = (normed * gain + shift).astype(low).T
    dhidden = jnp.zeros((rows, width), wide)
    bias_sums = []
    for block in range(3):
        cols = slice(block * width, (block + 1) * width)
        piece = djoined[:, cols]
        dhidden = dhidden + dot_nt(piece, weight_ref[:, cols])
        grad = dot_nn(hidden_t, piece)
        for target in range(shards):
            grads_ref[target, block * part : (block + 1) * part, :] = grad[
                target * part : (target + 1) * part, :
            ]
        if block != 1:
            bias_sums.append(jnp.sum(piece.astype(wide), axis=0, keepdims=True))
    through, gain_grad, shift_grad = norm_back(dhidden, normed, root, gain)
    dx_ref[...] = through
    sums = [gain_grad, shift_grad, sums_in[0:1, :], sums_in[1:2, :]] + bias_sums
    sums += [sums_in[row : row + 1, :] for row in range(2, 8)]
    per_shard = len(sums) // shards
    empty = [jnp.zeros((grads_ref.shape[1] - 3 * part - per_shard, width), wide)]
    for target in range(shards):
        rows_here = sums[target * per_shard : (target + 1) * per_shard]
        grads_ref[target, 3 * part :, :] = jnp.concatenate(rows_here + empty, axis=0)
    part_ways(grads_ref, keep_ref, send_ref, shard & 1)


def halve_kernel(bit, kept, *refs):
    arrived, (keep_ref, send_ref) = refs[:-2], refs[-2:]
    side = (lax.axis_index("dp") >> bit) & 1

    def total(index):
        value = kept[index]
        for piece in arrived:
            value = value + piece[index].astype(wide)
        return value

    for pair in range(keep_ref.shape[0]):
        keep_ref[pair] = total(2 * pair + side)
        send_ref[pair] = total(2 * pair + 1 - side).astype(low)


def piece_spans(total, tail, group):
    spans = [((total - tail) // group, 0, True)]
    if tail:
        spans.append((tail, total - tail, False))
    return spans


def quarter_kernel(tail, kept, arrived, keep_ref, beside_ref, across_ref, corner_ref, sum_ref):
    group = sum_ref.shape[1]
    for half in range(2):
        total = kept[half] + arrived[half].astype(wide)
        for index in range(group):
            row = 0
            for rows, first, moves in piece_spans(total.shape[0], tail, group):
                at = first + index * rows if moves else first
                sum_ref[half, index, row : row + rows, :] = total[at : at + rows, :]
                row += rows
    mine = (lax.axis_index("shard") >> 1) & 1
    side = lax.axis_index("dp") & 1
    for pair in range(group // 2):
        keep_ref[pair] = sum_ref[mine, 2 * pair + side]
        beside_ref[pair] = sum_ref[1 - mine, 2 * pair + side].astype(low)
        across_ref[pair] = sum_ref[mine, 2 * pair + 1 - side].astype(low)
        corner_ref[pair] = sum_ref[1 - mine, 2 * pair + 1 - side].astype(low)


def piece_kernel(*refs):
    parts = [
        mine[...].reshape(mine.shape[-2:]).astype(wide)
        + other[...].reshape(other.shape[-2:]).astype(wide)
        for mine, other in zip(refs[:-1:2], refs[1:-1:2])
    ]
    refs[-1][...] = jnp.concatenate(parts, axis=0).astype(low)


def adam_values(weight, grad, first, second, decay_rate):
    first_next = beta_one * first + (1.0 - beta_one) * grad
    second_next = beta_two * second + (1.0 - beta_two) * grad * grad
    first_fix = 1.0 - beta_one**STEP
    second_fix = 1.0 - beta_two**STEP
    update = (first_next * (1.0 / first_fix)) / (
        jnp.sqrt(second_next * (1.0 / second_fix)) + adam_eps
    )
    return first_next, second_next, weight - learn_rate * (update + decay_rate * weight)


def adam_kernel(group, spans, layout, *refs):
    pieces = refs[:group]
    count = len(layout)
    states = refs[group : group + 3 * count]
    results = refs[group + 3 * count : group + 6 * count]
    buffers = refs[group + 6 * count : group + 9 * count]
    grad_ref, sems = refs[-2:]
    copies = []
    for offset, piece in enumerate(pieces):
        value = piece[...].astype(wide)
        index = (lax.axis_index("dp") & (group - 1)) ^ offset
        for rows, first, row in spans:
            at = pl.multiple_of(first + index * rows, TILE_ROWS)
            grad_ref[pl.ds(at, rows), :] = value[row : row + rows, :]
    width = grad_ref.shape[1]
    for array, (first_row, stride, decay) in enumerate(layout):
        weight, first, second = states[3 * array : 3 * array + 3]
        new = buffers[3 * array : 3 * array + 3]
        vector = len(weight.shape) == 1
        rows = 1 if vector else weight.shape[0]
        for block in range(weight.shape[-1] // width):
            cols = slice(block * width, (block + 1) * width)
            where = cols if vector else (slice(None), cols)
            at = first_row + block * stride
            values = adam_values(
                weight[where].reshape(rows, width),
                grad_ref[at : at + rows, :],
                first[where].reshape(rows, width),
                second[where].reshape(rows, width),
                decay,
            )
            for target, value in zip(new, values):
                target[where] = value.reshape(width) if vector else value
        for index in range(3 * array, 3 * array + 3):
            copies.append(
                pltpu.make_async_copy(buffers[index], results[index], sems.at[index])
            )
            copies[-1].start()
    for copy in copies:
        copy.wait()


def local_call(kernel, outs, operands, scratch=(), flops=0, name=None, fetch=False, sems=0):
    in_space = pltpu.HBM if fetch else pltpu.VMEM
    out_space = pltpu.HBM if sems else pltpu.VMEM
    outs = [jax.ShapeDtypeStruct(*out) for out in outs]
    moved = sum(
        math.prod(item.shape) * item.dtype.itemsize for item in list(operands) + outs
    )
    scratch_shapes = [pltpu.VMEM(*item) for item in scratch]
    if fetch or sems:
        scratch_shapes.append(pltpu.SemaphoreType.DMA((sems or len(operands),)))
    limit = 56 if fetch else 40
    return pl.pallas_call(
        kernel,
        out_shape=outs,
        in_specs=[pl.BlockSpec(memory_space=in_space)] * len(operands),
        out_specs=[pl.BlockSpec(memory_space=out_space)] * len(outs),
        scratch_shapes=scratch_shapes,
        compiler_params=pltpu.CompilerParams(vmem_limit_bytes=limit * 1024 * 1024),
        cost_estimate=pl.CostEstimate(flops=flops, bytes_accessed=moved, transcendentals=0),
        name=name,
    )(*operands)


def exchange(values, axis, mask):
    count = lax.axis_size(axis)
    return lax.ppermute(values, axis, [(index, index ^ mask) for index in range(count)])


def gather_pieces(value, group):
    found = {0: value}
    near = min(group, 4)
    far = near
    while far < group:
        for offset in sorted(found):
            found[offset ^ far] = exchange(found[offset], "dp", far)
        far *= 2
    for offset in range(1, near):
        found[offset] = exchange(value, "dp", offset)
    if near < group:
        found[near], found[1] = lax.optimization_barrier((found[near], found[1]))
    for base in range(near, group, near):
        for offset in range(near - 1, 0, -1):
            found[base ^ offset] = exchange(found[base], "dp", offset)
    return [found[offset] for offset in range(group)]


def corner(values):
    replicas, shards = lax.axis_size("dp"), lax.axis_size("shard")
    pairs = [
        (replica * shards + shard, (replica ^ 1) * shards + (shard ^ 2))
        for replica in range(replicas)
        for shard in range(shards)
    ]
    return lax.ppermute(values, ("dp", "shard"), pairs)


def quarter_call(kept, arrived, tail, group, name):
    _, rows, width = kept.shape
    shape = (group // 2, (rows - tail) // group + tail, width)
    return local_call(
        functools.partial(quarter_kernel, tail),
        [(shape, wide)] + [(shape, low)] * 3,
        [kept, arrived],
        [((2, group) + shape[1:], wide)],
        name=name,
    )


def spread(beside, across, far):
    return [exchange(beside, "shard", 2), exchange(across, "dp", 1), corner(far)]


def spread_far_first(beside, across, far):
    return [corner(far), exchange(beside, "shard", 2), exchange(across, "dp", 1)]


def near_sum(flat):
    half = flat[0].shape[0]
    bit = 1
    while half > 1:
        half //= 2
        shape = (half,) + flat[0].shape[1:]
        keep, send = local_call(
            functools.partial(halve_kernel, bit),
            [(shape, wide), (shape, low)],
            flat,
            name="halve_dp",
        )
        flat = [keep, exchange(send, "dp", 1 << bit)]
        bit += 1
    return flat


def finish_sum(chunks, group):
    replicas = lax.axis_size("dp")
    flat = [item for chunk in chunks for item in near_sum(chunk)]
    width = flat[0].shape[-1]
    rows = sum(item.shape[1] for item in flat[::2])
    (piece,) = local_call(piece_kernel, [((rows, width), low)], flat, name="piece_sum")
    mask = group
    while mask < replicas:
        other = exchange(piece, "dp", mask)
        (piece,) = local_call(piece_kernel, [((rows, width), low)], [piece, other], name="far_sum")
        mask *= 2
    return gather_pieces(piece, group)


def adam_call(pieces, counts, tails, states, layout):
    group = len(pieces)
    width = pieces[0].shape[1]
    spans = []
    first = row = 0
    for total, tail in zip(counts, tails):
        for rows, start, moves in piece_spans(total, tail, group):
            spans.append((rows, first + start, row))
            row += rows
            first += rows * (group - 1) * (not moves)
        first += total
    outs = [(state[0].shape, wide) for state in states for _ in range(3)]
    return local_call(
        functools.partial(adam_kernel, group, spans, layout),
        outs,
        pieces + [item for state in states for item in state],
        outs + [((first, width), wide)],
        name="adam",
        sems=len(outs),
    )


def shards_program(
    tokens,
    cotangent,
    lengths,
    seq_owner,
    qkv_weight,
    out_weight,
    up_weight,
    down_weight,
    gains_biases,
    qkv_first,
    qkv_second,
    out_first,
    out_second,
    up_first,
    up_second,
    down_first,
    down_second,
    small_first,
    small_second,
):
    rows, width = tokens.shape
    shards = lax.axis_size("shard")
    heads = width // HEAD
    part = qkv_weight.shape[0]
    hidden_count = up_weight.shape[1]
    group = min(GROUP, lax.axis_size("dp"))
    lengths = lengths.reshape(1, -1)
    seq_owner = seq_owner.reshape(1, -1)
    first_rows = 3 * part + SMALL_PAD
    second_rows = part + up_weight.size // width + down_weight.shape[0]
    (first_pack,) = local_call(
        pack_first_kernel,
        [((first_rows, width), low)],
        [qkv_weight, gains_biases],
        [(qkv_weight.shape, wide), (gains_biases.shape, wide)],
        name="pack_first",
        fetch=True,
    )
    firsts = {0: first_pack}
    firsts[2] = exchange(first_pack, "shard", 2)
    firsts[1] = exchange(first_pack, "shard", 1)
    first_pack, matrices = lax.optimization_barrier(
        (first_pack, [out_weight, up_weight, down_weight])
    )
    (second_pack,) = local_call(
        pack_second_kernel,
        [((second_rows, width), low)],
        matrices,
        [(item.shape, wide) for item in matrices],
        name="pack_second",
        fetch=True,
    )
    early_tokens, second_pack = lax.optimization_barrier((tokens, second_pack))
    square = (rows, rows)
    bias, normed, root, seed = local_call(
        functools.partial(prepare_kernel, shards),
        [(square, wide), ((rows, width), wide), ((rows, 1), wide), ((rows, width), low)],
        [early_tokens, cotangent, lengths, seq_owner],
        name="prepare",
    )
    seconds = {0: second_pack}
    seconds[2] = exchange(second_pack, "shard", 2)
    seconds[1] = exchange(second_pack, "shard", 1)
    firsts[2], bias, normed, root, seed = lax.optimization_barrier(
        (firsts[2], bias, normed, root, seed)
    )
    firsts[3] = exchange(firsts[2], "shard", 1)
    firsts = [firsts[offset] for offset in range(shards)]
    joined, attended, log_sums, mixed = local_call(
        functools.partial(attend_kernel, shards),
        [
            ((rows, 3 * width), low),
            ((rows, width), low),
            ((heads, rows), wide),
            ((width, rows), wide),
        ],
        [normed, bias] + firsts,
        [((width, 3 * width), low), ((shards, SMALL_PAD, width), wide)],
        flops=heads * rows * rows * 640,
        name="attend",
    )
    attended, seconds[2] = lax.optimization_barrier((attended, seconds[2]))
    seconds[3] = exchange(seconds[2], "shard", 1)
    seconds = [seconds[offset] for offset in range(shards)]
    pair = (shards // 2, second_rows, width)
    result, middle_grad, attended_grad, sums, kept_ffn, send_ffn = local_call(
        functools.partial(feed_kernel, shards),
        [
            ((rows, width), wide),
            ((rows, width), wide),
            ((rows, width), low),
            ((SMALL_PAD, width), wide),
            (pair, wide),
            (pair, low),
        ],
        [tokens, attended, seed] + firsts + seconds,
        [
            ((shards, SMALL_PAD, width), wide),
            ((width, width), low),
            ((width, hidden_count), low),
            ((hidden_count, width), low),
            ((shards, second_rows, width), wide),
        ],
        flops=rows * width * (hidden_count * 12 + width * 6),
        name="feed",
    )
    arrived_ffn = exchange(send_ffn, "shard", 1)
    shared = [joined, attended_grad, log_sums, bias, mixed]
    tile_scratch = [((LANES, rows), low), ((rows, LANES), wide), ((rows, LANES), wide)]
    per_tile = LANES // HEAD
    groups = [list(range(at, at + per_tile)) for at in range(0, heads, per_tile)]
    groups = [groups[0][:3], groups[0][3:]] + groups[1:]
    first_query, first_key, first_value = local_call(
        functools.partial(back_first_kernel, groups[0]),
        tile_scratch,
        shared,
        flops=heads * rows * rows * 256 * 5 // 2,
        name="back_first",
    )
    first_query, arrived_ffn = lax.optimization_barrier((first_query, arrived_ffn))
    tail = TILE_ROWS
    keep_ffn, *sends_ffn = quarter_call(kept_ffn, arrived_ffn, 0, group, "quarter_ffn")
    first_query, sends_ffn = lax.optimization_barrier((first_query, sends_ffn))
    arrived_ffn = spread(*sends_ffn)
    att_rows = 3 * part + tail
    pair = (shards // 2, att_rows, width)
    through, kept_att, send_att = local_call(
        functools.partial(back_last_kernel, shards, groups[1:]),
        [((rows, width), wide), (pair, wide), (pair, low)],
        shared + [first_query, first_key, first_value, normed, root, middle_grad, sums] + firsts,
        [((width, 3 * width), low), ((shards, SMALL_PAD, width), wide)]
        + tile_scratch
        + [((rows, 3 * width), low), ((shards, att_rows, width), wide)],
        flops=heads * rows * rows * 256 * 6,
        name="back_last",
    )
    send_att, arrived_ffn[0], arrived_ffn[1] = lax.optimization_barrier(
        (send_att, arrived_ffn[0], arrived_ffn[1])
    )
    arrived_att = exchange(send_att, "shard", 1)
    keep_att, *sends_att = quarter_call(kept_att, arrived_att, tail, group, "quarter_att")
    arrived_att = spread_far_first(*sends_att)
    tails = (0, tail)
    pieces = finish_sum([[keep_ffn] + arrived_ffn, [keep_att] + arrived_att], group)
    blocks = hidden_count // width
    results = adam_call(
        pieces,
        (second_rows, att_rows),
        tails,
        [
            (qkv_weight, qkv_first, qkv_second),
            (out_weight, out_first, out_second),
            (up_weight, up_first, up_second),
            (down_weight, down_first, down_second),
            (gains_biases, small_first, small_second),
        ],
        [
            (second_rows, part, matrix_decay),
            (0, part, matrix_decay),
            (part, part, matrix_decay),
            (part + blocks * part, 0, matrix_decay),
            (second_rows + 3 * part, 1, 0.0),
        ],
    )
    return (result.astype(low), middle_grad + through, *results)


def solution(mesh):
    rows = P(("dp", "shard"), None)
    matrix = P("shard", None)
    vector = P("shard")
    return jax.shard_map(
        shards_program,
        mesh=mesh,
        in_specs=(rows, rows, P(), P())
        + (matrix,) * 4
        + (vector,)
        + (matrix,) * 8
        + (vector, vector),
        out_specs=(rows, rows) + (matrix,) * 12 + (vector,) * 3,
        check_vma=False,
    )
```

```python
import functools
import math

import jax
import jax.numpy as jnp
from jax import lax
from jax.experimental import pallas as pl
from jax.experimental.pallas import tpu as pltpu
from jax.sharding import PartitionSpec as P

HEAD = 32
STEP = 10
LANES = 128
GROUP = 8
SMALL_PAD = 16
TILE_ROWS = 8
CHUNK = 32

norm_eps = 1e-05
beta_one = 0.9
beta_two = 0.95
learn_rate = 0.1
adam_eps = 1e-08
matrix_decay = 0.1
masked_score = -1e30
low = jnp.bfloat16
wide = jnp.float32
log2_e = math.log2(math.e)
score_scale = 1.0 / math.sqrt(HEAD)
tanh_scale = math.sqrt(2.0 / math.pi)
cubic = 0.044715


def dot_nn(left, right):
    return jnp.dot(left, right, preferred_element_type=wide)


def dot_nt(left, right):
    return lax.dot_general(left, right, (((1,), (1,)), ((), ())), preferred_element_type=wide)


def standardize(values):
    centered = values - jnp.mean(values, axis=-1, keepdims=True)
    root_inv = lax.rsqrt(jnp.mean(centered * centered, axis=-1, keepdims=True) + norm_eps)
    return centered * root_inv, root_inv


def norm_back(upstream, normed, root_inv, gain):
    scaled = upstream * gain
    inner_mean = jnp.mean(scaled, axis=-1, keepdims=True)
    cross_mean = jnp.mean(scaled * normed, axis=-1, keepdims=True)
    through = root_inv * (scaled - inner_mean - normed * cross_mean)
    return (
        through,
        jnp.sum(upstream * normed, axis=0, keepdims=True),
        jnp.sum(upstream, axis=0, keepdims=True),
    )


def iota(shape, dim):
    return lax.broadcasted_iota(jnp.int32, shape, dim)


def own_row(lengths, owners, device):
    return jnp.where(owners == device, lengths, 0)


def ends_both(own):
    count = own.shape[1]
    shape = (count, count)
    rows, cols = iota(shape, 0), iota(shape, 1)
    spread = jnp.broadcast_to(own, shape)
    ends_col = jnp.sum(jnp.where(cols <= rows, spread, 0), axis=1, keepdims=True)
    own_col = jnp.sum(jnp.where(cols == rows, spread, 0), axis=1, keepdims=True)
    ends_row = jnp.sum(
        jnp.where(rows <= cols, jnp.broadcast_to(own_col, shape), 0), axis=0, keepdims=True
    )
    return ends_col, ends_row


def fill_mask(bias_ref, own, rows):
    ends_col, ends_row = ends_both(own)
    count = own.shape[1]
    seg_row = jnp.sum(
        (ends_col <= iota((count, rows), 1)).astype(jnp.int32), axis=0, keepdims=True
    )
    seg_col = jnp.sum(
        (ends_row <= iota((rows, count), 0)).astype(jnp.int32), axis=1, keepdims=True
    )
    allowed = (seg_row == seg_col) & (iota((rows, rows), 0) <= iota((rows, rows), 1))
    bias_ref[...] = jnp.where(allowed, 0.0, masked_score)


def fill_small(small_ref, shard, pieces, first_row):
    for offset, piece in enumerate(pieces):
        small_ref[shard ^ offset] = piece[first_row:, :].astype(wide)


def fill_cols(full_ref, shard, pieces, first_row, rows, width):
    blocks = full_ref.shape[1] // width
    for offset, piece in enumerate(pieces):
        at = pl.multiple_of((shard ^ offset) * rows, rows)
        for block in range(blocks):
            start = first_row + block * rows
            full_ref[pl.ds(at, rows), block * width : (block + 1) * width] = piece[
                start : start + rows, :
            ]


def head_mask(head):
    lane = iota((1, LANES), 1)
    first = head * HEAD % LANES
    return ((lane >= first) & (lane < first + HEAD)).astype(wide).astype(low)


def head_tile(head):
    first = head * HEAD // LANES * LANES
    return slice(first, first + LANES)


def query_blocks(rows):
    size = min(256, rows)
    return [(at, at + size) for at in range(0, rows, size)]


def put_blocks(target, row, source, width):
    rows = source.shape[0]
    for block in range(source.shape[1] // width):
        cols = slice(block * width, (block + 1) * width)
        target[row : row + rows, :] = source[:, cols].astype(low)
        row += rows
    return row


def fetch_all(sources, buffers, sems):
    copies = [
        pltpu.make_async_copy(source, buffer, sems.at[index])
        for index, (source, buffer) in enumerate(zip(sources, buffers))
    ]
    for copy in copies:
        copy.start()
    return copies


def pack_first_kernel(qkv_ref, small_ref, first_ref, qkv_buf, small_buf, sems):
    width = first_ref.shape[1]
    small_copy, qkv_copy = fetch_all((small_ref, qkv_ref), (small_buf, qkv_buf), sems)
    small_copy.wait()
    parts = [
        small_buf[block * width : (block + 1) * width].reshape(1, width)
        for block in range(small_buf.shape[0] // width)
    ]
    parts.append(jnp.zeros((SMALL_PAD - len(parts), width), wide))
    first_ref[first_ref.shape[0] - SMALL_PAD :, :] = jnp.concatenate(parts, axis=0).astype(low)
    qkv_copy.wait()
    put_blocks(first_ref, 0, qkv_buf, width)


def pack_second_kernel(out_ref, up_ref, down_ref, second_ref, out_buf, up_buf, down_buf, sems):
    width = second_ref.shape[1]
    buffers = (out_buf, up_buf, down_buf)
    copies = fetch_all((out_ref, up_ref, down_ref), buffers, sems)
    row = 0
    for copy, buffer in zip(copies, buffers):
        copy.wait()
        row = put_blocks(second_ref, row, buffer, width)


def prepare_kernel(shards, x_ref, seed_ref, len_ref, owner_ref, bias_ref, norm_ref, root_ref, low_ref):
    rows = x_ref.shape[0]
    device = lax.axis_index("dp") * shards + lax.axis_index("shard")
    own = own_row(len_ref[...], owner_ref[...], device)
    fill_mask(bias_ref, own, rows)
    normed, root = standardize(x_ref[...].astype(wide))
    norm_ref[...] = normed
    root_ref[...] = root
    live = jnp.sum(own, axis=1, keepdims=True)
    live_rows = (iota((rows, 1), 0) < live).astype(wide)
    low_ref[...] = (seed_ref[...].astype(wide) * live_rows).astype(low)


def attend_kernel(shards, *refs):
    norm_ref, bias_ref = refs[:2]
    pieces = refs[2 : 2 + shards]
    joined_ref, out_ref, log_ref, att_ref, weight_ref, small_ref = refs[2 + shards :]
    rows, width = norm_ref.shape
    shard = lax.axis_index("shard")
    part = width // shards
    fill_cols(weight_ref, shard, pieces, 0, part, width)
    fill_small(small_ref, shard, pieces, 3 * part)
    gain, shift = small_ref[0, 0:1, :], small_ref[0, 1:2, :]
    bias_query, bias_value = small_ref[1, 1:2, :], small_ref[1, 2:3, :]
    hidden = (norm_ref[...] * gain + shift).astype(low)
    for block, bias in enumerate((bias_query, None, bias_value)):
        cols = slice(block * width, (block + 1) * width)
        value = dot_nn(hidden, weight_ref[:, cols])
        if bias is not None:
            value = value + bias
        joined_ref[:, cols] = value.astype(low)
    values_t = joined_ref[:, 2 * width :].T
    units = [
        (head, start, stop) for head in range(width // HEAD) for start, stop in query_blocks(rows)
    ]

    def raw_scores(head, start, stop):
        tile = head_tile(head)
        key_tile = joined_ref[:stop, width + tile.start : width + tile.stop] * head_mask(head)
        return dot_nt(key_tile, joined_ref[start:stop, tile])

    ahead = raw_scores(*units[0])
    for index, (head, start, stop) in enumerate(units):
        raw = ahead
        if index + 1 < len(units):
            ahead = raw_scores(*units[index + 1])
        feature = slice(head * HEAD, (head + 1) * HEAD)
        scores = []
        top = None
        for at in range(0, stop, CHUNK):
            piece = raw[at : at + CHUNK] * (score_scale * log2_e)
            piece = piece + bias_ref[at : at + CHUNK, start:stop]
            scores.append(piece)
            top = piece if top is None else jnp.maximum(top, piece)
        top = jnp.max(top, axis=0, keepdims=True)
        exponents = []
        total = None
        for piece in scores:
            piece = jnp.exp2(piece - top)
            total = piece if total is None else total + piece
            exponents.append(piece.astype(low))
        total = jnp.sum(total, axis=0, keepdims=True)
        mixed = dot_nn(values_t[feature, :stop], jnp.concatenate(exponents, axis=0))
        att_ref[feature, start:stop] = mixed * (1.0 / total)
        log_ref[head : head + 1, start:stop] = top + jnp.log2(total)
    out_ref[...] = att_ref[...].astype(low).T


def feed_kernel(shards, *refs):
    x_ref, att_ref, seed_ref = refs[:3]
    firsts = refs[3 : 3 + shards]
    pieces = refs[3 + shards : 3 + 2 * shards]
    refs = refs[3 + 2 * shards :]
    out_ref, middle_ref, dattend_ref, sums_ref, keep_ref, send_ref = refs[:6]
    small_ref, out_w, up_w, down_w, grads_ref = refs[6:]
    rows, width = x_ref.shape
    hidden_count = up_w.shape[1]
    shard = lax.axis_index("shard")
    part = width // shards
    blocks = hidden_count // width
    down_part = hidden_count // shards
    fill_small(small_ref, shard, firsts, 3 * part)
    fill_cols(out_w, shard, pieces, 0, part, width)
    fill_cols(up_w, shard, pieces, part, part, width)
    fill_cols(down_w, shard, pieces, part + blocks * part, down_part, width)
    gain, shift = small_ref[0, 2:3, :], small_ref[1, 0:1, :]
    bias_out, bias_down = small_ref[2, 0:1, :], small_ref[2, 1:2, :]
    bias_up = [small_ref[2, 2:3, :]] + [small_ref[3, row : row + 1, :] for row in range(3)]
    seed_low = seed_ref[...]
    seed = seed_low.astype(wide)
    attended = att_ref[...]
    middle = x_ref[...].astype(wide) + (dot_nn(attended, out_w[...]) + bias_out)
    normed, root = standardize(middle)
    hidden = (normed * gain + shift).astype(low)
    hidden_t = hidden.T
    result = middle + bias_down
    dhidden = jnp.zeros((rows, width), wide)
    sums_ref[...] = jnp.zeros(sums_ref.shape, wide)

    def raw_products(block):
        cols = slice(block * width, (block + 1) * width)
        return dot_nn(hidden, up_w[:, cols]), dot_nt(seed_low, down_w[cols, :])

    ahead = raw_products(0)
    for block in range(blocks):
        cols = slice(block * width, (block + 1) * width)
        raw, dact = ahead
        if block + 1 < blocks:
            ahead = raw_products(block + 1)
        act, dpre = [], []
        for at in range(0, rows, CHUNK):
            pre = raw[at : at + CHUNK] + bias_up[block]
            square = pre * pre
            bend = jnp.tanh(pre * (tanh_scale + (tanh_scale * cubic) * square))
            half = 0.5 + 0.5 * bend
            act.append((pre * half).astype(low))
            slope = 0.5 * tanh_scale + (1.5 * tanh_scale * cubic) * square
            slope = half + (pre * slope) * (1.0 - bend * bend)
            dpre.append((dact[at : at + CHUNK] * slope).astype(low))
        act = jnp.concatenate(act, axis=0)
        dpre = jnp.concatenate(dpre, axis=0)
        result = result + dot_nn(act, down_w[cols, :])
        dhidden = dhidden + dot_nt(dpre, up_w[:, cols])
        grad_down = dot_nn(act.T, seed_low)
        grad_up = dot_nn(hidden_t, dpre)
        for piece in range(width // down_part):
            target = block * (width // down_part) + piece
            at = part + blocks * part
            grads_ref[target, at : at + down_part, :] = grad_down[
                piece * down_part : (piece + 1) * down_part, :
            ]
        for target in range(shards):
            at = part + block * part
            grads_ref[target, at : at + part, :] = grad_up[target * part : (target + 1) * part, :]
        sums_ref[4 + block : 5 + block, :] = jnp.sum(dpre.astype(wide), axis=0, keepdims=True)
    out_ref[...] = result
    through, gain_grad, shift_grad = norm_back(dhidden, normed, root, gain)
    dmiddle = seed + through
    middle_ref[...] = dmiddle
    dmiddle_low = dmiddle.astype(low)
    grad_out = dot_nn(attended.T, dmiddle_low)
    for target in range(shards):
        grads_ref[target, :part, :] = grad_out[target * part : (target + 1) * part, :]
    dattend_ref[...] = dot_nt(dmiddle_low, out_w[...]).astype(low)
    sums_ref[0:1, :] = gain_grad
    sums_ref[1:2, :] = shift_grad
    sums_ref[2:3, :] = jnp.sum(dmiddle_low.astype(wide), axis=0, keepdims=True)
    sums_ref[3:4, :] = jnp.sum(seed, axis=0, keepdims=True)
    part_ways(grads_ref, keep_ref, send_ref, shard & 1)


def part_ways(grads_ref, keep_ref, send_ref, side):
    for pair in range(keep_ref.shape[0]):
        keep_ref[pair] = grads_ref[2 * pair + side]
        send_ref[pair] = grads_ref[2 * pair + 1 - side].astype(low)


def back_heads(
    heads, joined_ref, dattend_ref, log_ref, bias_ref, mixed_ref, dquery_t, dkey, dvalue
):
    rows = joined_ref.shape[0]
    width = joined_ref.shape[1] // 3
    first = heads[0] * HEAD
    count = len(heads) * HEAD
    base = first // LANES * LANES
    tile = slice(base, base + LANES)
    inside = slice(first - base, first - base + count)
    keys_t = joined_ref[:, width + base : width + base + LANES].T
    datt_t = dattend_ref[:, tile].T[inside]
    inner = datt_t.astype(wide) * mixed_ref[first : first + count, :]
    units = [(head, start, stop) for head in heads for start, stop in query_blocks(rows)]

    def raw_products(head, start, stop):
        mask = head_mask(head)
        key_tile = joined_ref[:stop, width + base : width + base + LANES] * mask
        value_tile = joined_ref[:stop, 2 * width + base : 2 * width + base + LANES] * mask
        query = joined_ref[start:stop, tile]
        datt = dattend_ref[start:stop, tile]
        return dot_nt(key_tile, query), dot_nt(value_tile, datt), query * mask, datt * mask

    ahead = raw_products(*units[0])
    for index, (head, start, stop) in enumerate(units):
        raw, dprobs, query, datt = ahead
        if index + 1 < len(units):
            ahead = raw_products(*units[index + 1])
        local = head * HEAD - first
        feature = slice(local, local + HEAD)
        weighted = jnp.sum(inner[feature, start:stop], axis=0, keepdims=True)
        logs = log_ref[head : head + 1, start:stop]
        probs, dscores = [], []
        for at in range(0, stop, CHUNK):
            piece = raw[at : at + CHUNK] * (score_scale * log2_e)
            piece = jnp.exp2(piece + bias_ref[at : at + CHUNK, start:stop] - logs)
            probs.append(piece.astype(low))
            piece = piece * (dprobs[at : at + CHUNK] - weighted)
            dscores.append(piece.astype(low))
        probs = jnp.concatenate(probs, axis=0)
        dscores = jnp.concatenate(dscores, axis=0)
        depth = slice(head * HEAD - base, head * HEAD - base + HEAD)
        dquery_t[depth, start:stop] = (
            dot_nn(keys_t[depth, :stop], dscores) * score_scale
        ).astype(low)
        dvalue[:stop, :] += dot_nn(probs, datt)
        dkey[:stop, :] += dot_nn(dscores, query)


def back_first_kernel(heads, *refs):
    dquery_t, dkey, dvalue = refs[5:8]
    dkey[...] = jnp.zeros(dkey.shape, wide)
    dvalue[...] = jnp.zeros(dvalue.shape, wide)
    dquery_t[...] = jnp.zeros(dquery_t.shape, low)
    back_heads(heads, *refs)


def back_last_kernel(shards, head_groups, *refs):
    shared = refs[:5]
    earlier = refs[5:8]
    norm_ref, root_ref, middle_ref, sums_in = refs[8:12]
    pieces = refs[12 : 12 + shards]
    refs = refs[12 + shards :]
    dx_ref, keep_ref, send_ref = refs[:3]
    weight_ref, small_ref, dquery_t, dkey, dvalue, djoined, grads_ref = refs[3:]
    rows, width = norm_ref.shape
    shard = lax.axis_index("shard")
    part = width // shards
    fill_cols(weight_ref, shard, pieces, 0, part, width)
    fill_small(small_ref, shard, pieces, 3 * part)
    gain, shift = small_ref[0, 0:1, :], small_ref[0, 1:2, :]
    for target, value in zip((dquery_t, dkey, dvalue), earlier):
        target[...] = value[...]
    for heads in head_groups:
        back_heads(heads, *shared, dquery_t, dkey, dvalue)
        if (heads[-1] + 1) * HEAD % LANES == 0:
            first = (heads[-1] + 1) * HEAD - LANES
            values = (dquery_t[...].T, dkey[...] * score_scale, dvalue[...])
            for block, value in enumerate(values):
                at = block * width + first
                djoined[:, at : at + LANES] = value.astype(low)
            dkey[...] = jnp.zeros(dkey.shape, wide)
            dvalue[...] = jnp.zeros(dvalue.shape, wide)
    normed, root = norm_ref[...], root_ref[...]
    hidden_t = (normed * gain + shift).astype(low).T
    dhidden = jnp.zeros((rows, width), wide)
    bias_sums = []
    for block in range(3):
        cols = slice(block * width, (block + 1) * width)
        piece = djoined[:, cols]
        dhidden = dhidden + dot_nt(piece, weight_ref[:, cols])
        grad = dot_nn(hidden_t, piece)
        for target in range(shards):
            grads_ref[target, block * part : (block + 1) * part, :] = grad[
                target * part : (target + 1) * part, :
            ]
        if block != 1:
            bias_sums.append(jnp.sum(piece.astype(wide), axis=0, keepdims=True))
    through, gain_grad, shift_grad = norm_back(dhidden, normed, root, gain)
    dx_ref[...] = through
    sums = [gain_grad, shift_grad, sums_in[0:1, :], sums_in[1:2, :]] + bias_sums
    sums += [sums_in[row : row + 1, :] for row in range(2, 8)]
    per_shard = len(sums) // shards
    empty = [jnp.zeros((grads_ref.shape[1] - 3 * part - per_shard, width), wide)]
    for target in range(shards):
        rows_here = sums[target * per_shard : (target + 1) * per_shard]
        grads_ref[target, 3 * part :, :] = jnp.concatenate(rows_here + empty, axis=0)
    part_ways(grads_ref, keep_ref, send_ref, shard & 1)


def halve_kernel(bit, kept, *refs):
    arrived, (keep_ref, send_ref) = refs[:-2], refs[-2:]
    side = (lax.axis_index("dp") >> bit) & 1

    def total(index):
        value = kept[index]
        for piece in arrived:
            value = value + piece[index].astype(wide)
        return value

    for pair in range(keep_ref.shape[0]):
        keep_ref[pair] = total(2 * pair + side)
        send_ref[pair] = total(2 * pair + 1 - side).astype(low)


def piece_spans(total, tail, group):
    spans = [((total - tail) // group, 0, True)]
    if tail:
        spans.append((tail, total - tail, False))
    return spans


def quarter_kernel(tail, kept, arrived, keep_ref, beside_ref, across_ref, corner_ref, sum_ref):
    group = sum_ref.shape[1]
    for half in range(2):
        total = kept[half] + arrived[half].astype(wide)
        for index in range(group):
            row = 0
            for rows, first, moves in piece_spans(total.shape[0], tail, group):
                at = first + index * rows if moves else first
                sum_ref[half, index, row : row + rows, :] = total[at : at + rows, :]
                row += rows
    mine = (lax.axis_index("shard") >> 1) & 1
    side = lax.axis_index("dp") & 1
    for pair in range(group // 2):
        keep_ref[pair] = sum_ref[mine, 2 * pair + side]
        beside_ref[pair] = sum_ref[1 - mine, 2 * pair + side].astype(low)
        across_ref[pair] = sum_ref[mine, 2 * pair + 1 - side].astype(low)
        corner_ref[pair] = sum_ref[1 - mine, 2 * pair + 1 - side].astype(low)


def piece_kernel(*refs):
    parts = [
        mine[...].reshape(mine.shape[-2:]).astype(wide)
        + other[...].reshape(other.shape[-2:]).astype(wide)
        for mine, other in zip(refs[:-1:2], refs[1:-1:2])
    ]
    refs[-1][...] = jnp.concatenate(parts, axis=0).astype(low)


def adam_values(weight, grad, first, second, decay_rate):
    first_next = beta_one * first + (1.0 - beta_one) * grad
    second_next = beta_two * second + (1.0 - beta_two) * grad * grad
    first_fix = 1.0 - beta_one**STEP
    second_fix = 1.0 - beta_two**STEP
    update = (first_next * (1.0 / first_fix)) / (
        jnp.sqrt(second_next * (1.0 / second_fix)) + adam_eps
    )
    return first_next, second_next, weight - learn_rate * (update + decay_rate * weight)


def adam_kernel(group, spans, layout, *refs):
    pieces = refs[:group]
    count = len(layout)
    states = refs[group : group + 3 * count]
    results = refs[group + 3 * count : group + 6 * count]
    buffers = refs[group + 6 * count : group + 9 * count]
    grad_ref, sems = refs[-2:]
    copies = []
    for offset, piece in enumerate(pieces):
        value = piece[...].astype(wide)
        index = (lax.axis_index("dp") & (group - 1)) ^ offset
        for rows, first, row in spans:
            at = pl.multiple_of(first + index * rows, TILE_ROWS)
            grad_ref[pl.ds(at, rows), :] = value[row : row + rows, :]
    width = grad_ref.shape[1]
    for array, (first_row, stride, decay) in enumerate(layout):
        weight, first, second = states[3 * array : 3 * array + 3]
        new = buffers[3 * array : 3 * array + 3]
        vector = len(weight.shape) == 1
        rows = 1 if vector else weight.shape[0]
        for block in range(weight.shape[-1] // width):
            cols = slice(block * width, (block + 1) * width)
            where = cols if vector else (slice(None), cols)
            at = first_row + block * stride
            values = adam_values(
                weight[where].reshape(rows, width),
                grad_ref[at : at + rows, :],
                first[where].reshape(rows, width),
                second[where].reshape(rows, width),
                decay,
            )
            for target, value in zip(new, values):
                target[where] = value.reshape(width) if vector else value
        for index in range(3 * array, 3 * array + 3):
            copies.append(
                pltpu.make_async_copy(buffers[index], results[index], sems.at[index])
            )
            copies[-1].start()
    for copy in copies:
        copy.wait()


def local_call(kernel, outs, operands, scratch=(), flops=0, name=None, fetch=False, sems=0):
    in_space = pltpu.HBM if fetch else pltpu.VMEM
    out_space = pltpu.HBM if sems else pltpu.VMEM
    outs = [jax.ShapeDtypeStruct(*out) for out in outs]
    moved = sum(
        math.prod(item.shape) * item.dtype.itemsize for item in list(operands) + outs
    )
    scratch_shapes = [pltpu.VMEM(*item) for item in scratch]
    if fetch or sems:
        scratch_shapes.append(pltpu.SemaphoreType.DMA((sems or len(operands),)))
    limit = 56 if fetch else 40
    return pl.pallas_call(
        kernel,
        out_shape=outs,
        in_specs=[pl.BlockSpec(memory_space=in_space)] * len(operands),
        out_specs=[pl.BlockSpec(memory_space=out_space)] * len(outs),
        scratch_shapes=scratch_shapes,
        compiler_params=pltpu.CompilerParams(vmem_limit_bytes=limit * 1024 * 1024),
        cost_estimate=pl.CostEstimate(flops=flops, bytes_accessed=moved, transcendentals=0),
        name=name,
    )(*operands)


def exchange(values, axis, mask):
    count = lax.axis_size(axis)
    return lax.ppermute(values, axis, [(index, index ^ mask) for index in range(count)])


def gather_pieces(value, group):
    found = {0: value}
    near = min(group, 4)
    far = near
    while far < group:
        for offset in sorted(found):
            found[offset ^ far] = exchange(found[offset], "dp", far)
        far *= 2
    for offset in range(1, near):
        found[offset] = exchange(value, "dp", offset)
    if near < group:
        found[near], found[1] = lax.optimization_barrier((found[near], found[1]))
    for base in range(near, group, near):
        for offset in range(near - 1, 0, -1):
            found[base ^ offset] = exchange(found[base], "dp", offset)
    return [found[offset] for offset in range(group)]


def corner(values):
    replicas, shards = lax.axis_size("dp"), lax.axis_size("shard")
    pairs = [
        (replica * shards + shard, (replica ^ 1) * shards + (shard ^ 2))
        for replica in range(replicas)
        for shard in range(shards)
    ]
    return lax.ppermute(values, ("dp", "shard"), pairs)


def quarter_call(kept, arrived, tail, group, name):
    _, rows, width = kept.shape
    shape = (group // 2, (rows - tail) // group + tail, width)
    return local_call(
        functools.partial(quarter_kernel, tail),
        [(shape, wide)] + [(shape, low)] * 3,
        [kept, arrived],
        [((2, group) + shape[1:], wide)],
        name=name,
    )


def spread(beside, across, far):
    return [exchange(beside, "shard", 2), exchange(across, "dp", 1), corner(far)]


def near_sum(flat):
    half = flat[0].shape[0]
    bit = 1
    while half > 1:
        half //= 2
        shape = (half,) + flat[0].shape[1:]
        keep, send = local_call(
            functools.partial(halve_kernel, bit),
            [(shape, wide), (shape, low)],
            flat,
            name="halve_dp",
        )
        flat = [keep, exchange(send, "dp", 1 << bit)]
        bit += 1
    return flat


def finish_sum(chunks, group):
    replicas = lax.axis_size("dp")
    flat = [item for chunk in chunks for item in near_sum(chunk)]
    width = flat[0].shape[-1]
    rows = sum(item.shape[1] for item in flat[::2])
    (piece,) = local_call(piece_kernel, [((rows, width), low)], flat, name="piece_sum")
    mask = group
    while mask < replicas:
        other = exchange(piece, "dp", mask)
        (piece,) = local_call(piece_kernel, [((rows, width), low)], [piece, other], name="far_sum")
        mask *= 2
    return gather_pieces(piece, group)


def adam_call(pieces, counts, tails, states, layout):
    group = len(pieces)
    width = pieces[0].shape[1]
    spans = []
    first = row = 0
    for total, tail in zip(counts, tails):
        for rows, start, moves in piece_spans(total, tail, group):
            spans.append((rows, first + start, row))
            row += rows
            first += rows * (group - 1) * (not moves)
        first += total
    outs = [(state[0].shape, wide) for state in states for _ in range(3)]
    return local_call(
        functools.partial(adam_kernel, group, spans, layout),
        outs,
        pieces + [item for state in states for item in state],
        outs + [((first, width), wide)],
        name="adam",
        sems=len(outs),
    )


def shards_program(
    tokens,
    cotangent,
    lengths,
    seq_owner,
    qkv_weight,
    out_weight,
    up_weight,
    down_weight,
    gains_biases,
    qkv_first,
    qkv_second,
    out_first,
    out_second,
    up_first,
    up_second,
    down_first,
    down_second,
    small_first,
    small_second,
):
    rows, width = tokens.shape
    shards = lax.axis_size("shard")
    heads = width // HEAD
    part = qkv_weight.shape[0]
    hidden_count = up_weight.shape[1]
    group = min(GROUP, lax.axis_size("dp"))
    lengths = lengths.reshape(1, -1)
    seq_owner = seq_owner.reshape(1, -1)
    first_rows = 3 * part + SMALL_PAD
    second_rows = part + up_weight.size // width + down_weight.shape[0]
    (first_pack,) = local_call(
        pack_first_kernel,
        [((first_rows, width), low)],
        [qkv_weight, gains_biases],
        [(qkv_weight.shape, wide), (gains_biases.shape, wide)],
        name="pack_first",
        fetch=True,
    )
    firsts = {0: first_pack}
    firsts[2] = exchange(first_pack, "shard", 2)
    firsts[1] = exchange(first_pack, "shard", 1)
    first_pack, matrices = lax.optimization_barrier(
        (first_pack, [out_weight, up_weight, down_weight])
    )
    (second_pack,) = local_call(
        pack_second_kernel,
        [((second_rows, width), low)],
        matrices,
        [(item.shape, wide) for item in matrices],
        name="pack_second",
        fetch=True,
    )
    early_tokens, second_pack = lax.optimization_barrier((tokens, second_pack))
    square = (rows, rows)
    bias, normed, root, seed = local_call(
        functools.partial(prepare_kernel, shards),
        [(square, wide), ((rows, width), wide), ((rows, 1), wide), ((rows, width), low)],
        [early_tokens, cotangent, lengths, seq_owner],
        name="prepare",
    )
    seconds = {0: second_pack}
    seconds[2] = exchange(second_pack, "shard", 2)
    seconds[1] = exchange(second_pack, "shard", 1)
    firsts[2], bias, normed, root, seed = lax.optimization_barrier(
        (firsts[2], bias, normed, root, seed)
    )
    firsts[3] = exchange(firsts[2], "shard", 1)
    firsts = [firsts[offset] for offset in range(shards)]
    joined, attended, log_sums, mixed = local_call(
        functools.partial(attend_kernel, shards),
        [
            ((rows, 3 * width), low),
            ((rows, width), low),
            ((heads, rows), wide),
            ((width, rows), wide),
        ],
        [normed, bias] + firsts,
        [((width, 3 * width), low), ((shards, SMALL_PAD, width), wide)],
        flops=heads * rows * rows * 640,
        name="attend",
    )
    attended, seconds[2] = lax.optimization_barrier((attended, seconds[2]))
    seconds[3] = exchange(seconds[2], "shard", 1)
    seconds = [seconds[offset] for offset in range(shards)]
    pair = (shards // 2, second_rows, width)
    result, middle_grad, attended_grad, sums, kept_ffn, send_ffn = local_call(
        functools.partial(feed_kernel, shards),
        [
            ((rows, width), wide),
            ((rows, width), wide),
            ((rows, width), low),
            ((SMALL_PAD, width), wide),
            (pair, wide),
            (pair, low),
        ],
        [tokens, attended, seed] + firsts + seconds,
        [
            ((shards, SMALL_PAD, width), wide),
            ((width, width), low),
            ((width, hidden_count), low),
            ((hidden_count, width), low),
            ((shards, second_rows, width), wide),
        ],
        flops=rows * width * (hidden_count * 12 + width * 6),
        name="feed",
    )
    arrived_ffn = exchange(send_ffn, "shard", 1)
    shared = [joined, attended_grad, log_sums, bias, mixed]
    tile_scratch = [((LANES, rows), low), ((rows, LANES), wide), ((rows, LANES), wide)]
    per_tile = LANES // HEAD
    groups = [list(range(at, at + per_tile)) for at in range(0, heads, per_tile)]
    groups = [groups[0][:3], groups[0][3:]] + groups[1:]
    first_query, first_key, first_value = local_call(
        functools.partial(back_first_kernel, groups[0]),
        tile_scratch,
        shared,
        flops=heads * rows * rows * 256 * 5 // 2,
        name="back_first",
    )
    first_query, arrived_ffn = lax.optimization_barrier((first_query, arrived_ffn))
    tail = TILE_ROWS
    keep_ffn, *sends_ffn = quarter_call(kept_ffn, arrived_ffn, 0, group, "quarter_ffn")
    first_query, sends_ffn = lax.optimization_barrier((first_query, sends_ffn))
    arrived_ffn = spread(*sends_ffn)
    att_rows = 3 * part + tail
    pair = (shards // 2, att_rows, width)
    through, kept_att, send_att = local_call(
        functools.partial(back_last_kernel, shards, groups[1:]),
        [((rows, width), wide), (pair, wide), (pair, low)],
        shared + [first_query, first_key, first_value, normed, root, middle_grad, sums] + firsts,
        [((width, 3 * width), low), ((shards, SMALL_PAD, width), wide)]
        + tile_scratch
        + [((rows, 3 * width), low), ((shards, att_rows, width), wide)],
        flops=heads * rows * rows * 256 * 6,
        name="back_last",
    )
    send_att, arrived_ffn[0], arrived_ffn[1] = lax.optimization_barrier(
        (send_att, arrived_ffn[0], arrived_ffn[1])
    )
    arrived_att = exchange(send_att, "shard", 1)
    keep_att, *sends_att = quarter_call(kept_att, arrived_att, tail, group, "quarter_att")
    arrived_att = spread(*sends_att)
    tails = (0, tail)
    pieces = finish_sum([[keep_ffn] + arrived_ffn, [keep_att] + arrived_att], group)
    blocks = hidden_count // width
    results = adam_call(
        pieces,
        (second_rows, att_rows),
        tails,
        [
            (qkv_weight, qkv_first, qkv_second),
            (out_weight, out_first, out_second),
            (up_weight, up_first, up_second),
            (down_weight, down_first, down_second),
            (gains_biases, small_first, small_second),
        ],
        [
            (second_rows, part, matrix_decay),
            (0, part, matrix_decay),
            (part, part, matrix_decay),
            (part + blocks * part, 0, matrix_decay),
            (second_rows + 3 * part, 1, 0.0),
        ],
    )
    return (result.astype(low), middle_grad + through, *results)


def solution(mesh):
    rows = P(("dp", "shard"), None)
    matrix = P("shard", None)
    vector = P("shard")
    return jax.shard_map(
        shards_program,
        mesh=mesh,
        in_specs=(rows, rows, P(), P())
        + (matrix,) * 4
        + (vector,)
        + (matrix,) * 8
        + (vector, vector),
        out_specs=(rows, rows) + (matrix,) * 12 + (vector,) * 3,
        check_vma=False,
    )
```
